32 devices in a mesh: expert: 8 (over z, x), tensor: 4 (over y, core).
Axes of the slice: x: 2, y: 2, z: 4, core: 2. Of those that a mesh axis runs over, the one named last changes fastest.
Arguments:
- tokens: bfloat16 [8192, 768], P('expert'), may hold values from -6 to 6
- gain_attn: float32 [768], replicated, may hold values from 0.5 to 1.5
- w_qkv: bfloat16 [3, 768, 768], P(None, None, 'tensor'), may hold values from -0.21875 to 0.21875
- w_proj: bfloat16 [768, 768], P('tensor'), may hold values from -3.5 to 3.5
- rel_bias: float32 [12, 32], P('tensor'), may hold values from -1 to 1
- gain_ffn: float32 [768], replicated, may hold values from 0.5 to 1.5
- w_router: bfloat16 [768, 8], replicated, may hold values from -0.109375 to 0.109375
- w_in: bfloat16 [8, 768, 3072], P('expert', None, 'tensor'), may hold values from -0.21875 to 0.21875
- w_out: bfloat16 [8, 3072, 768], P('expert', 'tensor'), may hold values from -1.5 to 1.5
- routes: int32 [8192, 1], P('expert'), may hold values from 0 to 7; in each aligned block of 1024 rows (0 to 1023, 1024 to 2047, ...) at most 192 rows name the same one
- segment_ids: int32 [8, 1024], P('expert'), may hold values from 0 to 3, never falling along the last dimension, each value on 1 to 512 neighbouring positions
- cotangent: bfloat16 [8192, 768], P('expert'), may hold values from -6 to 6
Outputs:
- output: bfloat16 [8192, 768], P('expert')
- grad_input: float32 [8192, 768], P('expert')
- grad_gain_attn: float32 [768], replicated
- grad_qkv: float32 [3, 768, 768], P(None, None, 'tensor')
- grad_proj: float32 [768, 768], P('tensor')
- grad_rel: float32 [12, 32], P('tensor')
- grad_gain_ffn: float32 [768], replicated
- grad_router: float32 [768, 8], replicated
- grad_w_in: float32 [8, 768, 3072], P('expert', None, 'tensor')
- grad_w_out: float32 [8, 3072, 768], P('expert', 'tensor')
The draws below stay inside these ranges and needn't reach their ends.
Inputs may be any that keep to these rules, and one draw needn't show every extreme that they name: `routes`: among the 1024 tokens of one sequence no expert is named more than 192 times, a bound that some block reaches. `segment_ids`: within each sequence the document numbers never fall, each document has at most 512 positions.
All inputs are finite; a program needn't handle non-finite values.
Results may differ from the reference program's by a relative error of at most 0.017.
Values may be sent and summed in bfloat16 or wider, within the bound.
No kernel may reach another device: no remote copies, remote signals or barrier semaphores. Data moves between devices by JAX's collectives and lax.ppermute only.
A program may use at most 192 MiB of HBM per device.

```python
import math
import jax
import jax.numpy as jnp
import numpy as np
from jax import lax

D = 768
HEADS = 12
HD = 64
FF = 3072
BUCKETS = 32
TOK_DEV = 1024
INNER = 768
EXPERTS = 8
CAP = 192
SEQS = 8
TOKENS = 8192


def steps_of(rng, dims, cuts, low, top_value):
    def one(position, parts):
        heights = jax.random.uniform(jax.random.fold_in(jax.random.fold_in(rng, 6), position), (parts,), jnp.float32, low / len(cuts), top_value / len(cuts))
        return jnp.repeat(jnp.exp(heights), dims[position] // parts).reshape((-1,) + (1,) * (len(dims) - position - 1))

    loudness = one(*cuts[0])
    for cut in cuts[1:]:
        loudness = loudness * one(*cut)
    return loudness


def length_profile(number_of, total, bound, lean):
    portions = [(1 << 20) // math.isqrt(rank ** lean) + 1 for rank in range(2, number_of + 1)]
    surplus, holding = total - bound - (number_of - 1), [1] * (number_of - 1)
    while surplus > 0:
        candidates = [i for i in range(number_of - 1) if holding[i] < bound]
        mass, budget = sum([portions[i] for i in candidates]), surplus
        for i in candidates:
            addition = min(bound - holding[i], max(1, budget * portions[i] // mass), surplus)
            holding[i] = holding[i] + addition
            surplus = surplus - addition
    return np.array([bound] + holding)


def ragged_sizes(key, amount, total, reach, slope):
    if amount == 2:
        one = jax.random.randint(key, (), max(1, total - reach), min(reach, total - 1) + 1)
        return jnp.stack([one, total - one])
    tallies = jnp.asarray(length_profile(amount, total, reach, slope), jnp.int32)
    twos = (amount - 1) // 2
    donor, receiver = tallies[1:1 + 2 * twos:2], tallies[2:2 + 2 * twos:2]
    slack = jnp.minimum(donor - 1, reach - receiver)
    shifted = jax.random.randint(jax.random.fold_in(key, 1), (twos,), 0, 1 << 20) % (slack + 1)
    tallies = tallies.at[1:1 + 2 * twos:2].set(donor - shifted).at[2:2 + 2 * twos:2].set(receiver + shifted)
    return tallies[jax.random.permutation(jax.random.fold_in(key, 2), amount)]


def assign_block(stream_key, own, number, rows, count, top, reach, skew):
    order = jax.random.permutation(stream_key, count)
    crowded, common = load_shares(count, rows * top, reach, skew, True), load_shares(count, rows * top, reach, skew, False)
    places = jnp.arange(count)

    def named(sizes, offset_by):
        used = int((sizes > 0).sum())
        fixed = max(1, used // 4)
        passed = fixed + (places - fixed + offset_by * (used - fixed)) % max(1, count - fixed)
        return jnp.zeros((count,), jnp.int32).at[order[jnp.where(places < fixed, places, passed)]].set(jnp.asarray(sizes, jnp.int32))

    sizes = jnp.where(number % 4 == 0, named(crowded, number // 4), named(common, number - number // 4 - 1))
    mixed = jax.random.permutation(jax.random.fold_in(own, 3), count)
    source_of, taker = mixed[0:count // 2 * 2:2], mixed[1:count // 2 * 2:2]
    room = jnp.minimum(sizes[source_of] - 1, reach - sizes[taker]) // 2
    room = jnp.where((source_of == order[0]) | (taker == order[0]) | (sizes[taker] == 0), 0, jnp.maximum(room, 0))
    passed = jax.random.randint(jax.random.fold_in(own, 4), (count // 2,), 0, 1 << 20) % (room + 1)
    sizes = sizes.at[source_of].add(-passed).at[taker].add(passed)
    members = jnp.searchsorted(jnp.cumsum(sizes), jnp.arange(rows * top), side="right").astype(jnp.int32)
    listing = members.reshape(top, rows).T
    listing = listing[jax.random.permutation(jax.random.fold_in(own, 1), rows)]
    offset_by = jax.random.randint(jax.random.fold_in(own, 2), (rows, 1), 0, top)
    return jnp.take_along_axis(listing, (jnp.arange(top)[None, :] + offset_by) % top, axis=1)


def load_shares(count, total, bound, slope, full):
    loads = [(1 << 20) // math.isqrt(rank ** slope) + 1 for rank in range(1, count + 1)]
    largest = bound if full else min(bound, max(-(-total // count), total * loads[0] // sum(loads)))
    least = 1 if total - largest >= count - 1 else 0
    given, surplus = [largest] + [least] * (count - 1), total - largest - least * (count - 1)
    while surplus > 0:
        movable = [i for i in range(1, count) if given[i] < largest] or [i for i in range(1, count) if given[i] < bound]
        mass, budget = sum([loads[i] for i in movable]), surplus
        for i in movable:
            more = min(bound - given[i], max(1, budget * loads[i] // mass), surplus)
            given[i] = given[i] + more
            surplus = surplus - more
    return np.array(given)


def centred(rng, extent, scale, most, pieces=(), kind=jnp.bfloat16):
    level = steps_of(rng, extent, pieces, -0.22, 0.18) if pieces else 1.0
    entries = jax.random.normal(rng, extent, jnp.float32) * scale * level
    return jnp.minimum(jnp.maximum(entries, -most), most).astype(kind)


def setup_inputs(seed: int = 0) -> dict:
    splits = jax.random.split(jax.random.key(seed), 13)
    tokens = centred(splits[0], (TOKENS, D), 1.0, 6.0, ((0, 8),))
    gain_attn = jnp.clip(1.0 + 0.1 * jax.random.normal(splits[1], (D,), jnp.float32), 0.5, 1.5)
    w_qkv = centred(splits[2], (3, D, INNER), D ** -0.5, 0.21875, ((2, 4),))
    w_proj = centred(splits[3], (INNER, D), (max(1, INNER // 256)) ** -0.5, 3.5, ((0, 4),))
    rel_bias = jnp.clip(jax.random.uniform(splits[4], (HEADS, BUCKETS), jnp.float32, -1.0, 1.0) * steps_of(splits[4], (HEADS, BUCKETS), ((0, 4),), -0.4, 0.0), -1.0, 1.0)
    gain_ffn = jnp.clip(1.0 + 0.1 * jax.random.normal(splits[5], (D,), jnp.float32), 0.5, 1.5)
    w_router = centred(splits[6], (D, EXPERTS), (4 * D) ** -0.5, 0.109375)
    w_in = centred(splits[7], (EXPERTS, D, FF), D ** -0.5, 0.21875, ((0, 8), (2, 4)))
    w_out = centred(splits[8], (EXPERTS, FF, D), (EXPERTS / 32), 1.5, ((0, 8), (1, 4)))
    routes_keys = jax.random.split(jax.random.fold_in(splits[9], 1), TOKENS // TOK_DEV)
    routes_turns = jax.random.permutation(jax.random.fold_in(splits[9], 3), TOKENS // TOK_DEV)
    routes = jax.vmap(lambda own, number: assign_block(jax.random.fold_in(splits[9], 2), own, number, TOK_DEV, EXPERTS, 1, CAP, 1))(routes_keys, routes_turns).reshape((TOKENS, 1))
    segment_ids = jax.vmap(lambda own: jnp.searchsorted(jnp.cumsum(ragged_sizes(own, 4, TOK_DEV, TOK_DEV // 2, 0)), jnp.arange(TOK_DEV), side="right"))(jax.random.split(splits[10], SEQS)).reshape((SEQS, TOK_DEV)).astype(jnp.int32)
    cotangent = centred(splits[11], (TOKENS, D), 1.0, 6.0, ((0, 8),))
    return dict(tokens=tokens, gain_attn=gain_attn, w_qkv=w_qkv, w_proj=w_proj, rel_bias=rel_bias, gain_ffn=gain_ffn, w_router=w_router, w_in=w_in, w_out=w_out, routes=routes, segment_ids=segment_ids, cotangent=cotangent)


@jax.custom_vjp
def low(v):
    return lax.optimization_barrier(v.astype(jnp.bfloat16)).astype(jnp.float32)

@jax.custom_vjp
def low_back(v):
    return v

def low_keep(v):
    return (low(v), None)

def low_pass(kept, grad):
    return (grad,)

def back_keep(v):
    return (v, None)

def back_low(kept, grad):
    return (low(grad),)
low.defvjp(low_keep, low_pass)
low_back.defvjp(back_keep, back_low)
FAR_LIMITS = (12, 16, 23, 32, 46, 64, 91)
HIGH = lax.Precision.HIGHEST

def bucket_of(offset):
    distance = jnp.abs(offset)
    far_bucket = jnp.full_like(distance, 8)
    for limit in FAR_LIMITS:
        far_bucket = far_bucket + (distance >= limit).astype(jnp.int32)
    near_far = jnp.where(distance < 8, distance, far_bucket)
    return near_far + 16 * (offset > 0).astype(jnp.int32)

def norm_rows(values, gain):
    return values * lax.rsqrt(lax.optimization_barrier(jnp.mean(values * values, -1, keepdims=True)) + 1e-06) * gain

def attend(sequence, segments, gain_attn, w_qkv, w_proj, rel_bias):
    length = sequence.shape[0]
    normed1 = low(norm_rows(sequence, gain_attn))
    projected = low_back(low(jnp.einsum('sd,tdi->tsi', normed1, w_qkv, precision=HIGH)))
    queries = projected[0].reshape(length, HEADS, HD)
    keys = projected[1].reshape(length, HEADS, HD)
    values = projected[2].reshape(length, HEADS, HD)
    positions = jnp.arange(length, dtype=jnp.int32)
    buckets = bucket_of(positions[None, :] - positions[:, None])
    position_bias = rel_bias[:, buckets]
    scores = jnp.einsum('qhd,khd->hqk', queries, keys, precision=HIGH) * HD ** (-0.5) + position_bias
    same_doc = segments[:, None] == segments[None, :]
    scores = low_back(jnp.where(same_doc[None], scores, -1e+30))
    probs = jax.nn.softmax(scores, -1)
    attended = jnp.einsum('hqk,khd->qhd', low(probs), values, precision=HIGH).reshape(length, INNER)
    attended = low_back(low(attended))
    head_out = low_back(jnp.dot(attended, w_proj, precision=HIGH))
    return sequence + head_out

def reference(tokens, gain_attn, w_qkv, w_proj, rel_bias, gain_ffn, w_router, w_in, w_out, routes, segment_ids, cotangent):
    route = routes[:, 0].astype(jnp.int32)
    seq_of = (jnp.arange(TOKENS, dtype=jnp.int32) // TOK_DEV).astype(jnp.int32)
    onehot_int = (route[:, None] == jnp.arange(EXPERTS, dtype=jnp.int32)[None, :]).astype(jnp.int32)
    per_seq = onehot_int.reshape(SEQS, TOK_DEV, EXPERTS)
    slot = (lax.optimization_barrier(jnp.sum(jnp.cumsum(per_seq, 1) * per_seq, -1)) - 1).reshape(TOKENS).astype(jnp.int32)
    onehot = onehot_int.astype(jnp.float32)

    def forward(inputs, gain_attn, w_qkv, w_proj, rel_bias, gain_ffn, w_router, w_in, w_out):
        sequences = inputs.reshape(SEQS, TOK_DEV, D)

        def one_sequence(pair):
            return attend(pair[0], pair[1], gain_attn, w_qkv, w_proj, rel_bias)
        hidden1 = lax.map(jax.checkpoint(one_sequence), (sequences, segment_ids)).reshape(TOKENS, D)
        normed2 = low(norm_rows(hidden1, gain_ffn))
        router_probs = jax.nn.softmax(jnp.dot(normed2, w_router, precision=HIGH), -1)
        gate = lax.optimization_barrier(jnp.sum(router_probs * onehot, -1))
        sent = low_back(normed2)
        buffer = jnp.zeros((SEQS, EXPERTS, CAP, D), jnp.float32).at[seq_of, route, slot].set(sent)

        def one_expert(triple):
            rows, first, second = triple
            pre = low_back(jnp.einsum('scd,df->scf', rows, first, precision=HIGH))
            act = low(jax.nn.gelu(pre))
            result = jnp.einsum('scf,fd->scd', act, second, precision=HIGH)
            return low_back(low(result))
        reply = lax.map(jax.checkpoint(one_expert), (jnp.swapaxes(buffer, 0, 1), w_in, w_out))
        returned = reply[route, seq_of, slot]
        return hidden1 + gate[:, None] * returned
    primals = (tokens.astype(jnp.float32), gain_attn, w_qkv.astype(jnp.float32), w_proj.astype(jnp.float32), rel_bias, gain_ffn, w_router.astype(jnp.float32), w_in.astype(jnp.float32), w_out.astype(jnp.float32))
    result, pull = jax.vjp(forward, *primals)
    grads = pull(cotangent.astype(jnp.float32))
    return (result.astype(jnp.bfloat16), grads[0], grads[1], grads[2], grads[3], grads[4], grads[5], grads[6], grads[7], grads[8])
```

```python
import functools

import jax
import jax.numpy as jnp
from jax import lax
from jax.experimental import pallas as pl
from jax.experimental.pallas import tpu as pltpu
from jax.sharding import PartitionSpec as P

FAR_LIMITS = (12, 16, 23, 32, 46, 64, 91)
HIGH = lax.Precision.HIGHEST
F32 = jnp.float32
BF16 = jnp.bfloat16
MASKED = -1e30
QB = 256
PAD = 256
FAR = FAR_LIMITS[-1]

STEPS = (
    [(1 - limit, 14 - i) for i, limit in enumerate(reversed(FAR_LIMITS))]
    + [(-n, n) for n in range(7, -1, -1)]
    + [(n, 16 + n) for n in range(1, 8)]
    + [(8, 24)]
    + [(limit, 25 + i) for i, limit in enumerate(FAR_LIMITS)]
)


def norm_rows(values, gain):
    return values * lax.rsqrt(jnp.mean(values * values, -1, keepdims=True) + 1e-06) * gain


def nt_dot(left, right):
    return lax.dot_general(left, right, (((1,), (1,)), ((), ())), preferred_element_type=F32)


def nn_dot(left, right):
    return jnp.dot(left, right, preferred_element_type=F32)


def strip_shape(length):
    return 2 * length - QB


def near_rows(length):
    base = length - QB
    first = (base - FAR) // 32 * 32
    last = -(-(base + 127 + FAR) // 32) * 32
    return base, first, last


def build_strip(strip_ref, bias_ref, length, heads):
    total = strip_shape(length)
    base, first, last = near_rows(length)
    for h in range(heads):
        low = jnp.full((8, 128), bias_ref[h, 15], F32)
        high = jnp.full((8, 128), bias_ref[h, 31], F32)
        for half in range(QB // 128):
            cols = slice(half * 128, half * 128 + 128)
            lo_end, hi_start = first + half * 128, last + half * 128
            strip_ref[h, 0:lo_end, cols] = jnp.broadcast_to(low[:1], (lo_end, 128))
            strip_ref[h, hi_start:total, cols] = jnp.broadcast_to(high[:1], (total - hi_start, 128))
    for start in range(first, last, 32):
        offset = (
            lax.broadcasted_iota(jnp.int32, (32, 128), 0)
            - lax.broadcasted_iota(jnp.int32, (32, 128), 1)
            + (start - base)
        )
        tiles = [jnp.full((32, 128), bias_ref[h, 15], F32) for h in range(heads)]
        for begin, bucket in STEPS:
            reached = offset >= begin
            tiles = [jnp.where(reached, bias_ref[h, bucket], tiles[h]) for h in range(heads)]
        for h in range(heads):
            for half in range(QB // 128):
                at = start + half * 128
                strip_ref[h, at : at + 32, half * 128 : half * 128 + 128] = tiles[h]


def head_lanes(rows, h, dim, keep_tail, heads):
    lane = lax.broadcasted_iota(jnp.int32, (rows, PAD), 1)
    inside = (lane >= h * dim) & (lane < (h + 1) * dim)
    if keep_tail:
        inside = inside | (lane >= heads * dim)
    return inside


def attend_kernel(length, heads, dim, proj_ref, vt_ref, bias_ref, att_ref, lse_ref, kh_ref, strip_ref):
    build_strip(strip_ref, bias_ref, length, heads)
    keys = proj_ref[:, PAD : 2 * PAD]
    for h in range(heads):
        kh_ref[h] = jnp.where(head_lanes(length, h, dim, True, heads), keys, jnp.zeros_like(keys))

    def block(b, carry):
        at = pl.multiple_of(b * QB, QB)
        from_row = pl.multiple_of(length - QB - b * QB, QB)
        queries = proj_ref[pl.ds(at, QB), 0:PAD]
        for h in range(heads):
            scores = nt_dot(kh_ref[h], queries) + strip_ref[h, pl.ds(from_row, length), :]
            top = jnp.max(scores, 0, keepdims=True)
            probs = jnp.exp(scores - top)
            total = jnp.sum(probs, 0, keepdims=True)
            out = nn_dot(vt_ref[h * dim : (h + 1) * dim, :], probs.astype(BF16))
            att_ref[h * dim : (h + 1) * dim, pl.ds(at, QB)] = (out / total).astype(BF16)
            lse_ref[h : h + 1, pl.ds(at, QB)] = top + jnp.log(total)
        return carry

    lax.fori_loop(0, length // QB, block, 0)


def attend_back_kernel(
    length, heads, dim,
    proj_ref, kt_ref, lse_ref, da_ref, bias_ref,
    dqkv_ref, drel_ref,
    kh_ref, vh_ref, strip_ref, dstrip_ref, pcat_ref, dcat_ref, dacat_ref, qcat_ref, dk_ref, dv_ref, dqt_ref,
):
    inner = heads * dim
    scale = dim ** (-0.5)
    total = strip_shape(length)
    base, first, last = near_rows(length)
    build_strip(strip_ref, bias_ref, length, heads)
    dstrip_ref[...] = jnp.zeros_like(dstrip_ref)
    dk_ref[...] = jnp.zeros_like(dk_ref)
    dv_ref[...] = jnp.zeros_like(dv_ref)
    dqt_ref[...] = jnp.zeros_like(dqt_ref)
    keys = proj_ref[:, PAD : 2 * PAD]
    values = proj_ref[:, 2 * PAD : 3 * PAD]
    for h in range(heads):
        kh_ref[h] = jnp.where(head_lanes(length, h, dim, True, heads), keys, jnp.zeros_like(keys))
        vh_ref[h] = jnp.where(head_lanes(length, h, dim, False, heads), values, jnp.zeros_like(values))

    def block(b, carry):
        at = pl.multiple_of(b * QB, QB)
        from_row = pl.multiple_of(length - QB - b * QB, QB)
        queries = proj_ref[pl.ds(at, QB), 0:PAD]
        grads = da_ref[pl.ds(at, QB), :]
        for h in range(heads):
            mine = head_lanes(QB, h, dim, False, heads)
            cols = slice(h * QB, (h + 1) * QB)
            qcat_ref[cols, :] = jnp.where(mine, queries, jnp.zeros_like(queries))
            dacat_ref[cols, :] = jnp.where(mine, grads, jnp.zeros_like(grads))
            scores = nt_dot(kh_ref[h], queries) + strip_ref[h, pl.ds(from_row, length), :]
            probs = jnp.exp(scores - lse_ref[h : h + 1, pl.ds(at, QB)])
            weighted = probs * nt_dot(vh_ref[h], grads)
            delta = jnp.sum(weighted, 0, keepdims=True)
            dscore = weighted - probs * delta
            dstrip_ref[h, pl.ds(from_row, length), :] += dscore
            dlow = dscore.astype(BF16)
            pcat_ref[:, cols] = probs.astype(BF16)
            dcat_ref[:, cols] = dlow
            dqt_ref[h * dim : (h + 1) * dim, :] = nn_dot(kt_ref[h * dim : (h + 1) * dim, :], dlow) * scale
        dk_ref[...] += nn_dot(dcat_ref[...], qcat_ref[...])
        dv_ref[...] += nn_dot(pcat_ref[...], dacat_ref[...])
        dqkv_ref[0, pl.ds(at, QB), :] = dqt_ref[...].T[:, :inner].astype(BF16)
        return carry

    lax.fori_loop(0, length // QB, block, 0)
    dqkv_ref[1] = dk_ref[:, :inner].astype(BF16)
    dqkv_ref[2] = dv_ref[:, :inner].astype(BF16)

    offset = (
        lax.broadcasted_iota(jnp.int32, (last - first, 128), 0)
        - lax.broadcasted_iota(jnp.int32, (last - first, 128), 1)
        + (first - base)
    )
    begins = [-(1 << 20)] + [begin for begin, bucket in STEPS] + [1 << 20]
    buckets = [15] + [bucket for begin, bucket in STEPS]
    for h in range(heads):
        near = jnp.zeros((last - first, 128), F32)
        low = jnp.zeros((1, 128), F32)
        high = jnp.zeros((1, 128), F32)
        for half in range(QB // 128):
            cols = slice(half * 128, half * 128 + 128)
            lo_end, hi_start = first + half * 128, last + half * 128
            near = near + dstrip_ref[h, lo_end:hi_start, cols]
            low = low + jnp.sum(dstrip_ref[h, 0:lo_end, cols], 0, keepdims=True)
            high = high + jnp.sum(dstrip_ref[h, hi_start:total, cols], 0, keepdims=True)
        drel_ref[h, 16:17, :] = jnp.zeros((1, 128), F32)
        for i, bucket in enumerate(buckets):
            inside = (offset >= begins[i]) & (offset < begins[i + 1])
            row = jnp.sum(jnp.where(inside, near, 0.0), 0, keepdims=True)
            if bucket == 15:
                row = row + low
            if bucket == 31:
                row = row + high
            drel_ref[h, bucket : bucket + 1, :] = row


def whole_vmem(count):
    return [pl.BlockSpec(memory_space=pltpu.VMEM)] * count


def attend(proj, vt, rel_bias, dim):
    length = proj.shape[0]
    heads = rel_bias.shape[0]
    return pl.pallas_call(
        functools.partial(attend_kernel, length, heads, dim),
        out_shape=(
            jax.ShapeDtypeStruct((heads * dim, length), BF16),
            jax.ShapeDtypeStruct((8, length), F32),
        ),
        in_specs=whole_vmem(2) + [pl.BlockSpec(memory_space=pltpu.SMEM)],
        out_specs=tuple(whole_vmem(2)),
        scratch_shapes=[
            pltpu.VMEM((heads, length, PAD), BF16),
            pltpu.VMEM((heads, strip_shape(length), QB), F32),
        ],
        compiler_params=pltpu.CompilerParams(vmem_limit_bytes=40 << 20),
        cost_estimate=pl.CostEstimate(
            flops=4 * heads * length * length * dim,
            bytes_accessed=4 << 20,
            transcendentals=heads * length * length,
        ),
    )(proj, vt, rel_bias)


def attend_back(proj, kt, lse, da, rel_bias, dim):
    length = proj.shape[0]
    heads, buckets = rel_bias.shape
    return pl.pallas_call(
        functools.partial(attend_back_kernel, length, heads, dim),
        out_shape=(
            jax.ShapeDtypeStruct((3, length, heads * dim), BF16),
            jax.ShapeDtypeStruct((heads, buckets, 128), F32),
        ),
        in_specs=whole_vmem(4) + [pl.BlockSpec(memory_space=pltpu.SMEM)],
        out_specs=tuple(whole_vmem(2)),
        scratch_shapes=[
            pltpu.VMEM((heads, length, PAD), BF16),
            pltpu.VMEM((heads, length, PAD), BF16),
            pltpu.VMEM((heads, strip_shape(length), QB), F32),
            pltpu.VMEM((heads, strip_shape(length), QB), F32),
            pltpu.VMEM((length, heads * QB), BF16),
            pltpu.VMEM((length, heads * QB), BF16),
            pltpu.VMEM((heads * QB, PAD), BF16),
            pltpu.VMEM((heads * QB, PAD), BF16),
            pltpu.VMEM((length, PAD), F32),
            pltpu.VMEM((length, PAD), F32),
            pltpu.VMEM((PAD, QB), F32),
        ],
        compiler_params=pltpu.CompilerParams(vmem_limit_bytes=56 << 20),
        cost_estimate=pl.CostEstimate(
            flops=10 * heads * length * length * dim,
            bytes_accessed=6 << 20,
            transcendentals=heads * length * length,
        ),
    )(proj, kt, lse, da, rel_bias)


def shards(
    tokens,
    gain_attn,
    w_qkv,
    w_proj,
    rel_bias,
    gain_ffn,
    w_router,
    w_in,
    w_out,
    routes,
    segment_ids,
    cotangent,
):
    length, width = tokens.shape
    experts = w_router.shape[1]
    here = w_in.shape[0]
    capacity = max(2, 3 * length // (2 * experts))
    heads_here = rel_bias.shape[0]
    inner_here = w_proj.shape[0]
    head_dim = inner_here // heads_here
    scale = head_dim ** (-0.5)
    members = lax.axis_size("tensor")
    groups = lax.axis_size("expert")
    member = lax.axis_index("tensor")
    group = lax.axis_index("expert")
    share = capacity // members
    segments = segment_ids[0]
    route = routes[:, 0]

    def swap(value, bit):
        return lax.ppermute(value, "tensor", [(i, i ^ bit) for i in range(members)])

    bits = [1 << i for i in range(members.bit_length() - 1)]

    def gather_members(value):
        blocks = {0: value}
        for bit in reversed(bits):
            blocks.update({k ^ bit: swap(block, bit) for k, block in blocks.items()})
        return [blocks[k] for k in range(members)]

    def sum_members(parts):
        held = dict(enumerate(parts))
        for bit in bits:
            for k in [k for k in held if k & bit]:
                held[k ^ bit] = held[k ^ bit] + swap(held.pop(k).astype(BF16), bit).astype(F32)
        return held[0]

    paired = groups <= 8

    def owner_of(k):
        return group ^ k if paired else jnp.int32(k)

    def across(value, k):
        return lax.ppermute(value, "expert", [(i, i ^ k) for i in range(groups)])

    def exchange(value):
        if not paired:
            return lax.all_to_all(value, "expert", split_axis=0, concat_axis=0, tiled=True)
        far_first = sorted(range(1, groups), reverse=True)
        blocks = {k: across(value[k], k) for k in far_first}
        blocks[0] = value[0]
        return jnp.stack([blocks[k] for k in range(groups)])

    def gather_groups(value):
        if not paired:
            return lax.all_gather(value, "expert", axis=0)
        far_first = sorted(range(1, groups), reverse=True)
        blocks = {k: across(value, k) for k in far_first}
        blocks[0] = value
        return jnp.stack([blocks[k] for k in range(groups)])

    def in_order(value):
        if not paired:
            return value
        return jnp.stack([lax.dynamic_index_in_dim(value, group ^ k, 0, False) for k in range(groups)])

    def sum_groups(value, extra=None):
        rows, columns = value.shape
        cut = in_order(value.reshape(groups, rows // groups, columns)).astype(BF16)
        mine = jnp.sum(exchange(cut).astype(F32), 0).astype(BF16)
        if extra is not None:
            mine = jnp.concatenate([mine, extra.astype(BF16)], 0)
        every = gather_groups(mine)
        total = in_order(every[:, : rows // groups]).reshape(rows, columns).astype(F32)
        if extra is None:
            return total
        return total, jnp.sum(every[:, rows // groups :].astype(F32), 0)

    expert_ids = jnp.arange(experts, dtype=jnp.int32)
    onehot_low = (route[:, None] == expert_ids[None, :]).astype(BF16)
    onehot = onehot_low.astype(F32)
    positions = jnp.arange(length, dtype=jnp.int32)
    lower_ones = (positions[:, None] >= positions[None, :]).astype(BF16)
    running = nn_dot(lower_ones, onehot_low)
    slot = (jnp.sum(running * onehot, 1) - 1.0).astype(jnp.int32)
    flat_id = route * capacity + slot

    block_experts = jnp.stack([owner_of(k) for k in range(groups)])
    block_experts = (block_experts[:, None] * here + jnp.arange(here, dtype=jnp.int32)).reshape(-1)

    def ids_of(owner):
        slots = owner * share + jnp.arange(share, dtype=jnp.int32)
        return (block_experts[:, None] * capacity + slots[None, :]).reshape(-1)

    send_table = (ids_of(member)[:, None] == flat_id[None, :]).astype(BF16)
    all_ids = jnp.concatenate([ids_of(member ^ k) for k in range(members)])
    back_table = (flat_id[:, None] == all_ids[None, :]).astype(BF16)

    w_proj_all = jnp.concatenate(gather_members(w_proj), 0)

    residual = tokens.astype(F32)
    normed1 = norm_rows(residual, gain_attn).astype(BF16)
    tail = PAD - inner_here
    w_pad = jnp.pad(w_qkv, ((0, 0), (0, 0), (0, tail)))
    w_all = jnp.concatenate([w_pad[0], w_pad[1], w_pad[2]], 1)
    documents = segments[:, None] == jnp.arange(tail, dtype=jnp.int32)[None, :]
    first_lane = jnp.zeros((length, inner_here), F32)
    extra = jnp.concatenate(
        [
            first_lane,
            jnp.where(documents, 0.0, MASKED),
            first_lane,
            documents.astype(F32),
            jnp.zeros((length, PAD), F32),
        ],
        1,
    ).astype(BF16)
    factors = jnp.where(jnp.arange(3 * PAD) < PAD, scale, 1.0).astype(BF16)
    proj = nn_dot(normed1, w_all).astype(BF16) * factors[None, :] + extra
    kvt = jnp.einsum("tdi,sd->tis", w_qkv[1:], normed1, preferred_element_type=F32).astype(BF16)
    def dispatch(rows):
        out = nn_dot(send_table, rows).astype(BF16).reshape(groups, -1, width)
        return exchange(out).reshape(-1, width)

    cot_share = dispatch(cotangent)
    proj, cot_share, w_proj_all = lax.optimization_barrier((proj, cot_share, w_proj_all))
    attended_t, lse = attend(proj, kvt[1], rel_bias, head_dim)

    attended_all = jnp.concatenate(gather_members(attended_t), 0)
    attended_all, cot_share = lax.optimization_barrier((attended_all, cot_share))
    head_out = lax.dot_general(
        attended_all, w_proj_all, (((0,), (0,)), ((), ())), preferred_element_type=F32
    )
    hidden1 = residual + head_out
    normed2 = norm_rows(hidden1, gain_ffn).astype(BF16)
    logits = nn_dot(normed2, w_router)
    router_probs = jax.nn.softmax(logits, -1)
    gate = jnp.sum(router_probs * onehot, -1)
    grad_out = cotangent.astype(F32)

    share_rows = dispatch(normed2)
    cot_rows = jnp.concatenate(gather_members(cot_share), 0)
    share_rows, cot_rows = lax.optimization_barrier((share_rows, cot_rows))
    received = jnp.concatenate(gather_members(share_rows), 0)

    first, second = w_in[0], w_out[0]
    rows_here = received.shape[0] // members

    def cut(value):
        return [value[k * rows_here : (k + 1) * rows_here] for k in range(members)]

    def summed(value):
        return sum_members(cut(value)).astype(BF16)

    def home(value):
        back = exchange(value.reshape(groups, -1, width)).reshape(-1, width)
        return nn_dot(back_table, jnp.concatenate(gather_members(back), 0)).astype(BF16).astype(F32)

    slot_probs = jax.nn.softmax(nn_dot(received, w_router), -1)
    own = (expert_ids == group).astype(F32)[None, :]
    slot_gate = jnp.sum(slot_probs * own, -1, keepdims=True)
    cot_values = cot_rows.astype(F32)
    grad_received = (slot_gate * cot_values).astype(BF16)
    pre = nn_dot(received, first)
    act = jax.nn.gelu(pre).astype(BF16)
    expert_part = nn_dot(act, second)
    slot_gate_grad = jnp.sum(cot_values * expert_part, -1, keepdims=True)
    slot_logit_grad = (slot_probs * (own - slot_gate) * slot_gate_grad).astype(BF16)
    grad_act = nt_dot(grad_received, second)
    unused_act, gelu_pull = jax.vjp(jax.nn.gelu, pre)
    grad_pre = gelu_pull(grad_act)[0].astype(BF16)
    input_part = nt_dot(grad_pre, first) + nt_dot(slot_logit_grad, w_router)
    grad_share = summed(input_part)
    expert_part, grad_share = lax.optimization_barrier((expert_part, grad_share))
    grad_normed2 = home(grad_share)
    reply_share = summed(expert_part)
    returned = home(reply_share)
    grad_w_out = lax.dot_general(
        act, grad_received, (((0,), (0,)), ((), ())), preferred_element_type=F32
    )
    grad_w_in = lax.dot_general(
        received, grad_pre, (((0,), (0,)), ((), ())), preferred_element_type=F32
    )

    output = (hidden1 + gate[:, None] * returned).astype(BF16)
    gate_grad = jnp.sum(grad_out * returned, -1)
    prob_grad = onehot * gate_grad[:, None]
    logit_grad = router_probs * (prob_grad - jnp.sum(prob_grad * router_probs, -1, keepdims=True))
    grad_router = jnp.dot(normed2.astype(F32).T, logit_grad, precision=HIGH)
    unused_norm, norm_pull = jax.vjp(norm_rows, hidden1, gain_ffn)
    back_hidden, grad_gain_ffn = norm_pull(grad_normed2)
    grad_hidden1 = grad_out + back_hidden
    out_grad = grad_hidden1.astype(BF16)
    grad_proj = nn_dot(attended_t, out_grad)
    w_proj_pad = jnp.pad(w_proj, ((0, tail), (0, 0)))
    attended_grad = nt_dot(out_grad, w_proj_pad).astype(BF16)

    small = jnp.concatenate([grad_gain_ffn[None], grad_router.T], 0)
    grad_proj, small = sum_groups(grad_proj, small)
    grad_gain_ffn = small[0]
    grad_router = small[1:].T

    stacked_grad, rel_parts = attend_back(proj, kvt[0], lse, attended_grad, rel_bias, head_dim)
    normed1_part = jnp.einsum("tsi,tdi->sd", stacked_grad, w_qkv, preferred_element_type=F32)
    grad_qkv_t = jnp.einsum("tsi,sd->tid", stacked_grad, normed1, preferred_element_type=F32)
    rel_row = jnp.sum(rel_parts, -1).reshape(1, -1)
    rel_row = jnp.pad(rel_row, ((0, 0), (0, width - rel_row.shape[1])))
    grad_qkv_t, rel_row = sum_groups(grad_qkv_t.reshape(3 * inner_here, width), rel_row)
    grad_qkv = jnp.swapaxes(grad_qkv_t.reshape(3, inner_here, width), 1, 2)
    grad_rel = rel_row[0, : rel_bias.size].reshape(rel_bias.shape)
    inverse = lax.rsqrt(jnp.mean(residual * residual, -1, keepdims=True) + 1e-06)

    halves = normed1_part.reshape(2, length // 2, width)
    low_bit = member & 1
    kept = lax.dynamic_index_in_dim(halves, low_bit, 0, False)
    sent = lax.dynamic_index_in_dim(halves, 1 - low_bit, 0, False)
    kept = kept + swap(sent.astype(BF16), 1).astype(F32)
    for bit in bits[1:]:
        kept = kept + swap(kept.astype(BF16), bit).astype(F32)
    kept = kept.astype(BF16)
    other = swap(kept, 1)
    grad_normed1 = jnp.concatenate(
        [jnp.where(low_bit == 0, kept, other), jnp.where(low_bit == 0, other, kept)], 0
    ).astype(F32)
    gain_part = jnp.sum(grad_normed1 * residual * inverse, 0, keepdims=True)
    grad_gain_attn = jnp.sum(gather_groups(gain_part), (0, 1))
    scaled = gain_attn * grad_normed1
    correction = jnp.mean(residual * scaled, -1, keepdims=True)
    grad_input = grad_hidden1 + inverse * scaled - residual * (inverse**3 * correction)
    return (
        output,
        grad_input,
        grad_gain_attn,
        grad_qkv,
        grad_proj,
        grad_rel,
        grad_gain_ffn,
        grad_router,
        grad_w_in[None],
        grad_w_out[None],
    )


def solution(mesh):
    placed = (
        P("expert", None),
        P(),
        P(None, None, "tensor"),
        P("tensor", None),
        P("tensor", None),
        P(),
        P(),
        P("expert", None, "tensor"),
        P("expert", "tensor", None),
        P("expert", None),
        P("expert", None),
        P("expert", None),
    )
    return jax.shard_map(
        shards,
        mesh=mesh,
        in_specs=placed,
        out_specs=(
            P("expert", None),
            P("expert", None),
            P(),
            P(None, None, "tensor"),
            P("tensor", None),
            P("tensor", None),
            P(),
            P(),
            P("expert", None, "tensor"),
            P("expert", "tensor", None),
        ),
        check_vma=False,
    )
```

```python
import functools

import jax
import jax.numpy as jnp
from jax import lax
from jax.experimental import pallas as pl
from jax.experimental.pallas import tpu as pltpu
from jax.sharding import PartitionSpec as P

FAR_LIMITS = (12, 16, 23, 32, 46, 64, 91)
HIGH = lax.Precision.HIGHEST
F32 = jnp.float32
BF16 = jnp.bfloat16
MASKED = -1e30
QB = 256
PAD = 256
FAR = FAR_LIMITS[-1]

STEPS = (
    [(1 - limit, 14 - i) for i, limit in enumerate(reversed(FAR_LIMITS))]
    + [(-n, n) for n in range(7, -1, -1)]
    + [(n, 16 + n) for n in range(1, 8)]
    + [(8, 24)]
    + [(limit, 25 + i) for i, limit in enumerate(FAR_LIMITS)]
)


def norm_rows(values, gain):
    return values * lax.rsqrt(jnp.mean(values * values, -1, keepdims=True) + 1e-06) * gain


def nt_dot(left, right):
    return lax.dot_general(left, right, (((1,), (1,)), ((), ())), preferred_element_type=F32)


def nn_dot(left, right):
    return jnp.dot(left, right, preferred_element_type=F32)


def strip_shape(length):
    return 2 * length - QB


def near_rows(length):
    base = length - QB
    first = (base - FAR) // 32 * 32
    last = -(-(base + 127 + FAR) // 32) * 32
    return base, first, last


def build_strip(strip_ref, bias_ref, length, heads):
    total = strip_shape(length)
    base, first, last = near_rows(length)
    for h in range(heads):
        low = jnp.full((8, 128), bias_ref[h, 15], F32)
        high = jnp.full((8, 128), bias_ref[h, 31], F32)
        for half in range(QB // 128):
            cols = slice(half * 128, half * 128 + 128)
            lo_end, hi_start = first + half * 128, last + half * 128
            strip_ref[h, 0:lo_end, cols] = jnp.broadcast_to(low[:1], (lo_end, 128))
            strip_ref[h, hi_start:total, cols] = jnp.broadcast_to(high[:1], (total - hi_start, 128))
    for start in range(first, last, 32):
        offset = (
            lax.broadcasted_iota(jnp.int32, (32, 128), 0)
            - lax.broadcasted_iota(jnp.int32, (32, 128), 1)
            + (start - base)
        )
        tiles = [jnp.full((32, 128), bias_ref[h, 15], F32) for h in range(heads)]
        for begin, bucket in STEPS:
            reached = offset >= begin
            tiles = [jnp.where(reached, bias_ref[h, bucket], tiles[h]) for h in range(heads)]
        for h in range(heads):
            for half in range(QB // 128):
                at = start + half * 128
                strip_ref[h, at : at + 32, half * 128 : half * 128 + 128] = tiles[h]


def head_lanes(rows, h, dim, keep_tail, heads):
    lane = lax.broadcasted_iota(jnp.int32, (rows, PAD), 1)
    inside = (lane >= h * dim) & (lane < (h + 1) * dim)
    if keep_tail:
        inside = inside | (lane >= heads * dim)
    return inside


def attend_kernel(length, heads, dim, proj_ref, vt_ref, bias_ref, att_ref, lse_ref, kh_ref, strip_ref):
    build_strip(strip_ref, bias_ref, length, heads)
    keys = proj_ref[:, PAD : 2 * PAD]
    for h in range(heads):
        kh_ref[h] = jnp.where(head_lanes(length, h, dim, True, heads), keys, jnp.zeros_like(keys))

    def block(b, carry):
        at = pl.multiple_of(b * QB, QB)
        from_row = pl.multiple_of(length - QB - b * QB, QB)
        queries = proj_ref[pl.ds(at, QB), 0:PAD]
        for h in range(heads):
            scores = nt_dot(kh_ref[h], queries) + strip_ref[h, pl.ds(from_row, length), :]
            top = jnp.max(scores, 0, keepdims=True)
            probs = jnp.exp(scores - top)
            total = jnp.sum(probs, 0, keepdims=True)
            out = nn_dot(vt_ref[h * dim : (h + 1) * dim, :], probs.astype(BF16))
            att_ref[h * dim : (h + 1) * dim, pl.ds(at, QB)] = (out / total).astype(BF16)
            lse_ref[h : h + 1, pl.ds(at, QB)] = top + jnp.log(total)
        return carry

    lax.fori_loop(0, length // QB, block, 0)


def attend_back_kernel(
    length, heads, dim,
    proj_ref, kt_ref, lse_ref, da_ref, bias_ref,
    dqkv_ref, drel_ref,
    kh_ref, vh_ref, strip_ref, dstrip_ref, pcat_ref, dcat_ref, dacat_ref, qcat_ref, dk_ref, dv_ref, dqt_ref,
):
    inner = heads * dim
    scale = dim ** (-0.5)
    total = strip_shape(length)
    base, first, last = near_rows(length)
    build_strip(strip_ref, bias_ref, length, heads)
    dstrip_ref[...] = jnp.zeros_like(dstrip_ref)
    dk_ref[...] = jnp.zeros_like(dk_ref)
    dv_ref[...] = jnp.zeros_like(dv_ref)
    dqt_ref[...] = jnp.zeros_like(dqt_ref)
    keys = proj_ref[:, PAD : 2 * PAD]
    values = proj_ref[:, 2 * PAD : 3 * PAD]
    for h in range(heads):
        kh_ref[h] = jnp.where(head_lanes(length, h, dim, True, heads), keys, jnp.zeros_like(keys))
        vh_ref[h] = jnp.where(head_lanes(length, h, dim, False, heads), values, jnp.zeros_like(values))

    def block(b, carry):
        at = pl.multiple_of(b * QB, QB)
        from_row = pl.multiple_of(length - QB - b * QB, QB)
        queries = proj_ref[pl.ds(at, QB), 0:PAD]
        grads = da_ref[pl.ds(at, QB), :]
        for h in range(heads):
            mine = head_lanes(QB, h, dim, False, heads)
            cols = slice(h * QB, (h + 1) * QB)
            qcat_ref[cols, :] = jnp.where(mine, queries, jnp.zeros_like(queries))
            dacat_ref[cols, :] = jnp.where(mine, grads, jnp.zeros_like(grads))
            scores = nt_dot(kh_ref[h], queries) + strip_ref[h, pl.ds(from_row, length), :]
            probs = jnp.exp(scores - lse_ref[h : h + 1, pl.ds(at, QB)])
            weighted = probs * nt_dot(vh_ref[h], grads)
            delta = jnp.sum(weighted, 0, keepdims=True)
            dscore = weighted - probs * delta
            dstrip_ref[h, pl.ds(from_row, length), :] += dscore
            dlow = dscore.astype(BF16)
            pcat_ref[:, cols] = probs.astype(BF16)
            dcat_ref[:, cols] = dlow
            dqt_ref[h * dim : (h + 1) * dim, :] = nn_dot(kt_ref[h * dim : (h + 1) * dim, :], dlow) * scale
        dk_ref[...] += nn_dot(dcat_ref[...], qcat_ref[...])
        dv_ref[...] += nn_dot(pcat_ref[...], dacat_ref[...])
        dqkv_ref[0, pl.ds(at, QB), :] = dqt_ref[...].T[:, :inner].astype(BF16)
        return carry

    lax.fori_loop(0, length // QB, block, 0)
    dqkv_ref[1] = dk_ref[:, :inner].astype(BF16)
    dqkv_ref[2] = dv_ref[:, :inner].astype(BF16)

    offset = (
        lax.broadcasted_iota(jnp.int32, (last - first, 128), 0)
        - lax.broadcasted_iota(jnp.int32, (last - first, 128), 1)
        + (first - base)
    )
    begins = [-(1 << 20)] + [begin for begin, bucket in STEPS] + [1 << 20]
    buckets = [15] + [bucket for begin, bucket in STEPS]
    for h in range(heads):
        near = jnp.zeros((last - first, 128), F32)
        low = jnp.zeros((1, 128), F32)
        high = jnp.zeros((1, 128), F32)
        for half in range(QB // 128):
            cols = slice(half * 128, half * 128 + 128)
            lo_end, hi_start = first + half * 128, last + half * 128
            near = near + dstrip_ref[h, lo_end:hi_start, cols]
            low = low + jnp.sum(dstrip_ref[h, 0:lo_end, cols], 0, keepdims=True)
            high = high + jnp.sum(dstrip_ref[h, hi_start:total, cols], 0, keepdims=True)
        drel_ref[h, 16:17, :] = jnp.zeros((1, 128), F32)
        for i, bucket in enumerate(buckets):
            inside = (offset >= begins[i]) & (offset < begins[i + 1])
            row = jnp.sum(jnp.where(inside, near, 0.0), 0, keepdims=True)
            if bucket == 15:
                row = row + low
            if bucket == 31:
                row = row + high
            drel_ref[h, bucket : bucket + 1, :] = row


def whole_vmem(count):
    return [pl.BlockSpec(memory_space=pltpu.VMEM)] * count


def attend(proj, vt, rel_bias, dim):
    length = proj.shape[0]
    heads = rel_bias.shape[0]
    return pl.pallas_call(
        functools.partial(attend_kernel, length, heads, dim),
        out_shape=(
            jax.ShapeDtypeStruct((heads * dim, length), BF16),
            jax.ShapeDtypeStruct((8, length), F32),
        ),
        in_specs=whole_vmem(2) + [pl.BlockSpec(memory_space=pltpu.SMEM)],
        out_specs=tuple(whole_vmem(2)),
        scratch_shapes=[
            pltpu.VMEM((heads, length, PAD), BF16),
            pltpu.VMEM((heads, strip_shape(length), QB), F32),
        ],
        compiler_params=pltpu.CompilerParams(vmem_limit_bytes=40 << 20),
        cost_estimate=pl.CostEstimate(
            flops=4 * heads * length * length * dim,
            bytes_accessed=4 << 20,
            transcendentals=heads * length * length,
        ),
    )(proj, vt, rel_bias)


def attend_back(proj, kt, lse, da, rel_bias, dim):
    length = proj.shape[0]
    heads, buckets = rel_bias.shape
    return pl.pallas_call(
        functools.partial(attend_back_kernel, length, heads, dim),
        out_shape=(
            jax.ShapeDtypeStruct((3, length, heads * dim), BF16),
            jax.ShapeDtypeStruct((heads, buckets, 128), F32),
        ),
        in_specs=whole_vmem(4) + [pl.BlockSpec(memory_space=pltpu.SMEM)],
        out_specs=tuple(whole_vmem(2)),
        scratch_shapes=[
            pltpu.VMEM((heads, length, PAD), BF16),
            pltpu.VMEM((heads, length, PAD), BF16),
            pltpu.VMEM((heads, strip_shape(length), QB), F32),
            pltpu.VMEM((heads, strip_shape(length), QB), F32),
            pltpu.VMEM((length, heads * QB), BF16),
            pltpu.VMEM((length, heads * QB), BF16),
            pltpu.VMEM((heads * QB, PAD), BF16),
            pltpu.VMEM((heads * QB, PAD), BF16),
            pltpu.VMEM((length, PAD), F32),
            pltpu.VMEM((length, PAD), F32),
            pltpu.VMEM((PAD, QB), F32),
        ],
        compiler_params=pltpu.CompilerParams(vmem_limit_bytes=56 << 20),
        cost_estimate=pl.CostEstimate(
            flops=10 * heads * length * length * dim,
            bytes_accessed=6 << 20,
            transcendentals=heads * length * length,
        ),
    )(proj, kt, lse, da, rel_bias)


def shards(
    tokens,
    gain_attn,
    w_qkv,
    w_proj,
    rel_bias,
    gain_ffn,
    w_router,
    w_in,
    w_out,
    routes,
    segment_ids,
    cotangent,
):
    length, width = tokens.shape
    experts = w_router.shape[1]
    capacity = max(2, 3 * length // (2 * experts))
    heads_here = rel_bias.shape[0]
    inner_here = w_proj.shape[0]
    head_dim = inner_here // heads_here
    scale = head_dim ** (-0.5)
    members = lax.axis_size("tensor")
    groups = lax.axis_size("expert")
    member = lax.axis_index("tensor")
    group = lax.axis_index("expert")
    share = capacity // members
    segments = segment_ids[0]
    route = routes[:, 0]

    def swap(value, bit):
        return lax.ppermute(value, "tensor", [(i, i ^ bit) for i in range(members)])

    bits = [1 << i for i in range(members.bit_length() - 1)]

    def gather_members(value):
        blocks = {0: value}
        for bit in reversed(bits):
            blocks.update({k ^ bit: swap(block, bit) for k, block in blocks.items()})
        return [blocks[k] for k in range(members)]

    def sum_members(parts):
        held = dict(enumerate(parts))
        for bit in bits:
            for k in [k for k in held if k & bit]:
                held[k ^ bit] = held[k ^ bit] + swap(held.pop(k).astype(BF16), bit).astype(F32)
        return held[0]

    def gather_groups(value):
        copies = jnp.broadcast_to(value[None], (groups,) + value.shape)
        return exchange(copies)

    def exchange(value):
        return lax.all_to_all(value, "expert", split_axis=0, concat_axis=0, tiled=True)

    tie = lax.optimization_barrier

    expert_ids = jnp.arange(experts, dtype=jnp.int32)
    onehot_low = (route[:, None] == expert_ids[None, :]).astype(BF16)
    onehot = onehot_low.astype(F32)
    positions = jnp.arange(length, dtype=jnp.int32)
    lower_ones = (positions[:, None] >= positions[None, :]).astype(BF16)
    running = nn_dot(lower_ones, onehot_low)
    slot = (jnp.sum(running * onehot, 1) - 1.0).astype(jnp.int32)
    flat_id = route * capacity + slot

    def ids_of(owner):
        slots = owner * share + jnp.arange(share, dtype=jnp.int32)
        return (expert_ids[:, None] * capacity + slots[None, :]).reshape(-1)

    send_table = (ids_of(member)[:, None] == flat_id[None, :]).astype(BF16)
    all_ids = jnp.concatenate([ids_of(member ^ k) for k in range(members)])
    back_table = (flat_id[:, None] == all_ids[None, :]).astype(BF16)

    w_proj_all = jnp.concatenate(gather_members(w_proj), 0)

    residual = tokens.astype(F32)
    normed1 = norm_rows(residual, gain_attn).astype(BF16)
    tail = PAD - inner_here
    w_pad = jnp.pad(w_qkv, ((0, 0), (0, 0), (0, tail)))
    w_all = jnp.concatenate([w_pad[0], w_pad[1], w_pad[2]], 1)
    documents = segments[:, None] == jnp.arange(tail, dtype=jnp.int32)[None, :]
    first_lane = jnp.zeros((length, inner_here), F32)
    extra = jnp.concatenate(
        [
            first_lane,
            jnp.where(documents, 0.0, MASKED),
            first_lane,
            documents.astype(F32),
            jnp.zeros((length, PAD), F32),
        ],
        1,
    ).astype(BF16)
    factors = jnp.where(jnp.arange(3 * PAD) < PAD, scale, 1.0).astype(BF16)
    proj = nn_dot(normed1, w_all).astype(BF16) * factors[None, :] + extra
    kvt = jnp.einsum("tdi,sd->tis", w_qkv[1:], normed1, preferred_element_type=F32).astype(BF16)
    def dispatch(rows):
        out = nn_dot(send_table, rows).astype(BF16).reshape(groups, -1, width)
        return exchange(out).reshape(-1, width)

    cot_share = dispatch(cotangent)
    proj, cot_share, w_proj_all = tie((proj, cot_share, w_proj_all))
    attended_t, lse = attend(proj, kvt[1], rel_bias, head_dim)
    w_in_all = gather_members(w_in[0])
    attended_t, w_in_all = tie((attended_t, w_in_all))

    attended_blocks = gather_members(attended_t)
    attended_blocks, w_out_here = tie((attended_blocks, w_out[0]))
    attended_all = jnp.concatenate(attended_blocks, 0)
    head_out = lax.dot_general(
        attended_all, w_proj_all, (((0,), (0,)), ((), ())), preferred_element_type=F32
    )
    hidden1 = residual + head_out
    normed2 = norm_rows(hidden1, gain_ffn).astype(BF16)
    logits = nn_dot(normed2, w_router)
    router_probs = jax.nn.softmax(logits, -1)
    gate = jnp.sum(router_probs * onehot, -1)
    grad_out = cotangent.astype(F32)

    w_out_all = gather_members(w_out_here)
    rows = dispatch(normed2)
    rows, w_out_all = tie((rows, w_out_all))

    every = range(members)

    def tn_dot(left, right):
        return lax.dot_general(left, right, (((0,), (0,)), ((), ())), preferred_element_type=F32)

    def gathered(value):
        return gather_members(exchange(value.reshape(groups, -1, width)).reshape(-1, width))

    def home(blocks):
        return nn_dot(back_table, jnp.concatenate(blocks, 0)).astype(BF16).astype(F32)

    slot_probs = jax.nn.softmax(nn_dot(rows, w_router), -1)
    own = (expert_ids == group).astype(F32)[None, :]
    slot_gate = jnp.sum(slot_probs * own, -1, keepdims=True)
    cot_values = cot_share.astype(F32)
    grad_rows = (slot_gate * cot_values).astype(BF16)
    pre = [nn_dot(rows, w_in_all[k]) for k in every]
    act = [jax.nn.gelu(pre[k]).astype(BF16) for k in every]
    reply = sum(nn_dot(act[k], w_out_all[k]) for k in every).astype(BF16)
    slot_gate_grad = jnp.sum(cot_values * reply.astype(F32), -1, keepdims=True)
    slot_logit_grad = (slot_probs * (own - slot_gate) * slot_gate_grad).astype(BF16)
    grad_pre = []
    for k in every:
        unused_act, gelu_pull = jax.vjp(jax.nn.gelu, pre[k])
        grad_pre.append(gelu_pull(nt_dot(grad_rows, w_out_all[k]))[0].astype(BF16))
    grad_share = sum(nt_dot(grad_pre[k], w_in_all[k]) for k in every)
    grad_share = (grad_share + nt_dot(slot_logit_grad, w_router)).astype(BF16)
    grad_back = exchange(grad_share.reshape(groups, -1, width)).reshape(-1, width)
    grad_w_out = sum_members([tn_dot(act[k], grad_rows) for k in every])
    grad_back, grad_w_out = tie((grad_back, grad_w_out))
    grad_blocks = gather_members(grad_back)
    grad_blocks, rows_later, grad_pre = tie((grad_blocks, rows, grad_pre))
    grad_normed2 = home(grad_blocks)
    unused_norm, norm_pull = jax.vjp(norm_rows, hidden1, gain_ffn)
    back_hidden, grad_gain_ffn = norm_pull(grad_normed2)
    grad_hidden1 = grad_out + back_hidden
    out_grad = grad_hidden1.astype(BF16)
    w_proj_pad = jnp.pad(w_proj, ((0, tail), (0, 0)))
    attended_grad = nt_dot(out_grad, w_proj_pad).astype(BF16)
    attended_grad, reply = tie((attended_grad, reply))

    reply_back = exchange(reply.reshape(groups, -1, width)).reshape(-1, width)
    grad_w_in = sum_members([tn_dot(rows_later, grad_pre[k]) for k in every])
    grad_proj = nn_dot(attended_t, out_grad).astype(BF16)
    grad_proj = lax.psum(grad_proj, "expert").astype(F32)

    stacked_grad, rel_parts = attend_back(proj, kvt[0], lse, attended_grad, rel_bias, head_dim)
    stacked_grad, grad_w_in, reply_back = tie((stacked_grad, grad_w_in, reply_back))
    normed1_part = jnp.einsum("tsi,tdi->sd", stacked_grad, w_qkv, preferred_element_type=F32)
    grad_qkv_t = jnp.einsum("tsi,sd->tid", stacked_grad, normed1, preferred_element_type=F32)
    grad_qkv_t = lax.psum(grad_qkv_t.reshape(3 * inner_here, width).astype(BF16), "expert").astype(F32)
    grad_qkv = jnp.swapaxes(grad_qkv_t.reshape(3, inner_here, width), 1, 2)
    inverse = lax.rsqrt(jnp.mean(residual * residual, -1, keepdims=True) + 1e-06)

    halves = normed1_part.reshape(2, length // 2, width)
    low_bit = member & 1
    kept = lax.dynamic_index_in_dim(halves, low_bit, 0, False)
    sent = lax.dynamic_index_in_dim(halves, 1 - low_bit, 0, False)
    kept = kept + swap(sent.astype(BF16), 1).astype(F32)
    for bit in bits[1:]:
        kept = kept + swap(kept.astype(BF16), bit).astype(F32)
    kept, reply_back = tie((kept.astype(BF16), reply_back))
    other = swap(kept, 1)
    grad_normed1 = jnp.concatenate(
        [jnp.where(low_bit == 0, kept, other), jnp.where(low_bit == 0, other, kept)], 0
    ).astype(F32)
    gain_part = jnp.sum(grad_normed1 * residual * inverse, 0, keepdims=True)
    scaled = gain_attn * grad_normed1
    correction = jnp.mean(residual * scaled, -1, keepdims=True)
    grad_input = grad_hidden1 + inverse * scaled - residual * (inverse**3 * correction)

    returned = home(gather_members(reply_back))
    output = (hidden1 + gate[:, None] * returned).astype(BF16)
    gate_grad = jnp.sum(grad_out * returned, -1)
    prob_grad = onehot * gate_grad[:, None]
    logit_grad = router_probs * (prob_grad - jnp.sum(prob_grad * router_probs, -1, keepdims=True))
    grad_router = jnp.dot(normed2.astype(F32).T, logit_grad, precision=HIGH)
    rel_row = jnp.sum(rel_parts, -1).reshape(1, -1)
    rel_row = jnp.pad(rel_row, ((0, 0), (0, width - rel_row.shape[1])))
    small = jnp.concatenate([grad_gain_ffn[None], gain_part, rel_row, grad_router.T], 0)
    small = jnp.sum(gather_groups(small), 0)
    grad_gain_ffn, grad_gain_attn = small[0], small[1]
    grad_rel = small[2, : rel_bias.size].reshape(rel_bias.shape)
    grad_router = small[3:].T
    return (
        output,
        grad_input,
        grad_gain_attn,
        grad_qkv,
        grad_proj,
        grad_rel,
        grad_gain_ffn,
        grad_router,
        grad_w_in[None],
        grad_w_out[None],
    )


def solution(mesh):
    placed = (
        P("expert", None),
        P(),
        P(None, None, "tensor"),
        P("tensor", None),
        P("tensor", None),
        P(),
        P(),
        P("expert", None, "tensor"),
        P("expert", "tensor", None),
        P("expert", None),
        P("expert", None),
        P("expert", None),
    )
    return jax.shard_map(
        shards,
        mesh=mesh,
        in_specs=placed,
        out_specs=(
            P("expert", None),
            P("expert", None),
            P(),
            P(None, None, "tensor"),
            P("tensor", None),
            P("tensor", None),
            P(),
            P(),
            P("expert", None, "tensor"),
            P("expert", "tensor", None),
        ),
        check_vma=False,
    )
```

```python
import functools

import jax
import jax.numpy as jnp
from jax import lax
from jax.experimental import pallas as pl
from jax.experimental.pallas import tpu as pltpu
from jax.sharding import PartitionSpec as P

FAR_LIMITS = (12, 16, 23, 32, 46, 64, 91)
HIGH = lax.Precision.HIGHEST
F32 = jnp.float32
BF16 = jnp.bfloat16
MASKED = -1e30
QB = 256
PAD = 256
FAR = FAR_LIMITS[-1]

STEPS = (
    [(1 - limit, 14 - i) for i, limit in enumerate(reversed(FAR_LIMITS))]
    + [(-n, n) for n in range(7, -1, -1)]
    + [(n, 16 + n) for n in range(1, 8)]
    + [(8, 24)]
    + [(limit, 25 + i) for i, limit in enumerate(FAR_LIMITS)]
)


def norm_rows(values, gain):
    return values * lax.rsqrt(jnp.mean(values * values, -1, keepdims=True) + 1e-06) * gain


def nt_dot(left, right):
    return lax.dot_general(left, right, (((1,), (1,)), ((), ())), preferred_element_type=F32)


def nn_dot(left, right):
    return jnp.dot(left, right, preferred_element_type=F32)


def strip_shape(length):
    return 2 * length - QB


def near_rows(length):
    base = length - QB
    first = (base - FAR) // 32 * 32
    last = -(-(base + 127 + FAR) // 32) * 32
    return base, first, last


def build_strip(strip_ref, bias_ref, length, heads):
    total = strip_shape(length)
    base, first, last = near_rows(length)
    for h in range(heads):
        low = jnp.full((8, 128), bias_ref[h, 15], F32)
        high = jnp.full((8, 128), bias_ref[h, 31], F32)
        for half in range(QB // 128):
            cols = slice(half * 128, half * 128 + 128)
            lo_end, hi_start = first + half * 128, last + half * 128
            strip_ref[h, 0:lo_end, cols] = jnp.broadcast_to(low[:1], (lo_end, 128))
            strip_ref[h, hi_start:total, cols] = jnp.broadcast_to(high[:1], (total - hi_start, 128))
    for start in range(first, last, 32):
        offset = (
            lax.broadcasted_iota(jnp.int32, (32, 128), 0)
            - lax.broadcasted_iota(jnp.int32, (32, 128), 1)
            + (start - base)
        )
        tiles = [jnp.full((32, 128), bias_ref[h, 15], F32) for h in range(heads)]
        for begin, bucket in STEPS:
            reached = offset >= begin
            tiles = [jnp.where(reached, bias_ref[h, bucket], tiles[h]) for h in range(heads)]
        for h in range(heads):
            for half in range(QB // 128):
                at = start + half * 128
                strip_ref[h, at : at + 32, half * 128 : half * 128 + 128] = tiles[h]


def head_lanes(rows, h, dim, keep_tail, heads):
    lane = lax.broadcasted_iota(jnp.int32, (rows, PAD), 1)
    inside = (lane >= h * dim) & (lane < (h + 1) * dim)
    if keep_tail:
        inside = inside | (lane >= heads * dim)
    return inside


def attend_kernel(
    length, heads, dim,
    x_ref, gain_ref, w_ref, doc_ref, bias_ref,
    att_ref, lse_ref, proj_ref, kt_ref, normed_ref,
    kh_ref, strip_ref, vt_ref, pad_ref,
):
    inner = heads * dim
    build_strip(strip_ref, bias_ref, length, heads)
    lane = lax.broadcasted_iota(jnp.int32, (QB, PAD), 1) - inner
    pad_ref[...] = jnp.zeros_like(pad_ref)
    for t in range(3):
        pad_ref[:, t * PAD : t * PAD + inner] = w_ref[t]

    def project(b, carry):
        at = pl.multiple_of(b * QB, QB)
        here = x_ref[pl.ds(at, QB), :].astype(F32)
        normed = norm_rows(here, gain_ref[...]).astype(BF16)
        normed_ref[pl.ds(at, QB), :] = normed
        every = nn_dot(normed, pad_ref[...])
        same = doc_ref[pl.ds(at, QB), :] == lane
        queries = (every[:, 0:PAD].astype(BF16) * jnp.bfloat16(dim ** (-0.5))).astype(F32)
        queries = queries + jnp.where((lane < 0) | same, 0.0, MASKED)
        keys = every[:, PAD : 2 * PAD]
        values = every[:, 2 * PAD : 3 * PAD]
        proj_ref[pl.ds(at, QB), 0:PAD] = queries.astype(BF16)
        proj_ref[pl.ds(at, QB), PAD : 2 * PAD] = (keys + jnp.where(same, 1.0, 0.0)).astype(BF16)
        proj_ref[pl.ds(at, QB), 2 * PAD : 3 * PAD] = values.astype(BF16)
        kt_ref[:, pl.ds(at, QB)] = keys.T[:inner].astype(BF16)
        vt_ref[:, pl.ds(at, QB)] = values.T[:inner].astype(BF16)
        return carry

    lax.fori_loop(0, length // QB, project, 0)
    keys = proj_ref[:, PAD : 2 * PAD]
    for h in range(heads):
        kh_ref[h] = jnp.where(head_lanes(length, h, dim, True, heads), keys, jnp.zeros_like(keys))

    def block(b, carry):
        at = pl.multiple_of(b * QB, QB)
        from_row = pl.multiple_of(length - QB - b * QB, QB)
        queries = proj_ref[pl.ds(at, QB), 0:PAD]
        for h in range(heads):
            scores = nt_dot(kh_ref[h], queries) + strip_ref[h, pl.ds(from_row, length), :]
            top = jnp.max(scores, 0, keepdims=True)
            probs = jnp.exp(scores - top)
            total = jnp.sum(probs, 0, keepdims=True)
            out = nn_dot(vt_ref[h * dim : (h + 1) * dim, :], probs.astype(BF16))
            att_ref[h * dim : (h + 1) * dim, pl.ds(at, QB)] = (out / total).astype(BF16)
            lse_ref[h : h + 1, pl.ds(at, QB)] = top + jnp.log(total)
        return carry

    lax.fori_loop(0, length // QB, block, 0)


def attend_back_kernel(
    length, heads, dim,
    proj_ref, kt_ref, lse_ref, da_ref, normed_ref, w_ref, bias_ref, low_ref,
    grad_ref, kept_ref, sent_ref, drel_ref,
    kh_ref, vh_ref, strip_ref, dstrip_ref, pcat_ref, dcat_ref, dacat_ref, qcat_ref, dk_ref, dv_ref, dqt_ref,
    dq_ref, pad_ref,
):
    inner = heads * dim
    scale = dim ** (-0.5)
    total = strip_shape(length)
    base, first, last = near_rows(length)
    build_strip(strip_ref, bias_ref, length, heads)
    dstrip_ref[...] = jnp.zeros_like(dstrip_ref)
    dk_ref[...] = jnp.zeros_like(dk_ref)
    dv_ref[...] = jnp.zeros_like(dv_ref)
    dqt_ref[...] = jnp.zeros_like(dqt_ref)
    keys = proj_ref[:, PAD : 2 * PAD]
    values = proj_ref[:, 2 * PAD : 3 * PAD]
    for h in range(heads):
        kh_ref[h] = jnp.where(head_lanes(length, h, dim, True, heads), keys, jnp.zeros_like(keys))
        vh_ref[h] = jnp.where(head_lanes(length, h, dim, False, heads), values, jnp.zeros_like(values))

    def block(b, carry):
        at = pl.multiple_of(b * QB, QB)
        from_row = pl.multiple_of(length - QB - b * QB, QB)
        queries = proj_ref[pl.ds(at, QB), 0:PAD]
        grads = da_ref[pl.ds(at, QB), :]
        for h in range(heads):
            mine = head_lanes(QB, h, dim, False, heads)
            cols = slice(h * QB, (h + 1) * QB)
            qcat_ref[cols, :] = jnp.where(mine, queries, jnp.zeros_like(queries))
            dacat_ref[cols, :] = jnp.where(mine, grads, jnp.zeros_like(grads))
            scores = nt_dot(kh_ref[h], queries) + strip_ref[h, pl.ds(from_row, length), :]
            probs = jnp.exp(scores - lse_ref[h : h + 1, pl.ds(at, QB)])
            weighted = probs * nt_dot(vh_ref[h], grads)
            delta = jnp.sum(weighted, 0, keepdims=True)
            dscore = weighted - probs * delta
            dstrip_ref[h, pl.ds(from_row, length), :] += dscore
            dlow = dscore.astype(BF16)
            pcat_ref[:, cols] = probs.astype(BF16)
            dcat_ref[:, cols] = dlow
            dqt_ref[h * dim : (h + 1) * dim, :] = nn_dot(kt_ref[h * dim : (h + 1) * dim, :], dlow) * scale
        dk_ref[...] += nn_dot(dcat_ref[...], qcat_ref[...])
        dv_ref[...] += nn_dot(pcat_ref[...], dacat_ref[...])
        dq_ref[pl.ds(at, QB), :] = dqt_ref[...].T
        return carry

    lax.fori_loop(0, length // QB, block, 0)

    for t, ref in enumerate((dq_ref, dk_ref, dv_ref)):
        turned = ref[...].T[:inner].astype(BF16)
        grad_ref[t * inner : (t + 1) * inner, :] = nn_dot(turned, normed_ref[...]).astype(BF16)

    pad_ref[...] = jnp.zeros_like(pad_ref)
    for t in range(3):
        pad_ref[t, :, 0:inner] = w_ref[t]
    half = length // 2

    def part(start):
        total = jnp.zeros((QB, w_ref.shape[1]), F32)
        for t, ref in enumerate((dq_ref, dk_ref, dv_ref)):
            total = total + nt_dot(ref[pl.ds(start, QB), :].astype(BF16), pad_ref[t])
        return total

    for i in range(half // QB):
        rows = slice(i * QB, (i + 1) * QB)
        kept_ref[rows, :] = part(pl.multiple_of(low_ref[0] * half + i * QB, QB))
        sent_ref[rows, :] = part(pl.multiple_of((1 - low_ref[0]) * half + i * QB, QB)).astype(BF16)

    offset = (
        lax.broadcasted_iota(jnp.int32, (last - first, 128), 0)
        - lax.broadcasted_iota(jnp.int32, (last - first, 128), 1)
        + (first - base)
    )
    begins = [-(1 << 20)] + [begin for begin, bucket in STEPS] + [1 << 20]
    buckets = [15] + [bucket for begin, bucket in STEPS]
    for h in range(heads):
        near = jnp.zeros((last - first, 128), F32)
        low = jnp.zeros((1, 128), F32)
        high = jnp.zeros((1, 128), F32)
        for half in range(QB // 128):
            cols = slice(half * 128, half * 128 + 128)
            lo_end, hi_start = first + half * 128, last + half * 128
            near = near + dstrip_ref[h, lo_end:hi_start, cols]
            low = low + jnp.sum(dstrip_ref[h, 0:lo_end, cols], 0, keepdims=True)
            high = high + jnp.sum(dstrip_ref[h, hi_start:total, cols], 0, keepdims=True)
        drel_ref[h, 16:17, :] = jnp.zeros((1, 128), F32)
        for i, bucket in enumerate(buckets):
            inside = (offset >= begins[i]) & (offset < begins[i + 1])
            row = jnp.sum(jnp.where(inside, near, 0.0), 0, keepdims=True)
            if bucket == 15:
                row = row + low
            if bucket == 31:
                row = row + high
            drel_ref[h, bucket : bucket + 1, :] = row


def whole_vmem(count):
    return [pl.BlockSpec(memory_space=pltpu.VMEM)] * count


def attend(tokens, gain, w_qkv, segments, rel_bias):
    length, width = tokens.shape
    heads = rel_bias.shape[0]
    inner = w_qkv.shape[2]
    return pl.pallas_call(
        functools.partial(attend_kernel, length, heads, inner // heads),
        out_shape=(
            jax.ShapeDtypeStruct((inner, length), BF16),
            jax.ShapeDtypeStruct((8, length), F32),
            jax.ShapeDtypeStruct((length, 3 * PAD), BF16),
            jax.ShapeDtypeStruct((inner, length), BF16),
            jax.ShapeDtypeStruct((length, width), BF16),
        ),
        in_specs=whole_vmem(4) + [pl.BlockSpec(memory_space=pltpu.SMEM)],
        out_specs=tuple(whole_vmem(5)),
        scratch_shapes=[
            pltpu.VMEM((heads, length, PAD), BF16),
            pltpu.VMEM((heads, strip_shape(length), QB), F32),
            pltpu.VMEM((inner, length), BF16),
            pltpu.VMEM((width, 3 * PAD), BF16),
        ],
        compiler_params=pltpu.CompilerParams(vmem_limit_bytes=48 << 20),
        cost_estimate=pl.CostEstimate(
            flops=4 * heads * length * length * PAD + 6 * length * width * PAD,
            bytes_accessed=8 << 20,
            transcendentals=heads * length * length,
        ),
    )(tokens, gain[None, :], w_qkv, segments[:, None], rel_bias)


def attend_back(proj, kt, lse, da, normed, w_qkv, rel_bias, low_bit):
    length, width = normed.shape
    heads, buckets = rel_bias.shape
    inner = w_qkv.shape[2]
    return pl.pallas_call(
        functools.partial(attend_back_kernel, length, heads, inner // heads),
        out_shape=(
            jax.ShapeDtypeStruct((3 * inner, width), BF16),
            jax.ShapeDtypeStruct((length // 2, width), F32),
            jax.ShapeDtypeStruct((length // 2, width), BF16),
            jax.ShapeDtypeStruct((heads, buckets, 128), F32),
        ),
        in_specs=whole_vmem(6) + [pl.BlockSpec(memory_space=pltpu.SMEM)] * 2,
        out_specs=tuple(whole_vmem(4)),
        scratch_shapes=[
            pltpu.VMEM((heads, length, PAD), BF16),
            pltpu.VMEM((heads, length, PAD), BF16),
            pltpu.VMEM((heads, strip_shape(length), QB), F32),
            pltpu.VMEM((heads, strip_shape(length), QB), F32),
            pltpu.VMEM((length, heads * QB), BF16),
            pltpu.VMEM((length, heads * QB), BF16),
            pltpu.VMEM((heads * QB, PAD), BF16),
            pltpu.VMEM((heads * QB, PAD), BF16),
            pltpu.VMEM((length, PAD), F32),
            pltpu.VMEM((length, PAD), F32),
            pltpu.VMEM((PAD, QB), F32),
            pltpu.VMEM((length, PAD), F32),
            pltpu.VMEM((3, width, PAD), BF16),
        ],
        compiler_params=pltpu.CompilerParams(vmem_limit_bytes=56 << 20),
        cost_estimate=pl.CostEstimate(
            flops=10 * heads * length * length * PAD + 12 * length * width * PAD,
            bytes_accessed=12 << 20,
            transcendentals=heads * length * length,
        ),
    )(proj, kt, lse, da, normed, w_qkv, rel_bias, low_bit)


def gelu_pair(v):
    inner = 0.7978845608028654 * (v + 0.044715 * (v * v * v))
    bend = jnp.tanh(inner)
    half = 0.5 * (1.0 + bend)
    slope = half + 0.5 * v * (1.0 - bend * bend) * (0.7978845608028654 * (1.0 + 0.134145 * (v * v)))
    return v * half, slope


def expert_kernel(
    members, experts,
    rows_ref, cot_ref, router_ref, group_ref, *refs,
):
    first, second = refs[:members], refs[members : 2 * members]
    reply_ref, share_ref, act_ref, gpre_ref, grad_ref, grouter_ref = refs[2 * members :]
    rows = rows_ref[...]
    count = rows.shape[0]
    lane = lax.broadcasted_iota(jnp.int32, (count, 128), 1)
    logits = jnp.where(lane < experts, nn_dot(rows, router_ref[...]), MASKED)
    raised = jnp.exp(logits - jnp.max(logits, -1, keepdims=True))
    probs = raised / jnp.sum(raised, -1, keepdims=True)
    own = jnp.where(lane == group_ref[0], 1.0, 0.0)
    gate = jnp.sum(probs * own, -1, keepdims=True)
    cot = cot_ref[...].astype(F32)
    grads = (gate * cot).astype(BF16)
    grad_ref[...] = grads
    reply = jnp.zeros(rows.shape, F32)
    share = jnp.zeros(rows.shape, F32)
    for k in range(members):
        act, slope = gelu_pair(nn_dot(rows, first[k][...]))
        act = act.astype(BF16)
        act_ref[k] = act
        reply = reply + nn_dot(act, second[k][...])
        gpre = (nt_dot(grads, second[k][...]) * slope).astype(BF16)
        gpre_ref[k] = gpre
        share = share + nt_dot(gpre, first[k][...])
    reply = reply.astype(BF16)
    reply_ref[...] = reply
    gate_grad = jnp.sum(cot * reply.astype(F32), -1, keepdims=True)
    logit_grad = probs * (own - gate) * gate_grad
    share_ref[...] = (share + nt_dot(logit_grad.astype(BF16), router_ref[...])).astype(BF16)
    grouter_ref[...] = nn_dot(logit_grad.T.astype(BF16), rows)


def expert_step(rows, cot, w_router, group, first, second):
    members = len(first)
    count, width = rows.shape
    hidden = first[0].shape[1]
    experts = w_router.shape[1]
    router = jnp.pad(w_router, ((0, 0), (0, 128 - experts)))
    return pl.pallas_call(
        functools.partial(expert_kernel, members, experts),
        out_shape=(
            jax.ShapeDtypeStruct((count, width), BF16),
            jax.ShapeDtypeStruct((count, width), BF16),
            jax.ShapeDtypeStruct((members, count, hidden), BF16),
            jax.ShapeDtypeStruct((members, count, hidden), BF16),
            jax.ShapeDtypeStruct((count, width), BF16),
            jax.ShapeDtypeStruct((128, width), F32),
        ),
        in_specs=whole_vmem(3) + [pl.BlockSpec(memory_space=pltpu.SMEM)] + whole_vmem(2 * members),
        out_specs=tuple(whole_vmem(6)),
        compiler_params=pltpu.CompilerParams(vmem_limit_bytes=48 << 20),
        cost_estimate=pl.CostEstimate(
            flops=8 * members * count * width * hidden,
            bytes_accessed=20 << 20,
            transcendentals=members * count * hidden,
        ),
    )(rows, cot, router, group, *first, *second)


def shards(
    tokens,
    gain_attn,
    w_qkv,
    w_proj,
    rel_bias,
    gain_ffn,
    w_router,
    w_in,
    w_out,
    routes,
    segment_ids,
    cotangent,
):
    length, width = tokens.shape
    experts = w_router.shape[1]
    capacity = max(2, 3 * length // (2 * experts))
    heads_here = rel_bias.shape[0]
    inner_here = w_proj.shape[0]
    head_dim = inner_here // heads_here
    scale = head_dim ** (-0.5)
    members = lax.axis_size("tensor")
    groups = lax.axis_size("expert")
    member = lax.axis_index("tensor")
    group = lax.axis_index("expert")
    share = capacity // members
    segments = segment_ids[0]
    route = routes[:, 0]

    def swap(value, bit):
        return lax.ppermute(value, "tensor", [(i, i ^ bit) for i in range(members)])

    bits = [1 << i for i in range(members.bit_length() - 1)]

    def gather_far(value):
        blocks = {0: value}
        for bit in reversed(bits[1:]):
            blocks.update({k ^ bit: swap(block, bit) for k, block in blocks.items()})
        return blocks

    def gather_near(blocks):
        blocks = dict(blocks)
        for bit in bits[:1]:
            blocks.update({k ^ bit: swap(block, bit) for k, block in blocks.items()})
        return [blocks[k] for k in range(members)]

    def gather_members(value):
        return gather_near(gather_far(value))

    def sum_near(parts):
        held = dict(enumerate(parts))
        for bit in bits[:1]:
            for k in [k for k in held if k & bit]:
                held[k ^ bit] = held[k ^ bit] + swap(held.pop(k).astype(BF16), bit).astype(F32)
        return held

    def sum_far(held, sent):
        held = dict(held)
        for bit in bits[1:]:
            for k in [k for k in held if k & bit]:
                there = sent[k] if bit == bits[1] else held[k].astype(BF16)
                held[k ^ bit] = held[k ^ bit] + swap(there, bit).astype(F32)
                held.pop(k)
        return held[0]

    def gather_groups(value):
        copies = jnp.broadcast_to(value[None], (groups,) + value.shape)
        return exchange(copies)

    def exchange(value):
        return lax.all_to_all(value, "expert", split_axis=0, concat_axis=0, tiled=True)

    tie = lax.optimization_barrier

    expert_ids = jnp.arange(experts, dtype=jnp.int32)
    onehot_low = (route[:, None] == expert_ids[None, :]).astype(BF16)
    onehot = onehot_low.astype(F32)
    positions = jnp.arange(length, dtype=jnp.int32)
    lower_ones = (positions[:, None] >= positions[None, :]).astype(BF16)
    running = nn_dot(lower_ones, onehot_low)
    slot = (jnp.sum(running * onehot, 1) - 1.0).astype(jnp.int32)
    flat_id = route * capacity + slot

    def ids_of(owner):
        slots = owner * share + jnp.arange(share, dtype=jnp.int32)
        return (expert_ids[:, None] * capacity + slots[None, :]).reshape(-1)

    send_table = (ids_of(member)[:, None] == flat_id[None, :]).astype(BF16)
    all_ids = jnp.concatenate([ids_of(member ^ k) for k in range(members)])
    back_table = (flat_id[:, None] == all_ids[None, :]).astype(BF16)

    def dispatch(rows):
        out = nn_dot(send_table, rows).astype(BF16).reshape(groups, -1, width)
        return exchange(out).reshape(-1, width)

    residual = tokens.astype(F32)
    cot_share = dispatch(cotangent)
    w_proj_far = gather_far(w_proj)
    w_in_far = gather_far(w_in[0])
    attended_t, lse, proj, keys_t, normed1 = attend(tokens, gain_attn, w_qkv, segments, rel_bias)
    attended_t, w_proj_far, w_in_far, cot_share = tie((attended_t, w_proj_far, w_in_far, cot_share))

    attended_blocks = gather_members(attended_t)
    attended_blocks, w_out_here = tie((attended_blocks, w_out[0]))
    w_proj_all = jnp.concatenate(gather_near(w_proj_far), 0)
    w_in_all = gather_near(w_in_far)
    attended_all = jnp.concatenate(attended_blocks, 0)
    head_out = lax.dot_general(
        attended_all, w_proj_all, (((0,), (0,)), ((), ())), preferred_element_type=F32
    )
    hidden1 = residual + head_out
    normed2 = norm_rows(hidden1, gain_ffn).astype(BF16)
    logits = nn_dot(normed2, w_router)
    router_probs = jax.nn.softmax(logits, -1)
    gate = jnp.sum(router_probs * onehot, -1)
    grad_out = cotangent.astype(F32)

    w_out_far = gather_far(w_out_here)
    rows = dispatch(normed2)
    rows, w_out_far = tie((rows, w_out_far))
    w_out_all = gather_near(w_out_far)

    every = range(members)

    def tn_dot(left, right):
        return lax.dot_general(left, right, (((0,), (0,)), ((), ())), preferred_element_type=F32)

    def gathered(value):
        return gather_members(exchange(value.reshape(groups, -1, width)).reshape(-1, width))

    def home(blocks):
        return nn_dot(back_table, jnp.concatenate(blocks, 0)).astype(BF16).astype(F32)

    reply, grad_share, act, grad_pre, grad_rows, grad_router = expert_step(
        rows, cot_share, w_router, group[None], w_in_all, w_out_all
    )
    grad_back = exchange(grad_share.reshape(groups, -1, width)).reshape(-1, width)
    out_held = sum_near([tn_dot(act[k], grad_rows) for k in every])
    in_held = sum_near([tn_dot(rows, grad_pre[k]) for k in every])
    out_sent = {k: held.astype(BF16) for k, held in out_held.items() if k}
    in_sent = {k: held.astype(BF16) for k, held in in_held.items() if k}
    grad_back, out_sent, in_sent = tie((grad_back, out_sent, in_sent))
    grad_blocks = gather_members(grad_back)
    grad_blocks, out_sent, in_sent = tie((grad_blocks, out_sent, in_sent))
    grad_w_out = sum_far(out_held, out_sent)
    grad_w_in = sum_far(in_held, in_sent)
    grad_router = grad_router[:experts]
    for bit in bits:
        grad_router = grad_router + swap(grad_router, bit)
    grad_normed2 = home(grad_blocks)
    unused_norm, norm_pull = jax.vjp(norm_rows, hidden1, gain_ffn)
    back_hidden, grad_gain_ffn = norm_pull(grad_normed2)
    grad_hidden1 = grad_out + back_hidden
    out_grad = grad_hidden1.astype(BF16)
    w_proj_pad = jnp.pad(w_proj, ((0, PAD - inner_here), (0, 0)))
    attended_grad = nt_dot(out_grad, w_proj_pad).astype(BF16)
    attended_grad, reply = tie((attended_grad, reply))

    grad_proj = nn_dot(attended_t, out_grad).astype(BF16)
    riders = jnp.concatenate(
        [reply.reshape(groups, -1, width), grad_proj.reshape(groups, -1, width)], 1
    )
    riders = exchange(riders)

    low_bit = member & 1
    grad_qkv, kept, sent, rel_parts = attend_back(
        proj, keys_t, lse, attended_grad, normed1, w_qkv, rel_bias, low_bit[None]
    )
    grad_qkv, kept, sent, grad_w_in, grad_w_out, riders = tie(
        (grad_qkv, kept, sent, grad_w_in, grad_w_out, riders)
    )
    reply_back = riders[:, : reply.shape[0] // groups].reshape(-1, width)
    proj_mine = jnp.sum(riders[:, reply.shape[0] // groups :].astype(F32), 0).astype(BF16)
    qkv_mine = exchange(grad_qkv.reshape(groups, -1, width))
    qkv_mine = jnp.sum(qkv_mine.astype(F32), 0).astype(BF16)
    totals = gather_groups(jnp.concatenate([qkv_mine, proj_mine], 0))
    grad_qkv = totals[:, : qkv_mine.shape[0]].reshape(3, inner_here, width).astype(F32)
    grad_qkv = jnp.swapaxes(grad_qkv, 1, 2)
    grad_proj = totals[:, qkv_mine.shape[0] :].reshape(inner_here, width).astype(F32)

    inverse = lax.rsqrt(jnp.mean(residual * residual, -1, keepdims=True) + 1e-06)
    kept = kept + swap(sent, 1).astype(F32)
    for bit in bits[1:]:
        kept = kept + swap(kept.astype(BF16), bit).astype(F32)
    kept, reply_back = tie((kept.astype(BF16), reply_back))
    other = swap(kept, 1)
    grad_normed1 = jnp.concatenate(
        [jnp.where(low_bit == 0, kept, other), jnp.where(low_bit == 0, other, kept)], 0
    ).astype(F32)
    gain_part = jnp.sum(grad_normed1 * residual * inverse, 0, keepdims=True)
    scaled = gain_attn * grad_normed1
    correction = jnp.mean(residual * scaled, -1, keepdims=True)
    grad_input = grad_hidden1 + inverse * scaled - residual * (inverse**3 * correction)

    returned = home(gather_members(reply_back))
    output = (hidden1 + gate[:, None] * returned).astype(BF16)
    rel_row = jnp.sum(rel_parts, -1).reshape(1, -1)
    rel_row = jnp.pad(rel_row, ((0, 0), (0, width - rel_row.shape[1])))
    small = jnp.concatenate([grad_gain_ffn[None], gain_part, rel_row, grad_router], 0)
    small = jnp.sum(gather_groups(small), 0)
    grad_gain_ffn, grad_gain_attn = small[0], small[1]
    grad_rel = small[2, : rel_bias.size].reshape(rel_bias.shape)
    grad_router = small[3:].T
    return (
        output,
        grad_input,
        grad_gain_attn,
        grad_qkv,
        grad_proj,
        grad_rel,
        grad_gain_ffn,
        grad_router,
        grad_w_in[None],
        grad_w_out[None],
    )


def solution(mesh):
    placed = (
        P("expert", None),
        P(),
        P(None, None, "tensor"),
        P("tensor", None),
        P("tensor", None),
        P(),
        P(),
        P("expert", None, "tensor"),
        P("expert", "tensor", None),
        P("expert", None),
        P("expert", None),
        P("expert", None),
    )
    return jax.shard_map(
        shards,
        mesh=mesh,
        in_specs=placed,
        out_specs=(
            P("expert", None),
            P("expert", None),
            P(),
            P(None, None, "tensor"),
            P("tensor", None),
            P("tensor", None),
            P(),
            P(),
            P("expert", None, "tensor"),
            P("expert", "tensor", None),
        ),
        check_vma=False,
    )
```

```python
import functools

import jax
import jax.numpy as jnp
from jax import lax
from jax.experimental import pallas as pl
from jax.experimental.pallas import tpu as pltpu
from jax.sharding import PartitionSpec as P

FAR_LIMITS = (12, 16, 23, 32, 46, 64, 91)
HIGH = lax.Precision.HIGHEST
F32 = jnp.float32
BF16 = jnp.bfloat16
MASKED = -1e30
QB = 256
PAD = 256
FAR = FAR_LIMITS[-1]

STEPS = (
    [(1 - limit, 14 - i) for i, limit in enumerate(reversed(FAR_LIMITS))]
    + [(-n, n) for n in range(7, -1, -1)]
    + [(n, 16 + n) for n in range(1, 8)]
    + [(8, 24)]
    + [(limit, 25 + i) for i, limit in enumerate(FAR_LIMITS)]
)


def norm_rows(values, gain):
    return values * lax.rsqrt(jnp.mean(values * values, -1, keepdims=True) + 1e-06) * gain


def nt_dot(left, right):
    return lax.dot_general(left, right, (((1,), (1,)), ((), ())), preferred_element_type=F32)


def nn_dot(left, right):
    return jnp.dot(left, right, preferred_element_type=F32)


def strip_shape(length):
    return 2 * length - QB


def near_rows(length):
    base = length - QB
    first = (base - FAR) // 32 * 32
    last = -(-(base + 127 + FAR) // 32) * 32
    return base, first, last


def build_strip(strip_ref, bias_ref, length, heads):
    total = strip_shape(length)
    base, first, last = near_rows(length)
    for h in range(heads):
        low = jnp.full((8, 128), bias_ref[h, 15], F32)
        high = jnp.full((8, 128), bias_ref[h, 31], F32)
        for half in range(QB // 128):
            cols = slice(half * 128, half * 128 + 128)
            lo_end, hi_start = first + half * 128, last + half * 128
            strip_ref[h, 0:lo_end, cols] = jnp.broadcast_to(low[:1], (lo_end, 128))
            strip_ref[h, hi_start:total, cols] = jnp.broadcast_to(high[:1], (total - hi_start, 128))
    for start in range(first, last, 32):
        offset = (
            lax.broadcasted_iota(jnp.int32, (32, 128), 0)
            - lax.broadcasted_iota(jnp.int32, (32, 128), 1)
            + (start - base)
        )
        tiles = [jnp.full((32, 128), bias_ref[h, 15], F32) for h in range(heads)]
        for begin, bucket in STEPS:
            reached = offset >= begin
            tiles = [jnp.where(reached, bias_ref[h, bucket], tiles[h]) for h in range(heads)]
        for h in range(heads):
            for half in range(QB // 128):
                at = start + half * 128
                strip_ref[h, at : at + 32, half * 128 : half * 128 + 128] = tiles[h]


def head_lanes(rows, h, dim, keep_tail, heads):
    lane = lax.broadcasted_iota(jnp.int32, (rows, PAD), 1)
    inside = (lane >= h * dim) & (lane < (h + 1) * dim)
    if keep_tail:
        inside = inside | (lane >= heads * dim)
    return inside


def attend_kernel(
    length, heads, dim,
    x_ref, gain_ref, w_ref, doc_ref, bias_ref,
    att_ref, lse_ref, proj_ref, kt_ref, normed_ref,
    kh_ref, strip_ref, vt_ref, pad_ref,
):
    inner = heads * dim
    build_strip(strip_ref, bias_ref, length, heads)
    lane = lax.broadcasted_iota(jnp.int32, (QB, PAD), 1) - inner
    pad_ref[...] = jnp.zeros_like(pad_ref)
    for t in range(3):
        pad_ref[:, t * PAD : t * PAD + inner] = w_ref[t]

    def project(b, carry):
        at = pl.multiple_of(b * QB, QB)
        here = x_ref[pl.ds(at, QB), :].astype(F32)
        normed = norm_rows(here, gain_ref[...]).astype(BF16)
        normed_ref[pl.ds(at, QB), :] = normed
        every = nn_dot(normed, pad_ref[...])
        same = doc_ref[pl.ds(at, QB), :] == lane
        queries = (every[:, 0:PAD].astype(BF16) * jnp.bfloat16(dim ** (-0.5))).astype(F32)
        queries = queries + jnp.where((lane < 0) | same, 0.0, MASKED)
        keys = every[:, PAD : 2 * PAD]
        values = every[:, 2 * PAD : 3 * PAD]
        proj_ref[pl.ds(at, QB), 0:PAD] = queries.astype(BF16)
        proj_ref[pl.ds(at, QB), PAD : 2 * PAD] = (keys + jnp.where(same, 1.0, 0.0)).astype(BF16)
        proj_ref[pl.ds(at, QB), 2 * PAD : 3 * PAD] = values.astype(BF16)
        kt_ref[:, pl.ds(at, QB)] = keys.T[:inner].astype(BF16)
        vt_ref[:, pl.ds(at, QB)] = values.T[:inner].astype(BF16)
        return carry

    lax.fori_loop(0, length // QB, project, 0)
    keys = proj_ref[:, PAD : 2 * PAD]
    for h in range(heads):
        kh_ref[h] = jnp.where(head_lanes(length, h, dim, True, heads), keys, jnp.zeros_like(keys))

    def block(b, carry):
        at = pl.multiple_of(b * QB, QB)
        from_row = pl.multiple_of(length - QB - b * QB, QB)
        queries = proj_ref[pl.ds(at, QB), 0:PAD]
        for h in range(heads):
            scores = nt_dot(kh_ref[h], queries) + strip_ref[h, pl.ds(from_row, length), :]
            top = jnp.max(scores, 0, keepdims=True)
            probs = jnp.exp(scores - top)
            total = jnp.sum(probs, 0, keepdims=True)
            out = nn_dot(vt_ref[h * dim : (h + 1) * dim, :], probs.astype(BF16))
            att_ref[h * dim : (h + 1) * dim, pl.ds(at, QB)] = (out / total).astype(BF16)
            lse_ref[h : h + 1, pl.ds(at, QB)] = top + jnp.log(total)
        return carry

    lax.fori_loop(0, length // QB, block, 0)


def attend_back_kernel(
    length, heads, dim,
    proj_ref, kt_ref, lse_ref, da_ref, normed_ref, w_ref, gproj_ref, bias_ref, low_ref,
    grad_ref, kept_ref, sent_ref, drel_ref,
    kh_ref, vh_ref, strip_ref, dstrip_ref, pcat_ref, dcat_ref, dacat_ref, qcat_ref, dk_ref, dv_ref, dqt_ref,
    dq_ref, pad_ref,
):
    inner = heads * dim
    scale = dim ** (-0.5)
    total = strip_shape(length)
    base, first, last = near_rows(length)
    build_strip(strip_ref, bias_ref, length, heads)
    dstrip_ref[...] = jnp.zeros_like(dstrip_ref)
    dk_ref[...] = jnp.zeros_like(dk_ref)
    dv_ref[...] = jnp.zeros_like(dv_ref)
    dqt_ref[...] = jnp.zeros_like(dqt_ref)
    keys = proj_ref[:, PAD : 2 * PAD]
    values = proj_ref[:, 2 * PAD : 3 * PAD]
    for h in range(heads):
        kh_ref[h] = jnp.where(head_lanes(length, h, dim, True, heads), keys, jnp.zeros_like(keys))
        vh_ref[h] = jnp.where(head_lanes(length, h, dim, False, heads), values, jnp.zeros_like(values))

    def block(b, carry):
        at = pl.multiple_of(b * QB, QB)
        from_row = pl.multiple_of(length - QB - b * QB, QB)
        queries = proj_ref[pl.ds(at, QB), 0:PAD]
        grads = da_ref[pl.ds(at, QB), :]
        for h in range(heads):
            mine = head_lanes(QB, h, dim, False, heads)
            cols = slice(h * QB, (h + 1) * QB)
            qcat_ref[cols, :] = jnp.where(mine, queries, jnp.zeros_like(queries))
            dacat_ref[cols, :] = jnp.where(mine, grads, jnp.zeros_like(grads))
            scores = nt_dot(kh_ref[h], queries) + strip_ref[h, pl.ds(from_row, length), :]
            probs = jnp.exp(scores - lse_ref[h : h + 1, pl.ds(at, QB)])
            weighted = probs * nt_dot(vh_ref[h], grads)
            delta = jnp.sum(weighted, 0, keepdims=True)
            dscore = weighted - probs * delta
            dstrip_ref[h, pl.ds(from_row, length), :] += dscore
            dlow = dscore.astype(BF16)
            pcat_ref[:, cols] = probs.astype(BF16)
            dcat_ref[:, cols] = dlow
            dqt_ref[h * dim : (h + 1) * dim, :] = nn_dot(kt_ref[h * dim : (h + 1) * dim, :], dlow) * scale
        dk_ref[...] += nn_dot(dcat_ref[...], qcat_ref[...])
        dv_ref[...] += nn_dot(pcat_ref[...], dacat_ref[...])
        dq_ref[pl.ds(at, QB), :] = dqt_ref[...].T
        return carry

    lax.fori_loop(0, length // QB, block, 0)

    for t, ref in enumerate((dq_ref, dk_ref, dv_ref)):
        turned = ref[...].T[:inner].astype(BF16)
        grad_ref[t * inner : (t + 1) * inner, :] = nn_dot(turned, normed_ref[...]).astype(BF16)

    grad_ref[3 * inner :, :] = gproj_ref[...]

    pad_ref[...] = jnp.zeros_like(pad_ref)
    for t in range(3):
        pad_ref[t, :, 0:inner] = w_ref[t]
    half = length // 2

    def part(start):
        total = jnp.zeros((QB, w_ref.shape[1]), F32)
        for t, ref in enumerate((dq_ref, dk_ref, dv_ref)):
            total = total + nt_dot(ref[pl.ds(start, QB), :].astype(BF16), pad_ref[t])
        return total

    for i in range(half // QB):
        rows = slice(i * QB, (i + 1) * QB)
        kept_ref[rows, :] = part(pl.multiple_of(low_ref[0] * half + i * QB, QB))
        sent_ref[rows, :] = part(pl.multiple_of((1 - low_ref[0]) * half + i * QB, QB)).astype(BF16)

    offset = (
        lax.broadcasted_iota(jnp.int32, (last - first, 128), 0)
        - lax.broadcasted_iota(jnp.int32, (last - first, 128), 1)
        + (first - base)
    )
    begins = [-(1 << 20)] + [begin for begin, bucket in STEPS] + [1 << 20]
    buckets = [15] + [bucket for begin, bucket in STEPS]
    for h in range(heads):
        near = jnp.zeros((last - first, 128), F32)
        low = jnp.zeros((1, 128), F32)
        high = jnp.zeros((1, 128), F32)
        for half in range(QB // 128):
            cols = slice(half * 128, half * 128 + 128)
            lo_end, hi_start = first + half * 128, last + half * 128
            near = near + dstrip_ref[h, lo_end:hi_start, cols]
            low = low + jnp.sum(dstrip_ref[h, 0:lo_end, cols], 0, keepdims=True)
            high = high + jnp.sum(dstrip_ref[h, hi_start:total, cols], 0, keepdims=True)
        drel_ref[h, 16:17, :] = jnp.zeros((1, 128), F32)
        for i, bucket in enumerate(buckets):
            inside = (offset >= begins[i]) & (offset < begins[i + 1])
            row = jnp.sum(jnp.where(inside, near, 0.0), 0, keepdims=True)
            if bucket == 15:
                row = row + low
            if bucket == 31:
                row = row + high
            drel_ref[h, bucket : bucket + 1, :] = row


def whole_vmem(count):
    return [pl.BlockSpec(memory_space=pltpu.VMEM)] * count


def attend(tokens, gain, w_qkv, segments, rel_bias):
    length, width = tokens.shape
    heads = rel_bias.shape[0]
    inner = w_qkv.shape[2]
    return pl.pallas_call(
        functools.partial(attend_kernel, length, heads, inner // heads),
        out_shape=(
            jax.ShapeDtypeStruct((inner, length), BF16),
            jax.ShapeDtypeStruct((8, length), F32),
            jax.ShapeDtypeStruct((length, 3 * PAD), BF16),
            jax.ShapeDtypeStruct((inner, length), BF16),
            jax.ShapeDtypeStruct((length, width), BF16),
        ),
        in_specs=whole_vmem(4) + [pl.BlockSpec(memory_space=pltpu.SMEM)],
        out_specs=tuple(whole_vmem(5)),
        scratch_shapes=[
            pltpu.VMEM((heads, length, PAD), BF16),
            pltpu.VMEM((heads, strip_shape(length), QB), F32),
            pltpu.VMEM((inner, length), BF16),
            pltpu.VMEM((width, 3 * PAD), BF16),
        ],
        compiler_params=pltpu.CompilerParams(vmem_limit_bytes=48 << 20),
        cost_estimate=pl.CostEstimate(
            flops=4 * heads * length * length * PAD + 6 * length * width * PAD,
            bytes_accessed=8 << 20,
            transcendentals=heads * length * length,
        ),
    )(tokens, gain[None, :], w_qkv, segments[:, None], rel_bias)


def attend_back(proj, kt, lse, da, normed, w_qkv, grad_proj, rel_bias, low_bit):
    length, width = normed.shape
    heads, buckets = rel_bias.shape
    inner = w_qkv.shape[2]
    return pl.pallas_call(
        functools.partial(attend_back_kernel, length, heads, inner // heads),
        out_shape=(
            jax.ShapeDtypeStruct((4 * inner, width), BF16),
            jax.ShapeDtypeStruct((length // 2, width), F32),
            jax.ShapeDtypeStruct((length // 2, width), BF16),
            jax.ShapeDtypeStruct((heads, buckets, 128), F32),
        ),
        in_specs=whole_vmem(7) + [pl.BlockSpec(memory_space=pltpu.SMEM)] * 2,
        out_specs=tuple(whole_vmem(4)),
        scratch_shapes=[
            pltpu.VMEM((heads, length, PAD), BF16),
            pltpu.VMEM((heads, length, PAD), BF16),
            pltpu.VMEM((heads, strip_shape(length), QB), F32),
            pltpu.VMEM((heads, strip_shape(length), QB), F32),
            pltpu.VMEM((length, heads * QB), BF16),
            pltpu.VMEM((length, heads * QB), BF16),
            pltpu.VMEM((heads * QB, PAD), BF16),
            pltpu.VMEM((heads * QB, PAD), BF16),
            pltpu.VMEM((length, PAD), F32),
            pltpu.VMEM((length, PAD), F32),
            pltpu.VMEM((PAD, QB), F32),
            pltpu.VMEM((length, PAD), F32),
            pltpu.VMEM((3, width, PAD), BF16),
        ],
        compiler_params=pltpu.CompilerParams(vmem_limit_bytes=56 << 20),
        cost_estimate=pl.CostEstimate(
            flops=10 * heads * length * length * PAD + 12 * length * width * PAD,
            bytes_accessed=12 << 20,
            transcendentals=heads * length * length,
        ),
    )(proj, kt, lse, da, normed, w_qkv, grad_proj, rel_bias, low_bit)


def gelu_pair(v):
    inner = 0.7978845608028654 * (v + 0.044715 * (v * v * v))
    bend = jnp.tanh(inner)
    half = 0.5 * (1.0 + bend)
    slope = half + 0.5 * v * (1.0 - bend * bend) * (0.7978845608028654 * (1.0 + 0.134145 * (v * v)))
    return v * half, slope


def expert_kernel(
    members, experts,
    rows_ref, cot_ref, router_ref, group_ref, *refs,
):
    first, second = refs[:members], refs[members : 2 * members]
    reply_ref, share_ref, act_ref, gpre_ref, grad_ref, grouter_ref = refs[2 * members :]
    rows = rows_ref[...]
    count = rows.shape[0]
    lane = lax.broadcasted_iota(jnp.int32, (count, 128), 1)
    logits = jnp.where(lane < experts, nn_dot(rows, router_ref[...]), MASKED)
    raised = jnp.exp(logits - jnp.max(logits, -1, keepdims=True))
    probs = raised / jnp.sum(raised, -1, keepdims=True)
    own = jnp.where(lane == group_ref[0], 1.0, 0.0)
    gate = jnp.sum(probs * own, -1, keepdims=True)
    cot = cot_ref[...].astype(F32)
    grads = (gate * cot).astype(BF16)
    grad_ref[...] = grads
    reply = jnp.zeros(rows.shape, F32)
    share = jnp.zeros(rows.shape, F32)
    for k in range(members):
        act, slope = gelu_pair(nn_dot(rows, first[k][...]))
        act = act.astype(BF16)
        act_ref[k] = act
        reply = reply + nn_dot(act, second[k][...])
        gpre = (nt_dot(grads, second[k][...]) * slope).astype(BF16)
        gpre_ref[k] = gpre
        share = share + nt_dot(gpre, first[k][...])
    reply = reply.astype(BF16)
    reply_ref[...] = reply
    gate_grad = jnp.sum(cot * reply.astype(F32), -1, keepdims=True)
    logit_grad = probs * (own - gate) * gate_grad
    share_ref[...] = (share + nt_dot(logit_grad.astype(BF16), router_ref[...])).astype(BF16)
    grouter_ref[...] = nn_dot(logit_grad.T.astype(BF16), rows)


def expert_step(rows, cot, w_router, group, first, second):
    members = len(first)
    count, width = rows.shape
    hidden = first[0].shape[1]
    experts = w_router.shape[1]
    router = jnp.pad(w_router, ((0, 0), (0, 128 - experts)))
    return pl.pallas_call(
        functools.partial(expert_kernel, members, experts),
        out_shape=(
            jax.ShapeDtypeStruct((count, width), BF16),
            jax.ShapeDtypeStruct((count, width), BF16),
            jax.ShapeDtypeStruct((members, count, hidden), BF16),
            jax.ShapeDtypeStruct((members, count, hidden), BF16),
            jax.ShapeDtypeStruct((count, width), BF16),
            jax.ShapeDtypeStruct((128, width), F32),
        ),
        in_specs=whole_vmem(3) + [pl.BlockSpec(memory_space=pltpu.SMEM)] + whole_vmem(2 * members),
        out_specs=tuple(whole_vmem(6)),
        compiler_params=pltpu.CompilerParams(vmem_limit_bytes=48 << 20),
        cost_estimate=pl.CostEstimate(
            flops=8 * members * count * width * hidden,
            bytes_accessed=20 << 20,
            transcendentals=members * count * hidden,
        ),
    )(rows, cot, router, group, *first, *second)


def rows_of(count, columns):
    return pl.BlockSpec((count, columns), lambda i: (i, 0))


def whole_of(*shape):
    return pl.BlockSpec(shape, lambda i: (0,) * len(shape))


def enter_kernel(
    members, experts,
    x_ref, gain_ref, router_ref, route_ref, flat_ref, ids_ref, *refs,
):
    att, proj = refs[:members], refs[members : 2 * members]
    hidden_ref, gate_ref, leave_ref, total_ref = refs[2 * members :]
    step = pl.program_id(0)
    hidden = x_ref[...].astype(F32)
    for k in range(members):
        hidden = hidden + lax.dot_general(
            att[k][...], proj[k][...], (((0,), (0,)), ((), ())), preferred_element_type=F32
        )
    hidden_ref[...] = hidden
    normed = norm_rows(hidden, gain_ref[...]).astype(BF16)
    lane = lax.broadcasted_iota(jnp.int32, (QB, 128), 1)
    logits = jnp.where(lane < experts, nn_dot(normed, router_ref[...]), MASKED)
    raised = jnp.exp(logits - jnp.max(logits, -1, keepdims=True))
    chosen = jnp.sum(jnp.where(lane == route_ref[...], raised, 0.0), -1, keepdims=True)
    gate_ref[...] = chosen / jnp.sum(raised, -1, keepdims=True)
    table = jnp.where(ids_ref[...] == flat_ref[...], 1.0, 0.0).astype(BF16)

    @pl.when(step == 0)
    def _():
        total_ref[...] = jnp.zeros_like(total_ref)

    total_ref[...] += nn_dot(table, normed)

    @pl.when(step == pl.num_programs(0) - 1)
    def _():
        leave_ref[...] = total_ref[...].astype(BF16)


def enter_experts(tokens, gain, w_router, route, flat_id, ids, att, proj):
    length, width = tokens.shape
    experts = w_router.shape[1]
    members = len(att)
    inner = att[0].shape[0]
    count = ids.shape[0]
    return pl.pallas_call(
        functools.partial(enter_kernel, members, experts),
        grid=(length // QB,),
        out_shape=(
            jax.ShapeDtypeStruct((length, width), F32),
            jax.ShapeDtypeStruct((length, 1), F32),
            jax.ShapeDtypeStruct((count, width), BF16),
        ),
        in_specs=[
            rows_of(QB, width),
            whole_of(1, width),
            whole_of(width, 128),
            rows_of(QB, 1),
            pl.BlockSpec((1, QB), lambda i: (0, i)),
            whole_of(count, 1),
        ]
        + [pl.BlockSpec((inner, QB), lambda i: (0, i))] * members
        + [whole_of(inner, width)] * members,
        out_specs=(rows_of(QB, width), rows_of(QB, 1), whole_of(count, width)),
        scratch_shapes=[pltpu.VMEM((count, width), F32)],
        compiler_params=pltpu.CompilerParams(vmem_limit_bytes=40 << 20),
        cost_estimate=pl.CostEstimate(
            flops=2 * length * width * (members * inner + count),
            bytes_accessed=10 << 20,
            transcendentals=length * 128,
        ),
    )(
        tokens, gain[None, :], jnp.pad(w_router, ((0, 0), (0, 128 - experts))),
        route[:, None], flat_id[None, :], ids[:, None], *att, *proj,
    )


def weight_kernel(half, rows_ref, grads_ref, act_ref, gpre_ref, kept_ref, sent_ref):
    step = pl.program_id(0)
    dims = (((0,), (0,)), ((), ()))

    @pl.when(step < half)
    def _():
        k = 2 * step
        kept_ref[0] = lax.dot_general(act_ref[k], grads_ref[...], dims, preferred_element_type=F32)
        sent = lax.dot_general(act_ref[k + 1], grads_ref[...], dims, preferred_element_type=F32)
        sent_ref[0] = sent.astype(BF16)

    @pl.when(step >= half)
    def _():
        k = 2 * (step - half)
        kept_ref[0] = lax.dot_general(rows_ref[...], gpre_ref[k], dims, preferred_element_type=F32)
        sent = lax.dot_general(rows_ref[...], gpre_ref[k + 1], dims, preferred_element_type=F32)
        sent_ref[0] = sent.astype(BF16)


def weight_grads(rows, grads, act, gpre):
    members, count, hidden = act.shape
    width = rows.shape[1]
    assert hidden == width
    one = pl.BlockSpec((1, width, width), lambda i: (i, 0, 0))
    return pl.pallas_call(
        functools.partial(weight_kernel, members // 2),
        grid=(members,),
        out_shape=(
            jax.ShapeDtypeStruct((members, width, width), F32),
            jax.ShapeDtypeStruct((members, width, width), BF16),
        ),
        in_specs=[whole_of(count, width)] * 2 + [whole_of(members, count, hidden)] * 2,
        out_specs=(one, one),
        compiler_params=pltpu.CompilerParams(vmem_limit_bytes=48 << 20),
        cost_estimate=pl.CostEstimate(
            flops=4 * members * count * width * hidden, bytes_accessed=20 << 20, transcendentals=0
        ),
    )(rows, grads, act, gpre)


def leave_kernel(
    members,
    hidden_ref, cot_ref, gain_ref, flat_ref, ids_ref, wproj_ref, att_ref, *refs,
):
    blocks = refs[:members]
    gh_ref, da_ref, ggain_ref, gproj_ref, total_ref = refs[members:]
    step = pl.program_id(0)
    share = blocks[0].shape[0]
    grad = jnp.zeros(hidden_ref.shape, F32)
    for k in range(members):
        hit = flat_ref[...] == ids_ref[:, k * share : (k + 1) * share]
        grad = grad + nn_dot(jnp.where(hit, 1.0, 0.0).astype(BF16), blocks[k][...])
    hidden = hidden_ref[...]
    inverse = lax.rsqrt(jnp.mean(hidden * hidden, -1, keepdims=True) + 1e-06)
    unit = hidden * inverse
    scaled = gain_ref[...] * grad
    back = inverse * (scaled - unit * jnp.mean(unit * scaled, -1, keepdims=True))
    total = cot_ref[...].astype(F32) + back
    gh_ref[...] = total
    low = total.astype(BF16)
    da_ref[...] = nt_dot(low, wproj_ref[...]).astype(BF16)

    @pl.when(step == 0)
    def _():
        ggain_ref[...] = jnp.zeros_like(ggain_ref)
        total_ref[...] = jnp.zeros_like(total_ref)

    ggain_ref[...] += jnp.sum(grad * unit, 0, keepdims=True)
    total_ref[...] += nn_dot(att_ref[...], low)

    @pl.when(step == pl.num_programs(0) - 1)
    def _():
        gproj_ref[...] = total_ref[...].astype(BF16)


def leave_experts(hidden1, cotangent, gain, flat_id, ids, w_proj, attended_t, blocks):
    length, width = hidden1.shape
    inner = w_proj.shape[0]
    members = len(blocks)
    share = blocks[0].shape[0]
    return pl.pallas_call(
        functools.partial(leave_kernel, members),
        grid=(length // QB,),
        out_shape=(
            jax.ShapeDtypeStruct((length, width), F32),
            jax.ShapeDtypeStruct((length, PAD), BF16),
            jax.ShapeDtypeStruct((1, width), F32),
            jax.ShapeDtypeStruct((inner, width), BF16),
        ),
        in_specs=[
            rows_of(QB, width),
            rows_of(QB, width),
            whole_of(1, width),
            rows_of(QB, 1),
            whole_of(1, members * share),
            whole_of(PAD, width),
            pl.BlockSpec((inner, QB), lambda i: (0, i)),
        ]
        + [whole_of(share, width)] * members,
        out_specs=(
            rows_of(QB, width),
            rows_of(QB, PAD),
            whole_of(1, width),
            whole_of(inner, width),
        ),
        scratch_shapes=[pltpu.VMEM((inner, width), F32)],
        compiler_params=pltpu.CompilerParams(vmem_limit_bytes=40 << 20),
        cost_estimate=pl.CostEstimate(
            flops=2 * length * width * (members * share + 2 * PAD),
            bytes_accessed=13 << 20,
            transcendentals=length,
        ),
    )(
        hidden1, cotangent, gain[None, :], flat_id[:, None], ids[None, :],
        jnp.pad(w_proj, ((0, PAD - inner), (0, 0))), attended_t, *blocks,
    )


def input_kernel(halves, kept_ref, other_ref, x_ref, gain_ref, gh_ref, low_ref, out_ref, ggain_ref):
    step = pl.program_id(0)
    part = jnp.where(step // halves == low_ref[0], kept_ref[...].astype(F32), other_ref[...].astype(F32))
    x = x_ref[...].astype(F32)
    inverse = lax.rsqrt(jnp.mean(x * x, -1, keepdims=True) + 1e-06)
    unit = x * inverse
    scaled = gain_ref[...] * part
    out_ref[...] = gh_ref[...] + inverse * (scaled - unit * jnp.mean(unit * scaled, -1, keepdims=True))

    @pl.when(step == 0)
    def _():
        ggain_ref[...] = jnp.zeros_like(ggain_ref)

    ggain_ref[...] += jnp.sum(part * unit, 0, keepdims=True)


def input_grads(kept, other, tokens, gain, grad_hidden1, low_bit):
    length, width = tokens.shape
    halves = kept.shape[0] // QB
    half = pl.BlockSpec((QB, width), lambda i: (i % halves, 0))
    return pl.pallas_call(
        functools.partial(input_kernel, halves),
        grid=(length // QB,),
        out_shape=(
            jax.ShapeDtypeStruct((length, width), F32),
            jax.ShapeDtypeStruct((1, width), F32),
        ),
        in_specs=[
            half,
            half,
            rows_of(QB, width),
            whole_of(1, width),
            rows_of(QB, width),
            pl.BlockSpec(memory_space=pltpu.SMEM),
        ],
        out_specs=(rows_of(QB, width), whole_of(1, width)),
        compiler_params=pltpu.CompilerParams(vmem_limit_bytes=40 << 20),
        cost_estimate=pl.CostEstimate(flops=20 * length * width, bytes_accessed=11 << 20, transcendentals=length),
    )(kept, other, tokens, gain[None, :], grad_hidden1, low_bit)


def copies_kernel(came_ref, small_ref, ggain_ref, out_ref, mine_ref):
    groups, large = came_ref.shape[:2]

    @pl.when(pl.program_id(0) == 0)
    def _():
        total = came_ref[0].astype(F32)
        for g in range(1, groups):
            total = total + came_ref[g].astype(F32)
        mine_ref[:large, :] = total.astype(BF16)
        row = lax.broadcasted_iota(jnp.int32, small_ref.shape, 0)
        small = small_ref[...] + jnp.where(row == 1, ggain_ref[...], 0.0)
        mine_ref[large:, :] = small.astype(BF16)

    out_ref[0] = mine_ref[...]


def sum_copies(came, small, ggain):
    groups, large, width = came.shape
    count = large + small.shape[0]
    return pl.pallas_call(
        copies_kernel,
        grid=(groups,),
        out_shape=jax.ShapeDtypeStruct((groups, count, width), BF16),
        in_specs=[whole_of(groups, large, width), whole_of(*small.shape), whole_of(1, width)],
        out_specs=pl.BlockSpec((1, count, width), lambda i: (i, 0, 0)),
        scratch_shapes=[pltpu.VMEM((count, width), BF16)],
        compiler_params=pltpu.CompilerParams(vmem_limit_bytes=40 << 20),
    )(came, small, ggain)


def final_kernel(large, inner, totals_ref, qkv_ref, proj_ref, small_ref, all_ref):
    groups = totals_ref.shape[0]
    small = totals_ref[0, large:, :].astype(F32)
    for g in range(groups):
        all_ref[g * large : (g + 1) * large, :] = totals_ref[g, :large, :].astype(F32)
        if g:
            small = small + totals_ref[g, large:, :].astype(F32)
    small_ref[...] = small
    for t in range(3):
        qkv_ref[t] = all_ref[t * inner : (t + 1) * inner, :].T
    proj_ref[...] = all_ref[3 * inner :, :]


def final_weights(totals, large, inner):
    groups, count, width = totals.shape
    return pl.pallas_call(
        functools.partial(final_kernel, large, inner),
        out_shape=(
            jax.ShapeDtypeStruct((3, width, inner), F32),
            jax.ShapeDtypeStruct((inner, width), F32),
            jax.ShapeDtypeStruct((count - large, width), F32),
        ),
        in_specs=whole_vmem(1),
        out_specs=tuple(whole_vmem(3)),
        scratch_shapes=[pltpu.VMEM((groups * large, width), F32)],
        compiler_params=pltpu.CompilerParams(vmem_limit_bytes=40 << 20),
    )(totals)


def shards(
    tokens,
    gain_attn,
    w_qkv,
    w_proj,
    rel_bias,
    gain_ffn,
    w_router,
    w_in,
    w_out,
    routes,
    segment_ids,
    cotangent,
):
    length, width = tokens.shape
    experts = w_router.shape[1]
    capacity = max(2, 3 * length // (2 * experts))
    inner_here = w_proj.shape[0]
    members = lax.axis_size("tensor")
    groups = lax.axis_size("expert")
    member = lax.axis_index("tensor")
    group = lax.axis_index("expert")
    share = capacity // members
    segments = segment_ids[0]
    route = routes[:, 0]

    def swap(value, bit):
        return lax.ppermute(value, "tensor", [(i, i ^ bit) for i in range(members)])

    bits = [1 << i for i in range(members.bit_length() - 1)]

    def gather_far(value):
        blocks = {0: value}
        for bit in reversed(bits[1:]):
            blocks.update({k ^ bit: swap(block, bit) for k, block in blocks.items()})
        return blocks

    def gather_near(blocks):
        blocks = dict(blocks)
        for bit in bits[:1]:
            blocks.update({k ^ bit: swap(block, bit) for k, block in blocks.items()})
        return [blocks[k] for k in range(members)]

    def gather_members(value):
        return gather_near(gather_far(value))

    def gather_groups(value):
        copies = jnp.broadcast_to(value[None], (groups,) + value.shape)
        return exchange(copies)

    def exchange(value):
        return lax.all_to_all(value, "expert", split_axis=0, concat_axis=0, tiled=True)

    tie = lax.optimization_barrier

    expert_ids = jnp.arange(experts, dtype=jnp.int32)
    onehot_low = (route[:, None] == expert_ids[None, :]).astype(BF16)
    onehot = onehot_low.astype(F32)
    positions = jnp.arange(length, dtype=jnp.int32)
    lower_ones = (positions[:, None] >= positions[None, :]).astype(BF16)
    running = nn_dot(lower_ones, onehot_low)
    slot = (jnp.sum(running * onehot, 1) - 1.0).astype(jnp.int32)
    flat_id = route * capacity + slot

    def ids_of(owner):
        slots = owner * share + jnp.arange(share, dtype=jnp.int32)
        return (expert_ids[:, None] * capacity + slots[None, :]).reshape(-1)

    send_table = (ids_of(member)[:, None] == flat_id[None, :]).astype(BF16)
    all_ids = jnp.concatenate([ids_of(member ^ k) for k in range(members)])
    back_table = (flat_id[:, None] == all_ids[None, :]).astype(BF16)

    def dispatch(rows):
        out = nn_dot(send_table, rows).astype(BF16).reshape(groups, -1, width)
        return exchange(out).reshape(-1, width)

    cot_share = dispatch(cotangent)
    w_proj_far = gather_far(w_proj)
    w_in_far = gather_far(w_in[0])
    attended_t, lse, proj, keys_t, normed1 = attend(tokens, gain_attn, w_qkv, segments, rel_bias)
    attended_t, w_proj_far, cot_share = tie((attended_t, w_proj_far, cot_share))

    attended_far = gather_far(attended_t)
    attended_far, w_in_far, w_out_here = tie((attended_far, w_in_far, w_out[0]))
    attended_blocks = gather_near(attended_far)
    w_proj_blocks = gather_near(w_proj_far)
    w_in_all = gather_near(w_in_far)
    w_out_far = gather_far(w_out_here)
    hidden1, gate, leaving = enter_experts(
        tokens, gain_ffn, w_router, route, flat_id, ids_of(member), attended_blocks, w_proj_blocks
    )
    rows = exchange(leaving.reshape(groups, -1, width)).reshape(-1, width)
    rows, w_out_far = tie((rows, w_out_far))
    w_out_all = gather_near(w_out_far)

    reply, grad_share, act, grad_pre, grad_rows, grad_router = expert_step(
        rows, cot_share, w_router, group[None], w_in_all, w_out_all
    )
    grad_back = exchange(grad_share.reshape(groups, -1, width)).reshape(-1, width)
    kept_weights, sent_weights = weight_grads(rows, grad_rows, act, grad_pre)
    weights = kept_weights + swap(sent_weights, 1).astype(F32)
    out_sent, in_sent = weights[1].astype(BF16), weights[3].astype(BF16)
    grad_back, reply, out_sent, in_sent = tie((grad_back, reply, out_sent, in_sent))
    grad_blocks = gather_members(grad_back)
    reply_back = exchange(reply.reshape(groups, -1, width)).reshape(-1, width)
    grad_blocks, out_sent = tie((grad_blocks, out_sent))
    out_came = swap(out_sent, 2)
    grad_hidden1, attended_grad, grad_gain_ffn, grad_proj = leave_experts(
        hidden1, cotangent, gain_ffn, flat_id, all_ids, w_proj, attended_t, grad_blocks
    )

    low_bit = (member & 1)[None]
    grads, kept, sent, rel_parts = attend_back(
        proj, keys_t, lse, attended_grad, normed1, w_qkv, grad_proj, rel_bias, low_bit
    )
    grads, kept, sent, out_came, reply_back, in_sent = tie(
        (grads, kept, sent, out_came, reply_back, in_sent)
    )
    in_came = swap(in_sent, 2)
    came = exchange(grads.reshape(groups, -1, width))
    kept = kept + swap(sent, 1).astype(F32)
    kept = kept + swap(kept.astype(BF16), 2).astype(F32)
    kept, reply_back, out_came = tie((kept.astype(BF16), reply_back, out_came))
    other = swap(kept, 1)
    grad_input, gain_part = input_grads(kept, other, tokens, gain_attn, grad_hidden1, low_bit)

    grad_router = grad_router[:experts]
    for bit in bits:
        grad_router = grad_router + swap(grad_router, bit)
    rel_row = jnp.sum(rel_parts, -1).reshape(1, -1)
    rel_row = jnp.pad(rel_row, ((0, 0), (0, width - rel_row.shape[1])))
    small = jnp.concatenate([grad_gain_ffn, jnp.zeros((1, width), F32), rel_row, grad_router], 0)
    small = jnp.pad(small, ((0, -small.shape[0] % 16), (0, 0)))
    large = came.shape[1]
    if large % 16 == 0:
        totals = exchange(sum_copies(came, small, gain_part))
        grad_qkv, grad_proj, small = final_weights(totals, large, inner_here)
    else:
        mine = jnp.sum(came.astype(F32), 0)
        small = small.at[1].add(gain_part[0])
        totals = gather_groups(jnp.concatenate([mine, small], 0).astype(BF16))
        shared = totals[:, :large].reshape(-1, width).astype(F32)
        grad_qkv = jnp.swapaxes(shared[: 3 * inner_here].reshape(3, inner_here, width), 1, 2)
        grad_proj = shared[3 * inner_here :]
        small = jnp.sum(totals[:, large:].astype(F32), 0)
    grad_gain_ffn, grad_gain_attn = small[0], small[1]
    grad_rel = small[2, : rel_bias.size].reshape(rel_bias.shape)
    grad_router = small[3 : 3 + experts].T

    reply_rows = jnp.concatenate(gather_members(reply_back), 0)
    returned = nn_dot(back_table, reply_rows)
    output = (hidden1 + gate * returned).astype(BF16)
    grad_w_out = weights[0] + out_came.astype(F32)
    grad_w_in = weights[2] + in_came.astype(F32)
    return (
        output,
        grad_input,
        grad_gain_attn,
        grad_qkv,
        grad_proj,
        grad_rel,
        grad_gain_ffn,
        grad_router,
        grad_w_in[None],
        grad_w_out[None],
    )


def solution(mesh):
    placed = (
        P("expert", None),
        P(),
        P(None, None, "tensor"),
        P("tensor", None),
        P("tensor", None),
        P(),
        P(),
        P("expert", None, "tensor"),
        P("expert", "tensor", None),
        P("expert", None),
        P("expert", None),
        P("expert", None),
    )
    return jax.shard_map(
        shards,
        mesh=mesh,
        in_specs=placed,
        out_specs=(
            P("expert", None),
            P("expert", None),
            P(),
            P(None, None, "tensor"),
            P("tensor", None),
            P("tensor", None),
            P(),
            P(),
            P("expert", None, "tensor"),
            P("expert", "tensor", None),
        ),
        check_vma=False,
    )
```

```python
import functools

import jax
import jax.numpy as jnp
from jax import lax
from jax.experimental import pallas as pl
from jax.experimental.pallas import tpu as pltpu
from jax.sharding import PartitionSpec as P

FAR_LIMITS = (12, 16, 23, 32, 46, 64, 91)
HIGH = lax.Precision.HIGHEST
F32 = jnp.float32
BF16 = jnp.bfloat16
MASKED = -1e30
QB = 256
PAD = 256
FAR = FAR_LIMITS[-1]
SMALL = pl.CostEstimate(flops=1 << 20, bytes_accessed=1 << 16, transcendentals=0)

STEPS = (
    [(1 - limit, 14 - i) for i, limit in enumerate(reversed(FAR_LIMITS))]
    + [(-n, n) for n in range(7, -1, -1)]
    + [(n, 16 + n) for n in range(1, 8)]
    + [(8, 24)]
    + [(limit, 25 + i) for i, limit in enumerate(FAR_LIMITS)]
)


def norm_rows(values, gain):
    return values * lax.rsqrt(jnp.mean(values * values, -1, keepdims=True) + 1e-06) * gain


def nt_dot(left, right):
    return lax.dot_general(left, right, (((1,), (1,)), ((), ())), preferred_element_type=F32)


def nn_dot(left, right):
    return jnp.dot(left, right, preferred_element_type=F32)


def strip_shape(length):
    return 2 * length - QB


def near_rows(length):
    base = length - QB
    first = (base - FAR) // 32 * 32
    last = -(-(base + 127 + FAR) // 32) * 32
    return base, first, last


def build_strip(strip_ref, bias_ref, length, heads):
    total = strip_shape(length)
    base, first, last = near_rows(length)
    for h in range(heads):
        low = jnp.full((8, 128), bias_ref[h, 15], F32)
        high = jnp.full((8, 128), bias_ref[h, 31], F32)
        for half in range(QB // 128):
            cols = slice(half * 128, half * 128 + 128)
            lo_end, hi_start = first + half * 128, last + half * 128
            strip_ref[h, 0:lo_end, cols] = jnp.broadcast_to(low[:1], (lo_end, 128))
            strip_ref[h, hi_start:total, cols] = jnp.broadcast_to(high[:1], (total - hi_start, 128))
    for start in range(first, last, 32):
        offset = (
            lax.broadcasted_iota(jnp.int32, (32, 128), 0)
            - lax.broadcasted_iota(jnp.int32, (32, 128), 1)
            + (start - base)
        )
        tiles = [jnp.full((32, 128), bias_ref[h, 15], F32) for h in range(heads)]
        for begin, bucket in STEPS:
            reached = offset >= begin
            tiles = [jnp.where(reached, bias_ref[h, bucket], tiles[h]) for h in range(heads)]
        for h in range(heads):
            for half in range(QB // 128):
                at = start + half * 128
                strip_ref[h, at : at + 32, half * 128 : half * 128 + 128] = tiles[h]


def head_lanes(rows, h, dim, keep_tail, heads):
    lane = lax.broadcasted_iota(jnp.int32, (rows, PAD), 1)
    inside = (lane >= h * dim) & (lane < (h + 1) * dim)
    if keep_tail:
        inside = inside | (lane >= heads * dim)
    return inside


def attend_kernel(
    length, heads, dim,
    x_ref, gain_ref, w_ref, doc_ref, bias_ref,
    att_ref, lse_ref, proj_ref, kt_ref, normed_ref,
    kh_ref, strip_ref, vt_ref, pad_ref,
):
    inner = heads * dim
    build_strip(strip_ref, bias_ref, length, heads)
    lane = lax.broadcasted_iota(jnp.int32, (QB, PAD), 1) - inner
    pad_ref[...] = jnp.zeros_like(pad_ref)
    for t in range(3):
        pad_ref[t * PAD : t * PAD + inner, :] = w_ref[t]

    def project(b, carry):
        at = pl.multiple_of(b * QB, QB)
        here = x_ref[pl.ds(at, QB), :].astype(F32)
        normed = norm_rows(here, gain_ref[...]).astype(BF16)
        normed_ref[pl.ds(at, QB), :] = normed
        every = nt_dot(normed, pad_ref[...])
        same = doc_ref[pl.ds(at, QB), :] == lane
        queries = (every[:, 0:PAD].astype(BF16) * jnp.bfloat16(dim ** (-0.5))).astype(F32)
        queries = queries + jnp.where((lane < 0) | same, 0.0, MASKED)
        keys = every[:, PAD : 2 * PAD]
        values = every[:, 2 * PAD : 3 * PAD]
        proj_ref[pl.ds(at, QB), 0:PAD] = queries.astype(BF16)
        proj_ref[pl.ds(at, QB), PAD : 2 * PAD] = (keys + jnp.where(same, 1.0, 0.0)).astype(BF16)
        proj_ref[pl.ds(at, QB), 2 * PAD : 3 * PAD] = values.astype(BF16)
        kt_ref[:, pl.ds(at, QB)] = keys.T[:inner].astype(BF16)
        vt_ref[:, pl.ds(at, QB)] = values.T[:inner].astype(BF16)
        return carry

    lax.fori_loop(0, length // QB, project, 0)
    keys = proj_ref[:, PAD : 2 * PAD]
    for h in range(heads):
        kh_ref[h] = jnp.where(head_lanes(length, h, dim, True, heads), keys, jnp.zeros_like(keys))

    def block(b, carry):
        at = pl.multiple_of(b * QB, QB)
        from_row = pl.multiple_of(length - QB - b * QB, QB)
        queries = proj_ref[pl.ds(at, QB), 0:PAD]
        for h in range(heads):
            scores = nt_dot(kh_ref[h], queries) + strip_ref[h, pl.ds(from_row, length), :]
            top = jnp.max(scores, 0, keepdims=True)
            probs = jnp.exp(scores - top)
            total = jnp.sum(probs, 0, keepdims=True)
            out = nn_dot(vt_ref[h * dim : (h + 1) * dim, :], probs.astype(BF16))
            att_ref[h * dim : (h + 1) * dim, pl.ds(at, QB)] = (out / total).astype(BF16)
            lse_ref[h : h + 1, pl.ds(at, QB)] = top + jnp.log(total)
        return carry

    lax.fori_loop(0, length // QB, block, 0)


def attend_back_kernel(
    length, heads, dim,
    proj_ref, kt_ref, lse_ref, da_ref, normed_ref, w_ref, gproj_ref, bias_ref, low_ref,
    grad_ref, kept_ref, sent_ref, drel_ref,
    kh_ref, vh_ref, strip_ref, dstrip_ref, pcat_ref, dcat_ref, dacat_ref, qcat_ref, dk_ref, dv_ref, dqt_ref,
    dq_ref, pad_ref,
):
    inner = heads * dim
    scale = dim ** (-0.5)
    total = strip_shape(length)
    base, first, last = near_rows(length)
    build_strip(strip_ref, bias_ref, length, heads)
    dstrip_ref[...] = jnp.zeros_like(dstrip_ref)
    dk_ref[...] = jnp.zeros_like(dk_ref)
    dv_ref[...] = jnp.zeros_like(dv_ref)
    dqt_ref[...] = jnp.zeros_like(dqt_ref)
    keys = proj_ref[:, PAD : 2 * PAD]
    values = proj_ref[:, 2 * PAD : 3 * PAD]
    for h in range(heads):
        kh_ref[h] = jnp.where(head_lanes(length, h, dim, True, heads), keys, jnp.zeros_like(keys))
        vh_ref[h] = jnp.where(head_lanes(length, h, dim, False, heads), values, jnp.zeros_like(values))

    def block(b, carry):
        at = pl.multiple_of(b * QB, QB)
        from_row = pl.multiple_of(length - QB - b * QB, QB)
        queries = proj_ref[pl.ds(at, QB), 0:PAD]
        grads = da_ref[pl.ds(at, QB), :]
        for h in range(heads):
            mine = head_lanes(QB, h, dim, False, heads)
            cols = slice(h * QB, (h + 1) * QB)
            qcat_ref[cols, :] = jnp.where(mine, queries, jnp.zeros_like(queries))
            dacat_ref[cols, :] = jnp.where(mine, grads, jnp.zeros_like(grads))
            scores = nt_dot(kh_ref[h], queries) + strip_ref[h, pl.ds(from_row, length), :]
            probs = jnp.exp(scores - lse_ref[h : h + 1, pl.ds(at, QB)])
            weighted = probs * nt_dot(vh_ref[h], grads)
            delta = jnp.sum(weighted, 0, keepdims=True)
            dscore = weighted - probs * delta
            dstrip_ref[h, pl.ds(from_row, length), :] += dscore
            dlow = dscore.astype(BF16)
            pcat_ref[:, cols] = probs.astype(BF16)
            dcat_ref[:, cols] = dlow
            dqt_ref[h * dim : (h + 1) * dim, :] = nn_dot(kt_ref[h * dim : (h + 1) * dim, :], dlow) * scale
        dk_ref[...] += nn_dot(dcat_ref[...], qcat_ref[...])
        dv_ref[...] += nn_dot(pcat_ref[...], dacat_ref[...])
        dq_ref[pl.ds(at, QB), :] = dqt_ref[...].T
        return carry

    lax.fori_loop(0, length // QB, block, 0)

    for t, ref in enumerate((dq_ref, dk_ref, dv_ref)):
        turned = ref[...].T[:inner].astype(BF16)
        grad_ref[t * inner : (t + 1) * inner, :] = nn_dot(turned, normed_ref[...]).astype(BF16)

    grad_ref[3 * inner :, :] = gproj_ref[...]

    pad_ref[...] = jnp.zeros_like(pad_ref)
    for t in range(3):
        pad_ref[t, 0:inner, :] = w_ref[t]
    half = length // 2

    def part(start):
        total = jnp.zeros((QB, w_ref.shape[2]), F32)
        for t, ref in enumerate((dq_ref, dk_ref, dv_ref)):
            total = total + nn_dot(ref[pl.ds(start, QB), :].astype(BF16), pad_ref[t])
        return total

    for i in range(half // QB):
        rows = slice(i * QB, (i + 1) * QB)
        kept_ref[rows, :] = part(pl.multiple_of(low_ref[0] * half + i * QB, QB))
        sent_ref[rows, :] = part(pl.multiple_of((1 - low_ref[0]) * half + i * QB, QB)).astype(BF16)

    offset = (
        lax.broadcasted_iota(jnp.int32, (last - first, 128), 0)
        - lax.broadcasted_iota(jnp.int32, (last - first, 128), 1)
        + (first - base)
    )
    begins = [-(1 << 20)] + [begin for begin, bucket in STEPS] + [1 << 20]
    buckets = [15] + [bucket for begin, bucket in STEPS]
    for h in range(heads):
        near = jnp.zeros((last - first, 128), F32)
        low = jnp.zeros((1, 128), F32)
        high = jnp.zeros((1, 128), F32)
        for half in range(QB // 128):
            cols = slice(half * 128, half * 128 + 128)
            lo_end, hi_start = first + half * 128, last + half * 128
            near = near + dstrip_ref[h, lo_end:hi_start, cols]
            low = low + jnp.sum(dstrip_ref[h, 0:lo_end, cols], 0, keepdims=True)
            high = high + jnp.sum(dstrip_ref[h, hi_start:total, cols], 0, keepdims=True)
        drel_ref[h, 16:17, :] = jnp.zeros((1, 128), F32)
        for i, bucket in enumerate(buckets):
            inside = (offset >= begins[i]) & (offset < begins[i + 1])
            row = jnp.sum(jnp.where(inside, near, 0.0), 0, keepdims=True)
            if bucket == 15:
                row = row + low
            if bucket == 31:
                row = row + high
            drel_ref[h, bucket : bucket + 1, :] = row


def whole_vmem(count):
    return [pl.BlockSpec(memory_space=pltpu.VMEM)] * count


def attend(tokens, gain, w_qkv, segments, rel_bias):
    length, width = tokens.shape
    heads = rel_bias.shape[0]
    inner = w_qkv.shape[1]
    return pl.pallas_call(
        functools.partial(attend_kernel, length, heads, inner // heads),
        out_shape=(
            jax.ShapeDtypeStruct((inner, length), BF16),
            jax.ShapeDtypeStruct((8, length), F32),
            jax.ShapeDtypeStruct((length, 3 * PAD), BF16),
            jax.ShapeDtypeStruct((inner, length), BF16),
            jax.ShapeDtypeStruct((length, width), BF16),
        ),
        in_specs=whole_vmem(4) + [pl.BlockSpec(memory_space=pltpu.SMEM)],
        out_specs=tuple(whole_vmem(5)),
        scratch_shapes=[
            pltpu.VMEM((heads, length, PAD), BF16),
            pltpu.VMEM((heads, strip_shape(length), QB), F32),
            pltpu.VMEM((inner, length), BF16),
            pltpu.VMEM((3 * PAD, width), BF16),
        ],
        compiler_params=pltpu.CompilerParams(vmem_limit_bytes=48 << 20),
        cost_estimate=SMALL,
    )(tokens, gain[None, :], w_qkv, segments[:, None], rel_bias)


def attend_back(proj, kt, lse, da, normed, w_qkv, grad_proj, rel_bias, low_bit):
    length, width = normed.shape
    heads, buckets = rel_bias.shape
    inner = w_qkv.shape[1]
    return pl.pallas_call(
        functools.partial(attend_back_kernel, length, heads, inner // heads),
        out_shape=(
            jax.ShapeDtypeStruct((4 * inner, width), BF16),
            jax.ShapeDtypeStruct((length // 2, width), F32),
            jax.ShapeDtypeStruct((length // 2, width), BF16),
            jax.ShapeDtypeStruct((heads, buckets, 128), F32),
        ),
        in_specs=whole_vmem(7) + [pl.BlockSpec(memory_space=pltpu.SMEM)] * 2,
        out_specs=tuple(whole_vmem(4)),
        scratch_shapes=[
            pltpu.VMEM((heads, length, PAD), BF16),
            pltpu.VMEM((heads, length, PAD), BF16),
            pltpu.VMEM((heads, strip_shape(length), QB), F32),
            pltpu.VMEM((heads, strip_shape(length), QB), F32),
            pltpu.VMEM((length, heads * QB), BF16),
            pltpu.VMEM((length, heads * QB), BF16),
            pltpu.VMEM((heads * QB, PAD), BF16),
            pltpu.VMEM((heads * QB, PAD), BF16),
            pltpu.VMEM((length, PAD), F32),
            pltpu.VMEM((length, PAD), F32),
            pltpu.VMEM((PAD, QB), F32),
            pltpu.VMEM((length, PAD), F32),
            pltpu.VMEM((3, PAD, width), BF16),
        ],
        compiler_params=pltpu.CompilerParams(vmem_limit_bytes=56 << 20),
        cost_estimate=SMALL,
    )(proj, kt, lse, da, normed, w_qkv, grad_proj, rel_bias, low_bit)


def gelu_pair(v):
    inner = 0.7978845608028654 * (v + 0.044715 * (v * v * v))
    bend = jnp.tanh(inner)
    half = 0.5 * (1.0 + bend)
    slope = half + 0.5 * v * (1.0 - bend * bend) * (0.7978845608028654 * (1.0 + 0.134145 * (v * v)))
    return v * half, slope


def expert_kernel(
    members, experts,
    rows_ref, cot_ref, router_ref, group_ref, *refs,
):
    first, second = refs[:members], refs[members : 2 * members]
    reply_ref, share_ref, act_ref, gpre_ref, grad_ref, grouter_ref = refs[2 * members :]
    rows = rows_ref[...]
    count = rows.shape[0]
    lane = lax.broadcasted_iota(jnp.int32, (count, 128), 1)
    logits = jnp.where(lane < experts, nn_dot(rows, router_ref[...]), MASKED)
    raised = jnp.exp(logits - jnp.max(logits, -1, keepdims=True))
    probs = raised / jnp.sum(raised, -1, keepdims=True)
    own = jnp.where(lane == group_ref[0], 1.0, 0.0)
    gate = jnp.sum(probs * own, -1, keepdims=True)
    cot = cot_ref[...].astype(F32)
    grads = (gate * cot).astype(BF16)
    grad_ref[...] = grads
    reply = jnp.zeros(rows.shape, F32)
    share = jnp.zeros(rows.shape, F32)
    for k in range(members):
        act, slope = gelu_pair(nn_dot(rows, first[k][...]))
        act = act.astype(BF16)
        act_ref[k] = act
        reply = reply + nn_dot(act, second[k][...])
        gpre = (nt_dot(grads, second[k][...]) * slope).astype(BF16)
        gpre_ref[k] = gpre
        share = share + nt_dot(gpre, first[k][...])
    reply = reply.astype(BF16)
    reply_ref[...] = reply
    gate_grad = jnp.sum(cot * reply.astype(F32), -1, keepdims=True)
    logit_grad = probs * (own - gate) * gate_grad
    share_ref[...] = (share + nt_dot(logit_grad.astype(BF16), router_ref[...])).astype(BF16)
    grouter_ref[...] = nn_dot(logit_grad.T.astype(BF16), rows)


def expert_step(rows, cot, experts, router, group, first, second):
    members = len(first)
    count, width = rows.shape
    hidden = first[0].shape[1]
    return pl.pallas_call(
        functools.partial(expert_kernel, members, experts),
        out_shape=(
            jax.ShapeDtypeStruct((count, width), BF16),
            jax.ShapeDtypeStruct((count, width), BF16),
            jax.ShapeDtypeStruct((members, count, hidden), BF16),
            jax.ShapeDtypeStruct((members, count, hidden), BF16),
            jax.ShapeDtypeStruct((count, width), BF16),
            jax.ShapeDtypeStruct((128, width), F32),
        ),
        in_specs=whole_vmem(3) + [pl.BlockSpec(memory_space=pltpu.SMEM)] + whole_vmem(2 * members),
        out_specs=tuple(whole_vmem(6)),
        compiler_params=pltpu.CompilerParams(vmem_limit_bytes=48 << 20),
        cost_estimate=SMALL,
    )(rows, cot, router, group, *first, *second)


def rows_of(count, columns):
    return pl.BlockSpec((count, columns), lambda i: (i, 0))


def whole_of(*shape):
    return pl.BlockSpec(shape, lambda i: (0,) * len(shape))


def enter_kernel(
    members, experts,
    x_ref, gain_ref, router_ref, route_ref, flat_ref, ids_ref, *refs,
):
    att, proj = refs[:members], refs[members : 2 * members]
    hidden_ref, gate_ref, leave_ref, total_ref = refs[2 * members :]
    step = pl.program_id(0)
    hidden = x_ref[...].astype(F32)
    for k in range(members):
        hidden = hidden + lax.dot_general(
            att[k][...], proj[k][...], (((0,), (0,)), ((), ())), preferred_element_type=F32
        )
    hidden_ref[...] = hidden
    normed = norm_rows(hidden, gain_ref[...]).astype(BF16)
    lane = lax.broadcasted_iota(jnp.int32, (QB, 128), 1)
    logits = jnp.where(lane < experts, nn_dot(normed, router_ref[...]), MASKED)
    raised = jnp.exp(logits - jnp.max(logits, -1, keepdims=True))
    chosen = jnp.sum(jnp.where(lane == route_ref[...], raised, 0.0), -1, keepdims=True)
    gate_ref[...] = chosen / jnp.sum(raised, -1, keepdims=True)
    table = jnp.where(ids_ref[...] == flat_ref[...], 1.0, 0.0).astype(BF16)

    @pl.when(step == 0)
    def _():
        total_ref[...] = jnp.zeros_like(total_ref)

    total_ref[...] += nn_dot(table, normed)

    @pl.when(step == pl.num_programs(0) - 1)
    def _():
        leave_ref[...] = total_ref[...].astype(BF16)


def enter_experts(tokens, experts, gain, router, route, flat_id, ids, att, proj):
    length, width = tokens.shape
    members = len(att)
    inner = att[0].shape[0]
    count = ids.shape[0]
    return pl.pallas_call(
        functools.partial(enter_kernel, members, experts),
        grid=(length // QB,),
        out_shape=(
            jax.ShapeDtypeStruct((length, width), F32),
            jax.ShapeDtypeStruct((length, 1), F32),
            jax.ShapeDtypeStruct((count, width), BF16),
        ),
        in_specs=[
            rows_of(QB, width),
            whole_of(1, width),
            whole_of(width, 128),
            rows_of(QB, 1),
            pl.BlockSpec((1, QB), lambda i: (0, i)),
            whole_of(count, 1),
        ]
        + [pl.BlockSpec((inner, QB), lambda i: (0, i))] * members
        + [whole_of(inner, width)] * members,
        out_specs=(rows_of(QB, width), rows_of(QB, 1), whole_of(count, width)),
        scratch_shapes=[pltpu.VMEM((count, width), F32)],
        compiler_params=pltpu.CompilerParams(vmem_limit_bytes=40 << 20),
        cost_estimate=SMALL,
    )(
        tokens, gain, router, route, flat_id, ids, *att, *proj,
    )


def weight_kernel(half, rows_ref, grads_ref, act_ref, gpre_ref, kept_ref, sent_ref):
    step = pl.program_id(0)

    def product(left, right):
        return lax.dot_general(
            left, right, (((0,), (0,)), ((), ())), preferred_element_type=F32
        ).astype(BF16)

    @pl.when(step < half)
    def _():
        k = 2 * step
        kept_ref[0] = product(act_ref[k], grads_ref[...])
        sent_ref[0] = product(act_ref[k + 1], grads_ref[...])

    @pl.when(step >= half)
    def _():
        k = 2 * (step - half)
        kept_ref[0] = product(rows_ref[...], gpre_ref[k])
        sent_ref[0] = product(rows_ref[...], gpre_ref[k + 1])


def weight_grads(rows, grads, act, gpre):
    members, count, hidden = act.shape
    width = rows.shape[1]
    assert hidden == width
    one = pl.BlockSpec((1, width, width), lambda i: (i, 0, 0))
    return pl.pallas_call(
        functools.partial(weight_kernel, members // 2),
        grid=(members,),
        out_shape=(
            jax.ShapeDtypeStruct((members, width, width), BF16),
            jax.ShapeDtypeStruct((members, width, width), BF16),
        ),
        in_specs=[whole_of(count, width)] * 2 + [whole_of(members, count, hidden)] * 2,
        out_specs=(one, one),
        compiler_params=pltpu.CompilerParams(vmem_limit_bytes=48 << 20),
        cost_estimate=SMALL,
    )(rows, grads, act, gpre)


def leave_kernel(
    members,
    hidden_ref, cot_ref, gain_ref, flat_ref, ids_ref, wproj_ref, att_ref, *refs,
):
    blocks = refs[:members]
    gh_ref, da_ref, ggain_ref, gproj_ref, total_ref = refs[members:]
    step = pl.program_id(0)
    share = blocks[0].shape[0]
    grad = jnp.zeros(hidden_ref.shape, F32)
    for k in range(members):
        hit = flat_ref[...] == ids_ref[:, k * share : (k + 1) * share]
        grad = grad + nn_dot(jnp.where(hit, 1.0, 0.0).astype(BF16), blocks[k][...])
    hidden = hidden_ref[...]
    inverse = lax.rsqrt(jnp.mean(hidden * hidden, -1, keepdims=True) + 1e-06)
    unit = hidden * inverse
    scaled = gain_ref[...] * grad
    back = inverse * (scaled - unit * jnp.mean(unit * scaled, -1, keepdims=True))
    total = cot_ref[...].astype(F32) + back
    gh_ref[...] = total
    low = total.astype(BF16)
    da_ref[...] = nt_dot(low, wproj_ref[...]).astype(BF16)

    @pl.when(step == 0)
    def _():
        ggain_ref[...] = jnp.zeros_like(ggain_ref)
        total_ref[...] = jnp.zeros_like(total_ref)

    ggain_ref[...] += jnp.sum(grad * unit, 0, keepdims=True)
    total_ref[...] += nn_dot(att_ref[...], low)

    @pl.when(step == pl.num_programs(0) - 1)
    def _():
        gproj_ref[...] = total_ref[...].astype(BF16)


def leave_experts(hidden1, cotangent, gain, flat_id, ids, w_proj, attended_t, blocks):
    length, width = hidden1.shape
    inner = attended_t.shape[0]
    members = len(blocks)
    share = blocks[0].shape[0]
    return pl.pallas_call(
        functools.partial(leave_kernel, members),
        grid=(length // QB,),
        out_shape=(
            jax.ShapeDtypeStruct((length, width), F32),
            jax.ShapeDtypeStruct((length, PAD), BF16),
            jax.ShapeDtypeStruct((1, width), F32),
            jax.ShapeDtypeStruct((inner, width), BF16),
        ),
        in_specs=[
            rows_of(QB, width),
            rows_of(QB, width),
            whole_of(1, width),
            rows_of(QB, 1),
            whole_of(1, members * share),
            whole_of(PAD, width),
            pl.BlockSpec((inner, QB), lambda i: (0, i)),
        ]
        + [whole_of(share, width)] * members,
        out_specs=(
            rows_of(QB, width),
            rows_of(QB, PAD),
            whole_of(1, width),
            whole_of(inner, width),
        ),
        scratch_shapes=[pltpu.VMEM((inner, width), F32)],
        compiler_params=pltpu.CompilerParams(vmem_limit_bytes=40 << 20),
        cost_estimate=SMALL,
    )(
        hidden1, cotangent, gain, flat_id, ids, w_proj, attended_t, *blocks,
    )


def input_kernel(halves, kept_ref, other_ref, x_ref, gain_ref, gh_ref, low_ref, out_ref, ggain_ref):
    step = pl.program_id(0)
    part = jnp.where(step // halves == low_ref[0], kept_ref[...].astype(F32), other_ref[...].astype(F32))
    x = x_ref[...].astype(F32)
    inverse = lax.rsqrt(jnp.mean(x * x, -1, keepdims=True) + 1e-06)
    unit = x * inverse
    scaled = gain_ref[...] * part
    out_ref[...] = gh_ref[...] + inverse * (scaled - unit * jnp.mean(unit * scaled, -1, keepdims=True))

    @pl.when(step == 0)
    def _():
        ggain_ref[...] = jnp.zeros_like(ggain_ref)

    ggain_ref[...] += jnp.sum(part * unit, 0, keepdims=True)


def input_grads(kept, other, tokens, gain, grad_hidden1, low_bit):
    length, width = tokens.shape
    halves = kept.shape[0] // QB
    half = pl.BlockSpec((QB, width), lambda i: (i % halves, 0))
    return pl.pallas_call(
        functools.partial(input_kernel, halves),
        grid=(length // QB,),
        out_shape=(
            jax.ShapeDtypeStruct((length, width), F32),
            jax.ShapeDtypeStruct((1, width), F32),
        ),
        in_specs=[
            half,
            half,
            rows_of(QB, width),
            whole_of(1, width),
            rows_of(QB, width),
            pl.BlockSpec(memory_space=pltpu.SMEM),
        ],
        out_specs=(rows_of(QB, width), whole_of(1, width)),
        compiler_params=pltpu.CompilerParams(vmem_limit_bytes=40 << 20),
        cost_estimate=SMALL,
    )(kept, other, tokens, gain[None, :], grad_hidden1, low_bit)


def copies_kernel(came_ref, small_ref, out_ref, mine_ref):
    groups, large = came_ref.shape[:2]

    @pl.when(pl.program_id(0) == 0)
    def _():
        total = came_ref[0].astype(F32)
        for g in range(1, groups):
            total = total + came_ref[g].astype(F32)
        mine_ref[:large, :] = total.astype(BF16)
        mine_ref[large:, :] = small_ref[...].astype(BF16)

    out_ref[0] = mine_ref[...]


def sum_copies(came, small):
    groups, large, width = came.shape
    count = large + small.shape[0]
    return pl.pallas_call(
        copies_kernel,
        grid=(groups,),
        out_shape=jax.ShapeDtypeStruct((groups, count, width), BF16),
        in_specs=[whole_of(groups, large, width), whole_of(*small.shape)],
        out_specs=pl.BlockSpec((1, count, width), lambda i: (i, 0, 0)),
        scratch_shapes=[pltpu.VMEM((count, width), BF16)],
        compiler_params=pltpu.CompilerParams(vmem_limit_bytes=40 << 20),
        cost_estimate=SMALL,
    )(came, small)


def final_kernel(large, inner, totals_ref, qkv_ref, proj_ref, small_ref):
    groups = totals_ref.shape[0]
    split = 3 * inner
    small = totals_ref[0, large:, :].astype(F32)
    for g in range(groups):
        start, stop = g * large, (g + 1) * large
        if start < split:
            count = min(stop, split) - start
            qkv_ref[start : start + count, :] = totals_ref[g, :count, :].astype(F32)
        if stop > split:
            skip = max(start, split) - start
            proj_ref[start + skip - split : stop - split, :] = totals_ref[g, skip:large, :].astype(F32)
        if g:
            small = small + totals_ref[g, large:, :].astype(F32)
    small_ref[...] = small


def final_weights(totals, large, inner):
    groups, count, width = totals.shape
    return pl.pallas_call(
        functools.partial(final_kernel, large, inner),
        out_shape=(
            jax.ShapeDtypeStruct((3 * inner, width), F32),
            jax.ShapeDtypeStruct((inner, width), F32),
            jax.ShapeDtypeStruct((count - large, width), F32),
        ),
        in_specs=whole_vmem(1),
        out_specs=tuple(whole_vmem(3)),
        compiler_params=pltpu.CompilerParams(vmem_limit_bytes=40 << 20),
        cost_estimate=SMALL,
    )(totals)


def shards(
    tokens,
    gain_attn,
    w_qkv,
    w_proj,
    rel_bias,
    gain_ffn,
    w_router,
    w_in,
    w_out,
    routes,
    segment_ids,
    cotangent,
):
    length, width = tokens.shape
    experts = w_router.shape[1]
    capacity = max(2, 3 * length // (2 * experts))
    inner_here = w_proj.shape[0]
    members = lax.axis_size("tensor")
    groups = lax.axis_size("expert")
    member = lax.axis_index("tensor")
    group = lax.axis_index("expert")
    share = capacity // members
    segments = segment_ids[0]
    route = routes[:, 0]

    def swap(value, bit):
        return lax.ppermute(value, "tensor", [(i, i ^ bit) for i in range(members)])

    bits = [1 << i for i in range(members.bit_length() - 1)]

    def gather_far(value):
        blocks = {0: value}
        for bit in reversed(bits[1:]):
            blocks.update({k ^ bit: swap(block, bit) for k, block in blocks.items()})
        return blocks

    def gather_near(blocks):
        blocks = dict(blocks)
        for bit in bits[:1]:
            blocks.update({k ^ bit: swap(block, bit) for k, block in blocks.items()})
        return [blocks[k] for k in range(members)]

    def gather_members(value):
        return gather_near(gather_far(value))

    def gather_groups(value):
        copies = jnp.broadcast_to(value[None], (groups,) + value.shape)
        return exchange(copies)

    def exchange(value):
        return lax.all_to_all(value, "expert", split_axis=0, concat_axis=0, tiled=True)

    tie = lax.optimization_barrier

    expert_ids = jnp.arange(experts, dtype=jnp.int32)
    onehot_low = (route[:, None] == expert_ids[None, :]).astype(BF16)
    onehot = onehot_low.astype(F32)
    positions = jnp.arange(length, dtype=jnp.int32)
    lower_ones = (positions[:, None] >= positions[None, :]).astype(BF16)
    running = nn_dot(lower_ones, onehot_low)
    slot = (jnp.sum(running * onehot, 1) - 1.0).astype(jnp.int32)
    flat_id = route * capacity + slot

    def ids_of(owner):
        slots = owner * share + jnp.arange(share, dtype=jnp.int32)
        return (expert_ids[:, None] * capacity + slots[None, :]).reshape(-1)

    send_table = (ids_of(member)[:, None] == flat_id[None, :]).astype(BF16)
    all_ids = jnp.concatenate([ids_of(member ^ k) for k in range(members)])
    back_table = (flat_id[:, None] == all_ids[None, :]).astype(BF16)

    def dispatch(rows):
        out = nn_dot(send_table, rows).astype(BF16).reshape(groups, -1, width)
        return exchange(out).reshape(-1, width)

    cot_share = dispatch(cotangent)
    w_far = gather_far(jnp.concatenate([w_proj, w_in[0]], 0))
    w_qkv_t = jnp.swapaxes(w_qkv, 1, 2)
    attended_t, lse, proj, keys_t, normed1 = attend(tokens, gain_attn, w_qkv_t, segments, rel_bias)
    attended_t, w_far, cot_share = tie((attended_t, w_far, cot_share))

    attended_far = gather_far(attended_t)
    gain_row = gain_ffn[None, :]
    router = jnp.pad(w_router, ((0, 0), (0, 128 - experts)))
    w_proj_pad = jnp.pad(w_proj, ((0, PAD - inner_here), (0, 0)))
    flat_row, flat_column = flat_id[None, :], flat_id[:, None]
    send_ids, back_ids = ids_of(member)[:, None], all_ids[None, :]
    attended_far, w_out_here, gain_row, router, w_proj_pad, flat_row, flat_column, send_ids, back_ids = tie(
        (attended_far, w_out[0], gain_row, router, w_proj_pad, flat_row, flat_column, send_ids, back_ids)
    )
    attended_blocks = gather_near(attended_far)
    w_near = gather_near(w_far)
    w_proj_blocks = [block[:inner_here] for block in w_near]
    w_in_all = [block[inner_here:] for block in w_near]
    w_out_far = gather_far(w_out_here)
    hidden1, gate, leaving = enter_experts(
        tokens, experts, gain_row, router, routes, flat_row, send_ids, attended_blocks, w_proj_blocks
    )
    rows = exchange(leaving.reshape(groups, -1, width)).reshape(-1, width)
    rows, w_out_far, w_in_all = tie((rows, w_out_far, w_in_all))
    w_out_all = gather_near(w_out_far)

    reply, grad_share, act, grad_pre, grad_rows, grad_router = expert_step(
        rows, cot_share, experts, router, group[None], w_in_all, w_out_all
    )
    grad_back = exchange(grad_share.reshape(groups, -1, width)).reshape(-1, width)
    kept_weights, sent_weights = weight_grads(rows, grad_rows, act, grad_pre)
    near_weights = swap(sent_weights, 1)
    grad_router = grad_router[:experts]
    for bit in bits:
        grad_router = grad_router + swap(grad_router, bit)
    grad_back, reply, near_weights, grad_router = tie((grad_back, reply, near_weights, grad_router))
    grad_far = gather_far(grad_back)
    out_sent = (kept_weights[1].astype(F32) + near_weights[1].astype(F32)).astype(BF16)
    in_sent = (kept_weights[3].astype(F32) + near_weights[3].astype(F32)).astype(BF16)
    grad_far, out_sent, in_sent = tie((grad_far, out_sent, in_sent))
    out_came, in_came = swap(out_sent, 2), swap(in_sent, 2)
    grad_blocks = gather_near(grad_far)
    reply_back = exchange(reply.reshape(groups, -1, width)).reshape(-1, width)
    grad_hidden1, attended_grad, grad_gain_ffn, grad_proj = leave_experts(
        hidden1, cotangent, gain_row, flat_column, back_ids, w_proj_pad, attended_t, grad_blocks
    )

    low_bit = (member & 1)[None]
    grads, kept, sent, rel_parts = attend_back(
        proj, keys_t, lse, attended_grad, normed1, w_qkv_t, grad_proj, rel_bias, low_bit
    )
    grads, kept, sent, reply_back, out_came, in_came = tie(
        (grads, kept, sent, reply_back, out_came, in_came)
    )
    came = exchange(grads.reshape(groups, -1, width))
    kept = kept + swap(sent, 1).astype(F32)
    kept = kept + swap(kept.astype(BF16), 2).astype(F32)

    rel_row = jnp.sum(rel_parts, -1).reshape(1, -1)
    rel_row = jnp.pad(rel_row, ((0, 0), (0, width - rel_row.shape[1])))
    small = jnp.concatenate([grad_gain_ffn, rel_row, grad_router], 0)
    small = jnp.pad(small, ((0, -small.shape[0] % 16), (0, 0)))
    large = came.shape[1]
    came, small = tie((came, small))
    if large % 16 == 0:
        totals = exchange(sum_copies(came, small))
        grad_qkv_t, grad_proj, small = final_weights(totals, large, inner_here)
    else:
        mine = jnp.sum(came.astype(F32), 0)
        totals = gather_groups(jnp.concatenate([mine, small], 0).astype(BF16))
        shared = totals[:, :large].reshape(-1, width).astype(F32)
        grad_qkv_t, grad_proj = shared[: 3 * inner_here], shared[3 * inner_here :]
        small = jnp.sum(totals[:, large:].astype(F32), 0)
    grad_qkv = jnp.swapaxes(grad_qkv_t.reshape(3, inner_here, width), 1, 2)
    grad_gain_ffn = small[0]
    grad_rel = small[1, : rel_bias.size].reshape(rel_bias.shape)
    grad_router = small[2 : 2 + experts].T

    kept, reply_back, out_came, in_came = tie((kept.astype(BF16), reply_back, out_came, in_came))
    other = swap(kept, 1)
    grad_input, gain_part = input_grads(kept, other, tokens, gain_attn, grad_hidden1, low_bit)
    grad_gain_attn = jnp.sum(gather_groups(gain_part), (0, 1))

    reply_rows = jnp.concatenate(gather_members(reply_back), 0)
    returned = nn_dot(back_table, reply_rows)
    output = (hidden1 + gate * returned).astype(BF16)
    grad_w_out = kept_weights[0].astype(F32) + near_weights[0].astype(F32) + out_came.astype(F32)
    grad_w_in = kept_weights[2].astype(F32) + near_weights[2].astype(F32) + in_came.astype(F32)
    return (
        output,
        grad_input,
        grad_gain_attn,
        grad_qkv,
        grad_proj,
        grad_rel,
        grad_gain_ffn,
        grad_router,
        grad_w_in[None],
        grad_w_out[None],
    )


def solution(mesh):
    placed = (
        P("expert", None),
        P(),
        P(None, None, "tensor"),
        P("tensor", None),
        P("tensor", None),
        P(),
        P(),
        P("expert", None, "tensor"),
        P("expert", "tensor", None),
        P("expert", None),
        P("expert", None),
        P("expert", None),
    )
    return jax.shard_map(
        shards,
        mesh=mesh,
        in_specs=placed,
        out_specs=(
            P("expert", None),
            P("expert", None),
            P(),
            P(None, None, "tensor"),
            P("tensor", None),
            P("tensor", None),
            P(),
            P(),
            P("expert", None, "tensor"),
            P("expert", "tensor", None),
        ),
        check_vma=False,
    )
```

```python
import functools

import jax
import jax.numpy as jnp
from jax import lax
from jax.experimental import pallas as pl
from jax.experimental.pallas import tpu as pltpu
from jax.sharding import PartitionSpec as P

FAR_LIMITS = (12, 16, 23, 32, 46, 64, 91)
HIGH = lax.Precision.HIGHEST
F32 = jnp.float32
BF16 = jnp.bfloat16
MASKED = -1e30
QB = 256
PAD = 256
FAR = FAR_LIMITS[-1]
SMALL = pl.CostEstimate(flops=1 << 20, bytes_accessed=1 << 16, transcendentals=0)

STEPS = (
    [(1 - limit, 14 - i) for i, limit in enumerate(reversed(FAR_LIMITS))]
    + [(-n, n) for n in range(7, -1, -1)]
    + [(n, 16 + n) for n in range(1, 8)]
    + [(8, 24)]
    + [(limit, 25 + i) for i, limit in enumerate(FAR_LIMITS)]
)


def norm_rows(values, gain):
    return values * lax.rsqrt(jnp.mean(values * values, -1, keepdims=True) + 1e-06) * gain


def nt_dot(left, right):
    return lax.dot_general(left, right, (((1,), (1,)), ((), ())), preferred_element_type=F32)


def nn_dot(left, right):
    return jnp.dot(left, right, preferred_element_type=F32)


def strip_shape(length):
    return 2 * length - QB


def near_rows(length):
    base = length - QB
    first = (base - FAR) // 32 * 32
    last = -(-(base + 127 + FAR) // 32) * 32
    return base, first, last


def build_strip(strip_ref, bias_ref, length, heads):
    total = strip_shape(length)
    base, first, last = near_rows(length)
    for h in range(heads):
        low = jnp.full((8, 128), bias_ref[h, 15], F32)
        high = jnp.full((8, 128), bias_ref[h, 31], F32)
        for half in range(QB // 128):
            cols = slice(half * 128, half * 128 + 128)
            lo_end, hi_start = first + half * 128, last + half * 128
            strip_ref[h, 0:lo_end, cols] = jnp.broadcast_to(low[:1], (lo_end, 128))
            strip_ref[h, hi_start:total, cols] = jnp.broadcast_to(high[:1], (total - hi_start, 128))
    for start in range(first, last, 32):
        offset = (
            lax.broadcasted_iota(jnp.int32, (32, 128), 0)
            - lax.broadcasted_iota(jnp.int32, (32, 128), 1)
            + (start - base)
        )
        tiles = [jnp.full((32, 128), bias_ref[h, 15], F32) for h in range(heads)]
        for begin, bucket in STEPS:
            reached = offset >= begin
            tiles = [jnp.where(reached, bias_ref[h, bucket], tiles[h]) for h in range(heads)]
        for h in range(heads):
            for half in range(QB // 128):
                at = start + half * 128
                strip_ref[h, at : at + 32, half * 128 : half * 128 + 128] = tiles[h]


def head_lanes(rows, h, dim, keep_tail, heads):
    lane = lax.broadcasted_iota(jnp.int32, (rows, PAD), 1)
    inside = (lane >= h * dim) & (lane < (h + 1) * dim)
    if keep_tail:
        inside = inside | (lane >= heads * dim)
    return inside


def attend_kernel(
    length, heads, dim,
    x_ref, gain_ref, w_ref, doc_ref, bias_ref,
    att_ref, lse_ref, proj_ref, kt_ref, normed_ref,
    kh_ref, strip_ref, vt_ref, pad_ref,
):
    inner = heads * dim
    build_strip(strip_ref, bias_ref, length, heads)
    lane = lax.broadcasted_iota(jnp.int32, (QB, PAD), 1) - inner
    pad_ref[...] = jnp.zeros_like(pad_ref)
    for t in range(3):
        pad_ref[t * PAD : t * PAD + inner, :] = w_ref[t]

    def project(b, carry):
        at = pl.multiple_of(b * QB, QB)
        here = x_ref[pl.ds(at, QB), :].astype(F32)
        normed = norm_rows(here, gain_ref[...]).astype(BF16)
        normed_ref[pl.ds(at, QB), :] = normed
        every = nt_dot(normed, pad_ref[...])
        same = doc_ref[pl.ds(at, QB), :] == lane
        queries = (every[:, 0:PAD].astype(BF16) * jnp.bfloat16(dim ** (-0.5))).astype(F32)
        queries = queries + jnp.where((lane < 0) | same, 0.0, MASKED)
        keys = every[:, PAD : 2 * PAD]
        values = every[:, 2 * PAD : 3 * PAD]
        proj_ref[pl.ds(at, QB), 0:PAD] = queries.astype(BF16)
        proj_ref[pl.ds(at, QB), PAD : 2 * PAD] = (keys + jnp.where(same, 1.0, 0.0)).astype(BF16)
        proj_ref[pl.ds(at, QB), 2 * PAD : 3 * PAD] = values.astype(BF16)
        kt_ref[:, pl.ds(at, QB)] = keys.T[:inner].astype(BF16)
        vt_ref[:, pl.ds(at, QB)] = values.T[:inner].astype(BF16)
        return carry

    lax.fori_loop(0, length // QB, project, 0)
    keys = proj_ref[:, PAD : 2 * PAD]
    for h in range(heads):
        kh_ref[h] = jnp.where(head_lanes(length, h, dim, True, heads), keys, jnp.zeros_like(keys))

    def block(b, carry):
        at = pl.multiple_of(b * QB, QB)
        from_row = pl.multiple_of(length - QB - b * QB, QB)
        queries = proj_ref[pl.ds(at, QB), 0:PAD]
        for h in range(heads):
            scores = nt_dot(kh_ref[h], queries) + strip_ref[h, pl.ds(from_row, length), :]
            top = jnp.max(scores, 0, keepdims=True)
            probs = jnp.exp(scores - top)
            total = jnp.sum(probs, 0, keepdims=True)
            out = nn_dot(vt_ref[h * dim : (h + 1) * dim, :], probs.astype(BF16))
            att_ref[h * dim : (h + 1) * dim, pl.ds(at, QB)] = (out / total).astype(BF16)
            lse_ref[h : h + 1, pl.ds(at, QB)] = top + jnp.log(total)
        return carry

    lax.fori_loop(0, length // QB, block, 0)


def attend_back_kernel(
    length, heads, dim,
    proj_ref, kt_ref, lse_ref, da_ref, normed_ref, w_ref, gproj_ref, bias_ref, low_ref,
    grad_ref, kept_ref, sent_ref, drel_ref,
    kh_ref, vh_ref, strip_ref, dstrip_ref, pcat_ref, dcat_ref, dacat_ref, qcat_ref, dk_ref, dv_ref, dqt_ref,
    dq_ref, pad_ref,
):
    inner = heads * dim
    scale = dim ** (-0.5)
    total = strip_shape(length)
    base, first, last = near_rows(length)
    build_strip(strip_ref, bias_ref, length, heads)
    dstrip_ref[...] = jnp.zeros_like(dstrip_ref)
    dk_ref[...] = jnp.zeros_like(dk_ref)
    dv_ref[...] = jnp.zeros_like(dv_ref)
    dqt_ref[...] = jnp.zeros_like(dqt_ref)
    keys = proj_ref[:, PAD : 2 * PAD]
    values = proj_ref[:, 2 * PAD : 3 * PAD]
    for h in range(heads):
        kh_ref[h] = jnp.where(head_lanes(length, h, dim, True, heads), keys, jnp.zeros_like(keys))
        vh_ref[h] = jnp.where(head_lanes(length, h, dim, False, heads), values, jnp.zeros_like(values))

    def block(b, carry):
        at = pl.multiple_of(b * QB, QB)
        from_row = pl.multiple_of(length - QB - b * QB, QB)
        queries = proj_ref[pl.ds(at, QB), 0:PAD]
        grads = da_ref[pl.ds(at, QB), :]
        for h in range(heads):
            mine = head_lanes(QB, h, dim, False, heads)
            cols = slice(h * QB, (h + 1) * QB)
            qcat_ref[cols, :] = jnp.where(mine, queries, jnp.zeros_like(queries))
            dacat_ref[cols, :] = jnp.where(mine, grads, jnp.zeros_like(grads))
            scores = nt_dot(kh_ref[h], queries) + strip_ref[h, pl.ds(from_row, length), :]
            probs = jnp.exp(scores - lse_ref[h : h + 1, pl.ds(at, QB)])
            weighted = probs * nt_dot(vh_ref[h], grads)
            delta = jnp.sum(weighted, 0, keepdims=True)
            dscore = weighted - probs * delta
            dstrip_ref[h, pl.ds(from_row, length), :] += dscore
            dlow = dscore.astype(BF16)
            pcat_ref[:, cols] = probs.astype(BF16)
            dcat_ref[:, cols] = dlow
            dqt_ref[h * dim : (h + 1) * dim, :] = nn_dot(kt_ref[h * dim : (h + 1) * dim, :], dlow) * scale
        dk_ref[...] += nn_dot(dcat_ref[...], qcat_ref[...])
        dv_ref[...] += nn_dot(pcat_ref[...], dacat_ref[...])
        dq_ref[pl.ds(at, QB), :] = dqt_ref[...].T
        return carry

    lax.fori_loop(0, length // QB, block, 0)

    for t, ref in enumerate((dq_ref, dk_ref, dv_ref)):
        turned = ref[...].T[:inner].astype(BF16)
        grad_ref[t * inner : (t + 1) * inner, :] = nn_dot(turned, normed_ref[...]).astype(BF16)

    grad_ref[3 * inner :, :] = gproj_ref[...]

    pad_ref[...] = jnp.zeros_like(pad_ref)
    for t in range(3):
        pad_ref[t, 0:inner, :] = w_ref[t]
    half = length // 2

    def part(start):
        total = jnp.zeros((QB, w_ref.shape[2]), F32)
        for t, ref in enumerate((dq_ref, dk_ref, dv_ref)):
            total = total + nn_dot(ref[pl.ds(start, QB), :].astype(BF16), pad_ref[t])
        return total

    for i in range(half // QB):
        rows = slice(i * QB, (i + 1) * QB)
        kept_ref[rows, :] = part(pl.multiple_of(low_ref[0] * half + i * QB, QB))
        sent_ref[rows, :] = part(pl.multiple_of((1 - low_ref[0]) * half + i * QB, QB)).astype(BF16)

    offset = (
        lax.broadcasted_iota(jnp.int32, (last - first, 128), 0)
        - lax.broadcasted_iota(jnp.int32, (last - first, 128), 1)
        + (first - base)
    )
    begins = [-(1 << 20)] + [begin for begin, bucket in STEPS] + [1 << 20]
    buckets = [15] + [bucket for begin, bucket in STEPS]
    for h in range(heads):
        near = jnp.zeros((last - first, 128), F32)
        low = jnp.zeros((1, 128), F32)
        high = jnp.zeros((1, 128), F32)
        for half in range(QB // 128):
            cols = slice(half * 128, half * 128 + 128)
            lo_end, hi_start = first + half * 128, last + half * 128
            near = near + dstrip_ref[h, lo_end:hi_start, cols]
            low = low + jnp.sum(dstrip_ref[h, 0:lo_end, cols], 0, keepdims=True)
            high = high + jnp.sum(dstrip_ref[h, hi_start:total, cols], 0, keepdims=True)
        drel_ref[h, 16:17, :] = jnp.zeros((1, 128), F32)
        for i, bucket in enumerate(buckets):
            inside = (offset >= begins[i]) & (offset < begins[i + 1])
            row = jnp.sum(jnp.where(inside, near, 0.0), 0, keepdims=True)
            if bucket == 15:
                row = row + low
            if bucket == 31:
                row = row + high
            drel_ref[h, bucket : bucket + 1, :] = row


def whole_vmem(count):
    return [pl.BlockSpec(memory_space=pltpu.VMEM)] * count


def attend(tokens, gain, w_qkv, segments, rel_bias):
    length, width = tokens.shape
    heads = rel_bias.shape[0]
    inner = w_qkv.shape[1]
    return pl.pallas_call(
        functools.partial(attend_kernel, length, heads, inner // heads),
        out_shape=(
            jax.ShapeDtypeStruct((inner, length), BF16),
            jax.ShapeDtypeStruct((8, length), F32),
            jax.ShapeDtypeStruct((length, 3 * PAD), BF16),
            jax.ShapeDtypeStruct((inner, length), BF16),
            jax.ShapeDtypeStruct((length, width), BF16),
        ),
        in_specs=whole_vmem(4) + [pl.BlockSpec(memory_space=pltpu.SMEM)],
        out_specs=tuple(whole_vmem(5)),
        scratch_shapes=[
            pltpu.VMEM((heads, length, PAD), BF16),
            pltpu.VMEM((heads, strip_shape(length), QB), F32),
            pltpu.VMEM((inner, length), BF16),
            pltpu.VMEM((3 * PAD, width), BF16),
        ],
        compiler_params=pltpu.CompilerParams(vmem_limit_bytes=20 << 20),
        cost_estimate=SMALL,
    )(tokens, gain[None, :], w_qkv, segments[:, None], rel_bias)


def attend_back(proj, kt, lse, da, normed, w_qkv, grad_proj, rel_bias, low_bit):
    length, width = normed.shape
    heads, buckets = rel_bias.shape
    inner = w_qkv.shape[1]
    return pl.pallas_call(
        functools.partial(attend_back_kernel, length, heads, inner // heads),
        out_shape=(
            jax.ShapeDtypeStruct((4 * inner, width), BF16),
            jax.ShapeDtypeStruct((length // 2, width), F32),
            jax.ShapeDtypeStruct((length // 2, width), BF16),
            jax.ShapeDtypeStruct((heads, buckets, 128), F32),
        ),
        in_specs=whole_vmem(7) + [pl.BlockSpec(memory_space=pltpu.SMEM)] * 2,
        out_specs=tuple(whole_vmem(4)),
        scratch_shapes=[
            pltpu.VMEM((heads, length, PAD), BF16),
            pltpu.VMEM((heads, length, PAD), BF16),
            pltpu.VMEM((heads, strip_shape(length), QB), F32),
            pltpu.VMEM((heads, strip_shape(length), QB), F32),
            pltpu.VMEM((length, heads * QB), BF16),
            pltpu.VMEM((length, heads * QB), BF16),
            pltpu.VMEM((heads * QB, PAD), BF16),
            pltpu.VMEM((heads * QB, PAD), BF16),
            pltpu.VMEM((length, PAD), F32),
            pltpu.VMEM((length, PAD), F32),
            pltpu.VMEM((PAD, QB), F32),
            pltpu.VMEM((length, PAD), F32),
            pltpu.VMEM((3, PAD, width), BF16),
        ],
        compiler_params=pltpu.CompilerParams(vmem_limit_bytes=36 << 20),
        cost_estimate=SMALL,
    )(proj, kt, lse, da, normed, w_qkv, grad_proj, rel_bias, low_bit)


def gelu_pair(v):
    inner = 0.7978845608028654 * (v + 0.044715 * (v * v * v))
    bend = jnp.tanh(inner)
    half = 0.5 * (1.0 + bend)
    slope = half + 0.5 * v * (1.0 - bend * bend) * (0.7978845608028654 * (1.0 + 0.134145 * (v * v)))
    return v * half, slope


def expert_kernel(
    members, experts,
    rows_ref, cot_ref, router_ref, group_ref, *refs,
):
    first, second = refs[:members], refs[members : 2 * members]
    reply_ref, share_ref, act_ref, gpre_ref, grad_ref, grouter_ref = refs[2 * members :]
    rows = rows_ref[...]
    count = rows.shape[0]
    lane = lax.broadcasted_iota(jnp.int32, (count, 128), 1)
    logits = jnp.where(lane < experts, nn_dot(rows, router_ref[...]), MASKED)
    raised = jnp.exp(logits - jnp.max(logits, -1, keepdims=True))
    probs = raised / jnp.sum(raised, -1, keepdims=True)
    own = jnp.where(lane == group_ref[0], 1.0, 0.0)
    gate = jnp.sum(probs * own, -1, keepdims=True)
    cot = cot_ref[...].astype(F32)
    grads = (gate * cot).astype(BF16)
    grad_ref[...] = grads
    reply = jnp.zeros(rows.shape, F32)
    share = jnp.zeros(rows.shape, F32)
    for k in range(members):
        act, slope = gelu_pair(nn_dot(rows, first[k][...]))
        act = act.astype(BF16)
        act_ref[k] = act
        reply = reply + nn_dot(act, second[k][...])
        gpre = (nt_dot(grads, second[k][...]) * slope).astype(BF16)
        gpre_ref[k] = gpre
        share = share + nt_dot(gpre, first[k][...])
    reply = reply.astype(BF16)
    reply_ref[...] = reply
    gate_grad = jnp.sum(cot * reply.astype(F32), -1, keepdims=True)
    logit_grad = probs * (own - gate) * gate_grad
    share_ref[...] = (share + nt_dot(logit_grad.astype(BF16), router_ref[...])).astype(BF16)
    grouter_ref[...] = nn_dot(logit_grad.T.astype(BF16), rows)


def expert_step(rows, cot, experts, router, group, first, second):
    members = len(first)
    count, width = rows.shape
    hidden = first[0].shape[1]
    return pl.pallas_call(
        functools.partial(expert_kernel, members, experts),
        out_shape=(
            jax.ShapeDtypeStruct((count, width), BF16),
            jax.ShapeDtypeStruct((count, width), BF16),
            jax.ShapeDtypeStruct((members, count, hidden), BF16),
            jax.ShapeDtypeStruct((members, count, hidden), BF16),
            jax.ShapeDtypeStruct((count, width), BF16),
            jax.ShapeDtypeStruct((128, width), F32),
        ),
        in_specs=whole_vmem(3) + [pl.BlockSpec(memory_space=pltpu.SMEM)] + whole_vmem(2 * members),
        out_specs=tuple(whole_vmem(6)),
        compiler_params=pltpu.CompilerParams(vmem_limit_bytes=24 << 20),
        cost_estimate=SMALL,
    )(rows, cot, router, group, *first, *second)


def rows_of(count, columns):
    return pl.BlockSpec((count, columns), lambda i: (i, 0))


def whole_of(*shape):
    return pl.BlockSpec(shape, lambda i: (0,) * len(shape))


def enter_kernel(
    members, experts,
    x_ref, gain_ref, router_ref, route_ref, flat_ref, ids_ref, *refs,
):
    att, proj = refs[:members], refs[members : 2 * members]
    hidden_ref, gate_ref, leave_ref, total_ref = refs[2 * members :]
    step = pl.program_id(0)
    hidden = x_ref[...].astype(F32)
    for k in range(members):
        hidden = hidden + lax.dot_general(
            att[k][...], proj[k][...], (((0,), (0,)), ((), ())), preferred_element_type=F32
        )
    hidden_ref[...] = hidden
    normed = norm_rows(hidden, gain_ref[...]).astype(BF16)
    lane = lax.broadcasted_iota(jnp.int32, (QB, 128), 1)
    logits = jnp.where(lane < experts, nn_dot(normed, router_ref[...]), MASKED)
    raised = jnp.exp(logits - jnp.max(logits, -1, keepdims=True))
    chosen = jnp.sum(jnp.where(lane == route_ref[...], raised, 0.0), -1, keepdims=True)
    gate_ref[...] = chosen / jnp.sum(raised, -1, keepdims=True)
    table = jnp.where(ids_ref[...] == flat_ref[...], 1.0, 0.0).astype(BF16)

    @pl.when(step == 0)
    def _():
        total_ref[...] = jnp.zeros_like(total_ref)

    total_ref[...] += nn_dot(table, normed)

    @pl.when(step == pl.num_programs(0) - 1)
    def _():
        leave_ref[...] = total_ref[...].astype(BF16)


def enter_experts(tokens, experts, gain, router, route, flat_id, ids, att, proj):
    length, width = tokens.shape
    members = len(att)
    inner = att[0].shape[0]
    count = ids.shape[0]
    return pl.pallas_call(
        functools.partial(enter_kernel, members, experts),
        grid=(length // QB,),
        out_shape=(
            jax.ShapeDtypeStruct((length, width), F32),
            jax.ShapeDtypeStruct((length, 1), F32),
            jax.ShapeDtypeStruct((count, width), BF16),
        ),
        in_specs=[
            rows_of(QB, width),
            whole_of(1, width),
            whole_of(width, 128),
            rows_of(QB, 1),
            pl.BlockSpec((1, QB), lambda i: (0, i)),
            whole_of(count, 1),
        ]
        + [pl.BlockSpec((inner, QB), lambda i: (0, i))] * members
        + [whole_of(inner, width)] * members,
        out_specs=(rows_of(QB, width), rows_of(QB, 1), whole_of(count, width)),
        scratch_shapes=[pltpu.VMEM((count, width), F32)],
        compiler_params=pltpu.CompilerParams(vmem_limit_bytes=20 << 20),
        cost_estimate=SMALL,
    )(
        tokens, gain, router, route, flat_id, ids, *att, *proj,
    )


def weight_kernel(half, rows_ref, grads_ref, act_ref, gpre_ref, kept_ref, sent_ref):
    step = pl.program_id(0)

    def product(left, right):
        return lax.dot_general(
            left, right, (((0,), (0,)), ((), ())), preferred_element_type=F32
        ).astype(BF16)

    @pl.when(step < half)
    def _():
        k = 2 * step
        kept_ref[0] = product(act_ref[k], grads_ref[...])
        sent_ref[0] = product(act_ref[k + 1], grads_ref[...])

    @pl.when(step >= half)
    def _():
        k = 2 * (step - half)
        kept_ref[0] = product(rows_ref[...], gpre_ref[k])
        sent_ref[0] = product(rows_ref[...], gpre_ref[k + 1])


def weight_grads(rows, grads, act, gpre):
    members, count, hidden = act.shape
    width = rows.shape[1]
    assert hidden == width
    one = pl.BlockSpec((1, width, width), lambda i: (i, 0, 0))
    return pl.pallas_call(
        functools.partial(weight_kernel, members // 2),
        grid=(members,),
        out_shape=(
            jax.ShapeDtypeStruct((members, width, width), BF16),
            jax.ShapeDtypeStruct((members, width, width), BF16),
        ),
        in_specs=[whole_of(count, width)] * 2 + [whole_of(members, count, hidden)] * 2,
        out_specs=(one, one),
        compiler_params=pltpu.CompilerParams(vmem_limit_bytes=24 << 20),
        cost_estimate=SMALL,
    )(rows, grads, act, gpre)


def leave_kernel(
    members,
    hidden_ref, cot_ref, gain_ref, flat_ref, ids_ref, wproj_ref, att_ref, *refs,
):
    blocks = refs[:members]
    gh_ref, da_ref, ggain_ref, gproj_ref, total_ref = refs[members:]
    step = pl.program_id(0)
    share = blocks[0].shape[0]
    grad = jnp.zeros(hidden_ref.shape, F32)
    for k in range(members):
        hit = flat_ref[...] == ids_ref[:, k * share : (k + 1) * share]
        grad = grad + nn_dot(jnp.where(hit, 1.0, 0.0).astype(BF16), blocks[k][...])
    hidden = hidden_ref[...]
    inverse = lax.rsqrt(jnp.mean(hidden * hidden, -1, keepdims=True) + 1e-06)
    unit = hidden * inverse
    scaled = gain_ref[...] * grad
    back = inverse * (scaled - unit * jnp.mean(unit * scaled, -1, keepdims=True))
    total = cot_ref[...].astype(F32) + back
    gh_ref[...] = total
    low = total.astype(BF16)
    da_ref[...] = nt_dot(low, wproj_ref[...]).astype(BF16)

    @pl.when(step == 0)
    def _():
        ggain_ref[...] = jnp.zeros_like(ggain_ref)
        total_ref[...] = jnp.zeros_like(total_ref)

    ggain_ref[...] += jnp.sum(grad * unit, 0, keepdims=True)
    total_ref[...] += nn_dot(att_ref[...], low)

    @pl.when(step == pl.num_programs(0) - 1)
    def _():
        gproj_ref[...] = total_ref[...].astype(BF16)


def leave_experts(hidden1, cotangent, gain, flat_id, ids, w_proj, attended_t, blocks):
    length, width = hidden1.shape
    inner = attended_t.shape[0]
    members = len(blocks)
    share = blocks[0].shape[0]
    return pl.pallas_call(
        functools.partial(leave_kernel, members),
        grid=(length // QB,),
        out_shape=(
            jax.ShapeDtypeStruct((length, width), F32),
            jax.ShapeDtypeStruct((length, PAD), BF16),
            jax.ShapeDtypeStruct((1, width), F32),
            jax.ShapeDtypeStruct((inner, width), BF16),
        ),
        in_specs=[
            rows_of(QB, width),
            rows_of(QB, width),
            whole_of(1, width),
            rows_of(QB, 1),
            whole_of(1, members * share),
            whole_of(PAD, width),
            pl.BlockSpec((inner, QB), lambda i: (0, i)),
        ]
        + [whole_of(share, width)] * members,
        out_specs=(
            rows_of(QB, width),
            rows_of(QB, PAD),
            whole_of(1, width),
            whole_of(inner, width),
        ),
        scratch_shapes=[pltpu.VMEM((inner, width), F32)],
        compiler_params=pltpu.CompilerParams(vmem_limit_bytes=24 << 20),
        cost_estimate=SMALL,
    )(
        hidden1, cotangent, gain, flat_id, ids, w_proj, attended_t, *blocks,
    )


def output_kernel(members, hidden_ref, gate_ref, flat_ref, ids_ref, *refs):
    blocks, out_ref = refs[:members], refs[members]
    share = blocks[0].shape[0]
    reply = jnp.zeros(hidden_ref.shape, F32)
    for k in range(members):
        hit = flat_ref[...] == ids_ref[:, k * share : (k + 1) * share]
        reply = reply + nn_dot(jnp.where(hit, 1.0, 0.0).astype(BF16), blocks[k][...])
    out_ref[...] = (hidden_ref[...] + gate_ref[...] * reply).astype(BF16)


def output_rows(hidden1, gate, flat_id, ids, blocks):
    length, width = hidden1.shape
    members = len(blocks)
    share = blocks[0].shape[0]
    return pl.pallas_call(
        functools.partial(output_kernel, members),
        grid=(length // QB,),
        out_shape=jax.ShapeDtypeStruct((length, width), BF16),
        in_specs=[rows_of(QB, width), rows_of(QB, 1), rows_of(QB, 1), whole_of(1, members * share)]
        + [whole_of(share, width)] * members,
        out_specs=rows_of(QB, width),
        compiler_params=pltpu.CompilerParams(vmem_limit_bytes=20 << 20),
        cost_estimate=SMALL,
    )(hidden1, gate, flat_id, ids, *blocks)


def input_kernel(halves, kept_ref, other_ref, x_ref, gain_ref, gh_ref, low_ref, out_ref, ggain_ref):
    step = pl.program_id(0)
    part = jnp.where(step // halves == low_ref[0], kept_ref[...].astype(F32), other_ref[...].astype(F32))
    x = x_ref[...].astype(F32)
    inverse = lax.rsqrt(jnp.mean(x * x, -1, keepdims=True) + 1e-06)
    unit = x * inverse
    scaled = gain_ref[...] * part
    out_ref[...] = gh_ref[...] + inverse * (scaled - unit * jnp.mean(unit * scaled, -1, keepdims=True))

    @pl.when(step == 0)
    def _():
        ggain_ref[...] = jnp.zeros_like(ggain_ref)

    ggain_ref[...] += jnp.sum(part * unit, 0, keepdims=True)


def input_grads(kept, other, tokens, gain, grad_hidden1, low_bit):
    length, width = tokens.shape
    halves = kept.shape[0] // QB
    half = pl.BlockSpec((QB, width), lambda i: (i % halves, 0))
    return pl.pallas_call(
        functools.partial(input_kernel, halves),
        grid=(length // QB,),
        out_shape=(
            jax.ShapeDtypeStruct((length, width), F32),
            jax.ShapeDtypeStruct((1, width), F32),
        ),
        in_specs=[
            half,
            half,
            rows_of(QB, width),
            whole_of(1, width),
            rows_of(QB, width),
            pl.BlockSpec(memory_space=pltpu.SMEM),
        ],
        out_specs=(rows_of(QB, width), whole_of(1, width)),
        compiler_params=pltpu.CompilerParams(vmem_limit_bytes=16 << 20),
        cost_estimate=SMALL,
    )(kept, other, tokens, gain[None, :], grad_hidden1, low_bit)


def copies_kernel(came_ref, small_ref, out_ref, mine_ref):
    groups, large = came_ref.shape[:2]

    @pl.when(pl.program_id(0) == 0)
    def _():
        total = came_ref[0].astype(F32)
        for g in range(1, groups):
            total = total + came_ref[g].astype(F32)
        mine_ref[:large, :] = total.astype(BF16)
        mine_ref[large:, :] = small_ref[...].astype(BF16)

    out_ref[0] = mine_ref[...]


def sum_copies(came, small):
    groups, large, width = came.shape
    count = large + small.shape[0]
    return pl.pallas_call(
        copies_kernel,
        grid=(groups,),
        out_shape=jax.ShapeDtypeStruct((groups, count, width), BF16),
        in_specs=[whole_of(groups, large, width), whole_of(*small.shape)],
        out_specs=pl.BlockSpec((1, count, width), lambda i: (i, 0, 0)),
        scratch_shapes=[pltpu.VMEM((count, width), BF16)],
        compiler_params=pltpu.CompilerParams(vmem_limit_bytes=12 << 20),
        cost_estimate=SMALL,
    )(came, small)


def final_kernel(large, inner, totals_ref, qkv_ref, proj_ref, small_ref):
    groups = totals_ref.shape[0]
    split = 3 * inner
    small = totals_ref[0, large:, :].astype(F32)
    for g in range(groups):
        start, stop = g * large, (g + 1) * large
        if start < split:
            count = min(stop, split) - start
            qkv_ref[start : start + count, :] = totals_ref[g, :count, :].astype(F32)
        if stop > split:
            skip = max(start, split) - start
            proj_ref[start + skip - split : stop - split, :] = totals_ref[g, skip:large, :].astype(F32)
        if g:
            small = small + totals_ref[g, large:, :].astype(F32)
    small_ref[...] = small


def final_weights(totals, large, inner):
    groups, count, width = totals.shape
    return pl.pallas_call(
        functools.partial(final_kernel, large, inner),
        out_shape=(
            jax.ShapeDtypeStruct((3 * inner, width), F32),
            jax.ShapeDtypeStruct((inner, width), F32),
            jax.ShapeDtypeStruct((count - large, width), F32),
        ),
        in_specs=whole_vmem(1),
        out_specs=tuple(whole_vmem(3)),
        compiler_params=pltpu.CompilerParams(vmem_limit_bytes=8 << 20),
        cost_estimate=SMALL,
    )(totals)


def shards(
    tokens,
    gain_attn,
    w_qkv,
    w_proj,
    rel_bias,
    gain_ffn,
    w_router,
    w_in,
    w_out,
    routes,
    segment_ids,
    cotangent,
):
    length, width = tokens.shape
    experts = w_router.shape[1]
    capacity = max(2, 3 * length // (2 * experts))
    inner_here = w_proj.shape[0]
    members = lax.axis_size("tensor")
    groups = lax.axis_size("expert")
    member = lax.axis_index("tensor")
    group = lax.axis_index("expert")
    share = capacity // members
    segments = segment_ids[0]
    route = routes[:, 0]

    def swap(value, bit):
        return lax.ppermute(value, "tensor", [(i, i ^ bit) for i in range(members)])

    bits = [1 << i for i in range(members.bit_length() - 1)]

    def gather_far(value):
        blocks = {0: value}
        for bit in reversed(bits[1:]):
            blocks.update({k ^ bit: swap(block, bit) for k, block in blocks.items()})
        return blocks

    def gather_near(blocks):
        blocks = dict(blocks)
        for bit in bits[:1]:
            blocks.update({k ^ bit: swap(block, bit) for k, block in blocks.items()})
        return [blocks[k] for k in range(members)]

    def gather_members(value):
        return gather_near(gather_far(value))

    def gather_groups(value):
        copies = jnp.broadcast_to(value[None], (groups,) + value.shape)
        return exchange(copies)

    def exchange(value):
        return lax.all_to_all(value, "expert", split_axis=0, concat_axis=0, tiled=True)

    tie = lax.optimization_barrier

    expert_ids = jnp.arange(experts, dtype=jnp.int32)
    onehot_low = (route[:, None] == expert_ids[None, :]).astype(BF16)
    onehot = onehot_low.astype(F32)
    positions = jnp.arange(length, dtype=jnp.int32)
    lower_ones = (positions[:, None] >= positions[None, :]).astype(BF16)
    running = nn_dot(lower_ones, onehot_low)
    slot = (jnp.sum(running * onehot, 1) - 1.0).astype(jnp.int32)
    flat_id = route * capacity + slot

    def ids_of(owner):
        slots = owner * share + jnp.arange(share, dtype=jnp.int32)
        return (expert_ids[:, None] * capacity + slots[None, :]).reshape(-1)

    send_table = (ids_of(member)[:, None] == flat_id[None, :]).astype(BF16)
    all_ids = jnp.concatenate([ids_of(member ^ k) for k in range(members)])

    def dispatch(rows):
        out = nn_dot(send_table, rows).astype(BF16).reshape(groups, -1, width)
        return exchange(out).reshape(-1, width)

    cot_share = dispatch(cotangent)
    w_proj_far = gather_far(w_proj)
    w_in_far = gather_far(w_in[0])
    w_qkv_t = jnp.swapaxes(w_qkv, 1, 2)
    attended_t, lse, proj, keys_t, normed1 = attend(tokens, gain_attn, w_qkv_t, segments, rel_bias)
    attended_t, w_in_far, cot_share = tie((attended_t, w_in_far, cot_share))

    attended_far = gather_far(attended_t)
    gain_row = gain_ffn[None, :]
    router = jnp.pad(w_router, ((0, 0), (0, 128 - experts)))
    w_proj_pad = jnp.pad(w_proj, ((0, PAD - inner_here), (0, 0)))
    flat_row, flat_column = flat_id[None, :], flat_id[:, None]
    send_ids, back_ids = ids_of(member)[:, None], all_ids[None, :]
    (
        attended_far, w_proj_far, w_out_here, gain_row, router, w_proj_pad,
        flat_row, flat_column, send_ids, back_ids,
    ) = tie((
        attended_far, w_proj_far, w_out[0], gain_row, router, w_proj_pad,
        flat_row, flat_column, send_ids, back_ids,
    ))
    attended_blocks = gather_near(attended_far)
    w_proj_blocks = gather_near(w_proj_far)
    w_in_all = gather_near(w_in_far)
    w_out_far = gather_far(w_out_here)
    hidden1, gate, leaving = enter_experts(
        tokens, experts, gain_row, router, routes, flat_row, send_ids, attended_blocks, w_proj_blocks
    )
    rows = exchange(leaving.reshape(groups, -1, width)).reshape(-1, width)
    rows, w_out_far, w_in_all = tie((rows, w_out_far, w_in_all))
    w_out_all = gather_near(w_out_far)

    reply, grad_share, act, grad_pre, grad_rows, grad_router = expert_step(
        rows, cot_share, experts, router, group[None], w_in_all, w_out_all
    )
    grad_back = exchange(grad_share.reshape(groups, -1, width)).reshape(-1, width)
    grad_router = grad_router[:experts]
    grad_router = grad_router + swap(grad_router, 1)
    grad_router, rows, grad_rows, act, grad_pre = tie((grad_router, rows, grad_rows, act, grad_pre))
    kept_weights, sent_weights = weight_grads(rows, grad_rows, act, grad_pre)
    near_weights = swap(sent_weights, 1)
    for bit in bits[1:]:
        grad_router = grad_router + swap(grad_router, bit)
    grad_back, reply, near_weights, grad_router = tie((grad_back, reply, near_weights, grad_router))
    grad_far = gather_far(grad_back)
    out_sent = (kept_weights[1].astype(F32) + near_weights[1].astype(F32)).astype(BF16)
    in_sent = (kept_weights[3].astype(F32) + near_weights[3].astype(F32)).astype(BF16)
    grad_far, out_sent, in_sent = tie((grad_far, out_sent, in_sent))
    out_came, in_came = swap(out_sent, 2), swap(in_sent, 2)
    grad_blocks = gather_near(grad_far)
    reply_back = exchange(reply.reshape(groups, -1, width)).reshape(-1, width)
    grad_hidden1, attended_grad, grad_gain_ffn, grad_proj = leave_experts(
        hidden1, cotangent, gain_row, flat_column, back_ids, w_proj_pad, attended_t, grad_blocks
    )

    low_bit = (member & 1)[None]
    grads, kept, sent, rel_parts = attend_back(
        proj, keys_t, lse, attended_grad, normed1, w_qkv_t, grad_proj, rel_bias, low_bit
    )
    grads, kept, sent, reply_back, out_came, in_came = tie(
        (grads, kept, sent, reply_back, out_came, in_came)
    )
    kept = kept + swap(sent, 1).astype(F32)
    kept_low, grads = tie((kept.astype(BF16), grads))
    far = swap(kept_low, 2)
    came = exchange(grads.reshape(groups, -1, width))
    reply_far = gather_far(reply_back)
    grad_w_out = kept_weights[0].astype(F32) + near_weights[0].astype(F32) + out_came.astype(F32)
    grad_w_in = kept_weights[2].astype(F32) + near_weights[2].astype(F32) + in_came.astype(F32)

    rel_row = jnp.sum(rel_parts, -1).reshape(1, -1)
    rel_row = jnp.pad(rel_row, ((0, 0), (0, width - rel_row.shape[1])))
    small = jnp.concatenate([grad_gain_ffn, rel_row, grad_router], 0)
    small = jnp.pad(small, ((0, -small.shape[0] % 16), (0, 0)))
    large = came.shape[1]
    if large % 16 == 0:
        copies = sum_copies(came, small)
    else:
        copies = jnp.concatenate([jnp.sum(came.astype(F32), 0), small], 0).astype(BF16)
        copies = jnp.broadcast_to(copies[None], (groups,) + copies.shape)
    far, copies, grad_w_out, grad_w_in, reply_far = tie((far, copies, grad_w_out, grad_w_in, reply_far))
    totals = exchange(copies)
    kept = (kept + far.astype(F32)).astype(BF16)
    other = swap(kept, 1)
    grad_input, gain_part = input_grads(kept, other, tokens, gain_attn, grad_hidden1, low_bit)
    grad_gain_attn = jnp.sum(gather_groups(gain_part), (0, 1))
    output = output_rows(hidden1, gate, flat_column, back_ids, gather_near(reply_far))
    if large % 16 == 0:
        grad_qkv_t, grad_proj, small = final_weights(totals, large, inner_here)
    else:
        shared = totals[:, :large].reshape(-1, width).astype(F32)
        grad_qkv_t, grad_proj = shared[: 3 * inner_here], shared[3 * inner_here :]
        small = jnp.sum(totals[:, large:].astype(F32), 0)
    grad_qkv = jnp.swapaxes(grad_qkv_t.reshape(3, inner_here, width), 1, 2)
    grad_gain_ffn = small[0]
    grad_rel = small[1, : rel_bias.size].reshape(rel_bias.shape)
    grad_router = small[2 : 2 + experts].T
    return (
        output,
        grad_input,
        grad_gain_attn,
        grad_qkv,
        grad_proj,
        grad_rel,
        grad_gain_ffn,
        grad_router,
        grad_w_in[None],
        grad_w_out[None],
    )


def solution(mesh):
    placed = (
        P("expert", None),
        P(),
        P(None, None, "tensor"),
        P("tensor", None),
        P("tensor", None),
        P(),
        P(),
        P("expert", None, "tensor"),
        P("expert", "tensor", None),
        P("expert", None),
        P("expert", None),
        P("expert", None),
    )
    return jax.shard_map(
        shards,
        mesh=mesh,
        in_specs=placed,
        out_specs=(
            P("expert", None),
            P("expert", None),
            P(),
            P(None, None, "tensor"),
            P("tensor", None),
            P("tensor", None),
            P(),
            P(),
            P("expert", None, "tensor"),
            P("expert", "tensor", None),
        ),
        check_vma=False,
    )
```

```python
import functools

import jax
import jax.numpy as jnp
from jax import lax
from jax.experimental import pallas as pl
from jax.experimental.pallas import tpu as pltpu
from jax.sharding import PartitionSpec as P

FAR_LIMITS = (12, 16, 23, 32, 46, 64, 91)
HIGH = lax.Precision.HIGHEST
F32 = jnp.float32
BF16 = jnp.bfloat16
MASKED = -1e30
QB = 256
PAD = 256
FAR = FAR_LIMITS[-1]
SMALL = pl.CostEstimate(flops=1 << 20, bytes_accessed=1 << 16, transcendentals=0)

STEPS = (
    [(1 - limit, 14 - i) for i, limit in enumerate(reversed(FAR_LIMITS))]
    + [(-n, n) for n in range(7, -1, -1)]
    + [(n, 16 + n) for n in range(1, 8)]
    + [(8, 24)]
    + [(limit, 25 + i) for i, limit in enumerate(FAR_LIMITS)]
)


def norm_rows(values, gain):
    return values * lax.rsqrt(jnp.mean(values * values, -1, keepdims=True) + 1e-06) * gain


def nt_dot(left, right):
    return lax.dot_general(left, right, (((1,), (1,)), ((), ())), preferred_element_type=F32)


def nn_dot(left, right):
    return jnp.dot(left, right, preferred_element_type=F32)


def strip_shape(length):
    return 2 * length - QB


def near_rows(length):
    base = length - QB
    first = (base - FAR) // 32 * 32
    last = -(-(base + 127 + FAR) // 32) * 32
    return base, first, last


def build_strip(strip_ref, bias_ref, length, heads):
    total = strip_shape(length)
    base, first, last = near_rows(length)
    for h in range(heads):
        low = jnp.full((8, 128), bias_ref[h, 15], F32)
        high = jnp.full((8, 128), bias_ref[h, 31], F32)
        for half in range(QB // 128):
            cols = slice(half * 128, half * 128 + 128)
            lo_end, hi_start = first + half * 128, last + half * 128
            strip_ref[h, 0:lo_end, cols] = jnp.broadcast_to(low[:1], (lo_end, 128))
            strip_ref[h, hi_start:total, cols] = jnp.broadcast_to(high[:1], (total - hi_start, 128))
    for start in range(first, last, 32):
        offset = (
            lax.broadcasted_iota(jnp.int32, (32, 128), 0)
            - lax.broadcasted_iota(jnp.int32, (32, 128), 1)
            + (start - base)
        )
        tiles = [jnp.full((32, 128), bias_ref[h, 15], F32) for h in range(heads)]
        for begin, bucket in STEPS:
            reached = offset >= begin
            tiles = [jnp.where(reached, bias_ref[h, bucket], tiles[h]) for h in range(heads)]
        for h in range(heads):
            for half in range(QB // 128):
                at = start + half * 128
                strip_ref[h, at : at + 32, half * 128 : half * 128 + 128] = tiles[h]


def head_lanes(rows, h, dim, keep_tail, heads):
    lane = lax.broadcasted_iota(jnp.int32, (rows, PAD), 1)
    inside = (lane >= h * dim) & (lane < (h + 1) * dim)
    if keep_tail:
        inside = inside | (lane >= heads * dim)
    return inside


def attend_kernel(
    length, heads, dim,
    x_ref, gain_ref, w_ref, doc_ref, bias_ref,
    att_ref, lse_ref, proj_ref, kt_ref, normed_ref,
    kh_ref, strip_ref, vt_ref, pad_ref,
):
    inner = heads * dim
    build_strip(strip_ref, bias_ref, length, heads)
    lane = lax.broadcasted_iota(jnp.int32, (QB, PAD), 1) - inner
    pad_ref[...] = jnp.zeros_like(pad_ref)
    for t in range(3):
        pad_ref[t * PAD : t * PAD + inner, :] = w_ref[t]

    def project(b, carry):
        at = pl.multiple_of(b * QB, QB)
        here = x_ref[pl.ds(at, QB), :].astype(F32)
        normed = norm_rows(here, gain_ref[...]).astype(BF16)
        normed_ref[pl.ds(at, QB), :] = normed
        every = nt_dot(normed, pad_ref[...])
        same = doc_ref[pl.ds(at, QB), :] == lane
        queries = (every[:, 0:PAD].astype(BF16) * jnp.bfloat16(dim ** (-0.5))).astype(F32)
        queries = queries + jnp.where((lane < 0) | same, 0.0, MASKED)
        keys = every[:, PAD : 2 * PAD]
        values = every[:, 2 * PAD : 3 * PAD]
        proj_ref[pl.ds(at, QB), 0:PAD] = queries.astype(BF16)
        proj_ref[pl.ds(at, QB), PAD : 2 * PAD] = (keys + jnp.where(same, 1.0, 0.0)).astype(BF16)
        proj_ref[pl.ds(at, QB), 2 * PAD : 3 * PAD] = values.astype(BF16)
        kt_ref[:, pl.ds(at, QB)] = keys.T[:inner].astype(BF16)
        vt_ref[:, pl.ds(at, QB)] = values.T[:inner].astype(BF16)
        return carry

    lax.fori_loop(0, length // QB, project, 0)
    keys = proj_ref[:, PAD : 2 * PAD]
    for h in range(heads):
        kh_ref[h] = jnp.where(head_lanes(length, h, dim, True, heads), keys, jnp.zeros_like(keys))

    def block(b, carry):
        at = pl.multiple_of(b * QB, QB)
        from_row = pl.multiple_of(length - QB - b * QB, QB)
        queries = proj_ref[pl.ds(at, QB), 0:PAD]
        for h in range(heads):
            scores = nt_dot(kh_ref[h], queries) + strip_ref[h, pl.ds(from_row, length), :]
            top = jnp.max(scores, 0, keepdims=True)
            probs = jnp.exp(scores - top)
            total = jnp.sum(probs, 0, keepdims=True)
            out = nn_dot(vt_ref[h * dim : (h + 1) * dim, :], probs.astype(BF16))
            att_ref[h * dim : (h + 1) * dim, pl.ds(at, QB)] = (out / total).astype(BF16)
            lse_ref[h : h + 1, pl.ds(at, QB)] = top + jnp.log(total)
        return carry

    lax.fori_loop(0, length // QB, block, 0)


def attend_back_kernel(
    length, heads, dim,
    proj_ref, kt_ref, lse_ref, da_ref, normed_ref, w_ref, gproj_ref, bias_ref, low_ref,
    grad_ref, kept_ref, sent_ref, drel_ref,
    kh_ref, vh_ref, strip_ref, dstrip_ref, pcat_ref, dcat_ref, dacat_ref, qcat_ref, dk_ref, dv_ref, dqt_ref,
    dq_ref, pad_ref,
):
    inner = heads * dim
    scale = dim ** (-0.5)
    total = strip_shape(length)
    base, first, last = near_rows(length)
    build_strip(strip_ref, bias_ref, length, heads)
    dstrip_ref[...] = jnp.zeros_like(dstrip_ref)
    dk_ref[...] = jnp.zeros_like(dk_ref)
    dv_ref[...] = jnp.zeros_like(dv_ref)
    dqt_ref[...] = jnp.zeros_like(dqt_ref)
    keys = proj_ref[:, PAD : 2 * PAD]
    values = proj_ref[:, 2 * PAD : 3 * PAD]
    for h in range(heads):
        kh_ref[h] = jnp.where(head_lanes(length, h, dim, True, heads), keys, jnp.zeros_like(keys))
        vh_ref[h] = jnp.where(head_lanes(length, h, dim, False, heads), values, jnp.zeros_like(values))

    def block(b, carry):
        at = pl.multiple_of(b * QB, QB)
        from_row = pl.multiple_of(length - QB - b * QB, QB)
        queries = proj_ref[pl.ds(at, QB), 0:PAD]
        grads = da_ref[pl.ds(at, QB), :]
        for h in range(heads):
            mine = head_lanes(QB, h, dim, False, heads)
            cols = slice(h * QB, (h + 1) * QB)
            qcat_ref[cols, :] = jnp.where(mine, queries, jnp.zeros_like(queries))
            dacat_ref[cols, :] = jnp.where(mine, grads, jnp.zeros_like(grads))
            scores = nt_dot(kh_ref[h], queries) + strip_ref[h, pl.ds(from_row, length), :]
            probs = jnp.exp(scores - lse_ref[h : h + 1, pl.ds(at, QB)])
            weighted = probs * nt_dot(vh_ref[h], grads)
            delta = jnp.sum(weighted, 0, keepdims=True)
            dscore = weighted - probs * delta
            dstrip_ref[h, pl.ds(from_row, length), :] += dscore
            dlow = dscore.astype(BF16)
            pcat_ref[:, cols] = probs.astype(BF16)
            dcat_ref[:, cols] = dlow
            dqt_ref[h * dim : (h + 1) * dim, :] = nn_dot(kt_ref[h * dim : (h + 1) * dim, :], dlow) * scale
        dk_ref[...] += nn_dot(dcat_ref[...], qcat_ref[...])
        dv_ref[...] += nn_dot(pcat_ref[...], dacat_ref[...])
        dq_ref[pl.ds(at, QB), :] = dqt_ref[...].T
        return carry

    lax.fori_loop(0, length // QB, block, 0)

    for t, ref in enumerate((dq_ref, dk_ref, dv_ref)):
        turned = ref[...].T[:inner].astype(BF16)
        grad_ref[t * inner : (t + 1) * inner, :] = nn_dot(turned, normed_ref[...]).astype(BF16)

    grad_ref[3 * inner :, :] = gproj_ref[...]

    pad_ref[...] = jnp.zeros_like(pad_ref)
    for t in range(3):
        pad_ref[t, 0:inner, :] = w_ref[t]
    half = length // 2

    def part(start):
        total = jnp.zeros((QB, w_ref.shape[2]), F32)
        for t, ref in enumerate((dq_ref, dk_ref, dv_ref)):
            total = total + nn_dot(ref[pl.ds(start, QB), :].astype(BF16), pad_ref[t])
        return total

    for i in range(half // QB):
        rows = slice(i * QB, (i + 1) * QB)
        kept_ref[rows, :] = part(pl.multiple_of(low_ref[0] * half + i * QB, QB))
        sent_ref[rows, :] = part(pl.multiple_of((1 - low_ref[0]) * half + i * QB, QB)).astype(BF16)

    offset = (
        lax.broadcasted_iota(jnp.int32, (last - first, 128), 0)
        - lax.broadcasted_iota(jnp.int32, (last - first, 128), 1)
        + (first - base)
    )
    begins = [-(1 << 20)] + [begin for begin, bucket in STEPS] + [1 << 20]
    buckets = [15] + [bucket for begin, bucket in STEPS]
    for h in range(heads):
        near = jnp.zeros((last - first, 128), F32)
        low = jnp.zeros((1, 128), F32)
        high = jnp.zeros((1, 128), F32)
        for half in range(QB // 128):
            cols = slice(half * 128, half * 128 + 128)
            lo_end, hi_start = first + half * 128, last + half * 128
            near = near + dstrip_ref[h, lo_end:hi_start, cols]
            low = low + jnp.sum(dstrip_ref[h, 0:lo_end, cols], 0, keepdims=True)
            high = high + jnp.sum(dstrip_ref[h, hi_start:total, cols], 0, keepdims=True)
        drel_ref[h, 16:17, :] = jnp.zeros((1, 128), F32)
        for i, bucket in enumerate(buckets):
            inside = (offset >= begins[i]) & (offset < begins[i + 1])
            row = jnp.sum(jnp.where(inside, near, 0.0), 0, keepdims=True)
            if bucket == 15:
                row = row + low
            if bucket == 31:
                row = row + high
            drel_ref[h, bucket : bucket + 1, :] = row


def rows_of(count, columns):
    return pl.BlockSpec((count, columns), lambda i: (i, 0))


def whole_of(*shape):
    return pl.BlockSpec(shape, lambda i: (0,) * len(shape))


def whole_like(*arrays):
    return [whole_of(*array.shape) for array in arrays]


def attend(tokens, gain, w_qkv, segments, rel_bias):
    length, width = tokens.shape
    heads = rel_bias.shape[0]
    inner = w_qkv.shape[1]
    operands = (tokens, gain[None, :], w_qkv, segments[:, None])
    results = (
        jax.ShapeDtypeStruct((inner, length), BF16),
        jax.ShapeDtypeStruct((8, length), F32),
        jax.ShapeDtypeStruct((length, 3 * PAD), BF16),
        jax.ShapeDtypeStruct((inner, length), BF16),
        jax.ShapeDtypeStruct((length, width), BF16),
    )
    return pl.pallas_call(
        functools.partial(attend_kernel, length, heads, inner // heads),
        grid=(1,),
        out_shape=results,
        in_specs=whole_like(*operands) + [pl.BlockSpec(memory_space=pltpu.SMEM)],
        out_specs=tuple(whole_like(*results)),
        scratch_shapes=[
            pltpu.VMEM((heads, length, PAD), BF16),
            pltpu.VMEM((heads, strip_shape(length), QB), F32),
            pltpu.VMEM((inner, length), BF16),
            pltpu.VMEM((3 * PAD, width), BF16),
        ],
        compiler_params=pltpu.CompilerParams(vmem_limit_bytes=60 << 20),
        cost_estimate=SMALL,
    )(*operands, rel_bias)


def attend_back(proj, kt, lse, da, normed, w_qkv, grad_proj, rel_bias, low_bit):
    length, width = normed.shape
    heads, buckets = rel_bias.shape
    inner = w_qkv.shape[1]
    operands = (proj, kt, lse, da, normed, w_qkv, grad_proj)
    results = (
        jax.ShapeDtypeStruct((4 * inner, width), BF16),
        jax.ShapeDtypeStruct((length // 2, width), F32),
        jax.ShapeDtypeStruct((length // 2, width), BF16),
        jax.ShapeDtypeStruct((heads, buckets, 128), F32),
    )
    return pl.pallas_call(
        functools.partial(attend_back_kernel, length, heads, inner // heads),
        grid=(1,),
        out_shape=results,
        in_specs=whole_like(*operands) + [pl.BlockSpec(memory_space=pltpu.SMEM)] * 2,
        out_specs=tuple(whole_like(*results)),
        scratch_shapes=[
            pltpu.VMEM((heads, length, PAD), BF16),
            pltpu.VMEM((heads, length, PAD), BF16),
            pltpu.VMEM((heads, strip_shape(length), QB), F32),
            pltpu.VMEM((heads, strip_shape(length), QB), F32),
            pltpu.VMEM((length, heads * QB), BF16),
            pltpu.VMEM((length, heads * QB), BF16),
            pltpu.VMEM((heads * QB, PAD), BF16),
            pltpu.VMEM((heads * QB, PAD), BF16),
            pltpu.VMEM((length, PAD), F32),
            pltpu.VMEM((length, PAD), F32),
            pltpu.VMEM((PAD, QB), F32),
            pltpu.VMEM((length, PAD), F32),
            pltpu.VMEM((3, PAD, width), BF16),
        ],
        compiler_params=pltpu.CompilerParams(vmem_limit_bytes=60 << 20),
        cost_estimate=SMALL,
    )(*operands, rel_bias, low_bit)


def gelu_pair(v):
    inner = 0.7978845608028654 * (v + 0.044715 * (v * v * v))
    bend = jnp.tanh(inner)
    half = 0.5 * (1.0 + bend)
    slope = half + 0.5 * v * (1.0 - bend * bend) * (0.7978845608028654 * (1.0 + 0.134145 * (v * v)))
    return v * half, slope


def expert_kernel(
    members, experts,
    rows_ref, cot_ref, router_ref, group_ref, *refs,
):
    first, second = refs[:members], refs[members : 2 * members]
    reply_ref, share_ref, act_ref, gpre_ref, grad_ref, grouter_ref = refs[2 * members :]
    rows = rows_ref[...]
    count = rows.shape[0]
    lane = lax.broadcasted_iota(jnp.int32, (count, 128), 1)
    logits = jnp.where(lane < experts, nn_dot(rows, router_ref[...]), MASKED)
    raised = jnp.exp(logits - jnp.max(logits, -1, keepdims=True))
    probs = raised / jnp.sum(raised, -1, keepdims=True)
    own = jnp.where(lane == group_ref[0], 1.0, 0.0)
    gate = jnp.sum(probs * own, -1, keepdims=True)
    cot = cot_ref[...].astype(F32)
    grads = (gate * cot).astype(BF16)
    grad_ref[...] = grads
    reply = jnp.zeros(rows.shape, F32)
    share = jnp.zeros(rows.shape, F32)
    for k in range(members):
        act, slope = gelu_pair(nn_dot(rows, first[k][...]))
        act = act.astype(BF16)
        act_ref[k] = act
        reply = reply + nn_dot(act, second[k][...])
        gpre = (nt_dot(grads, second[k][...]) * slope).astype(BF16)
        gpre_ref[k] = gpre
        share = share + nt_dot(gpre, first[k][...])
    reply = reply.astype(BF16)
    reply_ref[...] = reply
    gate_grad = jnp.sum(cot * reply.astype(F32), -1, keepdims=True)
    logit_grad = probs * (own - gate) * gate_grad
    share_ref[...] = (share + nt_dot(logit_grad.astype(BF16), router_ref[...])).astype(BF16)
    grouter_ref[...] = nn_dot(logit_grad.T.astype(BF16), rows)


def expert_step(rows, cot, experts, router, group, first, second):
    members = len(first)
    count, width = rows.shape
    hidden = first[0].shape[1]
    weights = (*first, *second)
    results = (
        jax.ShapeDtypeStruct((count, width), BF16),
        jax.ShapeDtypeStruct((count, width), BF16),
        jax.ShapeDtypeStruct((members, count, hidden), BF16),
        jax.ShapeDtypeStruct((members, count, hidden), BF16),
        jax.ShapeDtypeStruct((count, width), BF16),
        jax.ShapeDtypeStruct((128, width), F32),
    )
    return pl.pallas_call(
        functools.partial(expert_kernel, members, experts),
        grid=(1,),
        out_shape=results,
        in_specs=whole_like(rows, cot, router)
        + [pl.BlockSpec(memory_space=pltpu.SMEM)]
        + whole_like(*weights),
        out_specs=tuple(whole_like(*results)),
        compiler_params=pltpu.CompilerParams(vmem_limit_bytes=60 << 20),
        cost_estimate=SMALL,
    )(rows, cot, router, group, *weights)


def enter_kernel(
    members, experts,
    x_ref, gain_ref, router_ref, route_ref, flat_ref, ids_ref, *refs,
):
    att, proj = refs[:members], refs[members : 2 * members]
    hidden_ref, gate_ref, leave_ref, total_ref = refs[2 * members :]
    step = pl.program_id(0)
    hidden = x_ref[...].astype(F32)
    for k in range(members):
        hidden = hidden + lax.dot_general(
            att[k][...], proj[k][...], (((0,), (0,)), ((), ())), preferred_element_type=F32
        )
    hidden_ref[...] = hidden
    normed = norm_rows(hidden, gain_ref[...]).astype(BF16)
    lane = lax.broadcasted_iota(jnp.int32, (QB, 128), 1)
    logits = jnp.where(lane < experts, nn_dot(normed, router_ref[...]), MASKED)
    raised = jnp.exp(logits - jnp.max(logits, -1, keepdims=True))
    chosen = jnp.sum(jnp.where(lane == route_ref[...], raised, 0.0), -1, keepdims=True)
    gate_ref[...] = chosen / jnp.sum(raised, -1, keepdims=True)
    table = jnp.where(ids_ref[...] == flat_ref[...], 1.0, 0.0).astype(BF16)

    @pl.when(step == 0)
    def _():
        total_ref[...] = jnp.zeros_like(total_ref)

    total_ref[...] += nn_dot(table, normed)

    @pl.when(step == pl.num_programs(0) - 1)
    def _():
        leave_ref[...] = total_ref[...].astype(BF16)


def enter_experts(tokens, experts, gain, router, route, flat_id, ids, att, proj):
    length, width = tokens.shape
    members = len(att)
    inner = att[0].shape[0]
    count = ids.shape[0]
    return pl.pallas_call(
        functools.partial(enter_kernel, members, experts),
        grid=(length // QB,),
        out_shape=(
            jax.ShapeDtypeStruct((length, width), F32),
            jax.ShapeDtypeStruct((length, 1), F32),
            jax.ShapeDtypeStruct((count, width), BF16),
        ),
        in_specs=[
            rows_of(QB, width),
            whole_of(1, width),
            whole_of(width, 128),
            rows_of(QB, 1),
            pl.BlockSpec((1, QB), lambda i: (0, i)),
            whole_of(count, 1),
        ]
        + [pl.BlockSpec((inner, QB), lambda i: (0, i))] * members
        + [whole_of(inner, width)] * members,
        out_specs=(rows_of(QB, width), rows_of(QB, 1), whole_of(count, width)),
        scratch_shapes=[pltpu.VMEM((count, width), F32)],
        compiler_params=pltpu.CompilerParams(vmem_limit_bytes=60 << 20),
        cost_estimate=SMALL,
    )(
        tokens, gain, router, route, flat_id, ids, *att, *proj,
    )


def weight_kernel(half, rows_ref, grads_ref, act_ref, gpre_ref, kept_ref, sent_ref):
    step = pl.program_id(0)

    def product(left, right):
        return lax.dot_general(
            left, right, (((0,), (0,)), ((), ())), preferred_element_type=F32
        ).astype(BF16)

    @pl.when(step < half)
    def _():
        k = 2 * step
        kept_ref[0] = product(act_ref[k], grads_ref[...])
        sent_ref[0] = product(act_ref[k + 1], grads_ref[...])

    @pl.when(step >= half)
    def _():
        k = 2 * (step - half)
        kept_ref[0] = product(rows_ref[...], gpre_ref[k])
        sent_ref[0] = product(rows_ref[...], gpre_ref[k + 1])


def weight_grads(rows, grads, act, gpre):
    members, count, hidden = act.shape
    width = rows.shape[1]
    assert hidden == width
    one = pl.BlockSpec((1, width, width), lambda i: (i, 0, 0))
    return pl.pallas_call(
        functools.partial(weight_kernel, members // 2),
        grid=(members,),
        out_shape=(
            jax.ShapeDtypeStruct((members, width, width), BF16),
            jax.ShapeDtypeStruct((members, width, width), BF16),
        ),
        in_specs=[whole_of(count, width)] * 2 + [whole_of(members, count, hidden)] * 2,
        out_specs=(one, one),
        compiler_params=pltpu.CompilerParams(vmem_limit_bytes=60 << 20),
        cost_estimate=SMALL,
    )(rows, grads, act, gpre)


def leave_kernel(
    members,
    hidden_ref, cot_ref, gain_ref, flat_ref, ids_ref, wproj_ref, att_ref, *refs,
):
    blocks = refs[:members]
    gh_ref, da_ref, ggain_ref, gproj_ref, total_ref = refs[members:]
    step = pl.program_id(0)
    share = blocks[0].shape[0]
    grad = jnp.zeros(hidden_ref.shape, F32)
    for k in range(members):
        hit = flat_ref[...] == ids_ref[:, k * share : (k + 1) * share]
        grad = grad + nn_dot(jnp.where(hit, 1.0, 0.0).astype(BF16), blocks[k][...])
    hidden = hidden_ref[...]
    inverse = lax.rsqrt(jnp.mean(hidden * hidden, -1, keepdims=True) + 1e-06)
    unit = hidden * inverse
    scaled = gain_ref[...] * grad
    back = inverse * (scaled - unit * jnp.mean(unit * scaled, -1, keepdims=True))
    total = cot_ref[...].astype(F32) + back
    gh_ref[...] = total
    low = total.astype(BF16)
    da_ref[...] = nt_dot(low, wproj_ref[...]).astype(BF16)

    @pl.when(step == 0)
    def _():
        ggain_ref[...] = jnp.zeros_like(ggain_ref)
        total_ref[...] = jnp.zeros_like(total_ref)

    ggain_ref[...] += jnp.sum(grad * unit, 0, keepdims=True)
    total_ref[...] += nn_dot(att_ref[...], low)

    @pl.when(step == pl.num_programs(0) - 1)
    def _():
        gproj_ref[...] = total_ref[...].astype(BF16)


def leave_experts(hidden1, cotangent, gain, flat_id, ids, w_proj, attended_t, blocks):
    length, width = hidden1.shape
    inner = attended_t.shape[0]
    members = len(blocks)
    share = blocks[0].shape[0]
    return pl.pallas_call(
        functools.partial(leave_kernel, members),
        grid=(length // QB,),
        out_shape=(
            jax.ShapeDtypeStruct((length, width), F32),
            jax.ShapeDtypeStruct((length, PAD), BF16),
            jax.ShapeDtypeStruct((1, width), F32),
            jax.ShapeDtypeStruct((inner, width), BF16),
        ),
        in_specs=[
            rows_of(QB, width),
            rows_of(QB, width),
            whole_of(1, width),
            rows_of(QB, 1),
            whole_of(1, members * share),
            whole_of(PAD, width),
            pl.BlockSpec((inner, QB), lambda i: (0, i)),
        ]
        + [whole_of(share, width)] * members,
        out_specs=(
            rows_of(QB, width),
            rows_of(QB, PAD),
            whole_of(1, width),
            whole_of(inner, width),
        ),
        scratch_shapes=[pltpu.VMEM((inner, width), F32)],
        compiler_params=pltpu.CompilerParams(vmem_limit_bytes=60 << 20),
        cost_estimate=SMALL,
    )(
        hidden1, cotangent, gain, flat_id, ids, w_proj, attended_t, *blocks,
    )


def output_kernel(members, hidden_ref, gate_ref, flat_ref, ids_ref, *refs):
    blocks, out_ref = refs[:members], refs[members]
    share = blocks[0].shape[0]
    reply = jnp.zeros(hidden_ref.shape, F32)
    for k in range(members):
        hit = flat_ref[...] == ids_ref[:, k * share : (k + 1) * share]
        reply = reply + nn_dot(jnp.where(hit, 1.0, 0.0).astype(BF16), blocks[k][...])
    out_ref[...] = (hidden_ref[...] + gate_ref[...] * reply).astype(BF16)


def output_rows(hidden1, gate, flat_id, ids, blocks):
    length, width = hidden1.shape
    members = len(blocks)
    share = blocks[0].shape[0]
    return pl.pallas_call(
        functools.partial(output_kernel, members),
        grid=(length // QB,),
        out_shape=jax.ShapeDtypeStruct((length, width), BF16),
        in_specs=[rows_of(QB, width), rows_of(QB, 1), rows_of(QB, 1), whole_of(1, members * share)]
        + [whole_of(share, width)] * members,
        out_specs=rows_of(QB, width),
        compiler_params=pltpu.CompilerParams(vmem_limit_bytes=60 << 20),
        cost_estimate=SMALL,
    )(hidden1, gate, flat_id, ids, *blocks)


def input_kernel(halves, kept_ref, other_ref, x_ref, gain_ref, gh_ref, low_ref, out_ref, ggain_ref):
    step = pl.program_id(0)
    part = jnp.where(step // halves == low_ref[0], kept_ref[...].astype(F32), other_ref[...].astype(F32))
    x = x_ref[...].astype(F32)
    inverse = lax.rsqrt(jnp.mean(x * x, -1, keepdims=True) + 1e-06)
    unit = x * inverse
    scaled = gain_ref[...] * part
    out_ref[...] = gh_ref[...] + inverse * (scaled - unit * jnp.mean(unit * scaled, -1, keepdims=True))

    @pl.when(step == 0)
    def _():
        ggain_ref[...] = jnp.zeros_like(ggain_ref)

    ggain_ref[...] += jnp.sum(part * unit, 0, keepdims=True)


def input_grads(kept, other, tokens, gain, grad_hidden1, low_bit):
    length, width = tokens.shape
    halves = kept.shape[0] // QB
    half = pl.BlockSpec((QB, width), lambda i: (i % halves, 0))
    return pl.pallas_call(
        functools.partial(input_kernel, halves),
        grid=(length // QB,),
        out_shape=(
            jax.ShapeDtypeStruct((length, width), F32),
            jax.ShapeDtypeStruct((1, width), F32),
        ),
        in_specs=[
            half,
            half,
            rows_of(QB, width),
            whole_of(1, width),
            rows_of(QB, width),
            pl.BlockSpec(memory_space=pltpu.SMEM),
        ],
        out_specs=(rows_of(QB, width), whole_of(1, width)),
        compiler_params=pltpu.CompilerParams(vmem_limit_bytes=60 << 20),
        cost_estimate=SMALL,
    )(kept, other, tokens, gain[None, :], grad_hidden1, low_bit)


def copies_kernel(came_ref, small_ref, ggain_ref, out_ref, mine_ref):
    groups, large = came_ref.shape[:2]

    @pl.when(pl.program_id(0) == 0)
    def _():
        total = came_ref[0].astype(F32)
        for g in range(1, groups):
            total = total + came_ref[g].astype(F32)
        mine_ref[:large, :] = total.astype(BF16)
        row = lax.broadcasted_iota(jnp.int32, small_ref.shape, 0)
        mine_ref[large:, :] = (small_ref[...] + jnp.where(row == 2, ggain_ref[...], 0.0)).astype(BF16)

    out_ref[0] = mine_ref[...]


def sum_copies(came, small, ggain):
    groups, large, width = came.shape
    count = large + small.shape[0]
    return pl.pallas_call(
        copies_kernel,
        grid=(groups,),
        out_shape=jax.ShapeDtypeStruct((groups, count, width), BF16),
        in_specs=whole_like(came, small, ggain),
        out_specs=pl.BlockSpec((1, count, width), lambda i: (i, 0, 0)),
        scratch_shapes=[pltpu.VMEM((count, width), BF16)],
        compiler_params=pltpu.CompilerParams(vmem_limit_bytes=60 << 20),
        cost_estimate=SMALL,
    )(came, small, ggain)


def final_kernel(large, inner, totals_ref, qkv_ref, proj_ref, small_ref):
    groups = totals_ref.shape[0]
    split = 3 * inner
    small = totals_ref[0, large:, :].astype(F32)
    for g in range(groups):
        start, stop = g * large, (g + 1) * large
        if start < split:
            count = min(stop, split) - start
            qkv_ref[start : start + count, :] = totals_ref[g, :count, :].astype(F32)
        if stop > split:
            skip = max(start, split) - start
            proj_ref[start + skip - split : stop - split, :] = totals_ref[g, skip:large, :].astype(F32)
        if g:
            small = small + totals_ref[g, large:, :].astype(F32)
    small_ref[...] = small


def final_weights(totals, large, inner):
    groups, count, width = totals.shape
    results = (
        jax.ShapeDtypeStruct((3 * inner, width), F32),
        jax.ShapeDtypeStruct((inner, width), F32),
        jax.ShapeDtypeStruct((count - large, width), F32),
    )
    return pl.pallas_call(
        functools.partial(final_kernel, large, inner),
        grid=(1,),
        out_shape=results,
        in_specs=whole_like(totals),
        out_specs=tuple(whole_like(*results)),
        compiler_params=pltpu.CompilerParams(vmem_limit_bytes=60 << 20),
        cost_estimate=SMALL,
    )(totals)


def shards(
    tokens,
    gain_attn,
    w_qkv,
    w_proj,
    rel_bias,
    gain_ffn,
    w_router,
    w_in,
    w_out,
    routes,
    segment_ids,
    cotangent,
):
    length, width = tokens.shape
    experts = w_router.shape[1]
    capacity = max(2, 3 * length // (2 * experts))
    inner_here = w_proj.shape[0]
    members = lax.axis_size("tensor")
    groups = lax.axis_size("expert")
    member = lax.axis_index("tensor")
    group = lax.axis_index("expert")
    share = capacity // members
    segments = segment_ids[0]
    route = routes[:, 0]

    def swap(value, bit):
        return lax.ppermute(value, "tensor", [(i, i ^ bit) for i in range(members)])

    bits = [1 << i for i in range(members.bit_length() - 1)]

    def gather_far(value):
        blocks = {0: value}
        for bit in reversed(bits[1:]):
            blocks.update({k ^ bit: swap(block, bit) for k, block in blocks.items()})
        return blocks

    def gather_near(blocks):
        blocks = dict(blocks)
        for bit in bits[:1]:
            blocks.update({k ^ bit: swap(block, bit) for k, block in blocks.items()})
        return [blocks[k] for k in range(members)]

    def gather_members(value):
        return gather_near(gather_far(value))

    def gather_groups(value):
        copies = jnp.broadcast_to(value[None], (groups,) + value.shape)
        return exchange(copies)

    def exchange(value):
        return lax.all_to_all(value, "expert", split_axis=0, concat_axis=0, tiled=True)

    tie = lax.optimization_barrier

    expert_ids = jnp.arange(experts, dtype=jnp.int32)
    onehot_low = (route[:, None] == expert_ids[None, :]).astype(BF16)
    onehot = onehot_low.astype(F32)
    positions = jnp.arange(length, dtype=jnp.int32)
    lower_ones = (positions[:, None] >= positions[None, :]).astype(BF16)
    running = nn_dot(lower_ones, onehot_low)
    slot = (jnp.sum(running * onehot, 1) - 1.0).astype(jnp.int32)
    flat_id = route * capacity + slot

    def ids_of(owner):
        slots = owner * share + jnp.arange(share, dtype=jnp.int32)
        return (expert_ids[:, None] * capacity + slots[None, :]).reshape(-1)

    send_table = (ids_of(member)[:, None] == flat_id[None, :]).astype(BF16)
    all_ids = jnp.concatenate([ids_of(member ^ k) for k in range(members)])

    def dispatch(rows):
        out = nn_dot(send_table, rows).astype(BF16).reshape(groups, -1, width)
        return exchange(out).reshape(-1, width)

    cot_share = dispatch(cotangent)
    w_proj_far = gather_far(w_proj)
    w_in_far = gather_far(w_in[0])
    w_qkv_t = jnp.swapaxes(w_qkv, 1, 2)
    attended_t, lse, proj, keys_t, normed1 = attend(tokens, gain_attn, w_qkv_t, segments, rel_bias)
    attended_t, w_in_far, cot_share = tie((attended_t, w_in_far, cot_share))

    attended_far = gather_far(attended_t)
    gain_row = gain_ffn[None, :]
    router = jnp.pad(w_router, ((0, 0), (0, 128 - experts)))
    w_proj_pad = jnp.pad(w_proj, ((0, PAD - inner_here), (0, 0)))
    flat_row, flat_column = flat_id[None, :], flat_id[:, None]
    send_ids, back_ids = ids_of(member)[:, None], all_ids[None, :]
    (
        attended_far, w_proj_far, w_out_here, gain_row, router, w_proj_pad,
        flat_row, flat_column, send_ids, back_ids,
    ) = tie((
        attended_far, w_proj_far, w_out[0], gain_row, router, w_proj_pad,
        flat_row, flat_column, send_ids, back_ids,
    ))
    attended_blocks = gather_near(attended_far)
    w_proj_blocks = gather_near(w_proj_far)
    w_in_all = gather_near(w_in_far)
    w_out_far = gather_far(w_out_here)
    hidden1, gate, leaving = enter_experts(
        tokens, experts, gain_row, router, routes, flat_row, send_ids, attended_blocks, w_proj_blocks
    )
    rows = exchange(leaving.reshape(groups, -1, width)).reshape(-1, width)
    rows, w_out_far, w_in_all = tie((rows, w_out_far, w_in_all))
    w_out_all = gather_near(w_out_far)

    reply, grad_share, act, grad_pre, grad_rows, grad_router = expert_step(
        rows, cot_share, experts, router, group[None], w_in_all, w_out_all
    )
    grad_back = exchange(grad_share.reshape(groups, -1, width)).reshape(-1, width)
    grad_router = grad_router[:experts]
    for bit in bits:
        grad_router = grad_router + swap(grad_router, bit)
    kept_weights, sent_weights = weight_grads(rows, grad_rows, act, grad_pre)
    grad_back, reply, kept_weights, sent_weights, grad_router = tie(
        (grad_back, reply, kept_weights, sent_weights, grad_router)
    )
    near_weights = swap(sent_weights, 1)
    grad_far = gather_far(grad_back)
    out_sent = (kept_weights[1].astype(F32) + near_weights[1].astype(F32)).astype(BF16)
    in_sent = (kept_weights[3].astype(F32) + near_weights[3].astype(F32)).astype(BF16)
    grad_far, out_sent, in_sent = tie((grad_far, out_sent, in_sent))
    out_came, in_came = swap(out_sent, 2), swap(in_sent, 2)
    grad_blocks = gather_near(grad_far)
    reply_back = exchange(reply.reshape(groups, -1, width)).reshape(-1, width)
    grad_hidden1, attended_grad, grad_gain_ffn, grad_proj = leave_experts(
        hidden1, cotangent, gain_row, flat_column, back_ids, w_proj_pad, attended_t, grad_blocks
    )

    low_bit = (member & 1)[None]
    grads, kept, sent, rel_parts = attend_back(
        proj, keys_t, lse, attended_grad, normed1, w_qkv_t, grad_proj, rel_bias, low_bit
    )
    grads, kept, sent, reply_back = tie((grads, kept, sent, reply_back))
    kept = kept + swap(sent, 1).astype(F32)
    kept_low, grads = tie((kept.astype(BF16), grads))
    far = swap(kept_low, 2)
    came = exchange(grads.reshape(groups, -1, width))
    reply_far = gather_far(reply_back)
    grad_w_out = kept_weights[0].astype(F32) + near_weights[0].astype(F32) + out_came.astype(F32)
    grad_w_in = kept_weights[2].astype(F32) + near_weights[2].astype(F32) + in_came.astype(F32)
    far, grad_w_out, grad_w_in, reply_far = tie((far, grad_w_out, grad_w_in, reply_far))
    kept = (kept + far.astype(F32)).astype(BF16)
    other = swap(kept, 1)
    grad_input, gain_part = input_grads(kept, other, tokens, gain_attn, grad_hidden1, low_bit)

    rel_row = jnp.sum(rel_parts, -1).reshape(1, -1)
    rel_row = jnp.pad(rel_row, ((0, 0), (0, width - rel_row.shape[1])))
    small = jnp.concatenate([grad_gain_ffn, rel_row, jnp.zeros((1, width), F32), grad_router], 0)
    small = jnp.pad(small, ((0, -small.shape[0] % 16), (0, 0)))
    large = came.shape[1]
    if large % 16 == 0:
        copies = sum_copies(came, small, gain_part)
    else:
        small = small.at[2].add(gain_part[0])
        copies = jnp.concatenate([jnp.sum(came.astype(F32), 0), small], 0).astype(BF16)
        copies = jnp.broadcast_to(copies[None], (groups,) + copies.shape)
    totals = exchange(copies)
    output = output_rows(hidden1, gate, flat_column, back_ids, gather_near(reply_far))
    if large % 16 == 0:
        grad_qkv_t, grad_proj, small = final_weights(totals, large, inner_here)
    else:
        shared = totals[:, :large].reshape(-1, width).astype(F32)
        grad_qkv_t, grad_proj = shared[: 3 * inner_here], shared[3 * inner_here :]
        small = jnp.sum(totals[:, large:].astype(F32), 0)
    grad_qkv = jnp.swapaxes(grad_qkv_t.reshape(3, inner_here, width), 1, 2)
    grad_gain_ffn = small[0]
    grad_rel = small[1, : rel_bias.size].reshape(rel_bias.shape)
    grad_gain_attn = small[2]
    grad_router = small[3 : 3 + experts].T
    return (
        output,
        grad_input,
        grad_gain_attn,
        grad_qkv,
        grad_proj,
        grad_rel,
        grad_gain_ffn,
        grad_router,
        grad_w_in[None],
        grad_w_out[None],
    )


def solution(mesh):
    placed = (
        P("expert", None),
        P(),
        P(None, None, "tensor"),
        P("tensor", None),
        P("tensor", None),
        P(),
        P(),
        P("expert", None, "tensor"),
        P("expert", "tensor", None),
        P("expert", None),
        P("expert", None),
        P("expert", None),
    )
    return jax.shard_map(
        shards,
        mesh=mesh,
        in_specs=placed,
        out_specs=(
            P("expert", None),
            P("expert", None),
            P(),
            P(None, None, "tensor"),
            P("tensor", None),
            P("tensor", None),
            P(),
            P(),
            P("expert", None, "tensor"),
            P("expert", "tensor", None),
        ),
        check_vma=False,
    )
```

```python
import functools

import jax
import jax.numpy as jnp
from jax import lax
from jax.experimental import pallas as pl
from jax.experimental.pallas import tpu as pltpu
from jax.sharding import PartitionSpec as P

FAR_LIMITS = (12, 16, 23, 32, 46, 64, 91)
HIGH = lax.Precision.HIGHEST
F32 = jnp.float32
BF16 = jnp.bfloat16
MASKED = -1e30
QB = 256
PAD = 256
FAR = FAR_LIMITS[-1]
SMALL = pl.CostEstimate(flops=1 << 20, bytes_accessed=1 << 16, transcendentals=0)

STEPS = (
    [(1 - limit, 14 - i) for i, limit in enumerate(reversed(FAR_LIMITS))]
    + [(-n, n) for n in range(7, -1, -1)]
    + [(n, 16 + n) for n in range(1, 8)]
    + [(8, 24)]
    + [(limit, 25 + i) for i, limit in enumerate(FAR_LIMITS)]
)


def norm_rows(values, gain):
    return values * lax.rsqrt(jnp.mean(values * values, -1, keepdims=True) + 1e-06) * gain


def nt_dot(left, right):
    return lax.dot_general(left, right, (((1,), (1,)), ((), ())), preferred_element_type=F32)


def nn_dot(left, right):
    return jnp.dot(left, right, preferred_element_type=F32)


def strip_shape(length):
    return 2 * length - QB


def near_rows(length):
    base = length - QB
    first = (base - FAR) // 32 * 32
    last = -(-(base + 127 + FAR) // 32) * 32
    return base, first, last


def build_strip(strip_ref, bias_ref, length, heads):
    total = strip_shape(length)
    base, first, last = near_rows(length)
    for h in range(heads):
        low = jnp.full((8, 128), bias_ref[h, 15], F32)
        high = jnp.full((8, 128), bias_ref[h, 31], F32)
        for half in range(QB // 128):
            cols = slice(half * 128, half * 128 + 128)
            lo_end, hi_start = first + half * 128, last + half * 128
            strip_ref[h, 0:lo_end, cols] = jnp.broadcast_to(low[:1], (lo_end, 128))
            strip_ref[h, hi_start:total, cols] = jnp.broadcast_to(high[:1], (total - hi_start, 128))
    for start in range(first, last, 32):
        offset = (
            lax.broadcasted_iota(jnp.int32, (32, 128), 0)
            - lax.broadcasted_iota(jnp.int32, (32, 128), 1)
            + (start - base)
        )
        tiles = [jnp.full((32, 128), bias_ref[h, 15], F32) for h in range(heads)]
        for begin, bucket in STEPS:
            reached = offset >= begin
            tiles = [jnp.where(reached, bias_ref[h, bucket], tiles[h]) for h in range(heads)]
        for h in range(heads):
            for half in range(QB // 128):
                at = start + half * 128
                strip_ref[h, at : at + 32, half * 128 : half * 128 + 128] = tiles[h]


def head_lanes(rows, h, dim, keep_tail, heads):
    lane = lax.broadcasted_iota(jnp.int32, (rows, PAD), 1)
    inside = (lane >= h * dim) & (lane < (h + 1) * dim)
    if keep_tail:
        inside = inside | (lane >= heads * dim)
    return inside


def attend_kernel(
    length, heads, dim,
    x_ref, gain_ref, w_ref, doc_ref, bias_ref,
    att_ref, lse_ref, proj_ref, kt_ref, normed_ref,
    kh_ref, strip_ref, vt_ref, pad_ref,
):
    inner = heads * dim
    build_strip(strip_ref, bias_ref, length, heads)
    lane = lax.broadcasted_iota(jnp.int32, (QB, PAD), 1) - inner
    pad_ref[...] = jnp.zeros_like(pad_ref)
    for t in range(3):
        pad_ref[t * PAD : t * PAD + inner, :] = w_ref[t]

    def project(b, carry):
        at = pl.multiple_of(b * QB, QB)
        here = x_ref[pl.ds(at, QB), :].astype(F32)
        normed = norm_rows(here, gain_ref[...]).astype(BF16)
        normed_ref[pl.ds(at, QB), :] = normed
        every = nt_dot(normed, pad_ref[...])
        same = doc_ref[pl.ds(at, QB), :] == lane
        queries = (every[:, 0:PAD].astype(BF16) * jnp.bfloat16(dim ** (-0.5))).astype(F32)
        queries = queries + jnp.where((lane < 0) | same, 0.0, MASKED)
        keys = every[:, PAD : 2 * PAD]
        values = every[:, 2 * PAD : 3 * PAD]
        proj_ref[pl.ds(at, QB), 0:PAD] = queries.astype(BF16)
        proj_ref[pl.ds(at, QB), PAD : 2 * PAD] = (keys + jnp.where(same, 1.0, 0.0)).astype(BF16)
        proj_ref[pl.ds(at, QB), 2 * PAD : 3 * PAD] = values.astype(BF16)
        kt_ref[:, pl.ds(at, QB)] = keys.T[:inner].astype(BF16)
        vt_ref[:, pl.ds(at, QB)] = values.T[:inner].astype(BF16)
        return carry

    lax.fori_loop(0, length // QB, project, 0)
    keys = proj_ref[:, PAD : 2 * PAD]
    for h in range(heads):
        kh_ref[h] = jnp.where(head_lanes(length, h, dim, True, heads), keys, jnp.zeros_like(keys))

    def block(b, carry):
        at = pl.multiple_of(b * QB, QB)
        from_row = pl.multiple_of(length - QB - b * QB, QB)
        queries = proj_ref[pl.ds(at, QB), 0:PAD]
        for h in range(heads):
            scores = nt_dot(kh_ref[h], queries) + strip_ref[h, pl.ds(from_row, length), :]
            top = jnp.max(scores, 0, keepdims=True)
            probs = jnp.exp(scores - top)
            total = jnp.sum(probs, 0, keepdims=True)
            out = nn_dot(vt_ref[h * dim : (h + 1) * dim, :], probs.astype(BF16))
            att_ref[h * dim : (h + 1) * dim, pl.ds(at, QB)] = (out / total).astype(BF16)
            lse_ref[h : h + 1, pl.ds(at, QB)] = top + jnp.log(total)
        return carry

    lax.fori_loop(0, length // QB, block, 0)


def attend_back_kernel(
    length, heads, dim,
    proj_ref, kt_ref, lse_ref, da_ref, normed_ref, w_ref, gproj_ref, bias_ref, low_ref,
    grad_ref, kept_ref, sent_ref, drel_ref,
    kh_ref, vh_ref, strip_ref, dstrip_ref, pcat_ref, dcat_ref, dacat_ref, qcat_ref, dk_ref, dv_ref, dqt_ref,
    dq_ref, pad_ref,
):
    inner = heads * dim
    scale = dim ** (-0.5)
    total = strip_shape(length)
    base, first, last = near_rows(length)
    build_strip(strip_ref, bias_ref, length, heads)
    dstrip_ref[...] = jnp.zeros_like(dstrip_ref)
    dk_ref[...] = jnp.zeros_like(dk_ref)
    dv_ref[...] = jnp.zeros_like(dv_ref)
    dqt_ref[...] = jnp.zeros_like(dqt_ref)
    keys = proj_ref[:, PAD : 2 * PAD]
    values = proj_ref[:, 2 * PAD : 3 * PAD]
    for h in range(heads):
        kh_ref[h] = jnp.where(head_lanes(length, h, dim, True, heads), keys, jnp.zeros_like(keys))
        vh_ref[h] = jnp.where(head_lanes(length, h, dim, False, heads), values, jnp.zeros_like(values))

    def block(b, carry):
        at = pl.multiple_of(b * QB, QB)
        from_row = pl.multiple_of(length - QB - b * QB, QB)
        queries = proj_ref[pl.ds(at, QB), 0:PAD]
        grads = da_ref[pl.ds(at, QB), :]
        for h in range(heads):
            mine = head_lanes(QB, h, dim, False, heads)
            cols = slice(h * QB, (h + 1) * QB)
            qcat_ref[cols, :] = jnp.where(mine, queries, jnp.zeros_like(queries))
            dacat_ref[cols, :] = jnp.where(mine, grads, jnp.zeros_like(grads))
            scores = nt_dot(kh_ref[h], queries) + strip_ref[h, pl.ds(from_row, length), :]
            probs = jnp.exp(scores - lse_ref[h : h + 1, pl.ds(at, QB)])
            weighted = probs * nt_dot(vh_ref[h], grads)
            delta = jnp.sum(weighted, 0, keepdims=True)
            dscore = weighted - probs * delta
            dstrip_ref[h, pl.ds(from_row, length), :] += dscore
            dlow = dscore.astype(BF16)
            pcat_ref[:, cols] = probs.astype(BF16)
            dcat_ref[:, cols] = dlow
            dqt_ref[h * dim : (h + 1) * dim, :] = nn_dot(kt_ref[h * dim : (h + 1) * dim, :], dlow) * scale
        dk_ref[...] += nn_dot(dcat_ref[...], qcat_ref[...])
        dv_ref[...] += nn_dot(pcat_ref[...], dacat_ref[...])
        dq_ref[pl.ds(at, QB), :] = dqt_ref[...].T
        return carry

    lax.fori_loop(0, length // QB, block, 0)

    for t, ref in enumerate((dq_ref, dk_ref, dv_ref)):
        turned = ref[...].T[:inner].astype(BF16)
        grad_ref[t * inner : (t + 1) * inner, :] = nn_dot(turned, normed_ref[...]).astype(BF16)

    grad_ref[3 * inner :, :] = gproj_ref[...]

    pad_ref[...] = jnp.zeros_like(pad_ref)
    for t in range(3):
        pad_ref[t, 0:inner, :] = w_ref[t]
    half = length // 2

    def part(start):
        total = jnp.zeros((QB, w_ref.shape[2]), F32)
        for t, ref in enumerate((dq_ref, dk_ref, dv_ref)):
            total = total + nn_dot(ref[pl.ds(start, QB), :].astype(BF16), pad_ref[t])
        return total

    for i in range(half // QB):
        rows = slice(i * QB, (i + 1) * QB)
        kept_ref[rows, :] = part(pl.multiple_of(low_ref[0] * half + i * QB, QB))
        sent_ref[rows, :] = part(pl.multiple_of((1 - low_ref[0]) * half + i * QB, QB)).astype(BF16)

    offset = (
        lax.broadcasted_iota(jnp.int32, (last - first, 128), 0)
        - lax.broadcasted_iota(jnp.int32, (last - first, 128), 1)
        + (first - base)
    )
    begins = [-(1 << 20)] + [begin for begin, bucket in STEPS] + [1 << 20]
    buckets = [15] + [bucket for begin, bucket in STEPS]
    for h in range(heads):
        near = jnp.zeros((last - first, 128), F32)
        low = jnp.zeros((1, 128), F32)
        high = jnp.zeros((1, 128), F32)
        for half in range(QB // 128):
            cols = slice(half * 128, half * 128 + 128)
            lo_end, hi_start = first + half * 128, last + half * 128
            near = near + dstrip_ref[h, lo_end:hi_start, cols]
            low = low + jnp.sum(dstrip_ref[h, 0:lo_end, cols], 0, keepdims=True)
            high = high + jnp.sum(dstrip_ref[h, hi_start:total, cols], 0, keepdims=True)
        drel_ref[h, 16:17, :] = jnp.zeros((1, 128), F32)
        for i, bucket in enumerate(buckets):
            inside = (offset >= begins[i]) & (offset < begins[i + 1])
            row = jnp.sum(jnp.where(inside, near, 0.0), 0, keepdims=True)
            if bucket == 15:
                row = row + low
            if bucket == 31:
                row = row + high
            drel_ref[h, bucket : bucket + 1, :] = row


def rows_of(count, columns):
    return pl.BlockSpec((count, columns), lambda i: (i, 0))


def whole_of(*shape):
    return pl.BlockSpec(shape, lambda i: (0,) * len(shape))


def whole_like(*arrays):
    return [whole_of(*array.shape) for array in arrays]


def attend(tokens, gain, w_qkv, segments, rel_bias):
    length, width = tokens.shape
    heads = rel_bias.shape[0]
    inner = w_qkv.shape[1]
    operands = (tokens, gain[None, :], w_qkv, segments[:, None])
    results = (
        jax.ShapeDtypeStruct((inner, length), BF16),
        jax.ShapeDtypeStruct((8, length), F32),
        jax.ShapeDtypeStruct((length, 3 * PAD), BF16),
        jax.ShapeDtypeStruct((inner, length), BF16),
        jax.ShapeDtypeStruct((length, width), BF16),
    )
    return pl.pallas_call(
        functools.partial(attend_kernel, length, heads, inner // heads),
        grid=(1,),
        out_shape=results,
        in_specs=whole_like(*operands) + [pl.BlockSpec(memory_space=pltpu.SMEM)],
        out_specs=tuple(whole_like(*results)),
        scratch_shapes=[
            pltpu.VMEM((heads, length, PAD), BF16),
            pltpu.VMEM((heads, strip_shape(length), QB), F32),
            pltpu.VMEM((inner, length), BF16),
            pltpu.VMEM((3 * PAD, width), BF16),
        ],
        compiler_params=pltpu.CompilerParams(vmem_limit_bytes=60 << 20),
        cost_estimate=SMALL,
    )(*operands, rel_bias)


def attend_back(proj, kt, lse, da, normed, w_qkv, grad_proj, rel_bias, low_bit):
    length, width = normed.shape
    heads, buckets = rel_bias.shape
    inner = w_qkv.shape[1]
    operands = (proj, kt, lse, da, normed, w_qkv, grad_proj)
    results = (
        jax.ShapeDtypeStruct((4 * inner, width), BF16),
        jax.ShapeDtypeStruct((length // 2, width), F32),
        jax.ShapeDtypeStruct((length // 2, width), BF16),
        jax.ShapeDtypeStruct((heads, buckets, 128), F32),
    )
    return pl.pallas_call(
        functools.partial(attend_back_kernel, length, heads, inner // heads),
        grid=(1,),
        out_shape=results,
        in_specs=whole_like(*operands) + [pl.BlockSpec(memory_space=pltpu.SMEM)] * 2,
        out_specs=tuple(whole_like(*results)),
        scratch_shapes=[
            pltpu.VMEM((heads, length, PAD), BF16),
            pltpu.VMEM((heads, length, PAD), BF16),
            pltpu.VMEM((heads, strip_shape(length), QB), F32),
            pltpu.VMEM((heads, strip_shape(length), QB), F32),
            pltpu.VMEM((length, heads * QB), BF16),
            pltpu.VMEM((length, heads * QB), BF16),
            pltpu.VMEM((heads * QB, PAD), BF16),
            pltpu.VMEM((heads * QB, PAD), BF16),
            pltpu.VMEM((length, PAD), F32),
            pltpu.VMEM((length, PAD), F32),
            pltpu.VMEM((PAD, QB), F32),
            pltpu.VMEM((length, PAD), F32),
            pltpu.VMEM((3, PAD, width), BF16),
        ],
        compiler_params=pltpu.CompilerParams(vmem_limit_bytes=60 << 20),
        cost_estimate=SMALL,
    )(*operands, rel_bias, low_bit)


def gelu_pair(v):
    inner = 0.7978845608028654 * (v + 0.044715 * (v * v * v))
    bend = jnp.tanh(inner)
    half = 0.5 * (1.0 + bend)
    slope = half + 0.5 * v * (1.0 - bend * bend) * (0.7978845608028654 * (1.0 + 0.134145 * (v * v)))
    return v * half, slope


def expert_kernel(
    members, experts,
    rows_ref, cot_ref, router_ref, group_ref, *refs,
):
    first, second = refs[:members], refs[members : 2 * members]
    reply_ref, share_ref, act_ref, gpre_ref, grad_ref, grouter_ref = refs[2 * members :]
    rows = rows_ref[...]
    count = rows.shape[0]
    lane = lax.broadcasted_iota(jnp.int32, (count, 128), 1)
    logits = jnp.where(lane < experts, nn_dot(rows, router_ref[...]), MASKED)
    raised = jnp.exp(logits - jnp.max(logits, -1, keepdims=True))
    probs = raised / jnp.sum(raised, -1, keepdims=True)
    own = jnp.where(lane == group_ref[0], 1.0, 0.0)
    gate = jnp.sum(probs * own, -1, keepdims=True)
    cot = cot_ref[...].astype(F32)
    grads = (gate * cot).astype(BF16)
    grad_ref[...] = grads
    reply = jnp.zeros(rows.shape, F32)
    share = jnp.zeros(rows.shape, F32)
    for k in range(members):
        act, slope = gelu_pair(nn_dot(rows, first[k][...]))
        act = act.astype(BF16)
        act_ref[k] = act
        reply = reply + nn_dot(act, second[k][...])
        gpre = (nt_dot(grads, second[k][...]) * slope).astype(BF16)
        gpre_ref[k] = gpre
        share = share + nt_dot(gpre, first[k][...])
    reply = reply.astype(BF16)
    reply_ref[...] = reply
    gate_grad = jnp.sum(cot * reply.astype(F32), -1, keepdims=True)
    logit_grad = probs * (own - gate) * gate_grad
    share_ref[...] = (share + nt_dot(logit_grad.astype(BF16), router_ref[...])).astype(BF16)
    grouter_ref[...] = nn_dot(logit_grad.T.astype(BF16), rows)


def expert_step(rows, cot, experts, router, group, first, second):
    members = len(first)
    count, width = rows.shape
    hidden = first[0].shape[1]
    weights = (*first, *second)
    results = (
        jax.ShapeDtypeStruct((count, width), BF16),
        jax.ShapeDtypeStruct((count, width), BF16),
        jax.ShapeDtypeStruct((members, count, hidden), BF16),
        jax.ShapeDtypeStruct((members, count, hidden), BF16),
        jax.ShapeDtypeStruct((count, width), BF16),
        jax.ShapeDtypeStruct((128, width), F32),
    )
    return pl.pallas_call(
        functools.partial(expert_kernel, members, experts),
        grid=(1,),
        out_shape=results,
        in_specs=whole_like(rows, cot, router)
        + [pl.BlockSpec(memory_space=pltpu.SMEM)]
        + whole_like(*weights),
        out_specs=tuple(whole_like(*results)),
        compiler_params=pltpu.CompilerParams(vmem_limit_bytes=60 << 20),
        cost_estimate=SMALL,
    )(rows, cot, router, group, *weights)


def enter_kernel(
    members, experts,
    x_ref, gain_ref, router_ref, route_ref, flat_ref, ids_ref, *refs,
):
    att, proj = refs[:members], refs[members : 2 * members]
    hidden_ref, gate_ref, leave_ref, total_ref = refs[2 * members :]
    step = pl.program_id(0)
    hidden = x_ref[...].astype(F32)
    for k in range(members):
        hidden = hidden + lax.dot_general(
            att[k][...], proj[k][...], (((0,), (0,)), ((), ())), preferred_element_type=F32
        )
    hidden_ref[...] = hidden
    normed = norm_rows(hidden, gain_ref[...]).astype(BF16)
    lane = lax.broadcasted_iota(jnp.int32, (QB, 128), 1)
    logits = jnp.where(lane < experts, nn_dot(normed, router_ref[...]), MASKED)
    raised = jnp.exp(logits - jnp.max(logits, -1, keepdims=True))
    chosen = jnp.sum(jnp.where(lane == route_ref[...], raised, 0.0), -1, keepdims=True)
    gate_ref[...] = chosen / jnp.sum(raised, -1, keepdims=True)
    table = jnp.where(ids_ref[...] == flat_ref[...], 1.0, 0.0).astype(BF16)

    @pl.when(step == 0)
    def _():
        total_ref[...] = jnp.zeros_like(total_ref)

    total_ref[...] += nn_dot(table, normed)

    @pl.when(step == pl.num_programs(0) - 1)
    def _():
        leave_ref[...] = total_ref[...].astype(BF16)


def enter_experts(tokens, experts, gain, router, route, flat_id, ids, att, proj):
    length, width = tokens.shape
    members = len(att)
    inner = att[0].shape[0]
    count = ids.shape[0]
    return pl.pallas_call(
        functools.partial(enter_kernel, members, experts),
        grid=(length // QB,),
        out_shape=(
            jax.ShapeDtypeStruct((length, width), F32),
            jax.ShapeDtypeStruct((length, 1), F32),
            jax.ShapeDtypeStruct((count, width), BF16),
        ),
        in_specs=[
            rows_of(QB, width),
            whole_of(1, width),
            whole_of(width, 128),
            rows_of(QB, 1),
            pl.BlockSpec((1, QB), lambda i: (0, i)),
            whole_of(count, 1),
        ]
        + [pl.BlockSpec((inner, QB), lambda i: (0, i))] * members
        + [whole_of(inner, width)] * members,
        out_specs=(rows_of(QB, width), rows_of(QB, 1), whole_of(count, width)),
        scratch_shapes=[pltpu.VMEM((count, width), F32)],
        compiler_params=pltpu.CompilerParams(vmem_limit_bytes=60 << 20),
        cost_estimate=SMALL,
    )(
        tokens, gain, router, route, flat_id, ids, *att, *proj,
    )


def weight_kernel(half, rows_ref, grads_ref, act_ref, gpre_ref, kept_ref, sent_ref):
    step = pl.program_id(0)

    def product(left, right):
        return lax.dot_general(
            left, right, (((0,), (0,)), ((), ())), preferred_element_type=F32
        ).astype(BF16)

    @pl.when(step < half)
    def _():
        k = 2 * step
        kept_ref[0] = product(act_ref[k], grads_ref[...])
        sent_ref[0] = product(act_ref[k + 1], grads_ref[...])

    @pl.when(step >= half)
    def _():
        k = 2 * (step - half)
        kept_ref[0] = product(rows_ref[...], gpre_ref[k])
        sent_ref[0] = product(rows_ref[...], gpre_ref[k + 1])


def weight_grads(rows, grads, act, gpre):
    members, count, hidden = act.shape
    width = rows.shape[1]
    assert hidden == width
    one = pl.BlockSpec((1, width, width), lambda i: (i, 0, 0))
    return pl.pallas_call(
        functools.partial(weight_kernel, members // 2),
        grid=(members,),
        out_shape=(
            jax.ShapeDtypeStruct((members, width, width), BF16),
            jax.ShapeDtypeStruct((members, width, width), BF16),
        ),
        in_specs=[whole_of(count, width)] * 2 + [whole_of(members, count, hidden)] * 2,
        out_specs=(one, one),
        compiler_params=pltpu.CompilerParams(vmem_limit_bytes=60 << 20),
        cost_estimate=SMALL,
    )(rows, grads, act, gpre)


def leave_kernel(
    members,
    hidden_ref, cot_ref, gain_ref, flat_ref, ids_ref, wproj_ref, att_ref, *refs,
):
    blocks = refs[:members]
    gh_ref, da_ref, ggain_ref, gproj_ref, total_ref = refs[members:]
    step = pl.program_id(0)
    share = blocks[0].shape[0]
    grad = jnp.zeros(hidden_ref.shape, F32)
    for k in range(members):
        hit = flat_ref[...] == ids_ref[:, k * share : (k + 1) * share]
        grad = grad + nn_dot(jnp.where(hit, 1.0, 0.0).astype(BF16), blocks[k][...])
    hidden = hidden_ref[...]
    inverse = lax.rsqrt(jnp.mean(hidden * hidden, -1, keepdims=True) + 1e-06)
    unit = hidden * inverse
    scaled = gain_ref[...] * grad
    back = inverse * (scaled - unit * jnp.mean(unit * scaled, -1, keepdims=True))
    total = cot_ref[...].astype(F32) + back
    gh_ref[...] = total
    low = total.astype(BF16)
    da_ref[...] = nt_dot(low, wproj_ref[...]).astype(BF16)

    @pl.when(step == 0)
    def _():
        ggain_ref[...] = jnp.zeros_like(ggain_ref)
        total_ref[...] = jnp.zeros_like(total_ref)

    ggain_ref[...] += jnp.sum(grad * unit, 0, keepdims=True)
    total_ref[...] += nn_dot(att_ref[...], low)

    @pl.when(step == pl.num_programs(0) - 1)
    def _():
        gproj_ref[...] = total_ref[...].astype(BF16)


def leave_experts(hidden1, cotangent, gain, flat_id, ids, w_proj, attended_t, blocks):
    length, width = hidden1.shape
    inner = attended_t.shape[0]
    members = len(blocks)
    share = blocks[0].shape[0]
    return pl.pallas_call(
        functools.partial(leave_kernel, members),
        grid=(length // QB,),
        out_shape=(
            jax.ShapeDtypeStruct((length, width), F32),
            jax.ShapeDtypeStruct((length, PAD), BF16),
            jax.ShapeDtypeStruct((1, width), F32),
            jax.ShapeDtypeStruct((inner, width), BF16),
        ),
        in_specs=[
            rows_of(QB, width),
            rows_of(QB, width),
            whole_of(1, width),
            rows_of(QB, 1),
            whole_of(1, members * share),
            whole_of(PAD, width),
            pl.BlockSpec((inner, QB), lambda i: (0, i)),
        ]
        + [whole_of(share, width)] * members,
        out_specs=(
            rows_of(QB, width),
            rows_of(QB, PAD),
            whole_of(1, width),
            whole_of(inner, width),
        ),
        scratch_shapes=[pltpu.VMEM((inner, width), F32)],
        compiler_params=pltpu.CompilerParams(vmem_limit_bytes=60 << 20),
        cost_estimate=SMALL,
    )(
        hidden1, cotangent, gain, flat_id, ids, w_proj, attended_t, *blocks,
    )


def output_kernel(members, hidden_ref, gate_ref, flat_ref, ids_ref, *refs):
    blocks, out_ref = refs[:members], refs[members]
    share = blocks[0].shape[0]
    reply = jnp.zeros(hidden_ref.shape, F32)
    for k in range(members):
        hit = flat_ref[...] == ids_ref[:, k * share : (k + 1) * share]
        reply = reply + nn_dot(jnp.where(hit, 1.0, 0.0).astype(BF16), blocks[k][...])
    out_ref[...] = (hidden_ref[...] + gate_ref[...] * reply).astype(BF16)


def output_rows(hidden1, gate, flat_id, ids, blocks):
    length, width = hidden1.shape
    members = len(blocks)
    share = blocks[0].shape[0]
    return pl.pallas_call(
        functools.partial(output_kernel, members),
        grid=(length // QB,),
        out_shape=jax.ShapeDtypeStruct((length, width), BF16),
        in_specs=[rows_of(QB, width), rows_of(QB, 1), rows_of(QB, 1), whole_of(1, members * share)]
        + [whole_of(share, width)] * members,
        out_specs=rows_of(QB, width),
        compiler_params=pltpu.CompilerParams(vmem_limit_bytes=60 << 20),
        cost_estimate=SMALL,
    )(hidden1, gate, flat_id, ids, *blocks)


def input_kernel(halves, kept_ref, other_ref, x_ref, gain_ref, gh_ref, low_ref, out_ref, ggain_ref):
    step = pl.program_id(0)
    part = jnp.where(step // halves == low_ref[0], kept_ref[...].astype(F32), other_ref[...].astype(F32))
    x = x_ref[...].astype(F32)
    inverse = lax.rsqrt(jnp.mean(x * x, -1, keepdims=True) + 1e-06)
    unit = x * inverse
    scaled = gain_ref[...] * part
    out_ref[...] = gh_ref[...] + inverse * (scaled - unit * jnp.mean(unit * scaled, -1, keepdims=True))

    @pl.when(step == 0)
    def _():
        ggain_ref[...] = jnp.zeros_like(ggain_ref)

    ggain_ref[...] += jnp.sum(part * unit, 0, keepdims=True)


def input_grads(kept, other, tokens, gain, grad_hidden1, low_bit):
    length, width = tokens.shape
    halves = kept.shape[0] // QB
    half = pl.BlockSpec((QB, width), lambda i: (i % halves, 0))
    return pl.pallas_call(
        functools.partial(input_kernel, halves),
        grid=(length // QB,),
        out_shape=(
            jax.ShapeDtypeStruct((length, width), F32),
            jax.ShapeDtypeStruct((1, width), F32),
        ),
        in_specs=[
            half,
            half,
            rows_of(QB, width),
            whole_of(1, width),
            rows_of(QB, width),
            pl.BlockSpec(memory_space=pltpu.SMEM),
        ],
        out_specs=(rows_of(QB, width), whole_of(1, width)),
        compiler_params=pltpu.CompilerParams(vmem_limit_bytes=60 << 20),
        cost_estimate=SMALL,
    )(kept, other, tokens, gain[None, :], grad_hidden1, low_bit)


def copies_kernel(came_ref, small_ref, ggain_ref, out_ref, mine_ref):
    groups, large = came_ref.shape[:2]

    @pl.when(pl.program_id(0) == 0)
    def _():
        total = came_ref[0].astype(F32)
        for g in range(1, groups):
            total = total + came_ref[g].astype(F32)
        mine_ref[:large, :] = total.astype(BF16)
        row = lax.broadcasted_iota(jnp.int32, small_ref.shape, 0)
        mine_ref[large:, :] = (small_ref[...] + jnp.where(row == 2, ggain_ref[...], 0.0)).astype(BF16)

    out_ref[0] = mine_ref[...]


def sum_copies(came, small, ggain):
    groups, large, width = came.shape
    count = large + small.shape[0]
    return pl.pallas_call(
        copies_kernel,
        grid=(groups,),
        out_shape=jax.ShapeDtypeStruct((groups, count, width), BF16),
        in_specs=whole_like(came, small, ggain),
        out_specs=pl.BlockSpec((1, count, width), lambda i: (i, 0, 0)),
        scratch_shapes=[pltpu.VMEM((count, width), BF16)],
        compiler_params=pltpu.CompilerParams(vmem_limit_bytes=60 << 20),
        cost_estimate=SMALL,
    )(came, small, ggain)


def final_kernel(large, inner, totals_ref, qkv_ref, proj_ref, gffn_ref, rel_ref, gattn_ref, router_ref):
    groups = totals_ref.shape[0]
    split = 3 * inner
    small = totals_ref[0, large:, :].astype(F32)
    for g in range(groups):
        start, stop = g * large, (g + 1) * large
        if start < split:
            count = min(stop, split) - start
            qkv_ref[start : start + count, :] = totals_ref[g, :count, :].astype(F32)
        if stop > split:
            skip = max(start, split) - start
            proj_ref[start + skip - split : stop - split, :] = totals_ref[g, skip:large, :].astype(F32)
        if g:
            small = small + totals_ref[g, large:, :].astype(F32)
    gffn_ref[...] = small[0:1]
    rel_ref[...] = small[1:2]
    gattn_ref[...] = small[2:3]
    router_ref[...] = small[3 : 3 + router_ref.shape[0]]


def final_weights(totals, large, inner, experts):
    groups, count, width = totals.shape
    results = (
        jax.ShapeDtypeStruct((3 * inner, width), F32),
        jax.ShapeDtypeStruct((inner, width), F32),
        jax.ShapeDtypeStruct((1, width), F32),
        jax.ShapeDtypeStruct((1, width), F32),
        jax.ShapeDtypeStruct((1, width), F32),
        jax.ShapeDtypeStruct((experts, width), F32),
    )
    return pl.pallas_call(
        functools.partial(final_kernel, large, inner),
        grid=(1,),
        out_shape=results,
        in_specs=whole_like(totals),
        out_specs=tuple(whole_like(*results)),
        compiler_params=pltpu.CompilerParams(vmem_limit_bytes=16 << 20),
        cost_estimate=SMALL,
    )(totals)


def shards(
    tokens,
    gain_attn,
    w_qkv,
    w_proj,
    rel_bias,
    gain_ffn,
    w_router,
    w_in,
    w_out,
    routes,
    segment_ids,
    cotangent,
):
    length, width = tokens.shape
    experts = w_router.shape[1]
    capacity = max(2, 3 * length // (2 * experts))
    inner_here = w_proj.shape[0]
    members = lax.axis_size("tensor")
    groups = lax.axis_size("expert")
    member = lax.axis_index("tensor")
    group = lax.axis_index("expert")
    share = capacity // members
    segments = segment_ids[0]
    route = routes[:, 0]

    def swap(value, bit):
        return lax.ppermute(value, "tensor", [(i, i ^ bit) for i in range(members)])

    bits = [1 << i for i in range(members.bit_length() - 1)]

    def gather_far(value):
        blocks = {0: value}
        for bit in reversed(bits[1:]):
            blocks.update({k ^ bit: swap(block, bit) for k, block in blocks.items()})
        return blocks

    def gather_near(blocks):
        blocks = dict(blocks)
        for bit in bits[:1]:
            blocks.update({k ^ bit: swap(block, bit) for k, block in blocks.items()})
        return [blocks[k] for k in range(members)]

    def gather_members(value):
        return gather_near(gather_far(value))

    def gather_groups(value):
        copies = jnp.broadcast_to(value[None], (groups,) + value.shape)
        return exchange(copies)

    def exchange(value):
        return lax.all_to_all(value, "expert", split_axis=0, concat_axis=0, tiled=True)

    tie = lax.optimization_barrier

    expert_ids = jnp.arange(experts, dtype=jnp.int32)
    onehot_low = (route[:, None] == expert_ids[None, :]).astype(BF16)
    onehot = onehot_low.astype(F32)
    positions = jnp.arange(length, dtype=jnp.int32)
    lower_ones = (positions[:, None] >= positions[None, :]).astype(BF16)
    running = nn_dot(lower_ones, onehot_low)
    slot = (jnp.sum(running * onehot, 1) - 1.0).astype(jnp.int32)
    flat_id = route * capacity + slot

    def ids_of(owner):
        slots = owner * share + jnp.arange(share, dtype=jnp.int32)
        return (expert_ids[:, None] * capacity + slots[None, :]).reshape(-1)

    send_table = (ids_of(member)[:, None] == flat_id[None, :]).astype(BF16)
    all_ids = jnp.concatenate([ids_of(member ^ k) for k in range(members)])

    def dispatch(rows):
        out = nn_dot(send_table, rows).astype(BF16).reshape(groups, -1, width)
        return exchange(out).reshape(-1, width)

    cot_share = dispatch(cotangent)
    w_proj_far = gather_far(w_proj)
    w_in_far = gather_far(w_in[0])
    w_qkv_t = jnp.swapaxes(w_qkv, 1, 2)
    attended_t, lse, proj, keys_t, normed1 = attend(tokens, gain_attn, w_qkv_t, segments, rel_bias)
    attended_t, w_in_far, cot_share = tie((attended_t, w_in_far, cot_share))

    attended_far = gather_far(attended_t)
    gain_row = gain_ffn[None, :]
    router = jnp.pad(w_router, ((0, 0), (0, 128 - experts)))
    w_proj_pad = jnp.pad(w_proj, ((0, PAD - inner_here), (0, 0)))
    flat_row, flat_column = flat_id[None, :], flat_id[:, None]
    send_ids, back_ids = ids_of(member)[:, None], all_ids[None, :]
    (
        attended_far, w_proj_far, w_out_here, gain_row, router, w_proj_pad,
        flat_row, flat_column, send_ids, back_ids,
    ) = tie((
        attended_far, w_proj_far, w_out[0], gain_row, router, w_proj_pad,
        flat_row, flat_column, send_ids, back_ids,
    ))
    attended_blocks = gather_near(attended_far)
    w_proj_blocks = gather_near(w_proj_far)
    w_in_all = gather_near(w_in_far)
    w_out_far = gather_far(w_out_here)
    hidden1, gate, leaving = enter_experts(
        tokens, experts, gain_row, router, routes, flat_row, send_ids, attended_blocks, w_proj_blocks
    )
    rows = exchange(leaving.reshape(groups, -1, width)).reshape(-1, width)
    rows, w_out_far, w_in_all = tie((rows, w_out_far, w_in_all))
    w_out_all = gather_near(w_out_far)

    reply, grad_share, act, grad_pre, grad_rows, grad_router = expert_step(
        rows, cot_share, experts, router, group[None], w_in_all, w_out_all
    )
    grad_back = exchange(grad_share.reshape(groups, -1, width)).reshape(-1, width)
    grad_router = grad_router[:experts]
    for bit in bits:
        grad_router = grad_router + swap(grad_router, bit)
    kept_weights, sent_weights = weight_grads(rows, grad_rows, act, grad_pre)
    grad_back, reply, kept_weights, sent_weights, grad_router = tie(
        (grad_back, reply, kept_weights, sent_weights, grad_router)
    )
    near_weights = swap(sent_weights, 1)
    grad_far = gather_far(grad_back)
    cut = width // 2

    def pair(k, rows_cut):
        return kept_weights[k, rows_cut].astype(F32) + near_weights[k, rows_cut].astype(F32)

    out_sent = pair(1, slice(0, width)).astype(BF16)
    fore_sent, rest_sent = pair(3, slice(0, cut)).astype(BF16), pair(3, slice(cut, width)).astype(BF16)
    grad_far, out_sent, fore_sent, rest_sent = tie((grad_far, out_sent, fore_sent, rest_sent))
    out_came, fore_came = swap(out_sent, 2), swap(fore_sent, 2)
    grad_blocks = gather_near(grad_far)
    reply_back = exchange(reply.reshape(groups, -1, width)).reshape(-1, width)
    grad_hidden1, attended_grad, grad_gain_ffn, grad_proj = leave_experts(
        hidden1, cotangent, gain_row, flat_column, back_ids, w_proj_pad, attended_t, grad_blocks
    )

    low_bit = (member & 1)[None]
    grads, kept, sent, rel_parts = attend_back(
        proj, keys_t, lse, attended_grad, normed1, w_qkv_t, grad_proj, rel_bias, low_bit
    )
    grads, kept, sent, reply_back, out_came, fore_came, rest_sent = tie(
        (grads, kept, sent, reply_back, out_came, fore_came, rest_sent)
    )
    kept = kept + swap(sent, 1).astype(F32)
    kept_low, grads = tie((kept.astype(BF16), grads))
    far = swap(kept_low, 2)
    came = exchange(grads.reshape(groups, -1, width))
    rest_came = swap(rest_sent, 2)
    grad_w_out = pair(0, slice(0, width)) + out_came.astype(F32)
    far, grad_w_out, reply_back = tie((far, grad_w_out, reply_back))
    reply_far = gather_far(reply_back)
    grad_w_in = pair(2, slice(0, width)) + jnp.concatenate([fore_came, rest_came], 0).astype(F32)
    kept = (kept + far.astype(F32)).astype(BF16)
    other = swap(kept, 1)
    grad_input, gain_part = input_grads(kept, other, tokens, gain_attn, grad_hidden1, low_bit)

    rel_row = jnp.sum(rel_parts, -1).reshape(1, -1)
    rel_row = jnp.pad(rel_row, ((0, 0), (0, width - rel_row.shape[1])))
    small = jnp.concatenate([grad_gain_ffn, rel_row, jnp.zeros((1, width), F32), grad_router], 0)
    small = jnp.pad(small, ((0, -small.shape[0] % 16), (0, 0)))
    large = came.shape[1]
    if large % 16 == 0:
        copies = sum_copies(came, small, gain_part)
    else:
        small = small.at[2].add(gain_part[0])
        copies = jnp.concatenate([jnp.sum(came.astype(F32), 0), small], 0).astype(BF16)
        copies = jnp.broadcast_to(copies[None], (groups,) + copies.shape)
    totals = exchange(copies)
    output = output_rows(hidden1, gate, flat_column, back_ids, gather_near(reply_far))
    if large % 16 == 0:
        grad_qkv_t, grad_proj, grad_gain_ffn, rel_row, grad_gain_attn, grad_router = final_weights(
            totals, large, inner_here, experts
        )
    else:
        shared = totals[:, :large].reshape(-1, width).astype(F32)
        grad_qkv_t, grad_proj = shared[: 3 * inner_here], shared[3 * inner_here :]
        small = jnp.sum(totals[:, large:].astype(F32), 0)
        grad_gain_ffn, rel_row, grad_gain_attn = small[0], small[1], small[2]
        grad_router = small[3 : 3 + experts]
    grad_qkv = jnp.swapaxes(grad_qkv_t.reshape(3, inner_here, width), 1, 2)
    grad_gain_ffn, grad_gain_attn = grad_gain_ffn.reshape(-1), grad_gain_attn.reshape(-1)
    grad_rel = rel_row.reshape(-1)[: rel_bias.size].reshape(rel_bias.shape)
    grad_router = grad_router.T
    return (
        output,
        grad_input,
        grad_gain_attn,
        grad_qkv,
        grad_proj,
        grad_rel,
        grad_gain_ffn,
        grad_router,
        grad_w_in[None],
        grad_w_out[None],
    )


def solution(mesh):
    placed = (
        P("expert", None),
        P(),
        P(None, None, "tensor"),
        P("tensor", None),
        P("tensor", None),
        P(),
        P(),
        P("expert", None, "tensor"),
        P("expert", "tensor", None),
        P("expert", None),
        P("expert", None),
        P("expert", None),
    )
    return jax.shard_map(
        shards,
        mesh=mesh,
        in_specs=placed,
        out_specs=(
            P("expert", None),
            P("expert", None),
            P(),
            P(None, None, "tensor"),
            P("tensor", None),
            P("tensor", None),
            P(),
            P(),
            P("expert", None, "tensor"),
            P("expert", "tensor", None),
        ),
        check_vma=False,
    )
```

```python
import functools

import jax
import jax.numpy as jnp
from jax import lax
from jax.experimental import pallas as pl
from jax.experimental.pallas import tpu as pltpu
from jax.sharding import PartitionSpec as P

FAR_LIMITS = (12, 16, 23, 32, 46, 64, 91)
HIGH = lax.Precision.HIGHEST
F32 = jnp.float32
BF16 = jnp.bfloat16
MASKED = -1e30
QB = 256
RB = 512
PAD = 256
FAR = FAR_LIMITS[-1]
SMALL = pl.CostEstimate(flops=1 << 20, bytes_accessed=1 << 16, transcendentals=0)

STEPS = (
    [(1 - limit, 14 - i) for i, limit in enumerate(reversed(FAR_LIMITS))]
    + [(-n, n) for n in range(7, -1, -1)]
    + [(n, 16 + n) for n in range(1, 8)]
    + [(8, 24)]
    + [(limit, 25 + i) for i, limit in enumerate(FAR_LIMITS)]
)


def norm_rows(values, gain):
    return values * lax.rsqrt(jnp.mean(values * values, -1, keepdims=True) + 1e-06) * gain


def nt_dot(left, right):
    return lax.dot_general(left, right, (((1,), (1,)), ((), ())), preferred_element_type=F32)


def nn_dot(left, right):
    return jnp.dot(left, right, preferred_element_type=F32)


def strip_shape(length):
    return 2 * length - QB


def near_rows(length):
    base = length - QB
    first = (base - FAR) // 32 * 32
    last = -(-(base + 127 + FAR) // 32) * 32
    return base, first, last


def build_strip(strip_ref, bias_ref, length, heads):
    total = strip_shape(length)
    base, first, last = near_rows(length)
    for h in range(heads):
        low = jnp.full((8, 128), bias_ref[h, 15], F32)
        high = jnp.full((8, 128), bias_ref[h, 31], F32)
        for half in range(QB // 128):
            cols = slice(half * 128, half * 128 + 128)
            lo_end, hi_start = first + half * 128, last + half * 128
            strip_ref[h, 0:lo_end, cols] = jnp.broadcast_to(low[:1], (lo_end, 128))
            strip_ref[h, hi_start:total, cols] = jnp.broadcast_to(high[:1], (total - hi_start, 128))
    for start in range(first, last, 32):
        offset = (
            lax.broadcasted_iota(jnp.int32, (32, 128), 0)
            - lax.broadcasted_iota(jnp.int32, (32, 128), 1)
            + (start - base)
        )
        tiles = [jnp.full((32, 128), bias_ref[h, 15], F32) for h in range(heads)]
        for begin, bucket in STEPS:
            reached = offset >= begin
            tiles = [jnp.where(reached, bias_ref[h, bucket], tiles[h]) for h in range(heads)]
        for h in range(heads):
            for half in range(QB // 128):
                at = start + half * 128
                strip_ref[h, at : at + 32, half * 128 : half * 128 + 128] = tiles[h]


def head_lanes(rows, h, dim, keep_tail, heads):
    lane = lax.broadcasted_iota(jnp.int32, (rows, PAD), 1)
    inside = (lane >= h * dim) & (lane < (h + 1) * dim)
    if keep_tail:
        inside = inside | (lane >= heads * dim)
    return inside


def shares(seg_ref, b, j):
    return (seg_ref[0, j * QB] <= seg_ref[0, b * QB + QB - 1]) & (
        seg_ref[0, b * QB] <= seg_ref[0, j * QB + QB - 1]
    )


def attend_kernel(
    length, heads, dim,
    x_ref, gain_ref, w_ref, doc_ref, bias_ref, seg_ref,
    att_ref, lse_ref, proj_ref, kt_ref, normed_ref,
    kh_ref, strip_ref, vt_ref, pad_ref, score_ref, top_ref, sum_ref, out_ref,
):
    inner = heads * dim
    build_strip(strip_ref, bias_ref, length, heads)
    lane = lax.broadcasted_iota(jnp.int32, (QB, PAD), 1) - inner
    pad_ref[...] = jnp.zeros_like(pad_ref)
    for t in range(3):
        pad_ref[t * PAD : t * PAD + inner, :] = w_ref[t]

    def project(b, carry):
        at = pl.multiple_of(b * QB, QB)
        here = x_ref[pl.ds(at, QB), :].astype(F32)
        normed = norm_rows(here, gain_ref[...]).astype(BF16)
        normed_ref[pl.ds(at, QB), :] = normed
        every = nt_dot(normed, pad_ref[...])
        same = doc_ref[pl.ds(at, QB), :] == lane
        queries = (every[:, 0:PAD].astype(BF16) * jnp.bfloat16(dim ** (-0.5))).astype(F32)
        queries = queries + jnp.where((lane < 0) | same, 0.0, MASKED)
        keys = every[:, PAD : 2 * PAD]
        values = every[:, 2 * PAD : 3 * PAD]
        proj_ref[pl.ds(at, QB), 0:PAD] = queries.astype(BF16)
        proj_ref[pl.ds(at, QB), PAD : 2 * PAD] = (keys + jnp.where(same, 1.0, 0.0)).astype(BF16)
        proj_ref[pl.ds(at, QB), 2 * PAD : 3 * PAD] = values.astype(BF16)
        kt_ref[:, pl.ds(at, QB)] = keys.T[:inner].astype(BF16)
        vt_ref[:, pl.ds(at, QB)] = values.T[:inner].astype(BF16)
        return carry

    lax.fori_loop(0, length // QB, project, 0)
    keys = proj_ref[:, PAD : 2 * PAD]
    for h in range(heads):
        kh_ref[h] = jnp.where(head_lanes(length, h, dim, True, heads), keys, jnp.zeros_like(keys))

    def block(b, carry):
        at = pl.multiple_of(b * QB, QB)
        queries = proj_ref[pl.ds(at, QB), 0:PAD]
        top_ref[...] = jnp.full_like(top_ref, -3e38)
        sum_ref[...] = jnp.zeros_like(sum_ref)
        out_ref[...] = jnp.zeros_like(out_ref)

        def score(j, carry):
            @pl.when(shares(seg_ref, b, j))
            def _():
                rows = pl.ds(pl.multiple_of(j * QB, QB), QB)
                bias = pl.ds(pl.multiple_of(length - QB + (j - b) * QB, QB), QB)
                for h in range(heads):
                    scores = nt_dot(kh_ref[h, rows, :], queries) + strip_ref[h, bias, :]
                    score_ref[h, rows, :] = scores
                    top = jnp.max(scores, 0, keepdims=True)
                    top_ref[h : h + 1, :] = jnp.maximum(top_ref[h : h + 1, :], top)

            return carry

        def spread(j, carry):
            @pl.when(shares(seg_ref, b, j))
            def _():
                rows = pl.ds(pl.multiple_of(j * QB, QB), QB)
                for h in range(heads):
                    probs = jnp.exp(score_ref[h, rows, :] - top_ref[h : h + 1, :])
                    sum_ref[h : h + 1, :] += jnp.sum(probs, 0, keepdims=True)
                    mine = slice(h * dim, (h + 1) * dim)
                    out_ref[mine, :] += nn_dot(vt_ref[mine, rows], probs.astype(BF16))

            return carry

        lax.fori_loop(0, length // QB, score, 0)
        lax.fori_loop(0, length // QB, spread, 0)
        for h in range(heads):
            mine = slice(h * dim, (h + 1) * dim)
            total = sum_ref[h : h + 1, :]
            att_ref[mine, pl.ds(at, QB)] = (out_ref[mine, :] / total).astype(BF16)
            lse_ref[h : h + 1, pl.ds(at, QB)] = top_ref[h : h + 1, :] + jnp.log(total)
        return carry

    lax.fori_loop(0, length // QB, block, 0)


def attend_back_kernel(
    length, heads, dim,
    proj_ref, kt_ref, lse_ref, da_ref, normed_ref, w_ref, gproj_ref, bias_ref, low_ref, seg_ref,
    grad_ref, kept_ref, sent_ref, drel_ref,
    kh_ref, vh_ref, strip_ref, dstrip_ref, pcat_ref, dcat_ref, dacat_ref, qcat_ref, dk_ref, dv_ref, dqt_ref,
    dq_ref, pad_ref, probs_ref, weighted_ref, delta_ref,
):
    inner = heads * dim
    scale = dim ** (-0.5)
    total = strip_shape(length)
    base, first, last = near_rows(length)
    build_strip(strip_ref, bias_ref, length, heads)
    dstrip_ref[...] = jnp.zeros_like(dstrip_ref)
    dk_ref[...] = jnp.zeros_like(dk_ref)
    dv_ref[...] = jnp.zeros_like(dv_ref)
    dqt_ref[...] = jnp.zeros_like(dqt_ref)
    keys = proj_ref[:, PAD : 2 * PAD]
    values = proj_ref[:, 2 * PAD : 3 * PAD]
    for h in range(heads):
        kh_ref[h] = jnp.where(head_lanes(length, h, dim, True, heads), keys, jnp.zeros_like(keys))
        vh_ref[h] = jnp.where(head_lanes(length, h, dim, False, heads), values, jnp.zeros_like(values))

    def block(b, carry):
        at = pl.multiple_of(b * QB, QB)
        queries = proj_ref[pl.ds(at, QB), 0:PAD]
        grads = da_ref[pl.ds(at, QB), :]
        delta_ref[...] = jnp.zeros_like(delta_ref)
        dqt_ref[...] = jnp.zeros_like(dqt_ref)
        for h in range(heads):
            mine = head_lanes(QB, h, dim, False, heads)
            cols = slice(h * QB, (h + 1) * QB)
            qcat_ref[cols, :] = jnp.where(mine, queries, jnp.zeros_like(queries))
            dacat_ref[cols, :] = jnp.where(mine, grads, jnp.zeros_like(grads))

        def weigh(j, carry):
            @pl.when(shares(seg_ref, b, j))
            def _():
                rows = pl.ds(pl.multiple_of(j * QB, QB), QB)
                bias = pl.ds(pl.multiple_of(length - QB + (j - b) * QB, QB), QB)
                for h in range(heads):
                    scores = nt_dot(kh_ref[h, rows, :], queries) + strip_ref[h, bias, :]
                    probs = jnp.exp(scores - lse_ref[h : h + 1, pl.ds(at, QB)])
                    weighted = probs * nt_dot(vh_ref[h, rows, :], grads)
                    delta_ref[h : h + 1, :] += jnp.sum(weighted, 0, keepdims=True)
                    probs_ref[h, rows, :] = probs
                    weighted_ref[h, rows, :] = weighted

            return carry

        def gather(j, carry):
            @pl.when(shares(seg_ref, b, j))
            def _():
                rows = pl.ds(pl.multiple_of(j * QB, QB), QB)
                bias = pl.ds(pl.multiple_of(length - QB + (j - b) * QB, QB), QB)
                for h in range(heads):
                    cols = slice(h * QB, (h + 1) * QB)
                    mine = slice(h * dim, (h + 1) * dim)
                    probs = probs_ref[h, rows, :]
                    dscore = weighted_ref[h, rows, :] - probs * delta_ref[h : h + 1, :]
                    dstrip_ref[h, bias, :] += dscore
                    dlow = dscore.astype(BF16)
                    pcat_ref[:, cols] = probs.astype(BF16)
                    dcat_ref[:, cols] = dlow
                    dqt_ref[mine, :] += nn_dot(kt_ref[mine, rows], dlow)
                dk_ref[rows, :] += nn_dot(dcat_ref[...], qcat_ref[...])
                dv_ref[rows, :] += nn_dot(pcat_ref[...], dacat_ref[...])

            return carry

        lax.fori_loop(0, length // QB, weigh, 0)
        lax.fori_loop(0, length // QB, gather, 0)
        dq_ref[pl.ds(at, QB), :] = dqt_ref[...].T * scale
        return carry

    lax.fori_loop(0, length // QB, block, 0)

    for t, ref in enumerate((dq_ref, dk_ref, dv_ref)):
        turned = ref[...].T[:inner].astype(BF16)
        grad_ref[t * inner : (t + 1) * inner, :] = nn_dot(turned, normed_ref[...]).astype(BF16)

    grad_ref[3 * inner :, :] = gproj_ref[...]

    pad_ref[...] = jnp.zeros_like(pad_ref)
    for t in range(3):
        pad_ref[t, 0:inner, :] = w_ref[t]
    half = length // 2

    def part(start):
        total = jnp.zeros((QB, w_ref.shape[2]), F32)
        for t, ref in enumerate((dq_ref, dk_ref, dv_ref)):
            total = total + nn_dot(ref[pl.ds(start, QB), :].astype(BF16), pad_ref[t])
        return total

    for i in range(half // QB):
        rows = slice(i * QB, (i + 1) * QB)
        kept_ref[rows, :] = part(pl.multiple_of(low_ref[0] * half + i * QB, QB))
        sent_ref[rows, :] = part(pl.multiple_of((1 - low_ref[0]) * half + i * QB, QB)).astype(BF16)

    offset = (
        lax.broadcasted_iota(jnp.int32, (last - first, 128), 0)
        - lax.broadcasted_iota(jnp.int32, (last - first, 128), 1)
        + (first - base)
    )
    begins = [-(1 << 20)] + [begin for begin, bucket in STEPS] + [1 << 20]
    buckets = [15] + [bucket for begin, bucket in STEPS]
    for h in range(heads):
        near = jnp.zeros((last - first, 128), F32)
        low = jnp.zeros((1, 128), F32)
        high = jnp.zeros((1, 128), F32)
        for half in range(QB // 128):
            cols = slice(half * 128, half * 128 + 128)
            lo_end, hi_start = first + half * 128, last + half * 128
            near = near + dstrip_ref[h, lo_end:hi_start, cols]
            low = low + jnp.sum(dstrip_ref[h, 0:lo_end, cols], 0, keepdims=True)
            high = high + jnp.sum(dstrip_ref[h, hi_start:total, cols], 0, keepdims=True)
        drel_ref[h, 16:17, :] = jnp.zeros((1, 128), F32)
        for i, bucket in enumerate(buckets):
            inside = (offset >= begins[i]) & (offset < begins[i + 1])
            row = jnp.sum(jnp.where(inside, near, 0.0), 0, keepdims=True)
            if bucket == 15:
                row = row + low
            if bucket == 31:
                row = row + high
            drel_ref[h, bucket : bucket + 1, :] = row


def rows_of(count, columns):
    return pl.BlockSpec((count, columns), lambda i: (i, 0))


def whole_of(*shape):
    return pl.BlockSpec(shape, lambda i: (0,) * len(shape))


def whole_like(*arrays):
    return [whole_of(*array.shape) for array in arrays]


def attend(tokens, gain, w_qkv, segments, rel_bias):
    length, width = tokens.shape
    heads = rel_bias.shape[0]
    inner = w_qkv.shape[1]
    operands = (tokens, gain[None, :], w_qkv, segments.reshape(-1, 1))
    results = (
        jax.ShapeDtypeStruct((inner, length), BF16),
        jax.ShapeDtypeStruct((8, length), F32),
        jax.ShapeDtypeStruct((length, 3 * PAD), BF16),
        jax.ShapeDtypeStruct((inner, length), BF16),
        jax.ShapeDtypeStruct((length, width), BF16),
    )
    return pl.pallas_call(
        functools.partial(attend_kernel, length, heads, inner // heads),
        grid=(1,),
        out_shape=results,
        in_specs=whole_like(*operands) + [pl.BlockSpec(memory_space=pltpu.SMEM)] * 2,
        out_specs=tuple(whole_like(*results)),
        scratch_shapes=[
            pltpu.VMEM((heads, length, PAD), BF16),
            pltpu.VMEM((heads, strip_shape(length), QB), F32),
            pltpu.VMEM((inner, length), BF16),
            pltpu.VMEM((3 * PAD, width), BF16),
            pltpu.VMEM((heads, length, QB), F32),
            pltpu.VMEM((8, QB), F32),
            pltpu.VMEM((8, QB), F32),
            pltpu.VMEM((inner, QB), F32),
        ],
        compiler_params=pltpu.CompilerParams(vmem_limit_bytes=60 << 20),
        cost_estimate=SMALL,
    )(*operands, rel_bias, segments)


def attend_back(proj, kt, lse, da, normed, w_qkv, grad_proj, rel_bias, low_bit, segments):
    length, width = normed.shape
    heads, buckets = rel_bias.shape
    inner = w_qkv.shape[1]
    operands = (proj, kt, lse, da, normed, w_qkv, grad_proj)
    results = (
        jax.ShapeDtypeStruct((4 * inner, width), BF16),
        jax.ShapeDtypeStruct((length // 2, width), F32),
        jax.ShapeDtypeStruct((length // 2, width), BF16),
        jax.ShapeDtypeStruct((heads, buckets, 128), F32),
    )
    return pl.pallas_call(
        functools.partial(attend_back_kernel, length, heads, inner // heads),
        grid=(1,),
        out_shape=results,
        in_specs=whole_like(*operands) + [pl.BlockSpec(memory_space=pltpu.SMEM)] * 3,
        out_specs=tuple(whole_like(*results)),
        scratch_shapes=[
            pltpu.VMEM((heads, length, PAD), BF16),
            pltpu.VMEM((heads, length, PAD), BF16),
            pltpu.VMEM((heads, strip_shape(length), QB), F32),
            pltpu.VMEM((heads, strip_shape(length), QB), F32),
            pltpu.VMEM((QB, heads * QB), BF16),
            pltpu.VMEM((QB, heads * QB), BF16),
            pltpu.VMEM((heads * QB, PAD), BF16),
            pltpu.VMEM((heads * QB, PAD), BF16),
            pltpu.VMEM((length, PAD), F32),
            pltpu.VMEM((length, PAD), F32),
            pltpu.VMEM((PAD, QB), F32),
            pltpu.VMEM((length, PAD), F32),
            pltpu.VMEM((3, PAD, width), BF16),
            pltpu.VMEM((heads, length, QB), F32),
            pltpu.VMEM((heads, length, QB), F32),
            pltpu.VMEM((8, QB), F32),
        ],
        compiler_params=pltpu.CompilerParams(vmem_limit_bytes=60 << 20),
        cost_estimate=SMALL,
    )(*operands, rel_bias, low_bit, segments)


def gelu_pair(v):
    inner = 0.7978845608028654 * (v + 0.044715 * (v * v * v))
    bend = jnp.tanh(inner)
    half = 0.5 * (1.0 + bend)
    slope = half + 0.5 * v * (1.0 - bend * bend) * (0.7978845608028654 * (1.0 + 0.134145 * (v * v)))
    return v * half, slope


def expert_kernel(
    members, experts,
    rows_ref, cot_ref, router_ref, group_ref, *refs,
):
    first, second = refs[:members], refs[members : 2 * members]
    reply_ref, share_ref, act_ref, gpre_ref, grad_ref, grouter_ref = refs[2 * members :]
    rows = rows_ref[...]
    count = rows.shape[0]
    lane = lax.broadcasted_iota(jnp.int32, (count, 128), 1)
    logits = jnp.where(lane < experts, nn_dot(rows, router_ref[...]), MASKED)
    raised = jnp.exp(logits - jnp.max(logits, -1, keepdims=True))
    probs = raised / jnp.sum(raised, -1, keepdims=True)
    own = jnp.where(lane == group_ref[0], 1.0, 0.0)
    gate = jnp.sum(probs * own, -1, keepdims=True)
    cot = cot_ref[...].astype(F32)
    grads = (gate * cot).astype(BF16)
    grad_ref[...] = grads
    reply = jnp.zeros(rows.shape, F32)
    share = jnp.zeros(rows.shape, F32)
    for k in range(members):
        act, slope = gelu_pair(nn_dot(rows, first[k][...]))
        act = act.astype(BF16)
        act_ref[k] = act
        reply = reply + nn_dot(act, second[k][...])
        gpre = (nt_dot(grads, second[k][...]) * slope).astype(BF16)
        gpre_ref[k] = gpre
        share = share + nt_dot(gpre, first[k][...])
    reply = reply.astype(BF16)
    reply_ref[...] = reply
    gate_grad = jnp.sum(cot * reply.astype(F32), -1, keepdims=True)
    logit_grad = probs * (own - gate) * gate_grad
    share_ref[...] = (share + nt_dot(logit_grad.astype(BF16), router_ref[...])).astype(BF16)
    grouter_ref[...] = nn_dot(logit_grad.T.astype(BF16), rows)


def expert_step(rows, cot, experts, router, group, first, second):
    members = len(first)
    count, width = rows.shape
    hidden = first[0].shape[1]
    weights = (*first, *second)
    results = (
        jax.ShapeDtypeStruct((count, width), BF16),
        jax.ShapeDtypeStruct((count, width), BF16),
        jax.ShapeDtypeStruct((members, count, hidden), BF16),
        jax.ShapeDtypeStruct((members, count, hidden), BF16),
        jax.ShapeDtypeStruct((count, width), BF16),
        jax.ShapeDtypeStruct((128, width), F32),
    )
    return pl.pallas_call(
        functools.partial(expert_kernel, members, experts),
        grid=(1,),
        out_shape=results,
        in_specs=whole_like(rows, cot, router)
        + [pl.BlockSpec(memory_space=pltpu.SMEM)]
        + whole_like(*weights),
        out_specs=tuple(whole_like(*results)),
        compiler_params=pltpu.CompilerParams(vmem_limit_bytes=60 << 20),
        cost_estimate=SMALL,
    )(rows, cot, router, group, *weights)


def enter_kernel(
    members, experts,
    x_ref, gain_ref, router_ref, route_ref, flat_ref, ids_ref, *refs,
):
    att, proj = refs[:members], refs[members : 2 * members]
    hidden_ref, gate_ref, leave_ref, total_ref = refs[2 * members :]
    step = pl.program_id(0)
    hidden = x_ref[...].astype(F32)
    for k in range(members):
        hidden = hidden + lax.dot_general(
            att[k][...], proj[k][...], (((0,), (0,)), ((), ())), preferred_element_type=F32
        )
    hidden_ref[...] = hidden
    normed = norm_rows(hidden, gain_ref[...]).astype(BF16)
    lane = lax.broadcasted_iota(jnp.int32, (RB, 128), 1)
    logits = jnp.where(lane < experts, nn_dot(normed, router_ref[...]), MASKED)
    raised = jnp.exp(logits - jnp.max(logits, -1, keepdims=True))
    chosen = jnp.sum(jnp.where(lane == route_ref[...], raised, 0.0), -1, keepdims=True)
    gate_ref[...] = chosen / jnp.sum(raised, -1, keepdims=True)
    table = jnp.where(ids_ref[...] == flat_ref[...], 1.0, 0.0).astype(BF16)

    @pl.when(step == 0)
    def _():
        total_ref[...] = jnp.zeros_like(total_ref)

    total_ref[...] += nn_dot(table, normed)

    @pl.when(step == pl.num_programs(0) - 1)
    def _():
        leave_ref[...] = total_ref[...].astype(BF16)


def enter_experts(tokens, experts, gain, router, route, flat_id, ids, att, proj):
    length, width = tokens.shape
    members = len(att)
    inner = att[0].shape[0]
    count = ids.shape[0]
    return pl.pallas_call(
        functools.partial(enter_kernel, members, experts),
        grid=(length // RB,),
        out_shape=(
            jax.ShapeDtypeStruct((length, width), F32),
            jax.ShapeDtypeStruct((length, 1), F32),
            jax.ShapeDtypeStruct((count, width), BF16),
        ),
        in_specs=[
            rows_of(RB, width),
            whole_of(1, width),
            whole_of(width, 128),
            rows_of(RB, 1),
            pl.BlockSpec((1, RB), lambda i: (0, i)),
            whole_of(count, 1),
        ]
        + [pl.BlockSpec((inner, RB), lambda i: (0, i))] * members
        + [whole_of(inner, width)] * members,
        out_specs=(rows_of(RB, width), rows_of(RB, 1), whole_of(count, width)),
        scratch_shapes=[pltpu.VMEM((count, width), F32)],
        compiler_params=pltpu.CompilerParams(vmem_limit_bytes=60 << 20),
        cost_estimate=SMALL,
    )(
        tokens, gain, router, route, flat_id, ids, *att, *proj,
    )


def weight_kernel(half, rows_ref, grads_ref, act_ref, gpre_ref, kept_ref, sent_ref):
    step = pl.program_id(0)

    def product(left, right):
        return lax.dot_general(
            left, right, (((0,), (0,)), ((), ())), preferred_element_type=F32
        ).astype(BF16)

    @pl.when(step < half)
    def _():
        k = 2 * step
        kept_ref[0] = product(act_ref[k], grads_ref[...])
        sent_ref[0] = product(act_ref[k + 1], grads_ref[...])

    @pl.when(step >= half)
    def _():
        k = 2 * (step - half)
        kept_ref[0] = product(rows_ref[...], gpre_ref[k])
        sent_ref[0] = product(rows_ref[...], gpre_ref[k + 1])


def weight_grads(rows, grads, act, gpre):
    members, count, hidden = act.shape
    width = rows.shape[1]
    assert hidden == width
    one = pl.BlockSpec((1, width, width), lambda i: (i, 0, 0))
    return pl.pallas_call(
        functools.partial(weight_kernel, members // 2),
        grid=(members,),
        out_shape=(
            jax.ShapeDtypeStruct((members, width, width), BF16),
            jax.ShapeDtypeStruct((members, width, width), BF16),
        ),
        in_specs=[whole_of(count, width)] * 2 + [whole_of(members, count, hidden)] * 2,
        out_specs=(one, one),
        compiler_params=pltpu.CompilerParams(vmem_limit_bytes=60 << 20),
        cost_estimate=SMALL,
    )(rows, grads, act, gpre)


def leave_kernel(
    members,
    hidden_ref, cot_ref, gain_ref, flat_ref, ids_ref, wproj_ref, att_ref, *refs,
):
    blocks = refs[:members]
    gh_ref, da_ref, ggain_ref, gproj_ref, total_ref = refs[members:]
    step = pl.program_id(0)
    share = blocks[0].shape[0]
    grad = jnp.zeros(hidden_ref.shape, F32)
    for k in range(members):
        hit = flat_ref[...] == ids_ref[:, k * share : (k + 1) * share]
        grad = grad + nn_dot(jnp.where(hit, 1.0, 0.0).astype(BF16), blocks[k][...])
    hidden = hidden_ref[...]
    inverse = lax.rsqrt(jnp.mean(hidden * hidden, -1, keepdims=True) + 1e-06)
    unit = hidden * inverse
    scaled = gain_ref[...] * grad
    back = inverse * (scaled - unit * jnp.mean(unit * scaled, -1, keepdims=True))
    total = cot_ref[...].astype(F32) + back
    gh_ref[...] = total
    low = total.astype(BF16)
    da_ref[...] = nt_dot(low, wproj_ref[...]).astype(BF16)

    @pl.when(step == 0)
    def _():
        ggain_ref[...] = jnp.zeros_like(ggain_ref)
        total_ref[...] = jnp.zeros_like(total_ref)

    ggain_ref[...] += jnp.sum(grad * unit, 0, keepdims=True)
    total_ref[...] += nn_dot(att_ref[...], low)

    @pl.when(step == pl.num_programs(0) - 1)
    def _():
        gproj_ref[...] = total_ref[...].astype(BF16)


def leave_experts(hidden1, cotangent, gain, flat_id, ids, w_proj, attended_t, blocks):
    length, width = hidden1.shape
    inner = attended_t.shape[0]
    members = len(blocks)
    share = blocks[0].shape[0]
    return pl.pallas_call(
        functools.partial(leave_kernel, members),
        grid=(length // RB,),
        out_shape=(
            jax.ShapeDtypeStruct((length, width), F32),
            jax.ShapeDtypeStruct((length, PAD), BF16),
            jax.ShapeDtypeStruct((1, width), F32),
            jax.ShapeDtypeStruct((inner, width), BF16),
        ),
        in_specs=[
            rows_of(RB, width),
            rows_of(RB, width),
            whole_of(1, width),
            rows_of(RB, 1),
            whole_of(1, members * share),
            whole_of(PAD, width),
            pl.BlockSpec((inner, RB), lambda i: (0, i)),
        ]
        + [whole_of(share, width)] * members,
        out_specs=(
            rows_of(RB, width),
            rows_of(RB, PAD),
            whole_of(1, width),
            whole_of(inner, width),
        ),
        scratch_shapes=[pltpu.VMEM((inner, width), F32)],
        compiler_params=pltpu.CompilerParams(vmem_limit_bytes=60 << 20),
        cost_estimate=SMALL,
    )(
        hidden1, cotangent, gain, flat_id, ids, w_proj, attended_t, *blocks,
    )


def output_kernel(members, hidden_ref, gate_ref, flat_ref, ids_ref, *refs):
    blocks, out_ref = refs[:members], refs[members]
    share = blocks[0].shape[0]
    reply = jnp.zeros(hidden_ref.shape, F32)
    for k in range(members):
        hit = flat_ref[...] == ids_ref[:, k * share : (k + 1) * share]
        reply = reply + nn_dot(jnp.where(hit, 1.0, 0.0).astype(BF16), blocks[k][...])
    out_ref[...] = (hidden_ref[...] + gate_ref[...] * reply).astype(BF16)


def output_rows(hidden1, gate, flat_id, ids, blocks):
    length, width = hidden1.shape
    members = len(blocks)
    share = blocks[0].shape[0]
    return pl.pallas_call(
        functools.partial(output_kernel, members),
        grid=(length // RB,),
        out_shape=jax.ShapeDtypeStruct((length, width), BF16),
        in_specs=[rows_of(RB, width), rows_of(RB, 1), rows_of(RB, 1), whole_of(1, members * share)]
        + [whole_of(share, width)] * members,
        out_specs=rows_of(RB, width),
        compiler_params=pltpu.CompilerParams(vmem_limit_bytes=60 << 20),
        cost_estimate=SMALL,
    )(hidden1, gate, flat_id, ids, *blocks)


def input_kernel(halves, kept_ref, other_ref, x_ref, gain_ref, gh_ref, low_ref, out_ref, ggain_ref):
    step = pl.program_id(0)
    part = jnp.where(step // halves == low_ref[0], kept_ref[...].astype(F32), other_ref[...].astype(F32))
    x = x_ref[...].astype(F32)
    inverse = lax.rsqrt(jnp.mean(x * x, -1, keepdims=True) + 1e-06)
    unit = x * inverse
    scaled = gain_ref[...] * part
    out_ref[...] = gh_ref[...] + inverse * (scaled - unit * jnp.mean(unit * scaled, -1, keepdims=True))

    @pl.when(step == 0)
    def _():
        ggain_ref[...] = jnp.zeros_like(ggain_ref)

    ggain_ref[...] += jnp.sum(part * unit, 0, keepdims=True)


def input_grads(kept, other, tokens, gain, grad_hidden1, low_bit):
    length, width = tokens.shape
    halves = kept.shape[0] // QB
    half = pl.BlockSpec((QB, width), lambda i: (i % halves, 0))
    return pl.pallas_call(
        functools.partial(input_kernel, halves),
        grid=(length // QB,),
        out_shape=(
            jax.ShapeDtypeStruct((length, width), F32),
            jax.ShapeDtypeStruct((1, width), F32),
        ),
        in_specs=[
            half,
            half,
            rows_of(QB, width),
            whole_of(1, width),
            rows_of(QB, width),
            pl.BlockSpec(memory_space=pltpu.SMEM),
        ],
        out_specs=(rows_of(QB, width), whole_of(1, width)),
        compiler_params=pltpu.CompilerParams(vmem_limit_bytes=60 << 20),
        cost_estimate=SMALL,
    )(kept, other, tokens, gain[None, :], grad_hidden1, low_bit)


def copies_kernel(came_ref, small_ref, ggain_ref, out_ref, mine_ref):
    groups, large = came_ref.shape[:2]

    @pl.when(pl.program_id(0) == 0)
    def _():
        total = came_ref[0].astype(F32)
        for g in range(1, groups):
            total = total + came_ref[g].astype(F32)
        mine_ref[:large, :] = total.astype(BF16)
        row = lax.broadcasted_iota(jnp.int32, small_ref.shape, 0)
        mine_ref[large:, :] = (small_ref[...] + jnp.where(row == 2, ggain_ref[...], 0.0)).astype(BF16)

    out_ref[0] = mine_ref[...]


def sum_copies(came, small, ggain):
    groups, large, width = came.shape
    count = large + small.shape[0]
    return pl.pallas_call(
        copies_kernel,
        grid=(groups,),
        out_shape=jax.ShapeDtypeStruct((groups, count, width), BF16),
        in_specs=whole_like(came, small, ggain),
        out_specs=pl.BlockSpec((1, count, width), lambda i: (i, 0, 0)),
        scratch_shapes=[pltpu.VMEM((count, width), BF16)],
        compiler_params=pltpu.CompilerParams(vmem_limit_bytes=60 << 20),
        cost_estimate=SMALL,
    )(came, small, ggain)


def final_kernel(large, inner, totals_ref, qkv_ref, proj_ref, gffn_ref, rel_ref, gattn_ref, router_ref):
    groups = totals_ref.shape[0]
    split = 3 * inner
    small = totals_ref[0, large:, :].astype(F32)
    for g in range(groups):
        start, stop = g * large, (g + 1) * large
        if start < split:
            count = min(stop, split) - start
            qkv_ref[start : start + count, :] = totals_ref[g, :count, :].astype(F32)
        if stop > split:
            skip = max(start, split) - start
            proj_ref[start + skip - split : stop - split, :] = totals_ref[g, skip:large, :].astype(F32)
        if g:
            small = small + totals_ref[g, large:, :].astype(F32)
    gffn_ref[...] = small[0:1]
    rel_ref[...] = small[1:2]
    gattn_ref[...] = small[2:3]
    router_ref[...] = small[3 : 3 + router_ref.shape[0]]


def final_weights(totals, large, inner, experts):
    groups, count, width = totals.shape
    results = (
        jax.ShapeDtypeStruct((3 * inner, width), F32),
        jax.ShapeDtypeStruct((inner, width), F32),
        jax.ShapeDtypeStruct((1, width), F32),
        jax.ShapeDtypeStruct((1, width), F32),
        jax.ShapeDtypeStruct((1, width), F32),
        jax.ShapeDtypeStruct((experts, width), F32),
    )
    return pl.pallas_call(
        functools.partial(final_kernel, large, inner),
        grid=(1,),
        out_shape=results,
        in_specs=whole_like(totals),
        out_specs=tuple(whole_like(*results)),
        compiler_params=pltpu.CompilerParams(vmem_limit_bytes=16 << 20),
        cost_estimate=SMALL,
    )(totals)


def shards(
    tokens,
    gain_attn,
    w_qkv,
    w_proj,
    rel_bias,
    gain_ffn,
    w_router,
    w_in,
    w_out,
    routes,
    segment_ids,
    cotangent,
):
    length, width = tokens.shape
    experts = w_router.shape[1]
    capacity = max(2, 3 * length // (2 * experts))
    inner_here = w_proj.shape[0]
    members = lax.axis_size("tensor")
    groups = lax.axis_size("expert")
    member = lax.axis_index("tensor")
    group = lax.axis_index("expert")
    share = capacity // members
    route = routes[:, 0]

    def swap(value, bit):
        return lax.ppermute(value, "tensor", [(i, i ^ bit) for i in range(members)])

    bits = [1 << i for i in range(members.bit_length() - 1)]

    def gather_far(value):
        blocks = {0: value}
        for bit in reversed(bits[1:]):
            blocks.update({k ^ bit: swap(block, bit) for k, block in blocks.items()})
        return blocks

    def gather_near(blocks):
        blocks = dict(blocks)
        for bit in bits[:1]:
            blocks.update({k ^ bit: swap(block, bit) for k, block in blocks.items()})
        return [blocks[k] for k in range(members)]

    def gather_members(value):
        return gather_near(gather_far(value))

    def gather_groups(value):
        copies = jnp.broadcast_to(value[None], (groups,) + value.shape)
        return exchange(copies)

    def exchange(value):
        return lax.all_to_all(value, "expert", split_axis=0, concat_axis=0, tiled=True)

    tie = lax.optimization_barrier

    expert_ids = jnp.arange(experts, dtype=jnp.int32)
    onehot_low = (route[:, None] == expert_ids[None, :]).astype(BF16)
    onehot = onehot_low.astype(F32)
    positions = jnp.arange(length, dtype=jnp.int32)
    lower_ones = (positions[:, None] >= positions[None, :]).astype(BF16)
    running = nn_dot(lower_ones, onehot_low)
    slot = (jnp.sum(running * onehot, 1) - 1.0).astype(jnp.int32)
    flat_id = route * capacity + slot

    def ids_of(owner):
        slots = owner * share + jnp.arange(share, dtype=jnp.int32)
        return (expert_ids[:, None] * capacity + slots[None, :]).reshape(-1)

    send_table = (ids_of(member)[:, None] == flat_id[None, :]).astype(BF16)
    all_ids = jnp.concatenate([ids_of(member ^ k) for k in range(members)])

    def dispatch(rows):
        out = nn_dot(send_table, rows).astype(BF16).reshape(groups, -1, width)
        return exchange(out).reshape(-1, width)

    cot_share = dispatch(cotangent)
    w_proj_far = gather_far(w_proj)
    w_in_far = gather_far(w_in[0])
    w_qkv_t = jnp.swapaxes(w_qkv, 1, 2)
    attended_t, lse, proj, keys_t, normed1 = attend(tokens, gain_attn, w_qkv_t, segment_ids, rel_bias)
    attended_t, w_in_far, cot_share = tie((attended_t, w_in_far, cot_share))

    attended_far = gather_far(attended_t)
    gain_row = gain_ffn[None, :]
    router = jnp.pad(w_router, ((0, 0), (0, 128 - experts)))
    w_proj_pad = jnp.pad(w_proj, ((0, PAD - inner_here), (0, 0)))
    flat_row, flat_column = flat_id[None, :], flat_id[:, None]
    send_ids, back_ids = ids_of(member)[:, None], all_ids[None, :]
    (
        attended_far, w_proj_far, w_out_here, gain_row, router, w_proj_pad,
        flat_row, flat_column, send_ids, back_ids,
    ) = tie((
        attended_far, w_proj_far, w_out[0], gain_row, router, w_proj_pad,
        flat_row, flat_column, send_ids, back_ids,
    ))
    attended_blocks = gather_near(attended_far)
    w_proj_blocks = gather_near(w_proj_far)
    w_in_all = gather_near(w_in_far)
    w_out_far = gather_far(w_out_here)
    hidden1, gate, leaving = enter_experts(
        tokens, experts, gain_row, router, routes, flat_row, send_ids, attended_blocks, w_proj_blocks
    )
    rows = exchange(leaving.reshape(groups, -1, width)).reshape(-1, width)
    rows, w_out_far, w_in_all = tie((rows, w_out_far, w_in_all))
    w_out_all = gather_near(w_out_far)

    reply, grad_share, act, grad_pre, grad_rows, grad_router = expert_step(
        rows, cot_share, experts, router, group[None], w_in_all, w_out_all
    )
    grad_back = exchange(grad_share.reshape(groups, -1, width)).reshape(-1, width)
    grad_router = grad_router[:experts]
    for bit in bits:
        grad_router = grad_router + swap(grad_router, bit)
    kept_weights, sent_weights = weight_grads(rows, grad_rows, act, grad_pre)
    grad_back, reply, kept_weights, sent_weights, grad_router = tie(
        (grad_back, reply, kept_weights, sent_weights, grad_router)
    )
    near_weights = swap(sent_weights, 1)
    grad_far = gather_far(grad_back)
    cut = width // 2

    def pair(k, rows_cut):
        return kept_weights[k, rows_cut].astype(F32) + near_weights[k, rows_cut].astype(F32)

    out_sent = pair(1, slice(0, width)).astype(BF16)
    fore_sent, rest_sent = pair(3, slice(0, cut)).astype(BF16), pair(3, slice(cut, width)).astype(BF16)
    grad_far, out_sent, fore_sent, rest_sent = tie((grad_far, out_sent, fore_sent, rest_sent))
    out_came, fore_came = swap(out_sent, 2), swap(fore_sent, 2)
    grad_blocks = gather_near(grad_far)
    reply_back = exchange(reply.reshape(groups, -1, width)).reshape(-1, width)
    grad_hidden1, attended_grad, grad_gain_ffn, grad_proj = leave_experts(
        hidden1, cotangent, gain_row, flat_column, back_ids, w_proj_pad, attended_t, grad_blocks
    )

    low_bit = (member & 1)[None]
    grads, kept, sent, rel_parts = attend_back(
        proj, keys_t, lse, attended_grad, normed1, w_qkv_t, grad_proj, rel_bias, low_bit, segment_ids
    )
    grads, kept, sent, reply_back, out_came, fore_came, rest_sent = tie(
        (grads, kept, sent, reply_back, out_came, fore_came, rest_sent)
    )
    kept = kept + swap(sent, 1).astype(F32)
    kept_low, grads = tie((kept.astype(BF16), grads))
    far = swap(kept_low, 2)
    came = exchange(grads.reshape(groups, -1, width))
    grad_w_out = pair(0, slice(0, width)) + out_came.astype(F32)
    far, grad_w_out, reply_back, rest_sent = tie((far, grad_w_out, reply_back, rest_sent))
    rest_came = swap(rest_sent, 2)
    kept = (kept + far.astype(F32)).astype(BF16)
    other = swap(kept, 1)
    grad_input, gain_part = input_grads(kept, other, tokens, gain_attn, grad_hidden1, low_bit)
    gain_part, rest_came, reply_back = tie((gain_part, rest_came, reply_back))
    reply_far = gather_far(reply_back)
    grad_w_in = pair(2, slice(0, width)) + jnp.concatenate([fore_came, rest_came], 0).astype(F32)

    rel_row = jnp.sum(rel_parts, -1).reshape(1, -1)
    rel_row = jnp.pad(rel_row, ((0, 0), (0, width - rel_row.shape[1])))
    small = jnp.concatenate([grad_gain_ffn, rel_row, jnp.zeros((1, width), F32), grad_router], 0)
    small = jnp.pad(small, ((0, -small.shape[0] % 16), (0, 0)))
    large = came.shape[1]
    if large % 16 == 0:
        copies = sum_copies(came, small, gain_part)
    else:
        small = small.at[2].add(gain_part[0])
        copies = jnp.concatenate([jnp.sum(came.astype(F32), 0), small], 0).astype(BF16)
        copies = jnp.broadcast_to(copies[None], (groups,) + copies.shape)
    totals = exchange(copies)
    output = output_rows(hidden1, gate, flat_column, back_ids, gather_near(reply_far))
    if large % 16 == 0:
        grad_qkv_t, grad_proj, grad_gain_ffn, rel_row, grad_gain_attn, grad_router = final_weights(
            totals, large, inner_here, experts
        )
    else:
        shared = totals[:, :large].reshape(-1, width).astype(F32)
        grad_qkv_t, grad_proj = shared[: 3 * inner_here], shared[3 * inner_here :]
        small = jnp.sum(totals[:, large:].astype(F32), 0)
        grad_gain_ffn, rel_row, grad_gain_attn = small[0], small[1], small[2]
        grad_router = small[3 : 3 + experts]
    grad_qkv = jnp.swapaxes(grad_qkv_t.reshape(3, inner_here, width), 1, 2)
    grad_gain_ffn, grad_gain_attn = grad_gain_ffn.reshape(-1), grad_gain_attn.reshape(-1)
    grad_rel = rel_row.reshape(-1)[: rel_bias.size].reshape(rel_bias.shape)
    grad_router = grad_router.T
    return (
        output,
        grad_input,
        grad_gain_attn,
        grad_qkv,
        grad_proj,
        grad_rel,
        grad_gain_ffn,
        grad_router,
        grad_w_in[None],
        grad_w_out[None],
    )


def solution(mesh):
    placed = (
        P("expert", None),
        P(),
        P(None, None, "tensor"),
        P("tensor", None),
        P("tensor", None),
        P(),
        P(),
        P("expert", None, "tensor"),
        P("expert", "tensor", None),
        P("expert", None),
        P("expert", None),
        P("expert", None),
    )
    return jax.shard_map(
        shards,
        mesh=mesh,
        in_specs=placed,
        out_specs=(
            P("expert", None),
            P("expert", None),
            P(),
            P(None, None, "tensor"),
            P("tensor", None),
            P("tensor", None),
            P(),
            P(),
            P("expert", None, "tensor"),
            P("expert", "tensor", None),
        ),
        check_vma=False,
    )
```

```python
import functools

import jax
import jax.numpy as jnp
from jax import lax
from jax.experimental import pallas as pl
from jax.experimental.pallas import tpu as pltpu
from jax.sharding import PartitionSpec as P

FAR_LIMITS = (12, 16, 23, 32, 46, 64, 91)
HIGH = lax.Precision.HIGHEST
F32 = jnp.float32
BF16 = jnp.bfloat16
MASKED = -1e30
QB = 256
RB = 512
PAD = 256
FAR = FAR_LIMITS[-1]
SMALL = pl.CostEstimate(flops=1 << 20, bytes_accessed=1 << 16, transcendentals=0)

STEPS = (
    [(1 - limit, 14 - i) for i, limit in enumerate(reversed(FAR_LIMITS))]
    + [(-n, n) for n in range(7, -1, -1)]
    + [(n, 16 + n) for n in range(1, 8)]
    + [(8, 24)]
    + [(limit, 25 + i) for i, limit in enumerate(FAR_LIMITS)]
)


def norm_rows(values, gain):
    return values * lax.rsqrt(jnp.mean(values * values, -1, keepdims=True) + 1e-06) * gain


def nt_dot(left, right):
    return lax.dot_general(left, right, (((1,), (1,)), ((), ())), preferred_element_type=F32)


def nn_dot(left, right):
    return jnp.dot(left, right, preferred_element_type=F32)


def strip_shape(length):
    return 2 * length - QB


def near_rows(length):
    base = length - QB
    first = (base - FAR) // 32 * 32
    last = -(-(base + 127 + FAR) // 32) * 32
    return base, first, last


def build_strip(strip_ref, bias_ref, length, heads):
    total = strip_shape(length)
    base, first, last = near_rows(length)
    for h in range(heads):
        low = jnp.full((8, 128), bias_ref[h, 15], F32)
        high = jnp.full((8, 128), bias_ref[h, 31], F32)
        for half in range(QB // 128):
            cols = slice(half * 128, half * 128 + 128)
            lo_end, hi_start = first + half * 128, last + half * 128
            strip_ref[h, 0:lo_end, cols] = jnp.broadcast_to(low[:1], (lo_end, 128))
            strip_ref[h, hi_start:total, cols] = jnp.broadcast_to(high[:1], (total - hi_start, 128))
    for start in range(first, last, 32):
        offset = (
            lax.broadcasted_iota(jnp.int32, (32, 128), 0)
            - lax.broadcasted_iota(jnp.int32, (32, 128), 1)
            + (start - base)
        )
        tiles = [jnp.full((32, 128), bias_ref[h, 15], F32) for h in range(heads)]
        for begin, bucket in STEPS:
            reached = offset >= begin
            tiles = [jnp.where(reached, bias_ref[h, bucket], tiles[h]) for h in range(heads)]
        for h in range(heads):
            for half in range(QB // 128):
                at = start + half * 128
                strip_ref[h, at : at + 32, half * 128 : half * 128 + 128] = tiles[h]


def head_lanes(rows, h, dim, keep_tail, heads):
    lane = lax.broadcasted_iota(jnp.int32, (rows, PAD), 1)
    inside = (lane >= h * dim) & (lane < (h + 1) * dim)
    if keep_tail:
        inside = inside | (lane >= heads * dim)
    return inside


def shares(seg_ref, b, j):
    return (seg_ref[0, j * QB] <= seg_ref[0, b * QB + QB - 1]) & (
        seg_ref[0, b * QB] <= seg_ref[0, j * QB + QB - 1]
    )


def attend_kernel(
    length, heads, dim,
    x_ref, gain_ref, w_ref, doc_ref, bias_ref, seg_ref,
    att_ref, lse_ref, proj_ref, kt_ref, normed_ref,
    kh_ref, strip_ref, vt_ref, pad_ref, score_ref, top_ref, sum_ref, out_ref,
):
    inner = heads * dim
    build_strip(strip_ref, bias_ref, length, heads)
    lane = lax.broadcasted_iota(jnp.int32, (QB, PAD), 1) - inner
    pad_ref[...] = jnp.zeros_like(pad_ref)
    for t in range(3):
        pad_ref[t * PAD : t * PAD + inner, :] = w_ref[t]

    def project(b, carry):
        at = pl.multiple_of(b * QB, QB)
        here = x_ref[pl.ds(at, QB), :].astype(F32)
        normed = norm_rows(here, gain_ref[...]).astype(BF16)
        normed_ref[pl.ds(at, QB), :] = normed
        every = nt_dot(normed, pad_ref[...])
        same = doc_ref[pl.ds(at, QB), :] == lane
        queries = (every[:, 0:PAD].astype(BF16) * jnp.bfloat16(dim ** (-0.5))).astype(F32)
        queries = queries + jnp.where((lane < 0) | same, 0.0, MASKED)
        keys = every[:, PAD : 2 * PAD]
        values = every[:, 2 * PAD : 3 * PAD]
        proj_ref[pl.ds(at, QB), 0:PAD] = queries.astype(BF16)
        proj_ref[pl.ds(at, QB), PAD : 2 * PAD] = (keys + jnp.where(same, 1.0, 0.0)).astype(BF16)
        proj_ref[pl.ds(at, QB), 2 * PAD : 3 * PAD] = values.astype(BF16)
        kt_ref[:, pl.ds(at, QB)] = keys.T[:inner].astype(BF16)
        vt_ref[:, pl.ds(at, QB)] = values.T[:inner].astype(BF16)
        return carry

    lax.fori_loop(0, length // QB, project, 0)
    keys = proj_ref[:, PAD : 2 * PAD]
    for h in range(heads):
        kh_ref[h] = jnp.where(head_lanes(length, h, dim, True, heads), keys, jnp.zeros_like(keys))

    def block(b, carry):
        at = pl.multiple_of(b * QB, QB)
        queries = proj_ref[pl.ds(at, QB), 0:PAD]
        top_ref[...] = jnp.full_like(top_ref, -3e38)
        sum_ref[...] = jnp.zeros_like(sum_ref)
        out_ref[...] = jnp.zeros_like(out_ref)

        def score(j, carry):
            @pl.when(shares(seg_ref, b, j))
            def _():
                rows = pl.ds(pl.multiple_of(j * QB, QB), QB)
                bias = pl.ds(pl.multiple_of(length - QB + (j - b) * QB, QB), QB)
                for h in range(heads):
                    scores = nt_dot(kh_ref[h, rows, :], queries) + strip_ref[h, bias, :]
                    score_ref[h, rows, :] = scores
                    top = jnp.max(scores, 0, keepdims=True)
                    top_ref[h : h + 1, :] = jnp.maximum(top_ref[h : h + 1, :], top)

            return carry

        def spread(j, carry):
            @pl.when(shares(seg_ref, b, j))
            def _():
                rows = pl.ds(pl.multiple_of(j * QB, QB), QB)
                for h in range(heads):
                    probs = jnp.exp(score_ref[h, rows, :] - top_ref[h : h + 1, :])
                    sum_ref[h : h + 1, :] += jnp.sum(probs, 0, keepdims=True)
                    mine = slice(h * dim, (h + 1) * dim)
                    out_ref[mine, :] += nn_dot(vt_ref[mine, rows], probs.astype(BF16))

            return carry

        lax.fori_loop(0, length // QB, score, 0)
        lax.fori_loop(0, length // QB, spread, 0)
        for h in range(heads):
            mine = slice(h * dim, (h + 1) * dim)
            total = sum_ref[h : h + 1, :]
            att_ref[mine, pl.ds(at, QB)] = (out_ref[mine, :] / total).astype(BF16)
            lse_ref[h : h + 1, pl.ds(at, QB)] = top_ref[h : h + 1, :] + jnp.log(total)
        return carry

    lax.fori_loop(0, length // QB, block, 0)


def attend_back_kernel(
    length, heads, dim,
    proj_ref, kt_ref, lse_ref, da_ref, normed_ref, w_ref, gproj_ref, bias_ref, low_ref, seg_ref,
    grad_ref, kept_ref, sent_ref, drel_ref,
    kh_ref, vh_ref, strip_ref, dstrip_ref, pcat_ref, dcat_ref, dacat_ref, qcat_ref, dk_ref, dv_ref, dqt_ref,
    dq_ref, pad_ref, probs_ref, weighted_ref, delta_ref,
):
    inner = heads * dim
    scale = dim ** (-0.5)
    total = strip_shape(length)
    base, first, last = near_rows(length)
    build_strip(strip_ref, bias_ref, length, heads)
    dstrip_ref[...] = jnp.zeros_like(dstrip_ref)
    dk_ref[...] = jnp.zeros_like(dk_ref)
    dv_ref[...] = jnp.zeros_like(dv_ref)
    dqt_ref[...] = jnp.zeros_like(dqt_ref)
    keys = proj_ref[:, PAD : 2 * PAD]
    values = proj_ref[:, 2 * PAD : 3 * PAD]
    for h in range(heads):
        kh_ref[h] = jnp.where(head_lanes(length, h, dim, True, heads), keys, jnp.zeros_like(keys))
        vh_ref[h] = jnp.where(head_lanes(length, h, dim, False, heads), values, jnp.zeros_like(values))

    def block(b, carry):
        at = pl.multiple_of(b * QB, QB)
        queries = proj_ref[pl.ds(at, QB), 0:PAD]
        grads = da_ref[pl.ds(at, QB), :]
        delta_ref[...] = jnp.zeros_like(delta_ref)
        dqt_ref[...] = jnp.zeros_like(dqt_ref)
        for h in range(heads):
            mine = head_lanes(QB, h, dim, False, heads)
            cols = slice(h * QB, (h + 1) * QB)
            qcat_ref[cols, :] = jnp.where(mine, queries, jnp.zeros_like(queries))
            dacat_ref[cols, :] = jnp.where(mine, grads, jnp.zeros_like(grads))

        def weigh(j, carry):
            @pl.when(shares(seg_ref, b, j))
            def _():
                rows = pl.ds(pl.multiple_of(j * QB, QB), QB)
                bias = pl.ds(pl.multiple_of(length - QB + (j - b) * QB, QB), QB)
                for h in range(heads):
                    scores = nt_dot(kh_ref[h, rows, :], queries) + strip_ref[h, bias, :]
                    probs = jnp.exp(scores - lse_ref[h : h + 1, pl.ds(at, QB)])
                    weighted = probs * nt_dot(vh_ref[h, rows, :], grads)
                    delta_ref[h : h + 1, :] += jnp.sum(weighted, 0, keepdims=True)
                    probs_ref[h, rows, :] = probs
                    weighted_ref[h, rows, :] = weighted

            return carry

        def gather(j, carry):
            @pl.when(shares(seg_ref, b, j))
            def _():
                rows = pl.ds(pl.multiple_of(j * QB, QB), QB)
                bias = pl.ds(pl.multiple_of(length - QB + (j - b) * QB, QB), QB)
                for h in range(heads):
                    cols = slice(h * QB, (h + 1) * QB)
                    mine = slice(h * dim, (h + 1) * dim)
                    probs = probs_ref[h, rows, :]
                    dscore = weighted_ref[h, rows, :] - probs * delta_ref[h : h + 1, :]
                    dstrip_ref[h, bias, :] += dscore
                    dlow = dscore.astype(BF16)
                    pcat_ref[:, cols] = probs.astype(BF16)
                    dcat_ref[:, cols] = dlow
                    dqt_ref[mine, :] += nn_dot(kt_ref[mine, rows], dlow)
                dk_ref[rows, :] += nn_dot(dcat_ref[...], qcat_ref[...])
                dv_ref[rows, :] += nn_dot(pcat_ref[...], dacat_ref[...])

            return carry

        lax.fori_loop(0, length // QB, weigh, 0)
        lax.fori_loop(0, length // QB, gather, 0)
        dq_ref[pl.ds(at, QB), :] = dqt_ref[...].T * scale
        return carry

    lax.fori_loop(0, length // QB, block, 0)

    for t, ref in enumerate((dq_ref, dk_ref, dv_ref)):
        turned = ref[...].T[:inner].astype(BF16)
        grad_ref[t * inner : (t + 1) * inner, :] = nn_dot(turned, normed_ref[...]).astype(BF16)

    grad_ref[3 * inner :, :] = gproj_ref[...]

    pad_ref[...] = jnp.zeros_like(pad_ref)
    for t in range(3):
        pad_ref[t, 0:inner, :] = w_ref[t]
    half = length // 2

    def part(start):
        total = jnp.zeros((QB, w_ref.shape[2]), F32)
        for t, ref in enumerate((dq_ref, dk_ref, dv_ref)):
            total = total + nn_dot(ref[pl.ds(start, QB), :].astype(BF16), pad_ref[t])
        return total

    for i in range(half // QB):
        rows = slice(i * QB, (i + 1) * QB)
        kept_ref[rows, :] = part(pl.multiple_of(low_ref[0] * half + i * QB, QB))
        sent_ref[rows, :] = part(pl.multiple_of((1 - low_ref[0]) * half + i * QB, QB)).astype(BF16)

    offset = (
        lax.broadcasted_iota(jnp.int32, (last - first, 128), 0)
        - lax.broadcasted_iota(jnp.int32, (last - first, 128), 1)
        + (first - base)
    )
    begins = [-(1 << 20)] + [begin for begin, bucket in STEPS] + [1 << 20]
    buckets = [15] + [bucket for begin, bucket in STEPS]
    for h in range(heads):
        near = jnp.zeros((last - first, 128), F32)
        low = jnp.zeros((1, 128), F32)
        high = jnp.zeros((1, 128), F32)
        for half in range(QB // 128):
            cols = slice(half * 128, half * 128 + 128)
            lo_end, hi_start = first + half * 128, last + half * 128
            near = near + dstrip_ref[h, lo_end:hi_start, cols]
            low = low + jnp.sum(dstrip_ref[h, 0:lo_end, cols], 0, keepdims=True)
            high = high + jnp.sum(dstrip_ref[h, hi_start:total, cols], 0, keepdims=True)
        drel_ref[h, 16:17, :] = jnp.zeros((1, 128), F32)
        for i, bucket in enumerate(buckets):
            inside = (offset >= begins[i]) & (offset < begins[i + 1])
            row = jnp.sum(jnp.where(inside, near, 0.0), 0, keepdims=True)
            if bucket == 15:
                row = row + low
            if bucket == 31:
                row = row + high
            drel_ref[h, bucket : bucket + 1, :] = row


def rows_of(count, columns):
    return pl.BlockSpec((count, columns), lambda i: (i, 0))


def whole_of(*shape):
    return pl.BlockSpec(shape, lambda i: (0,) * len(shape))


def whole_like(*arrays):
    return [whole_of(*array.shape) for array in arrays]


def attend(tokens, gain, w_qkv, segments, rel_bias):
    length, width = tokens.shape
    heads = rel_bias.shape[0]
    inner = w_qkv.shape[1]
    operands = (tokens, gain[None, :], w_qkv, segments.reshape(-1, 1))
    results = (
        jax.ShapeDtypeStruct((inner, length), BF16),
        jax.ShapeDtypeStruct((8, length), F32),
        jax.ShapeDtypeStruct((length, 3 * PAD), BF16),
        jax.ShapeDtypeStruct((inner, length), BF16),
        jax.ShapeDtypeStruct((length, width), BF16),
    )
    return pl.pallas_call(
        functools.partial(attend_kernel, length, heads, inner // heads),
        grid=(1,),
        out_shape=results,
        in_specs=whole_like(*operands) + [pl.BlockSpec(memory_space=pltpu.SMEM)] * 2,
        out_specs=tuple(whole_like(*results)),
        scratch_shapes=[
            pltpu.VMEM((heads, length, PAD), BF16),
            pltpu.VMEM((heads, strip_shape(length), QB), F32),
            pltpu.VMEM((inner, length), BF16),
            pltpu.VMEM((3 * PAD, width), BF16),
            pltpu.VMEM((heads, length, QB), F32),
            pltpu.VMEM((8, QB), F32),
            pltpu.VMEM((8, QB), F32),
            pltpu.VMEM((inner, QB), F32),
        ],
        compiler_params=pltpu.CompilerParams(vmem_limit_bytes=60 << 20),
        cost_estimate=SMALL,
    )(*operands, rel_bias, segments)


def attend_back(proj, kt, lse, da, normed, w_qkv, grad_proj, rel_bias, low_bit, segments):
    length, width = normed.shape
    heads, buckets = rel_bias.shape
    inner = w_qkv.shape[1]
    operands = (proj, kt, lse, da, normed, w_qkv, grad_proj)
    results = (
        jax.ShapeDtypeStruct((4 * inner, width), BF16),
        jax.ShapeDtypeStruct((length // 2, width), F32),
        jax.ShapeDtypeStruct((length // 2, width), BF16),
        jax.ShapeDtypeStruct((heads, buckets, 128), F32),
    )
    return pl.pallas_call(
        functools.partial(attend_back_kernel, length, heads, inner // heads),
        grid=(1,),
        out_shape=results,
        in_specs=whole_like(*operands) + [pl.BlockSpec(memory_space=pltpu.SMEM)] * 3,
        out_specs=tuple(whole_like(*results)),
        scratch_shapes=[
            pltpu.VMEM((heads, length, PAD), BF16),
            pltpu.VMEM((heads, length, PAD), BF16),
            pltpu.VMEM((heads, strip_shape(length), QB), F32),
            pltpu.VMEM((heads, strip_shape(length), QB), F32),
            pltpu.VMEM((QB, heads * QB), BF16),
            pltpu.VMEM((QB, heads * QB), BF16),
            pltpu.VMEM((heads * QB, PAD), BF16),
            pltpu.VMEM((heads * QB, PAD), BF16),
            pltpu.VMEM((length, PAD), F32),
            pltpu.VMEM((length, PAD), F32),
            pltpu.VMEM((PAD, QB), F32),
            pltpu.VMEM((length, PAD), F32),
            pltpu.VMEM((3, PAD, width), BF16),
            pltpu.VMEM((heads, length, QB), F32),
            pltpu.VMEM((heads, length, QB), F32),
            pltpu.VMEM((8, QB), F32),
        ],
        compiler_params=pltpu.CompilerParams(vmem_limit_bytes=60 << 20),
        cost_estimate=SMALL,
    )(*operands, rel_bias, low_bit, segments)


def gelu_pair(v):
    inner = 0.7978845608028654 * (v + 0.044715 * (v * v * v))
    bend = jnp.tanh(inner)
    half = 0.5 * (1.0 + bend)
    slope = half + 0.5 * v * (1.0 - bend * bend) * (0.7978845608028654 * (1.0 + 0.134145 * (v * v)))
    return v * half, slope


def expert_kernel(
    members, experts,
    rows_ref, cot_ref, router_ref, group_ref, *refs,
):
    first, second = refs[:members], refs[members : 2 * members]
    reply_ref, share_ref, act_ref, gpre_ref, grad_ref, grouter_ref = refs[2 * members :]
    rows = rows_ref[...]
    count = rows.shape[0]
    lane = lax.broadcasted_iota(jnp.int32, (count, 128), 1)
    logits = jnp.where(lane < experts, nn_dot(rows, router_ref[...]), MASKED)
    raised = jnp.exp(logits - jnp.max(logits, -1, keepdims=True))
    probs = raised / jnp.sum(raised, -1, keepdims=True)
    own = jnp.where(lane == group_ref[0], 1.0, 0.0)
    gate = jnp.sum(probs * own, -1, keepdims=True)
    cot = cot_ref[...].astype(F32)
    grads = (gate * cot).astype(BF16)
    grad_ref[...] = grads
    reply = jnp.zeros(rows.shape, F32)
    share = jnp.zeros(rows.shape, F32)
    for k in range(members):
        act, slope = gelu_pair(nn_dot(rows, first[k][...]))
        act = act.astype(BF16)
        act_ref[k] = act
        reply = reply + nn_dot(act, second[k][...])
        gpre = (nt_dot(grads, second[k][...]) * slope).astype(BF16)
        gpre_ref[k] = gpre
        share = share + nt_dot(gpre, first[k][...])
    reply = reply.astype(BF16)
    reply_ref[...] = reply
    gate_grad = jnp.sum(cot * reply.astype(F32), -1, keepdims=True)
    logit_grad = probs * (own - gate) * gate_grad
    share_ref[...] = (share + nt_dot(logit_grad.astype(BF16), router_ref[...])).astype(BF16)
    grouter_ref[...] = nn_dot(logit_grad.T.astype(BF16), rows)


def expert_step(rows, cot, experts, router, group, first, second):
    members = len(first)
    count, width = rows.shape
    hidden = first[0].shape[1]
    weights = (*first, *second)
    results = (
        jax.ShapeDtypeStruct((count, width), BF16),
        jax.ShapeDtypeStruct((count, width), BF16),
        jax.ShapeDtypeStruct((members, count, hidden), BF16),
        jax.ShapeDtypeStruct((members, count, hidden), BF16),
        jax.ShapeDtypeStruct((count, width), BF16),
        jax.ShapeDtypeStruct((128, width), F32),
    )
    return pl.pallas_call(
        functools.partial(expert_kernel, members, experts),
        grid=(1,),
        out_shape=results,
        in_specs=whole_like(rows, cot, router)
        + [pl.BlockSpec(memory_space=pltpu.SMEM)]
        + whole_like(*weights),
        out_specs=tuple(whole_like(*results)),
        compiler_params=pltpu.CompilerParams(vmem_limit_bytes=60 << 20),
        cost_estimate=SMALL,
    )(rows, cot, router, group, *weights)


def enter_kernel(
    members, experts,
    x_ref, gain_ref, router_ref, route_ref, flat_ref, ids_ref, *refs,
):
    att, proj = refs[:members], refs[members : 2 * members]
    hidden_ref, gate_ref, leave_ref, total_ref = refs[2 * members :]
    step = pl.program_id(0)
    hidden = x_ref[...].astype(F32)
    for k in range(members):
        hidden = hidden + lax.dot_general(
            att[k][...], proj[k][...], (((0,), (0,)), ((), ())), preferred_element_type=F32
        )
    hidden_ref[...] = hidden
    normed = norm_rows(hidden, gain_ref[...]).astype(BF16)
    lane = lax.broadcasted_iota(jnp.int32, (RB, 128), 1)
    logits = jnp.where(lane < experts, nn_dot(normed, router_ref[...]), MASKED)
    raised = jnp.exp(logits - jnp.max(logits, -1, keepdims=True))
    chosen = jnp.sum(jnp.where(lane == route_ref[...], raised, 0.0), -1, keepdims=True)
    gate_ref[...] = chosen / jnp.sum(raised, -1, keepdims=True)
    table = jnp.where(ids_ref[...] == flat_ref[...], 1.0, 0.0).astype(BF16)

    @pl.when(step == 0)
    def _():
        total_ref[...] = jnp.zeros_like(total_ref)

    total_ref[...] += nn_dot(table, normed)

    @pl.when(step == pl.num_programs(0) - 1)
    def _():
        leave_ref[...] = total_ref[...].astype(BF16)


def enter_experts(tokens, experts, gain, router, route, flat_id, ids, att, proj):
    length, width = tokens.shape
    members = len(att)
    inner = att[0].shape[0]
    count = ids.shape[0]
    return pl.pallas_call(
        functools.partial(enter_kernel, members, experts),
        grid=(length // RB,),
        out_shape=(
            jax.ShapeDtypeStruct((length, width), F32),
            jax.ShapeDtypeStruct((length, 1), F32),
            jax.ShapeDtypeStruct((count, width), BF16),
        ),
        in_specs=[
            rows_of(RB, width),
            whole_of(1, width),
            whole_of(width, 128),
            rows_of(RB, 1),
            pl.BlockSpec((1, RB), lambda i: (0, i)),
            whole_of(count, 1),
        ]
        + [pl.BlockSpec((inner, RB), lambda i: (0, i))] * members
        + [whole_of(inner, width)] * members,
        out_specs=(rows_of(RB, width), rows_of(RB, 1), whole_of(count, width)),
        scratch_shapes=[pltpu.VMEM((count, width), F32)],
        compiler_params=pltpu.CompilerParams(vmem_limit_bytes=60 << 20),
        cost_estimate=SMALL,
    )(
        tokens, gain, router, route, flat_id, ids, *att, *proj,
    )


def weight_kernel(half, rows_ref, grads_ref, act_ref, gpre_ref, kept_ref, sent_ref):
    step = pl.program_id(0)

    def product(left, right):
        return lax.dot_general(
            left, right, (((0,), (0,)), ((), ())), preferred_element_type=F32
        ).astype(BF16)

    @pl.when(step < half)
    def _():
        k = 2 * step
        kept_ref[0] = product(act_ref[k], grads_ref[...])
        sent_ref[0] = product(act_ref[k + 1], grads_ref[...])

    @pl.when(step >= half)
    def _():
        k = 2 * (step - half)
        kept_ref[0] = product(rows_ref[...], gpre_ref[k])
        sent_ref[0] = product(rows_ref[...], gpre_ref[k + 1])


def weight_grads(rows, grads, act, gpre):
    members, count, hidden = act.shape
    width = rows.shape[1]
    assert hidden == width
    one = pl.BlockSpec((1, width, width), lambda i: (i, 0, 0))
    return pl.pallas_call(
        functools.partial(weight_kernel, members // 2),
        grid=(members,),
        out_shape=(
            jax.ShapeDtypeStruct((members, width, width), BF16),
            jax.ShapeDtypeStruct((members, width, width), BF16),
        ),
        in_specs=[whole_of(count, width)] * 2 + [whole_of(members, count, hidden)] * 2,
        out_specs=(one, one),
        compiler_params=pltpu.CompilerParams(vmem_limit_bytes=60 << 20),
        cost_estimate=SMALL,
    )(rows, grads, act, gpre)


def leave_kernel(
    members,
    hidden_ref, cot_ref, gain_ref, flat_ref, ids_ref, wproj_ref, att_ref, *refs,
):
    blocks = refs[:members]
    gh_ref, da_ref, ggain_ref, gproj_ref, total_ref = refs[members:]
    step = pl.program_id(0)
    share = blocks[0].shape[0]
    grad = jnp.zeros(hidden_ref.shape, F32)
    for k in range(members):
        hit = flat_ref[...] == ids_ref[:, k * share : (k + 1) * share]
        grad = grad + nn_dot(jnp.where(hit, 1.0, 0.0).astype(BF16), blocks[k][...])
    hidden = hidden_ref[...]
    inverse = lax.rsqrt(jnp.mean(hidden * hidden, -1, keepdims=True) + 1e-06)
    unit = hidden * inverse
    scaled = gain_ref[...] * grad
    back = inverse * (scaled - unit * jnp.mean(unit * scaled, -1, keepdims=True))
    total = cot_ref[...].astype(F32) + back
    gh_ref[...] = total
    low = total.astype(BF16)
    da_ref[...] = nt_dot(low, wproj_ref[...]).astype(BF16)

    @pl.when(step == 0)
    def _():
        ggain_ref[...] = jnp.zeros_like(ggain_ref)
        total_ref[...] = jnp.zeros_like(total_ref)

    ggain_ref[...] += jnp.sum(grad * unit, 0, keepdims=True)
    total_ref[...] += nn_dot(att_ref[...], low)

    @pl.when(step == pl.num_programs(0) - 1)
    def _():
        gproj_ref[...] = total_ref[...].astype(BF16)


def leave_experts(hidden1, cotangent, gain, flat_id, ids, w_proj, attended_t, blocks):
    length, width = hidden1.shape
    inner = attended_t.shape[0]
    members = len(blocks)
    share = blocks[0].shape[0]
    return pl.pallas_call(
        functools.partial(leave_kernel, members),
        grid=(length // RB,),
        out_shape=(
            jax.ShapeDtypeStruct((length, width), F32),
            jax.ShapeDtypeStruct((length, PAD), BF16),
            jax.ShapeDtypeStruct((1, width), F32),
            jax.ShapeDtypeStruct((inner, width), BF16),
        ),
        in_specs=[
            rows_of(RB, width),
            rows_of(RB, width),
            whole_of(1, width),
            rows_of(RB, 1),
            whole_of(1, members * share),
            whole_of(PAD, width),
            pl.BlockSpec((inner, RB), lambda i: (0, i)),
        ]
        + [whole_of(share, width)] * members,
        out_specs=(
            rows_of(RB, width),
            rows_of(RB, PAD),
            whole_of(1, width),
            whole_of(inner, width),
        ),
        scratch_shapes=[pltpu.VMEM((inner, width), F32)],
        compiler_params=pltpu.CompilerParams(vmem_limit_bytes=60 << 20),
        cost_estimate=SMALL,
    )(
        hidden1, cotangent, gain, flat_id, ids, w_proj, attended_t, *blocks,
    )


def output_kernel(members, hidden_ref, gate_ref, flat_ref, ids_ref, *refs):
    blocks, out_ref = refs[:members], refs[members]
    share = blocks[0].shape[0]
    reply = jnp.zeros(hidden_ref.shape, F32)
    for k in range(members):
        hit = flat_ref[...] == ids_ref[:, k * share : (k + 1) * share]
        reply = reply + nn_dot(jnp.where(hit, 1.0, 0.0).astype(BF16), blocks[k][...])
    out_ref[...] = (hidden_ref[...] + gate_ref[...] * reply).astype(BF16)


def output_rows(hidden1, gate, flat_id, ids, blocks):
    length, width = hidden1.shape
    members = len(blocks)
    share = blocks[0].shape[0]
    return pl.pallas_call(
        functools.partial(output_kernel, members),
        grid=(length // RB,),
        out_shape=jax.ShapeDtypeStruct((length, width), BF16),
        in_specs=[rows_of(RB, width), rows_of(RB, 1), rows_of(RB, 1), whole_of(1, members * share)]
        + [whole_of(share, width)] * members,
        out_specs=rows_of(RB, width),
        compiler_params=pltpu.CompilerParams(vmem_limit_bytes=60 << 20),
        cost_estimate=SMALL,
    )(hidden1, gate, flat_id, ids, *blocks)


def input_kernel(halves, kept_ref, other_ref, x_ref, gain_ref, gh_ref, low_ref, out_ref, ggain_ref):
    step = pl.program_id(0)
    part = jnp.where(step // halves == low_ref[0], kept_ref[...].astype(F32), other_ref[...].astype(F32))
    x = x_ref[...].astype(F32)
    inverse = lax.rsqrt(jnp.mean(x * x, -1, keepdims=True) + 1e-06)
    unit = x * inverse
    scaled = gain_ref[...] * part
    out_ref[...] = gh_ref[...] + inverse * (scaled - unit * jnp.mean(unit * scaled, -1, keepdims=True))

    @pl.when(step == 0)
    def _():
        ggain_ref[...] = jnp.zeros_like(ggain_ref)

    ggain_ref[...] += jnp.sum(part * unit, 0, keepdims=True)


def input_grads(kept, other, tokens, gain, grad_hidden1, low_bit):
    length, width = tokens.shape
    halves = kept.shape[0] // QB
    half = pl.BlockSpec((QB, width), lambda i: (i % halves, 0))
    return pl.pallas_call(
        functools.partial(input_kernel, halves),
        grid=(length // QB,),
        out_shape=(
            jax.ShapeDtypeStruct((length, width), F32),
            jax.ShapeDtypeStruct((1, width), F32),
        ),
        in_specs=[
            half,
            half,
            rows_of(QB, width),
            whole_of(1, width),
            rows_of(QB, width),
            pl.BlockSpec(memory_space=pltpu.SMEM),
        ],
        out_specs=(rows_of(QB, width), whole_of(1, width)),
        compiler_params=pltpu.CompilerParams(vmem_limit_bytes=60 << 20),
        cost_estimate=SMALL,
    )(kept, other, tokens, gain[None, :], grad_hidden1, low_bit)


def copies_kernel(came_ref, small_ref, ggain_ref, out_ref, mine_ref):
    groups, large = came_ref.shape[:2]

    @pl.when(pl.program_id(0) == 0)
    def _():
        total = came_ref[0].astype(F32)
        for g in range(1, groups):
            total = total + came_ref[g].astype(F32)
        mine_ref[:large, :] = total.astype(BF16)
        row = lax.broadcasted_iota(jnp.int32, small_ref.shape, 0)
        mine_ref[large:, :] = (small_ref[...] + jnp.where(row == 2, ggain_ref[...], 0.0)).astype(BF16)

    out_ref[0] = mine_ref[...]


def sum_copies(came, small, ggain):
    groups, large, width = came.shape
    count = large + small.shape[0]
    return pl.pallas_call(
        copies_kernel,
        grid=(groups,),
        out_shape=jax.ShapeDtypeStruct((groups, count, width), BF16),
        in_specs=whole_like(came, small, ggain),
        out_specs=pl.BlockSpec((1, count, width), lambda i: (i, 0, 0)),
        scratch_shapes=[pltpu.VMEM((count, width), BF16)],
        compiler_params=pltpu.CompilerParams(vmem_limit_bytes=60 << 20),
        cost_estimate=SMALL,
    )(came, small, ggain)


def final_kernel(large, inner, totals_ref, qkv_ref, proj_ref, gffn_ref, rel_ref, gattn_ref, router_ref):
    groups = totals_ref.shape[0]
    split = 3 * inner
    small = totals_ref[0, large:, :].astype(F32)
    for g in range(groups):
        start, stop = g * large, (g + 1) * large
        if start < split:
            count = min(stop, split) - start
            qkv_ref[start : start + count, :] = totals_ref[g, :count, :].astype(F32)
        if stop > split:
            skip = max(start, split) - start
            proj_ref[start + skip - split : stop - split, :] = totals_ref[g, skip:large, :].astype(F32)
        if g:
            small = small + totals_ref[g, large:, :].astype(F32)
    gffn_ref[...] = small[0:1]
    rel_ref[...] = small[1:2]
    gattn_ref[...] = small[2:3]
    router_ref[...] = small[3 : 3 + router_ref.shape[0]]


def final_weights(totals, large, inner, experts):
    groups, count, width = totals.shape
    results = (
        jax.ShapeDtypeStruct((3 * inner, width), F32),
        jax.ShapeDtypeStruct((inner, width), F32),
        jax.ShapeDtypeStruct((1, width), F32),
        jax.ShapeDtypeStruct((1, width), F32),
        jax.ShapeDtypeStruct((1, width), F32),
        jax.ShapeDtypeStruct((experts, width), F32),
    )
    return pl.pallas_call(
        functools.partial(final_kernel, large, inner),
        grid=(1,),
        out_shape=results,
        in_specs=whole_like(totals),
        out_specs=tuple(whole_like(*results)),
        compiler_params=pltpu.CompilerParams(vmem_limit_bytes=16 << 20),
        cost_estimate=SMALL,
    )(totals)


def shards(
    tokens,
    gain_attn,
    w_qkv,
    w_proj,
    rel_bias,
    gain_ffn,
    w_router,
    w_in,
    w_out,
    routes,
    segment_ids,
    cotangent,
):
    length, width = tokens.shape
    experts = w_router.shape[1]
    capacity = max(2, 3 * length // (2 * experts))
    inner_here = w_proj.shape[0]
    members = lax.axis_size("tensor")
    groups = lax.axis_size("expert")
    member = lax.axis_index("tensor")
    group = lax.axis_index("expert")
    share = capacity // members
    route = routes[:, 0]

    def swap(value, bit):
        return lax.ppermute(value, "tensor", [(i, i ^ bit) for i in range(members)])

    bits = [1 << i for i in range(members.bit_length() - 1)]

    def gather_far(value):
        blocks = {0: value}
        for bit in reversed(bits[1:]):
            blocks.update({k ^ bit: swap(block, bit) for k, block in blocks.items()})
        return blocks

    def gather_near(blocks):
        blocks = dict(blocks)
        for bit in bits[:1]:
            blocks.update({k ^ bit: swap(block, bit) for k, block in blocks.items()})
        return [blocks[k] for k in range(members)]

    def gather_members(value):
        return gather_near(gather_far(value))

    def gather_groups(value):
        copies = jnp.broadcast_to(value[None], (groups,) + value.shape)
        return exchange(copies)

    def exchange(value):
        return lax.all_to_all(value, "expert", split_axis=0, concat_axis=0, tiled=True)

    tie = lax.optimization_barrier

    expert_ids = jnp.arange(experts, dtype=jnp.int32)
    onehot_low = (route[:, None] == expert_ids[None, :]).astype(BF16)
    onehot = onehot_low.astype(F32)
    positions = jnp.arange(length, dtype=jnp.int32)
    lower_ones = (positions[:, None] >= positions[None, :]).astype(BF16)
    running = nn_dot(lower_ones, onehot_low)
    slot = (jnp.sum(running * onehot, 1) - 1.0).astype(jnp.int32)
    flat_id = route * capacity + slot

    def ids_of(owner):
        slots = owner * share + jnp.arange(share, dtype=jnp.int32)
        return (expert_ids[:, None] * capacity + slots[None, :]).reshape(-1)

    send_table = (ids_of(member)[:, None] == flat_id[None, :]).astype(BF16)
    all_ids = jnp.concatenate([ids_of(member ^ k) for k in range(members)])

    def dispatch(rows):
        out = nn_dot(send_table, rows).astype(BF16).reshape(groups, -1, width)
        return exchange(out).reshape(-1, width)

    cot_share = dispatch(cotangent)
    w_proj_far = gather_far(w_proj)
    w_in_far = gather_far(w_in[0])
    w_qkv_t = jnp.swapaxes(w_qkv, 1, 2)
    attended_t, lse, proj, keys_t, normed1 = attend(tokens, gain_attn, w_qkv_t, segment_ids, rel_bias)
    attended_t, w_in_far, cot_share = tie((attended_t, w_in_far, cot_share))

    attended_far = gather_far(attended_t)
    gain_row = gain_ffn[None, :]
    router = jnp.pad(w_router, ((0, 0), (0, 128 - experts)))
    w_proj_pad = jnp.pad(w_proj, ((0, PAD - inner_here), (0, 0)))
    flat_row, flat_column = flat_id[None, :], flat_id[:, None]
    send_ids, back_ids = ids_of(member)[:, None], all_ids[None, :]
    (
        attended_far, w_proj_far, w_out_here, gain_row, router, w_proj_pad,
        flat_row, flat_column, send_ids, back_ids,
    ) = tie((
        attended_far, w_proj_far, w_out[0], gain_row, router, w_proj_pad,
        flat_row, flat_column, send_ids, back_ids,
    ))
    attended_blocks = gather_near(attended_far)
    w_proj_blocks = gather_near(w_proj_far)
    w_in_all = gather_near(w_in_far)
    w_out_far = gather_far(w_out_here)
    hidden1, gate, leaving = enter_experts(
        tokens, experts, gain_row, router, routes, flat_row, send_ids, attended_blocks, w_proj_blocks
    )
    rows = exchange(leaving.reshape(groups, -1, width)).reshape(-1, width)
    rows, w_out_far, w_in_all = tie((rows, w_out_far, w_in_all))
    w_out_all = gather_near(w_out_far)

    reply, grad_share, act, grad_pre, grad_rows, grad_router = expert_step(
        rows, cot_share, experts, router, group[None], w_in_all, w_out_all
    )
    grad_back = exchange(grad_share.reshape(groups, -1, width)).reshape(-1, width)
    grad_router = grad_router[:experts]
    for bit in bits:
        grad_router = grad_router + swap(grad_router, bit)
    kept_weights, sent_weights = weight_grads(rows, grad_rows, act, grad_pre)
    grad_back, reply, kept_weights, sent_weights, grad_router = tie(
        (grad_back, reply, kept_weights, sent_weights, grad_router)
    )
    near_weights = swap(sent_weights, 1)
    grad_far = gather_far(grad_back)
    cut = width // 3

    def pair(k, rows_cut):
        return kept_weights[k, rows_cut].astype(F32) + near_weights[k, rows_cut].astype(F32)

    out_sent = pair(1, slice(0, width)).astype(BF16)
    fore_sent, rest_sent = pair(3, slice(0, cut)).astype(BF16), pair(3, slice(cut, width)).astype(BF16)
    grad_far, out_sent, fore_sent, rest_sent = tie((grad_far, out_sent, fore_sent, rest_sent))
    out_came, fore_came = swap(out_sent, 2), swap(fore_sent, 2)
    grad_blocks = gather_near(grad_far)
    reply_back = exchange(reply.reshape(groups, -1, width)).reshape(-1, width)
    grad_hidden1, attended_grad, grad_gain_ffn, grad_proj = leave_experts(
        hidden1, cotangent, gain_row, flat_column, back_ids, w_proj_pad, attended_t, grad_blocks
    )

    low_bit = (member & 1)[None]
    grads, kept, sent, rel_parts = attend_back(
        proj, keys_t, lse, attended_grad, normed1, w_qkv_t, grad_proj, rel_bias, low_bit, segment_ids
    )
    grads, kept, sent, reply_back, out_came, fore_came, rest_sent = tie(
        (grads, kept, sent, reply_back, out_came, fore_came, rest_sent)
    )
    kept = kept + swap(sent, 1).astype(F32)
    far = swap(kept.astype(BF16), 2)
    came = exchange(grads.reshape(groups, -1, width))
    grad_w_out = pair(0, slice(0, width)) + out_came.astype(F32)
    far, grad_w_out, reply_back = tie((far, grad_w_out, reply_back))
    reply_far = gather_far(reply_back)
    reply_far, rest_sent = tie((reply_far, rest_sent))
    rest_came = swap(rest_sent, 2)
    kept = (kept + far.astype(F32)).astype(BF16)
    other = swap(kept, 1)
    grad_input, gain_part = input_grads(kept, other, tokens, gain_attn, grad_hidden1, low_bit)
    grad_w_in = pair(2, slice(0, width)) + jnp.concatenate([fore_came, rest_came], 0).astype(F32)

    rel_row = jnp.sum(rel_parts, -1).reshape(1, -1)
    rel_row = jnp.pad(rel_row, ((0, 0), (0, width - rel_row.shape[1])))
    small = jnp.concatenate([grad_gain_ffn, rel_row, jnp.zeros((1, width), F32), grad_router], 0)
    small = jnp.pad(small, ((0, -small.shape[0] % 16), (0, 0)))
    large = came.shape[1]
    if large % 16 == 0:
        copies = sum_copies(came, small, gain_part)
    else:
        small = small.at[2].add(gain_part[0])
        copies = jnp.concatenate([jnp.sum(came.astype(F32), 0), small], 0).astype(BF16)
        copies = jnp.broadcast_to(copies[None], (groups,) + copies.shape)
    totals = exchange(copies)
    output = output_rows(hidden1, gate, flat_column, back_ids, gather_near(reply_far))
    if large % 16 == 0:
        grad_qkv_t, grad_proj, grad_gain_ffn, rel_row, grad_gain_attn, grad_router = final_weights(
            totals, large, inner_here, experts
        )
    else:
        shared = totals[:, :large].reshape(-1, width).astype(F32)
        grad_qkv_t, grad_proj = shared[: 3 * inner_here], shared[3 * inner_here :]
        small = jnp.sum(totals[:, large:].astype(F32), 0)
        grad_gain_ffn, rel_row, grad_gain_attn = small[0], small[1], small[2]
        grad_router = small[3 : 3 + experts]
    grad_qkv = jnp.swapaxes(grad_qkv_t.reshape(3, inner_here, width), 1, 2)
    grad_gain_ffn, grad_gain_attn = grad_gain_ffn.reshape(-1), grad_gain_attn.reshape(-1)
    grad_rel = rel_row.reshape(-1)[: rel_bias.size].reshape(rel_bias.shape)
    grad_router = grad_router.T
    return (
        output,
        grad_input,
        grad_gain_attn,
        grad_qkv,
        grad_proj,
        grad_rel,
        grad_gain_ffn,
        grad_router,
        grad_w_in[None],
        grad_w_out[None],
    )


def solution(mesh):
    placed = (
        P("expert", None),
        P(),
        P(None, None, "tensor"),
        P("tensor", None),
        P("tensor", None),
        P(),
        P(),
        P("expert", None, "tensor"),
        P("expert", "tensor", None),
        P("expert", None),
        P("expert", None),
        P("expert", None),
    )
    return jax.shard_map(
        shards,
        mesh=mesh,
        in_specs=placed,
        out_specs=(
            P("expert", None),
            P("expert", None),
            P(),
            P(None, None, "tensor"),
            P("tensor", None),
            P("tensor", None),
            P(),
            P(),
            P("expert", None, "tensor"),
            P("expert", "tensor", None),
        ),
        check_vma=False,
    )
```

```python
import functools

import jax
import jax.numpy as jnp
from jax import lax
from jax.experimental import pallas as pl
from jax.experimental.pallas import tpu as pltpu
from jax.sharding import PartitionSpec as P

FAR_LIMITS = (12, 16, 23, 32, 46, 64, 91)
HIGH = lax.Precision.HIGHEST
F32 = jnp.float32
BF16 = jnp.bfloat16
MASKED = -1e30
QB = 256
RB = 512
PAD = 256
FAR = FAR_LIMITS[-1]
SMALL = pl.CostEstimate(flops=1 << 20, bytes_accessed=1 << 16, transcendentals=0)

STEPS = (
    [(1 - limit, 14 - i) for i, limit in enumerate(reversed(FAR_LIMITS))]
    + [(-n, n) for n in range(7, -1, -1)]
    + [(n, 16 + n) for n in range(1, 8)]
    + [(8, 24)]
    + [(limit, 25 + i) for i, limit in enumerate(FAR_LIMITS)]
)


def norm_rows(values, gain):
    return values * lax.rsqrt(jnp.mean(values * values, -1, keepdims=True) + 1e-06) * gain


def nt_dot(left, right):
    return lax.dot_general(left, right, (((1,), (1,)), ((), ())), preferred_element_type=F32)


def nn_dot(left, right):
    return jnp.dot(left, right, preferred_element_type=F32)


def strip_shape(length):
    return 2 * length - QB


def near_rows(length):
    base = length - QB
    first = (base - FAR) // 32 * 32
    last = -(-(base + 127 + FAR) // 32) * 32
    return base, first, last


def build_strip(strip_ref, bias_ref, length, heads):
    total = strip_shape(length)
    base, first, last = near_rows(length)
    for h in range(heads):
        low = jnp.full((8, 128), bias_ref[h, 15], F32)
        high = jnp.full((8, 128), bias_ref[h, 31], F32)
        for half in range(QB // 128):
            cols = slice(half * 128, half * 128 + 128)
            lo_end, hi_start = first + half * 128, last + half * 128
            strip_ref[h, 0:lo_end, cols] = jnp.broadcast_to(low[:1], (lo_end, 128))
            strip_ref[h, hi_start:total, cols] = jnp.broadcast_to(high[:1], (total - hi_start, 128))
    for start in range(first, last, 32):
        offset = (
            lax.broadcasted_iota(jnp.int32, (32, 128), 0)
            - lax.broadcasted_iota(jnp.int32, (32, 128), 1)
            + (start - base)
        )
        tiles = [jnp.full((32, 128), bias_ref[h, 15], F32) for h in range(heads)]
        for begin, bucket in STEPS:
            reached = offset >= begin
            tiles = [jnp.where(reached, bias_ref[h, bucket], tiles[h]) for h in range(heads)]
        for h in range(heads):
            for half in range(QB // 128):
                at = start + half * 128
                strip_ref[h, at : at + 32, half * 128 : half * 128 + 128] = tiles[h]


def head_lanes(rows, h, dim, keep_tail, heads):
    lane = lax.broadcasted_iota(jnp.int32, (rows, PAD), 1)
    inside = (lane >= h * dim) & (lane < (h + 1) * dim)
    if keep_tail:
        inside = inside | (lane >= heads * dim)
    return inside


def shares(seg_ref, b, j):
    return (seg_ref[0, j * QB] <= seg_ref[0, b * QB + QB - 1]) & (
        seg_ref[0, b * QB] <= seg_ref[0, j * QB + QB - 1]
    )


def attend_kernel(
    length, heads, dim,
    x_ref, gain_ref, w_ref, doc_ref, bias_ref, seg_ref,
    att_ref, lse_ref, proj_ref, kt_ref, normed_ref,
    kh_ref, strip_ref, vt_ref, pad_ref, score_ref, top_ref, sum_ref, out_ref,
):
    inner = heads * dim
    build_strip(strip_ref, bias_ref, length, heads)
    lane = lax.broadcasted_iota(jnp.int32, (QB, PAD), 1) - inner
    pad_ref[...] = jnp.zeros_like(pad_ref)
    for t in range(3):
        pad_ref[t * PAD : t * PAD + inner, :] = w_ref[t]

    def project(b, carry):
        at = pl.multiple_of(b * QB, QB)
        here = x_ref[pl.ds(at, QB), :].astype(F32)
        normed = norm_rows(here, gain_ref[...]).astype(BF16)
        normed_ref[pl.ds(at, QB), :] = normed
        every = nt_dot(normed, pad_ref[...])
        same = doc_ref[pl.ds(at, QB), :] == lane
        queries = (every[:, 0:PAD].astype(BF16) * jnp.bfloat16(dim ** (-0.5))).astype(F32)
        queries = queries + jnp.where((lane < 0) | same, 0.0, MASKED)
        keys = every[:, PAD : 2 * PAD]
        values = every[:, 2 * PAD : 3 * PAD]
        proj_ref[pl.ds(at, QB), 0:PAD] = queries.astype(BF16)
        proj_ref[pl.ds(at, QB), PAD : 2 * PAD] = (keys + jnp.where(same, 1.0, 0.0)).astype(BF16)
        proj_ref[pl.ds(at, QB), 2 * PAD : 3 * PAD] = values.astype(BF16)
        kt_ref[:, pl.ds(at, QB)] = keys.T[:inner].astype(BF16)
        vt_ref[:, pl.ds(at, QB)] = values.T[:inner].astype(BF16)
        return carry

    lax.fori_loop(0, length // QB, project, 0)
    keys = proj_ref[:, PAD : 2 * PAD]
    for h in range(heads):
        kh_ref[h] = jnp.where(head_lanes(length, h, dim, True, heads), keys, jnp.zeros_like(keys))

    def block(b, carry):
        at = pl.multiple_of(b * QB, QB)
        queries = proj_ref[pl.ds(at, QB), 0:PAD]
        top_ref[...] = jnp.full_like(top_ref, -3e38)
        sum_ref[...] = jnp.zeros_like(sum_ref)
        out_ref[...] = jnp.zeros_like(out_ref)

        def score(j, carry):
            @pl.when(shares(seg_ref, b, j))
            def _():
                rows = pl.ds(pl.multiple_of(j * QB, QB), QB)
                bias = pl.ds(pl.multiple_of(length - QB + (j - b) * QB, QB), QB)
                for h in range(heads):
                    scores = nt_dot(kh_ref[h, rows, :], queries) + strip_ref[h, bias, :]
                    score_ref[h, rows, :] = scores
                    top = jnp.max(scores, 0, keepdims=True)
                    top_ref[h : h + 1, :] = jnp.maximum(top_ref[h : h + 1, :], top)

            return carry

        def spread(j, carry):
            @pl.when(shares(seg_ref, b, j))
            def _():
                rows = pl.ds(pl.multiple_of(j * QB, QB), QB)
                for h in range(heads):
                    probs = jnp.exp(score_ref[h, rows, :] - top_ref[h : h + 1, :])
                    sum_ref[h : h + 1, :] += jnp.sum(probs, 0, keepdims=True)
                    mine = slice(h * dim, (h + 1) * dim)
                    out_ref[mine, :] += nn_dot(vt_ref[mine, rows], probs.astype(BF16))

            return carry

        lax.fori_loop(0, length // QB, score, 0)
        lax.fori_loop(0, length // QB, spread, 0)
        for h in range(heads):
            mine = slice(h * dim, (h + 1) * dim)
            total = sum_ref[h : h + 1, :]
            att_ref[mine, pl.ds(at, QB)] = (out_ref[mine, :] / total).astype(BF16)
            lse_ref[h : h + 1, pl.ds(at, QB)] = top_ref[h : h + 1, :] + jnp.log(total)
        return carry

    lax.fori_loop(0, length // QB, block, 0)


def attend_back_kernel(
    length, heads, dim,
    proj_ref, kt_ref, lse_ref, da_ref, normed_ref, w_ref, gproj_ref, bias_ref, low_ref, seg_ref,
    grad_ref, kept_ref, sent_ref, drel_ref,
    kh_ref, vh_ref, strip_ref, dstrip_ref, pcat_ref, dcat_ref, dacat_ref, qcat_ref, dk_ref, dv_ref, dqt_ref,
    dq_ref, pad_ref, probs_ref, weighted_ref, delta_ref,
):
    inner = heads * dim
    scale = dim ** (-0.5)
    total = strip_shape(length)
    base, first, last = near_rows(length)
    build_strip(strip_ref, bias_ref, length, heads)
    dstrip_ref[...] = jnp.zeros_like(dstrip_ref)
    dk_ref[...] = jnp.zeros_like(dk_ref)
    dv_ref[...] = jnp.zeros_like(dv_ref)
    dqt_ref[...] = jnp.zeros_like(dqt_ref)
    keys = proj_ref[:, PAD : 2 * PAD]
    values = proj_ref[:, 2 * PAD : 3 * PAD]
    for h in range(heads):
        kh_ref[h] = jnp.where(head_lanes(length, h, dim, True, heads), keys, jnp.zeros_like(keys))
        vh_ref[h] = jnp.where(head_lanes(length, h, dim, False, heads), values, jnp.zeros_like(values))

    def block(b, carry):
        at = pl.multiple_of(b * QB, QB)
        queries = proj_ref[pl.ds(at, QB), 0:PAD]
        grads = da_ref[pl.ds(at, QB), :]
        delta_ref[...] = jnp.zeros_like(delta_ref)
        dqt_ref[...] = jnp.zeros_like(dqt_ref)
        for h in range(heads):
            mine = head_lanes(QB, h, dim, False, heads)
            cols = slice(h * QB, (h + 1) * QB)
            qcat_ref[cols, :] = jnp.where(mine, queries, jnp.zeros_like(queries))
            dacat_ref[cols, :] = jnp.where(mine, grads, jnp.zeros_like(grads))

        def weigh(j, carry):
            @pl.when(shares(seg_ref, b, j))
            def _():
                rows = pl.ds(pl.multiple_of(j * QB, QB), QB)
                bias = pl.ds(pl.multiple_of(length - QB + (j - b) * QB, QB), QB)
                for h in range(heads):
                    scores = nt_dot(kh_ref[h, rows, :], queries) + strip_ref[h, bias, :]
                    probs = jnp.exp(scores - lse_ref[h : h + 1, pl.ds(at, QB)])
                    weighted = probs * nt_dot(vh_ref[h, rows, :], grads)
                    delta_ref[h : h + 1, :] += jnp.sum(weighted, 0, keepdims=True)
                    probs_ref[h, rows, :] = probs
                    weighted_ref[h, rows, :] = weighted

            return carry

        def gather(j, carry):
            @pl.when(shares(seg_ref, b, j))
            def _():
                rows = pl.ds(pl.multiple_of(j * QB, QB), QB)
                bias = pl.ds(pl.multiple_of(length - QB + (j - b) * QB, QB), QB)
                for h in range(heads):
                    cols = slice(h * QB, (h + 1) * QB)
                    mine = slice(h * dim, (h + 1) * dim)
                    probs = probs_ref[h, rows, :]
                    dscore = weighted_ref[h, rows, :] - probs * delta_ref[h : h + 1, :]
                    dstrip_ref[h, bias, :] += dscore
                    dlow = dscore.astype(BF16)
                    pcat_ref[:, cols] = probs.astype(BF16)
                    dcat_ref[:, cols] = dlow
                    dqt_ref[mine, :] += nn_dot(kt_ref[mine, rows], dlow)
                dk_ref[rows, :] += nn_dot(dcat_ref[...], qcat_ref[...])
                dv_ref[rows, :] += nn_dot(pcat_ref[...], dacat_ref[...])

            return carry

        lax.fori_loop(0, length // QB, weigh, 0)
        lax.fori_loop(0, length // QB, gather, 0)
        dq_ref[pl.ds(at, QB), :] = dqt_ref[...].T * scale
        return carry

    lax.fori_loop(0, length // QB, block, 0)

    for t, ref in enumerate((dq_ref, dk_ref, dv_ref)):
        turned = ref[...].T[:inner].astype(BF16)
        grad_ref[t * inner : (t + 1) * inner, :] = nn_dot(turned, normed_ref[...]).astype(BF16)

    grad_ref[3 * inner :, :] = gproj_ref[...]

    pad_ref[...] = jnp.zeros_like(pad_ref)
    for t in range(3):
        pad_ref[t, 0:inner, :] = w_ref[t]
    half = length // 2

    def part(start):
        total = jnp.zeros((QB, w_ref.shape[2]), F32)
        for t, ref in enumerate((dq_ref, dk_ref, dv_ref)):
            total = total + nn_dot(ref[pl.ds(start, QB), :].astype(BF16), pad_ref[t])
        return total

    for i in range(half // QB):
        rows = slice(i * QB, (i + 1) * QB)
        kept_ref[rows, :] = part(pl.multiple_of(low_ref[0] * half + i * QB, QB))
        sent_ref[rows, :] = part(pl.multiple_of((1 - low_ref[0]) * half + i * QB, QB)).astype(BF16)

    offset = (
        lax.broadcasted_iota(jnp.int32, (last - first, 128), 0)
        - lax.broadcasted_iota(jnp.int32, (last - first, 128), 1)
        + (first - base)
    )
    begins = [-(1 << 20)] + [begin for begin, bucket in STEPS] + [1 << 20]
    buckets = [15] + [bucket for begin, bucket in STEPS]
    for h in range(heads):
        near = jnp.zeros((last - first, 128), F32)
        low = jnp.zeros((1, 128), F32)
        high = jnp.zeros((1, 128), F32)
        for half in range(QB // 128):
            cols = slice(half * 128, half * 128 + 128)
            lo_end, hi_start = first + half * 128, last + half * 128
            near = near + dstrip_ref[h, lo_end:hi_start, cols]
            low = low + jnp.sum(dstrip_ref[h, 0:lo_end, cols], 0, keepdims=True)
            high = high + jnp.sum(dstrip_ref[h, hi_start:total, cols], 0, keepdims=True)
        drel_ref[h, 16:17, :] = jnp.zeros((1, 128), F32)
        for i, bucket in enumerate(buckets):
            inside = (offset >= begins[i]) & (offset < begins[i + 1])
            row = jnp.sum(jnp.where(inside, near, 0.0), 0, keepdims=True)
            if bucket == 15:
                row = row + low
            if bucket == 31:
                row = row + high
            drel_ref[h, bucket : bucket + 1, :] = row


def rows_of(count, columns):
    return pl.BlockSpec((count, columns), lambda i: (i, 0))


def whole_of(*shape):
    return pl.BlockSpec(shape, lambda i: (0,) * len(shape))


def whole_like(*arrays):
    return [whole_of(*array.shape) for array in arrays]


def attend(tokens, gain, w_qkv, segments, rel_bias):
    length, width = tokens.shape
    heads = rel_bias.shape[0]
    inner = w_qkv.shape[1]
    operands = (tokens, gain[None, :], w_qkv, segments.reshape(-1, 1))
    results = (
        jax.ShapeDtypeStruct((inner, length), BF16),
        jax.ShapeDtypeStruct((8, length), F32),
        jax.ShapeDtypeStruct((length, 3 * PAD), BF16),
        jax.ShapeDtypeStruct((inner, length), BF16),
        jax.ShapeDtypeStruct((length, width), BF16),
    )
    return pl.pallas_call(
        functools.partial(attend_kernel, length, heads, inner // heads),
        grid=(1,),
        out_shape=results,
        in_specs=whole_like(*operands) + [pl.BlockSpec(memory_space=pltpu.SMEM)] * 2,
        out_specs=tuple(whole_like(*results)),
        scratch_shapes=[
            pltpu.VMEM((heads, length, PAD), BF16),
            pltpu.VMEM((heads, strip_shape(length), QB), F32),
            pltpu.VMEM((inner, length), BF16),
            pltpu.VMEM((3 * PAD, width), BF16),
            pltpu.VMEM((heads, length, QB), F32),
            pltpu.VMEM((8, QB), F32),
            pltpu.VMEM((8, QB), F32),
            pltpu.VMEM((inner, QB), F32),
        ],
        compiler_params=pltpu.CompilerParams(vmem_limit_bytes=60 << 20),
        cost_estimate=SMALL,
    )(*operands, rel_bias, segments)


def attend_back(proj, kt, lse, da, normed, w_qkv, grad_proj, rel_bias, low_bit, segments):
    length, width = normed.shape
    heads, buckets = rel_bias.shape
    inner = w_qkv.shape[1]
    operands = (proj, kt, lse, da, normed, w_qkv, grad_proj)
    results = (
        jax.ShapeDtypeStruct((4 * inner, width), BF16),
        jax.ShapeDtypeStruct((length // 2, width), F32),
        jax.ShapeDtypeStruct((length // 2, width), BF16),
        jax.ShapeDtypeStruct((heads, buckets, 128), F32),
    )
    return pl.pallas_call(
        functools.partial(attend_back_kernel, length, heads, inner // heads),
        grid=(1,),
        out_shape=results,
        in_specs=whole_like(*operands) + [pl.BlockSpec(memory_space=pltpu.SMEM)] * 3,
        out_specs=tuple(whole_like(*results)),
        scratch_shapes=[
            pltpu.VMEM((heads, length, PAD), BF16),
            pltpu.VMEM((heads, length, PAD), BF16),
            pltpu.VMEM((heads, strip_shape(length), QB), F32),
            pltpu.VMEM((heads, strip_shape(length), QB), F32),
            pltpu.VMEM((QB, heads * QB), BF16),
            pltpu.VMEM((QB, heads * QB), BF16),
            pltpu.VMEM((heads * QB, PAD), BF16),
            pltpu.VMEM((heads * QB, PAD), BF16),
            pltpu.VMEM((length, PAD), F32),
            pltpu.VMEM((length, PAD), F32),
            pltpu.VMEM((PAD, QB), F32),
            pltpu.VMEM((length, PAD), F32),
            pltpu.VMEM((3, PAD, width), BF16),
            pltpu.VMEM((heads, length, QB), F32),
            pltpu.VMEM((heads, length, QB), F32),
            pltpu.VMEM((8, QB), F32),
        ],
        compiler_params=pltpu.CompilerParams(vmem_limit_bytes=60 << 20),
        cost_estimate=SMALL,
    )(*operands, rel_bias, low_bit, segments)


def gelu_pair(v):
    inner = 0.7978845608028654 * (v + 0.044715 * (v * v * v))
    bend = jnp.tanh(inner)
    half = 0.5 * (1.0 + bend)
    slope = half + 0.5 * v * (1.0 - bend * bend) * (0.7978845608028654 * (1.0 + 0.134145 * (v * v)))
    return v * half, slope


def expert_kernel(
    members, experts,
    rows_ref, cot_ref, router_ref, group_ref, *refs,
):
    first, second = refs[:members], refs[members : 2 * members]
    reply_ref, share_ref, act_ref, gpre_ref, grad_ref, grouter_ref = refs[2 * members :]
    rows = rows_ref[...]
    count = rows.shape[0]
    lane = lax.broadcasted_iota(jnp.int32, (count, 128), 1)
    logits = jnp.where(lane < experts, nn_dot(rows, router_ref[...]), MASKED)
    raised = jnp.exp(logits - jnp.max(logits, -1, keepdims=True))
    probs = raised / jnp.sum(raised, -1, keepdims=True)
    own = jnp.where(lane == group_ref[0], 1.0, 0.0)
    gate = jnp.sum(probs * own, -1, keepdims=True)
    cot = cot_ref[...].astype(F32)
    grads = (gate * cot).astype(BF16)
    grad_ref[...] = grads
    reply = jnp.zeros(rows.shape, F32)
    share = jnp.zeros(rows.shape, F32)
    for k in range(members):
        act, slope = gelu_pair(nn_dot(rows, first[k][...]))
        act = act.astype(BF16)
        act_ref[k] = act
        reply = reply + nn_dot(act, second[k][...])
        gpre = (nt_dot(grads, second[k][...]) * slope).astype(BF16)
        gpre_ref[k] = gpre
        share = share + nt_dot(gpre, first[k][...])
    reply = reply.astype(BF16)
    reply_ref[...] = reply
    gate_grad = jnp.sum(cot * reply.astype(F32), -1, keepdims=True)
    logit_grad = probs * (own - gate) * gate_grad
    share_ref[...] = (share + nt_dot(logit_grad.astype(BF16), router_ref[...])).astype(BF16)
    grouter_ref[...] = nn_dot(logit_grad.T.astype(BF16), rows)


def expert_step(rows, cot, experts, router, group, first, second):
    members = len(first)
    count, width = rows.shape
    hidden = first[0].shape[1]
    weights = (*first, *second)
    results = (
        jax.ShapeDtypeStruct((count, width), BF16),
        jax.ShapeDtypeStruct((count, width), BF16),
        jax.ShapeDtypeStruct((members, count, hidden), BF16),
        jax.ShapeDtypeStruct((members, count, hidden), BF16),
        jax.ShapeDtypeStruct((count, width), BF16),
        jax.ShapeDtypeStruct((128, width), F32),
    )
    return pl.pallas_call(
        functools.partial(expert_kernel, members, experts),
        grid=(1,),
        out_shape=results,
        in_specs=whole_like(rows, cot, router)
        + [pl.BlockSpec(memory_space=pltpu.SMEM)]
        + whole_like(*weights),
        out_specs=tuple(whole_like(*results)),
        compiler_params=pltpu.CompilerParams(vmem_limit_bytes=60 << 20),
        cost_estimate=SMALL,
    )(rows, cot, router, group, *weights)


def enter_kernel(
    members, experts,
    x_ref, gain_ref, router_ref, route_ref, flat_ref, ids_ref, *refs,
):
    att, proj = refs[:members], refs[members : 2 * members]
    hidden_ref, gate_ref, leave_ref, total_ref = refs[2 * members :]
    step = pl.program_id(0)
    hidden = x_ref[...].astype(F32)
    for k in range(members):
        hidden = hidden + lax.dot_general(
            att[k][...], proj[k][...], (((0,), (0,)), ((), ())), preferred_element_type=F32
        )
    hidden_ref[...] = hidden
    normed = norm_rows(hidden, gain_ref[...]).astype(BF16)
    lane = lax.broadcasted_iota(jnp.int32, (RB, 128), 1)
    logits = jnp.where(lane < experts, nn_dot(normed, router_ref[...]), MASKED)
    raised = jnp.exp(logits - jnp.max(logits, -1, keepdims=True))
    chosen = jnp.sum(jnp.where(lane == route_ref[...], raised, 0.0), -1, keepdims=True)
    gate_ref[...] = chosen / jnp.sum(raised, -1, keepdims=True)
    table = jnp.where(ids_ref[...] == flat_ref[...], 1.0, 0.0).astype(BF16)

    @pl.when(step == 0)
    def _():
        total_ref[...] = jnp.zeros_like(total_ref)

    total_ref[...] += nn_dot(table, normed)

    @pl.when(step == pl.num_programs(0) - 1)
    def _():
        leave_ref[...] = total_ref[...].astype(BF16)


def enter_experts(tokens, experts, gain, router, route, flat_id, ids, att, proj):
    length, width = tokens.shape
    members = len(att)
    inner = att[0].shape[0]
    count = ids.shape[0]
    return pl.pallas_call(
        functools.partial(enter_kernel, members, experts),
        grid=(length // RB,),
        out_shape=(
            jax.ShapeDtypeStruct((length, width), F32),
            jax.ShapeDtypeStruct((length, 1), F32),
            jax.ShapeDtypeStruct((count, width), BF16),
        ),
        in_specs=[
            rows_of(RB, width),
            whole_of(1, width),
            whole_of(width, 128),
            rows_of(RB, 1),
            pl.BlockSpec((1, RB), lambda i: (0, i)),
            whole_of(count, 1),
        ]
        + [pl.BlockSpec((inner, RB), lambda i: (0, i))] * members
        + [whole_of(inner, width)] * members,
        out_specs=(rows_of(RB, width), rows_of(RB, 1), whole_of(count, width)),
        scratch_shapes=[pltpu.VMEM((count, width), F32)],
        compiler_params=pltpu.CompilerParams(vmem_limit_bytes=60 << 20),
        cost_estimate=SMALL,
    )(
        tokens, gain, router, route, flat_id, ids, *att, *proj,
    )


def weight_kernel(half, rows_ref, grads_ref, act_ref, gpre_ref, kept_ref, sent_ref):
    step = pl.program_id(0)

    def product(left, right):
        return lax.dot_general(
            left, right, (((0,), (0,)), ((), ())), preferred_element_type=F32
        ).astype(BF16)

    @pl.when(step < half)
    def _():
        k = 2 * step
        kept_ref[0] = product(act_ref[k], grads_ref[...])
        sent_ref[0] = product(act_ref[k + 1], grads_ref[...])

    @pl.when(step >= half)
    def _():
        k = 2 * (step - half)
        kept_ref[0] = product(rows_ref[...], gpre_ref[k])
        sent_ref[0] = product(rows_ref[...], gpre_ref[k + 1])


def weight_grads(rows, grads, act, gpre):
    members, count, hidden = act.shape
    width = rows.shape[1]
    assert hidden == width
    one = pl.BlockSpec((1, width, width), lambda i: (i, 0, 0))
    return pl.pallas_call(
        functools.partial(weight_kernel, members // 2),
        grid=(members,),
        out_shape=(
            jax.ShapeDtypeStruct((members, width, width), BF16),
            jax.ShapeDtypeStruct((members, width, width), BF16),
        ),
        in_specs=[whole_of(count, width)] * 2 + [whole_of(members, count, hidden)] * 2,
        out_specs=(one, one),
        compiler_params=pltpu.CompilerParams(vmem_limit_bytes=60 << 20),
        cost_estimate=SMALL,
    )(rows, grads, act, gpre)


def leave_kernel(
    members,
    hidden_ref, cot_ref, gain_ref, flat_ref, ids_ref, wproj_ref, att_ref, *refs,
):
    blocks = refs[:members]
    gh_ref, da_ref, ggain_ref, gproj_ref, total_ref = refs[members:]
    step = pl.program_id(0)
    share = blocks[0].shape[0]
    grad = jnp.zeros(hidden_ref.shape, F32)
    for k in range(members):
        hit = flat_ref[...] == ids_ref[:, k * share : (k + 1) * share]
        grad = grad + nn_dot(jnp.where(hit, 1.0, 0.0).astype(BF16), blocks[k][...])
    hidden = hidden_ref[...]
    inverse = lax.rsqrt(jnp.mean(hidden * hidden, -1, keepdims=True) + 1e-06)
    unit = hidden * inverse
    scaled = gain_ref[...] * grad
    back = inverse * (scaled - unit * jnp.mean(unit * scaled, -1, keepdims=True))
    total = cot_ref[...].astype(F32) + back
    gh_ref[...] = total
    low = total.astype(BF16)
    da_ref[...] = nt_dot(low, wproj_ref[...]).astype(BF16)

    @pl.when(step == 0)
    def _():
        ggain_ref[...] = jnp.zeros_like(ggain_ref)
        total_ref[...] = jnp.zeros_like(total_ref)

    ggain_ref[...] += jnp.sum(grad * unit, 0, keepdims=True)
    total_ref[...] += nn_dot(att_ref[...], low)

    @pl.when(step == pl.num_programs(0) - 1)
    def _():
        gproj_ref[...] = total_ref[...].astype(BF16)


def leave_experts(hidden1, cotangent, gain, flat_id, ids, w_proj, attended_t, blocks):
    length, width = hidden1.shape
    inner = attended_t.shape[0]
    members = len(blocks)
    share = blocks[0].shape[0]
    return pl.pallas_call(
        functools.partial(leave_kernel, members),
        grid=(length // RB,),
        out_shape=(
            jax.ShapeDtypeStruct((length, width), F32),
            jax.ShapeDtypeStruct((length, PAD), BF16),
            jax.ShapeDtypeStruct((1, width), F32),
            jax.ShapeDtypeStruct((inner, width), BF16),
        ),
        in_specs=[
            rows_of(RB, width),
            rows_of(RB, width),
            whole_of(1, width),
            rows_of(RB, 1),
            whole_of(1, members * share),
            whole_of(PAD, width),
            pl.BlockSpec((inner, RB), lambda i: (0, i)),
        ]
        + [whole_of(share, width)] * members,
        out_specs=(
            rows_of(RB, width),
            rows_of(RB, PAD),
            whole_of(1, width),
            whole_of(inner, width),
        ),
        scratch_shapes=[pltpu.VMEM((inner, width), F32)],
        compiler_params=pltpu.CompilerParams(vmem_limit_bytes=60 << 20),
        cost_estimate=SMALL,
    )(
        hidden1, cotangent, gain, flat_id, ids, w_proj, attended_t, *blocks,
    )


def output_kernel(members, hidden_ref, gate_ref, flat_ref, ids_ref, *refs):
    blocks, out_ref = refs[:members], refs[members]
    share = blocks[0].shape[0]
    reply = jnp.zeros(hidden_ref.shape, F32)
    for k in range(members):
        hit = flat_ref[...] == ids_ref[:, k * share : (k + 1) * share]
        reply = reply + nn_dot(jnp.where(hit, 1.0, 0.0).astype(BF16), blocks[k][...])
    out_ref[...] = (hidden_ref[...] + gate_ref[...] * reply).astype(BF16)


def output_rows(hidden1, gate, flat_id, ids, blocks):
    length, width = hidden1.shape
    members = len(blocks)
    share = blocks[0].shape[0]
    return pl.pallas_call(
        functools.partial(output_kernel, members),
        grid=(length // RB,),
        out_shape=jax.ShapeDtypeStruct((length, width), BF16),
        in_specs=[rows_of(RB, width), rows_of(RB, 1), rows_of(RB, 1), whole_of(1, members * share)]
        + [whole_of(share, width)] * members,
        out_specs=rows_of(RB, width),
        compiler_params=pltpu.CompilerParams(vmem_limit_bytes=60 << 20),
        cost_estimate=SMALL,
    )(hidden1, gate, flat_id, ids, *blocks)


def chosen_half(halves, kept_ref, other_ref, low_ref):
    mine = pl.program_id(0) // halves == low_ref[0]
    return jnp.where(mine, kept_ref[...].astype(F32), other_ref[...].astype(F32))


def gain_kernel(halves, kept_ref, other_ref, x_ref, low_ref, ggain_ref):
    part = chosen_half(halves, kept_ref, other_ref, low_ref)
    x = x_ref[...].astype(F32)
    inverse = lax.rsqrt(jnp.mean(x * x, -1, keepdims=True) + 1e-06)

    @pl.when(pl.program_id(0) == 0)
    def _():
        ggain_ref[...] = jnp.zeros_like(ggain_ref)

    ggain_ref[...] += jnp.sum(part * (x * inverse), 0, keepdims=True)


def input_kernel(halves, kept_ref, other_ref, x_ref, gain_ref, gh_ref, low_ref, out_ref):
    part = chosen_half(halves, kept_ref, other_ref, low_ref)
    x = x_ref[...].astype(F32)
    inverse = lax.rsqrt(jnp.mean(x * x, -1, keepdims=True) + 1e-06)
    unit = x * inverse
    scaled = gain_ref[...] * part
    out_ref[...] = gh_ref[...] + inverse * (scaled - unit * jnp.mean(unit * scaled, -1, keepdims=True))


def gain_grads(kept, other, tokens, low_bit):
    length, width = tokens.shape
    halves = kept.shape[0] // QB
    half = pl.BlockSpec((QB, width), lambda i: (i % halves, 0))
    return pl.pallas_call(
        functools.partial(gain_kernel, halves),
        grid=(length // QB,),
        out_shape=jax.ShapeDtypeStruct((1, width), F32),
        in_specs=[half, half, rows_of(QB, width), pl.BlockSpec(memory_space=pltpu.SMEM)],
        out_specs=whole_of(1, width),
        compiler_params=pltpu.CompilerParams(vmem_limit_bytes=60 << 20),
        cost_estimate=SMALL,
    )(kept, other, tokens, low_bit)


def input_grads(kept, other, tokens, gain, grad_hidden1, low_bit):
    length, width = tokens.shape
    halves = kept.shape[0] // QB
    half = pl.BlockSpec((QB, width), lambda i: (i % halves, 0))
    return pl.pallas_call(
        functools.partial(input_kernel, halves),
        grid=(length // QB,),
        out_shape=jax.ShapeDtypeStruct((length, width), F32),
        in_specs=[
            half,
            half,
            rows_of(QB, width),
            whole_of(1, width),
            rows_of(QB, width),
            pl.BlockSpec(memory_space=pltpu.SMEM),
        ],
        out_specs=rows_of(QB, width),
        compiler_params=pltpu.CompilerParams(vmem_limit_bytes=60 << 20),
        cost_estimate=SMALL,
    )(kept, other, tokens, gain[None, :], grad_hidden1, low_bit)


def copies_kernel(came_ref, small_ref, ggain_ref, out_ref, mine_ref):
    groups, large = came_ref.shape[:2]

    @pl.when(pl.program_id(0) == 0)
    def _():
        total = came_ref[0].astype(F32)
        for g in range(1, groups):
            total = total + came_ref[g].astype(F32)
        mine_ref[:large, :] = total.astype(BF16)
        row = lax.broadcasted_iota(jnp.int32, small_ref.shape, 0)
        mine_ref[large:, :] = (small_ref[...] + jnp.where(row == 2, ggain_ref[...], 0.0)).astype(BF16)

    out_ref[0] = mine_ref[...]


def sum_copies(came, small, ggain):
    groups, large, width = came.shape
    count = large + small.shape[0]
    return pl.pallas_call(
        copies_kernel,
        grid=(groups,),
        out_shape=jax.ShapeDtypeStruct((groups, count, width), BF16),
        in_specs=whole_like(came, small, ggain),
        out_specs=pl.BlockSpec((1, count, width), lambda i: (i, 0, 0)),
        scratch_shapes=[pltpu.VMEM((count, width), BF16)],
        compiler_params=pltpu.CompilerParams(vmem_limit_bytes=60 << 20),
        cost_estimate=SMALL,
    )(came, small, ggain)


def final_kernel(large, inner, totals_ref, qkv_ref, proj_ref, gffn_ref, rel_ref, gattn_ref, router_ref):
    groups = totals_ref.shape[0]
    split = 3 * inner
    small = totals_ref[0, large:, :].astype(F32)
    for g in range(groups):
        start, stop = g * large, (g + 1) * large
        if start < split:
            count = min(stop, split) - start
            qkv_ref[start : start + count, :] = totals_ref[g, :count, :].astype(F32)
        if stop > split:
            skip = max(start, split) - start
            proj_ref[start + skip - split : stop - split, :] = totals_ref[g, skip:large, :].astype(F32)
        if g:
            small = small + totals_ref[g, large:, :].astype(F32)
    gffn_ref[...] = small[0:1]
    rel_ref[...] = small[1:2]
    gattn_ref[...] = small[2:3]
    router_ref[...] = small[3 : 3 + router_ref.shape[0]]


def final_weights(totals, large, inner, experts):
    groups, count, width = totals.shape
    results = (
        jax.ShapeDtypeStruct((3 * inner, width), F32),
        jax.ShapeDtypeStruct((inner, width), F32),
        jax.ShapeDtypeStruct((1, width), F32),
        jax.ShapeDtypeStruct((1, width), F32),
        jax.ShapeDtypeStruct((1, width), F32),
        jax.ShapeDtypeStruct((experts, width), F32),
    )
    return pl.pallas_call(
        functools.partial(final_kernel, large, inner),
        grid=(1,),
        out_shape=results,
        in_specs=whole_like(totals),
        out_specs=tuple(whole_like(*results)),
        compiler_params=pltpu.CompilerParams(vmem_limit_bytes=16 << 20),
        cost_estimate=SMALL,
    )(totals)


def shards(
    tokens,
    gain_attn,
    w_qkv,
    w_proj,
    rel_bias,
    gain_ffn,
    w_router,
    w_in,
    w_out,
    routes,
    segment_ids,
    cotangent,
):
    length, width = tokens.shape
    experts = w_router.shape[1]
    capacity = max(2, 3 * length // (2 * experts))
    inner_here = w_proj.shape[0]
    members = lax.axis_size("tensor")
    groups = lax.axis_size("expert")
    member = lax.axis_index("tensor")
    group = lax.axis_index("expert")
    share = capacity // members
    route = routes[:, 0]

    def swap(value, bit):
        return lax.ppermute(value, "tensor", [(i, i ^ bit) for i in range(members)])

    bits = [1 << i for i in range(members.bit_length() - 1)]

    def gather_far(value):
        blocks = {0: value}
        for bit in reversed(bits[1:]):
            blocks.update({k ^ bit: swap(block, bit) for k, block in blocks.items()})
        return blocks

    def gather_near(blocks):
        blocks = dict(blocks)
        for bit in bits[:1]:
            blocks.update({k ^ bit: swap(block, bit) for k, block in blocks.items()})
        return [blocks[k] for k in range(members)]

    def gather_members(value):
        return gather_near(gather_far(value))

    def gather_groups(value):
        copies = jnp.broadcast_to(value[None], (groups,) + value.shape)
        return exchange(copies)

    def exchange(value):
        return lax.all_to_all(value, "expert", split_axis=0, concat_axis=0, tiled=True)

    tie = lax.optimization_barrier

    expert_ids = jnp.arange(experts, dtype=jnp.int32)
    onehot_low = (route[:, None] == expert_ids[None, :]).astype(BF16)
    onehot = onehot_low.astype(F32)
    positions = jnp.arange(length, dtype=jnp.int32)
    lower_ones = (positions[:, None] >= positions[None, :]).astype(BF16)
    running = nn_dot(lower_ones, onehot_low)
    slot = (jnp.sum(running * onehot, 1) - 1.0).astype(jnp.int32)
    flat_id = route * capacity + slot

    def ids_of(owner):
        slots = owner * share + jnp.arange(share, dtype=jnp.int32)
        return (expert_ids[:, None] * capacity + slots[None, :]).reshape(-1)

    send_table = (ids_of(member)[:, None] == flat_id[None, :]).astype(BF16)
    all_ids = jnp.concatenate([ids_of(member ^ k) for k in range(members)])

    def dispatch(rows):
        out = nn_dot(send_table, rows).astype(BF16).reshape(groups, -1, width)
        return exchange(out).reshape(-1, width)

    cot_share = dispatch(cotangent)
    w_proj_far = gather_far(w_proj)
    w_in_far = gather_far(w_in[0])
    w_qkv_t = jnp.swapaxes(w_qkv, 1, 2)
    attended_t, lse, proj, keys_t, normed1 = attend(tokens, gain_attn, w_qkv_t, segment_ids, rel_bias)
    attended_t, w_in_far, cot_share = tie((attended_t, w_in_far, cot_share))

    attended_far = gather_far(attended_t)
    gain_row = gain_ffn[None, :]
    router = jnp.pad(w_router, ((0, 0), (0, 128 - experts)))
    w_proj_pad = jnp.pad(w_proj, ((0, PAD - inner_here), (0, 0)))
    flat_row, flat_column = flat_id[None, :], flat_id[:, None]
    send_ids, back_ids = ids_of(member)[:, None], all_ids[None, :]
    (
        attended_far, w_proj_far, w_out_here, gain_row, router, w_proj_pad,
        flat_row, flat_column, send_ids, back_ids,
    ) = tie((
        attended_far, w_proj_far, w_out[0], gain_row, router, w_proj_pad,
        flat_row, flat_column, send_ids, back_ids,
    ))
    attended_blocks = gather_near(attended_far)
    w_proj_blocks = gather_near(w_proj_far)
    w_in_all = gather_near(w_in_far)
    w_out_far = gather_far(w_out_here)
    hidden1, gate, leaving = enter_experts(
        tokens, experts, gain_row, router, routes, flat_row, send_ids, attended_blocks, w_proj_blocks
    )
    rows = exchange(leaving.reshape(groups, -1, width)).reshape(-1, width)
    rows, w_out_far, w_in_all = tie((rows, w_out_far, w_in_all))
    w_out_all = gather_near(w_out_far)

    reply, grad_share, act, grad_pre, grad_rows, grad_router = expert_step(
        rows, cot_share, experts, router, group[None], w_in_all, w_out_all
    )
    grad_back = exchange(grad_share.reshape(groups, -1, width)).reshape(-1, width)
    grad_router = grad_router[:experts]
    for bit in bits:
        grad_router = grad_router + swap(grad_router, bit)
    kept_weights, sent_weights = weight_grads(rows, grad_rows, act, grad_pre)
    grad_back, reply, kept_weights, sent_weights, grad_router = tie(
        (grad_back, reply, kept_weights, sent_weights, grad_router)
    )
    near_weights = swap(sent_weights, 1)
    grad_far = gather_far(grad_back)
    third = width // 3

    def pair(k, rows_cut):
        return kept_weights[k, rows_cut].astype(F32) + near_weights[k, rows_cut].astype(F32)

    out_sent = pair(1, slice(0, width)).astype(BF16)
    in_sent = [pair(3, slice(i * third, (i + 1) * third)).astype(BF16) for i in range(3)]
    grad_far, out_sent, in_sent = tie((grad_far, out_sent, in_sent))
    out_came, fore_came = swap(out_sent, 2), swap(in_sent[0], 2)
    grad_blocks = gather_near(grad_far)
    reply_back = exchange(reply.reshape(groups, -1, width)).reshape(-1, width)
    grad_hidden1, attended_grad, grad_gain_ffn, grad_proj = leave_experts(
        hidden1, cotangent, gain_row, flat_column, back_ids, w_proj_pad, attended_t, grad_blocks
    )

    low_bit = (member & 1)[None]
    grads, kept, sent, rel_parts = attend_back(
        proj, keys_t, lse, attended_grad, normed1, w_qkv_t, grad_proj, rel_bias, low_bit, segment_ids
    )
    grads, kept, sent, reply_back, out_came, fore_came, in_sent = tie(
        (grads, kept, sent, reply_back, out_came, fore_came, in_sent)
    )
    kept = kept + swap(sent, 1).astype(F32)
    far = swap(kept.astype(BF16), 2)
    came = exchange(grads.reshape(groups, -1, width))
    grad_w_out = pair(0, slice(0, width)) + out_came.astype(F32)
    rel_row = jnp.sum(rel_parts, -1).reshape(1, -1)
    rel_row = jnp.pad(rel_row, ((0, 0), (0, width - rel_row.shape[1])))
    small = jnp.concatenate([grad_gain_ffn, rel_row, jnp.zeros((1, width), F32), grad_router], 0)
    small = jnp.pad(small, ((0, -small.shape[0] % 16), (0, 0)))
    far, grad_w_out, reply_back, in_sent, small = tie((far, grad_w_out, reply_back, in_sent, small))
    middle_came = swap(in_sent[1], 2)
    kept = (kept + far.astype(F32)).astype(BF16)
    other = swap(kept, 1)
    gain_part = gain_grads(kept, other, tokens, low_bit)

    large = came.shape[1]
    if large % 16 == 0:
        copies = sum_copies(came, small, gain_part)
    else:
        small = small.at[2].add(gain_part[0])
        copies = jnp.concatenate([jnp.sum(came.astype(F32), 0), small], 0).astype(BF16)
        copies = jnp.broadcast_to(copies[None], (groups,) + copies.shape)
    copies, middle_came, reply_back, kept, other = tie((copies, middle_came, reply_back, kept, other))
    totals = exchange(copies)

    reply_far = gather_far(reply_back)
    reply_far, rest_sent = tie((reply_far, in_sent[2]))
    rest_came = swap(rest_sent, 2)
    grad_input = input_grads(kept, other, tokens, gain_attn, grad_hidden1, low_bit)
    in_came = jnp.concatenate([fore_came, middle_came, rest_came], 0)
    grad_w_in = pair(2, slice(0, width)) + in_came.astype(F32)
    output = output_rows(hidden1, gate, flat_column, back_ids, gather_near(reply_far))
    if large % 16 == 0:
        grad_qkv_t, grad_proj, grad_gain_ffn, rel_row, grad_gain_attn, grad_router = final_weights(
            totals, large, inner_here, experts
        )
    else:
        shared = totals[:, :large].reshape(-1, width).astype(F32)
        grad_qkv_t, grad_proj = shared[: 3 * inner_here], shared[3 * inner_here :]
        small = jnp.sum(totals[:, large:].astype(F32), 0)
        grad_gain_ffn, rel_row, grad_gain_attn = small[0], small[1], small[2]
        grad_router = small[3 : 3 + experts]
    grad_qkv = jnp.swapaxes(grad_qkv_t.reshape(3, inner_here, width), 1, 2)
    grad_gain_ffn, grad_gain_attn = grad_gain_ffn.reshape(-1), grad_gain_attn.reshape(-1)
    grad_rel = rel_row.reshape(-1)[: rel_bias.size].reshape(rel_bias.shape)
    grad_router = grad_router.T
    return (
        output,
        grad_input,
        grad_gain_attn,
        grad_qkv,
        grad_proj,
        grad_rel,
        grad_gain_ffn,
        grad_router,
        grad_w_in[None],
        grad_w_out[None],
    )


def solution(mesh):
    placed = (
        P("expert", None),
        P(),
        P(None, None, "tensor"),
        P("tensor", None),
        P("tensor", None),
        P(),
        P(),
        P("expert", None, "tensor"),
        P("expert", "tensor", None),
        P("expert", None),
        P("expert", None),
        P("expert", None),
    )
    return jax.shard_map(
        shards,
        mesh=mesh,
        in_specs=placed,
        out_specs=(
            P("expert", None),
            P("expert", None),
            P(),
            P(None, None, "tensor"),
            P("tensor", None),
            P("tensor", None),
            P(),
            P(),
            P("expert", None, "tensor"),
            P("expert", "tensor", None),
        ),
        check_vma=False,
    )
```

```python
import functools

import jax
import jax.numpy as jnp
from jax import lax
from jax.experimental import pallas as pl
from jax.experimental.pallas import tpu as pltpu
from jax.sharding import PartitionSpec as P

FAR_LIMITS = (12, 16, 23, 32, 46, 64, 91)
HIGH = lax.Precision.HIGHEST
F32 = jnp.float32
BF16 = jnp.bfloat16
MASKED = -1e30
QB = 256
RB = 512
PAD = 256
FAR = FAR_LIMITS[-1]
SMALL = pl.CostEstimate(flops=1 << 20, bytes_accessed=1 << 16, transcendentals=0)

STEPS = (
    [(1 - limit, 14 - i) for i, limit in enumerate(reversed(FAR_LIMITS))]
    + [(-n, n) for n in range(7, -1, -1)]
    + [(n, 16 + n) for n in range(1, 8)]
    + [(8, 24)]
    + [(limit, 25 + i) for i, limit in enumerate(FAR_LIMITS)]
)


def norm_rows(values, gain):
    return values * lax.rsqrt(jnp.mean(values * values, -1, keepdims=True) + 1e-06) * gain


def nt_dot(left, right):
    return lax.dot_general(left, right, (((1,), (1,)), ((), ())), preferred_element_type=F32)


def nn_dot(left, right):
    return jnp.dot(left, right, preferred_element_type=F32)


def strip_shape(length):
    return 2 * length - QB


def near_rows(length):
    base = length - QB
    first = (base - FAR) // 32 * 32
    last = -(-(base + 127 + FAR) // 32) * 32
    return base, first, last


def build_strip(strip_ref, bias_ref, length, heads):
    total = strip_shape(length)
    base, first, last = near_rows(length)
    for h in range(heads):
        low = jnp.full((8, 128), bias_ref[h, 15], F32)
        high = jnp.full((8, 128), bias_ref[h, 31], F32)
        for half in range(QB // 128):
            cols = slice(half * 128, half * 128 + 128)
            lo_end, hi_start = first + half * 128, last + half * 128
            strip_ref[h, 0:lo_end, cols] = jnp.broadcast_to(low[:1], (lo_end, 128))
            strip_ref[h, hi_start:total, cols] = jnp.broadcast_to(high[:1], (total - hi_start, 128))
    for start in range(first, last, 32):
        offset = (
            lax.broadcasted_iota(jnp.int32, (32, 128), 0)
            - lax.broadcasted_iota(jnp.int32, (32, 128), 1)
            + (start - base)
        )
        tiles = [jnp.full((32, 128), bias_ref[h, 15], F32) for h in range(heads)]
        for begin, bucket in STEPS:
            reached = offset >= begin
            tiles = [jnp.where(reached, bias_ref[h, bucket], tiles[h]) for h in range(heads)]
        for h in range(heads):
            for half in range(QB // 128):
                at = start + half * 128
                strip_ref[h, at : at + 32, half * 128 : half * 128 + 128] = tiles[h]


def head_lanes(rows, h, dim, keep_tail, heads):
    lane = lax.broadcasted_iota(jnp.int32, (rows, PAD), 1)
    inside = (lane >= h * dim) & (lane < (h + 1) * dim)
    if keep_tail:
        inside = inside | (lane >= heads * dim)
    return inside


def shares(seg_ref, b, j):
    return (seg_ref[0, j * QB] <= seg_ref[0, b * QB + QB - 1]) & (
        seg_ref[0, b * QB] <= seg_ref[0, j * QB + QB - 1]
    )


def attend_kernel(
    length, heads, dim,
    x_ref, gain_ref, w_ref, doc_ref, bias_ref, seg_ref,
    att_ref, lse_ref, proj_ref, kt_ref, normed_ref,
    kh_ref, strip_ref, vt_ref, pad_ref, score_ref, top_ref, sum_ref, out_ref,
):
    inner = heads * dim
    build_strip(strip_ref, bias_ref, length, heads)
    lane = lax.broadcasted_iota(jnp.int32, (QB, PAD), 1) - inner
    pad_ref[...] = jnp.zeros_like(pad_ref)
    for t in range(3):
        pad_ref[t * PAD : t * PAD + inner, :] = w_ref[t]

    def project(b, carry):
        at = pl.multiple_of(b * QB, QB)
        here = x_ref[pl.ds(at, QB), :].astype(F32)
        normed = norm_rows(here, gain_ref[...]).astype(BF16)
        normed_ref[pl.ds(at, QB), :] = normed
        every = nt_dot(normed, pad_ref[...])
        same = doc_ref[pl.ds(at, QB), :] == lane
        queries = (every[:, 0:PAD].astype(BF16) * jnp.bfloat16(dim ** (-0.5))).astype(F32)
        queries = queries + jnp.where((lane < 0) | same, 0.0, MASKED)
        keys = every[:, PAD : 2 * PAD]
        values = every[:, 2 * PAD : 3 * PAD]
        proj_ref[pl.ds(at, QB), 0:PAD] = queries.astype(BF16)
        proj_ref[pl.ds(at, QB), PAD : 2 * PAD] = (keys + jnp.where(same, 1.0, 0.0)).astype(BF16)
        proj_ref[pl.ds(at, QB), 2 * PAD : 3 * PAD] = values.astype(BF16)
        kt_ref[:, pl.ds(at, QB)] = keys.T[:inner].astype(BF16)
        vt_ref[:, pl.ds(at, QB)] = values.T[:inner].astype(BF16)
        return carry

    lax.fori_loop(0, length // QB, project, 0)
    keys = proj_ref[:, PAD : 2 * PAD]
    for h in range(heads):
        kh_ref[h] = jnp.where(head_lanes(length, h, dim, True, heads), keys, jnp.zeros_like(keys))

    def block(b, carry):
        at = pl.multiple_of(b * QB, QB)
        queries = proj_ref[pl.ds(at, QB), 0:PAD]
        top_ref[...] = jnp.full_like(top_ref, -3e38)
        sum_ref[...] = jnp.zeros_like(sum_ref)
        out_ref[...] = jnp.zeros_like(out_ref)

        def score(j, carry):
            @pl.when(shares(seg_ref, b, j))
            def _():
                rows = pl.ds(pl.multiple_of(j * QB, QB), QB)
                bias = pl.ds(pl.multiple_of(length - QB + (j - b) * QB, QB), QB)
                for h in range(heads):
                    scores = nt_dot(kh_ref[h, rows, :], queries) + strip_ref[h, bias, :]
                    score_ref[h, rows, :] = scores
                    top = jnp.max(scores, 0, keepdims=True)
                    top_ref[h : h + 1, :] = jnp.maximum(top_ref[h : h + 1, :], top)

            return carry

        def spread(j, carry):
            @pl.when(shares(seg_ref, b, j))
            def _():
                rows = pl.ds(pl.multiple_of(j * QB, QB), QB)
                for h in range(heads):
                    probs = jnp.exp(score_ref[h, rows, :] - top_ref[h : h + 1, :])
                    sum_ref[h : h + 1, :] += jnp.sum(probs, 0, keepdims=True)
                    mine = slice(h * dim, (h + 1) * dim)
                    out_ref[mine, :] += nn_dot(vt_ref[mine, rows], probs.astype(BF16))

            return carry

        lax.fori_loop(0, length // QB, score, 0)
        lax.fori_loop(0, length // QB, spread, 0)
        for h in range(heads):
            mine = slice(h * dim, (h + 1) * dim)
            total = sum_ref[h : h + 1, :]
            att_ref[mine, pl.ds(at, QB)] = (out_ref[mine, :] / total).astype(BF16)
            lse_ref[h : h + 1, pl.ds(at, QB)] = top_ref[h : h + 1, :] + jnp.log(total)
        return carry

    lax.fori_loop(0, length // QB, block, 0)


def attend_back_kernel(
    length, heads, dim,
    proj_ref, kt_ref, lse_ref, da_ref, normed_ref, w_ref, gproj_ref, bias_ref, low_ref, seg_ref,
    grad_ref, kept_ref, sent_ref, drel_ref,
    kh_ref, vh_ref, strip_ref, dstrip_ref, pcat_ref, dcat_ref, dacat_ref, qcat_ref, dk_ref, dv_ref, dqt_ref,
    dq_ref, pad_ref, probs_ref, weighted_ref, delta_ref,
):
    inner = heads * dim
    scale = dim ** (-0.5)
    total = strip_shape(length)
    base, first, last = near_rows(length)
    build_strip(strip_ref, bias_ref, length, heads)
    dstrip_ref[...] = jnp.zeros_like(dstrip_ref)
    dk_ref[...] = jnp.zeros_like(dk_ref)
    dv_ref[...] = jnp.zeros_like(dv_ref)
    dqt_ref[...] = jnp.zeros_like(dqt_ref)
    keys = proj_ref[:, PAD : 2 * PAD]
    values = proj_ref[:, 2 * PAD : 3 * PAD]
    for h in range(heads):
        kh_ref[h] = jnp.where(head_lanes(length, h, dim, True, heads), keys, jnp.zeros_like(keys))
        vh_ref[h] = jnp.where(head_lanes(length, h, dim, False, heads), values, jnp.zeros_like(values))

    def block(b, carry):
        at = pl.multiple_of(b * QB, QB)
        queries = proj_ref[pl.ds(at, QB), 0:PAD]
        grads = da_ref[pl.ds(at, QB), :]
        delta_ref[...] = jnp.zeros_like(delta_ref)
        dqt_ref[...] = jnp.zeros_like(dqt_ref)
        for h in range(heads):
            mine = head_lanes(QB, h, dim, False, heads)
            cols = slice(h * QB, (h + 1) * QB)
            qcat_ref[cols, :] = jnp.where(mine, queries, jnp.zeros_like(queries))
            dacat_ref[cols, :] = jnp.where(mine, grads, jnp.zeros_like(grads))

        def weigh(j, carry):
            @pl.when(shares(seg_ref, b, j))
            def _():
                rows = pl.ds(pl.multiple_of(j * QB, QB), QB)
                bias = pl.ds(pl.multiple_of(length - QB + (j - b) * QB, QB), QB)
                for h in range(heads):
                    scores = nt_dot(kh_ref[h, rows, :], queries) + strip_ref[h, bias, :]
                    probs = jnp.exp(scores - lse_ref[h : h + 1, pl.ds(at, QB)])
                    weighted = probs * nt_dot(vh_ref[h, rows, :], grads)
                    delta_ref[h : h + 1, :] += jnp.sum(weighted, 0, keepdims=True)
                    probs_ref[h, rows, :] = probs
                    weighted_ref[h, rows, :] = weighted

            return carry

        def gather(j, carry):
            @pl.when(shares(seg_ref, b, j))
            def _():
                rows = pl.ds(pl.multiple_of(j * QB, QB), QB)
                bias = pl.ds(pl.multiple_of(length - QB + (j - b) * QB, QB), QB)
                for h in range(heads):
                    cols = slice(h * QB, (h + 1) * QB)
                    mine = slice(h * dim, (h + 1) * dim)
                    probs = probs_ref[h, rows, :]
                    dscore = weighted_ref[h, rows, :] - probs * delta_ref[h : h + 1, :]
                    dstrip_ref[h, bias, :] += dscore
                    dlow = dscore.astype(BF16)
                    pcat_ref[:, cols] = probs.astype(BF16)
                    dcat_ref[:, cols] = dlow
                    dqt_ref[mine, :] += nn_dot(kt_ref[mine, rows], dlow)
                dk_ref[rows, :] += nn_dot(dcat_ref[...], qcat_ref[...])
                dv_ref[rows, :] += nn_dot(pcat_ref[...], dacat_ref[...])

            return carry

        lax.fori_loop(0, length // QB, weigh, 0)
        lax.fori_loop(0, length // QB, gather, 0)
        dq_ref[pl.ds(at, QB), :] = dqt_ref[...].T * scale
        return carry

    lax.fori_loop(0, length // QB, block, 0)

    for t, ref in enumerate((dq_ref, dk_ref, dv_ref)):
        turned = ref[...].T[:inner].astype(BF16)
        grad_ref[t * inner : (t + 1) * inner, :] = nn_dot(turned, normed_ref[...]).astype(BF16)

    grad_ref[3 * inner :, :] = gproj_ref[...]

    pad_ref[...] = jnp.zeros_like(pad_ref)
    for t in range(3):
        pad_ref[t, 0:inner, :] = w_ref[t]
    half = length // 2

    def part(start):
        total = jnp.zeros((QB, w_ref.shape[2]), F32)
        for t, ref in enumerate((dq_ref, dk_ref, dv_ref)):
            total = total + nn_dot(ref[pl.ds(start, QB), :].astype(BF16), pad_ref[t])
        return total

    for i in range(half // QB):
        rows = slice(i * QB, (i + 1) * QB)
        kept_ref[rows, :] = part(pl.multiple_of(low_ref[0] * half + i * QB, QB))
        sent_ref[rows, :] = part(pl.multiple_of((1 - low_ref[0]) * half + i * QB, QB)).astype(BF16)

    offset = (
        lax.broadcasted_iota(jnp.int32, (last - first, 128), 0)
        - lax.broadcasted_iota(jnp.int32, (last - first, 128), 1)
        + (first - base)
    )
    begins = [-(1 << 20)] + [begin for begin, bucket in STEPS] + [1 << 20]
    buckets = [15] + [bucket for begin, bucket in STEPS]
    for h in range(heads):
        near = jnp.zeros((last - first, 128), F32)
        low = jnp.zeros((1, 128), F32)
        high = jnp.zeros((1, 128), F32)
        for half in range(QB // 128):
            cols = slice(half * 128, half * 128 + 128)
            lo_end, hi_start = first + half * 128, last + half * 128
            near = near + dstrip_ref[h, lo_end:hi_start, cols]
            low = low + jnp.sum(dstrip_ref[h, 0:lo_end, cols], 0, keepdims=True)
            high = high + jnp.sum(dstrip_ref[h, hi_start:total, cols], 0, keepdims=True)
        drel_ref[h, 16:17, :] = jnp.zeros((1, 128), F32)
        for i, bucket in enumerate(buckets):
            inside = (offset >= begins[i]) & (offset < begins[i + 1])
            row = jnp.sum(jnp.where(inside, near, 0.0), 0, keepdims=True)
            if bucket == 15:
                row = row + low
            if bucket == 31:
                row = row + high
            drel_ref[h, bucket : bucket + 1, :] = row


def rows_of(count, columns):
    return pl.BlockSpec((count, columns), lambda i: (i, 0))


def whole_of(*shape):
    return pl.BlockSpec(shape, lambda i: (0,) * len(shape))


def whole_like(*arrays):
    return [whole_of(*array.shape) for array in arrays]


def attend(tokens, gain, w_qkv, segments, rel_bias):
    length, width = tokens.shape
    heads = rel_bias.shape[0]
    inner = w_qkv.shape[1]
    operands = (tokens, gain[None, :], w_qkv, segments.reshape(-1, 1))
    results = (
        jax.ShapeDtypeStruct((inner, length), BF16),
        jax.ShapeDtypeStruct((8, length), F32),
        jax.ShapeDtypeStruct((length, 3 * PAD), BF16),
        jax.ShapeDtypeStruct((inner, length), BF16),
        jax.ShapeDtypeStruct((length, width), BF16),
    )
    return pl.pallas_call(
        functools.partial(attend_kernel, length, heads, inner // heads),
        grid=(1,),
        out_shape=results,
        in_specs=whole_like(*operands) + [pl.BlockSpec(memory_space=pltpu.SMEM)] * 2,
        out_specs=tuple(whole_like(*results)),
        scratch_shapes=[
            pltpu.VMEM((heads, length, PAD), BF16),
            pltpu.VMEM((heads, strip_shape(length), QB), F32),
            pltpu.VMEM((inner, length), BF16),
            pltpu.VMEM((3 * PAD, width), BF16),
            pltpu.VMEM((heads, length, QB), F32),
            pltpu.VMEM((8, QB), F32),
            pltpu.VMEM((8, QB), F32),
            pltpu.VMEM((inner, QB), F32),
        ],
        compiler_params=pltpu.CompilerParams(vmem_limit_bytes=60 << 20),
        cost_estimate=SMALL,
    )(*operands, rel_bias, segments)


def attend_back(proj, kt, lse, da, normed, w_qkv, grad_proj, rel_bias, low_bit, segments):
    length, width = normed.shape
    heads, buckets = rel_bias.shape
    inner = w_qkv.shape[1]
    operands = (proj, kt, lse, da, normed, w_qkv, grad_proj)
    results = (
        jax.ShapeDtypeStruct((4 * inner, width), BF16),
        jax.ShapeDtypeStruct((length // 2, width), F32),
        jax.ShapeDtypeStruct((length // 2, width), BF16),
        jax.ShapeDtypeStruct((heads, buckets, 128), F32),
    )
    return pl.pallas_call(
        functools.partial(attend_back_kernel, length, heads, inner // heads),
        grid=(1,),
        out_shape=results,
        in_specs=whole_like(*operands) + [pl.BlockSpec(memory_space=pltpu.SMEM)] * 3,
        out_specs=tuple(whole_like(*results)),
        scratch_shapes=[
            pltpu.VMEM((heads, length, PAD), BF16),
            pltpu.VMEM((heads, length, PAD), BF16),
            pltpu.VMEM((heads, strip_shape(length), QB), F32),
            pltpu.VMEM((heads, strip_shape(length), QB), F32),
            pltpu.VMEM((QB, heads * QB), BF16),
            pltpu.VMEM((QB, heads * QB), BF16),
            pltpu.VMEM((heads * QB, PAD), BF16),
            pltpu.VMEM((heads * QB, PAD), BF16),
            pltpu.VMEM((length, PAD), F32),
            pltpu.VMEM((length, PAD), F32),
            pltpu.VMEM((PAD, QB), F32),
            pltpu.VMEM((length, PAD), F32),
            pltpu.VMEM((3, PAD, width), BF16),
            pltpu.VMEM((heads, length, QB), F32),
            pltpu.VMEM((heads, length, QB), F32),
            pltpu.VMEM((8, QB), F32),
        ],
        compiler_params=pltpu.CompilerParams(vmem_limit_bytes=60 << 20),
        cost_estimate=SMALL,
    )(*operands, rel_bias, low_bit, segments)


def gelu_pair(v):
    inner = 0.7978845608028654 * (v + 0.044715 * (v * v * v))
    bend = jnp.tanh(inner)
    half = 0.5 * (1.0 + bend)
    slope = half + 0.5 * v * (1.0 - bend * bend) * (0.7978845608028654 * (1.0 + 0.134145 * (v * v)))
    return v * half, slope


def expert_kernel(
    members, experts,
    rows_ref, cot_ref, router_ref, group_ref, *refs,
):
    first, second = refs[:members], refs[members : 2 * members]
    reply_ref, share_ref, act_ref, gpre_ref, grad_ref, grouter_ref = refs[2 * members :]
    rows = rows_ref[...]
    count = rows.shape[0]
    lane = lax.broadcasted_iota(jnp.int32, (count, 128), 1)
    logits = jnp.where(lane < experts, nn_dot(rows, router_ref[...]), MASKED)
    raised = jnp.exp(logits - jnp.max(logits, -1, keepdims=True))
    probs = raised / jnp.sum(raised, -1, keepdims=True)
    own = jnp.where(lane == group_ref[0], 1.0, 0.0)
    gate = jnp.sum(probs * own, -1, keepdims=True)
    cot = cot_ref[...].astype(F32)
    grads = (gate * cot).astype(BF16)
    grad_ref[...] = grads
    reply = jnp.zeros(rows.shape, F32)
    share = jnp.zeros(rows.shape, F32)
    for k in range(members):
        act, slope = gelu_pair(nn_dot(rows, first[k][...]))
        act = act.astype(BF16)
        act_ref[k] = act
        reply = reply + nn_dot(act, second[k][...])
        gpre = (nt_dot(grads, second[k][...]) * slope).astype(BF16)
        gpre_ref[k] = gpre
        share = share + nt_dot(gpre, first[k][...])
    reply = reply.astype(BF16)
    reply_ref[...] = reply
    gate_grad = jnp.sum(cot * reply.astype(F32), -1, keepdims=True)
    logit_grad = probs * (own - gate) * gate_grad
    share_ref[...] = (share + nt_dot(logit_grad.astype(BF16), router_ref[...])).astype(BF16)
    grouter_ref[...] = nn_dot(logit_grad.T.astype(BF16), rows)


def expert_step(rows, cot, experts, router, group, first, second):
    members = len(first)
    count, width = rows.shape
    hidden = first[0].shape[1]
    weights = (*first, *second)
    results = (
        jax.ShapeDtypeStruct((count, width), BF16),
        jax.ShapeDtypeStruct((count, width), BF16),
        jax.ShapeDtypeStruct((members, count, hidden), BF16),
        jax.ShapeDtypeStruct((members, count, hidden), BF16),
        jax.ShapeDtypeStruct((count, width), BF16),
        jax.ShapeDtypeStruct((128, width), F32),
    )
    return pl.pallas_call(
        functools.partial(expert_kernel, members, experts),
        grid=(1,),
        out_shape=results,
        in_specs=whole_like(rows, cot, router)
        + [pl.BlockSpec(memory_space=pltpu.SMEM)]
        + whole_like(*weights),
        out_specs=tuple(whole_like(*results)),
        compiler_params=pltpu.CompilerParams(vmem_limit_bytes=60 << 20),
        cost_estimate=SMALL,
    )(rows, cot, router, group, *weights)


def enter_kernel(
    members, experts,
    x_ref, gain_ref, router_ref, route_ref, flat_ref, ids_ref, *refs,
):
    att, proj = refs[:members], refs[members : 2 * members]
    hidden_ref, gate_ref, leave_ref, total_ref = refs[2 * members :]
    step = pl.program_id(0)
    hidden = x_ref[...].astype(F32)
    for k in range(members):
        hidden = hidden + lax.dot_general(
            att[k][...], proj[k][...], (((0,), (0,)), ((), ())), preferred_element_type=F32
        )
    hidden_ref[...] = hidden
    normed = norm_rows(hidden, gain_ref[...]).astype(BF16)
    lane = lax.broadcasted_iota(jnp.int32, (RB, 128), 1)
    logits = jnp.where(lane < experts, nn_dot(normed, router_ref[...]), MASKED)
    raised = jnp.exp(logits - jnp.max(logits, -1, keepdims=True))
    chosen = jnp.sum(jnp.where(lane == route_ref[...], raised, 0.0), -1, keepdims=True)
    gate_ref[...] = chosen / jnp.sum(raised, -1, keepdims=True)
    table = jnp.where(ids_ref[...] == flat_ref[...], 1.0, 0.0).astype(BF16)

    @pl.when(step == 0)
    def _():
        total_ref[...] = jnp.zeros_like(total_ref)

    total_ref[...] += nn_dot(table, normed)

    @pl.when(step == pl.num_programs(0) - 1)
    def _():
        leave_ref[...] = total_ref[...].astype(BF16)


def enter_experts(tokens, experts, gain, router, route, flat_id, ids, att, proj):
    length, width = tokens.shape
    members = len(att)
    inner = att[0].shape[0]
    count = ids.shape[0]
    return pl.pallas_call(
        functools.partial(enter_kernel, members, experts),
        grid=(length // RB,),
        out_shape=(
            jax.ShapeDtypeStruct((length, width), F32),
            jax.ShapeDtypeStruct((length, 1), F32),
            jax.ShapeDtypeStruct((count, width), BF16),
        ),
        in_specs=[
            rows_of(RB, width),
            whole_of(1, width),
            whole_of(width, 128),
            rows_of(RB, 1),
            pl.BlockSpec((1, RB), lambda i: (0, i)),
            whole_of(count, 1),
        ]
        + [pl.BlockSpec((inner, RB), lambda i: (0, i))] * members
        + [whole_of(inner, width)] * members,
        out_specs=(rows_of(RB, width), rows_of(RB, 1), whole_of(count, width)),
        scratch_shapes=[pltpu.VMEM((count, width), F32)],
        compiler_params=pltpu.CompilerParams(vmem_limit_bytes=60 << 20),
        cost_estimate=SMALL,
    )(
        tokens, gain, router, route, flat_id, ids, *att, *proj,
    )


def weight_kernel(half, rows_ref, grads_ref, act_ref, gpre_ref, kept_ref, sent_ref):
    step = pl.program_id(0)

    def product(left, right):
        return lax.dot_general(
            left, right, (((0,), (0,)), ((), ())), preferred_element_type=F32
        ).astype(BF16)

    @pl.when(step < half)
    def _():
        k = 2 * step
        kept_ref[0] = product(act_ref[k], grads_ref[...])
        sent_ref[0] = product(act_ref[k + 1], grads_ref[...])

    @pl.when(step >= half)
    def _():
        k = 2 * (step - half)
        kept_ref[0] = product(rows_ref[...], gpre_ref[k])
        sent_ref[0] = product(rows_ref[...], gpre_ref[k + 1])


def weight_grads(rows, grads, act, gpre):
    members, count, hidden = act.shape
    width = rows.shape[1]
    assert hidden == width
    one = pl.BlockSpec((1, width, width), lambda i: (i, 0, 0))
    return pl.pallas_call(
        functools.partial(weight_kernel, members // 2),
        grid=(members,),
        out_shape=(
            jax.ShapeDtypeStruct((members, width, width), BF16),
            jax.ShapeDtypeStruct((members, width, width), BF16),
        ),
        in_specs=[whole_of(count, width)] * 2 + [whole_of(members, count, hidden)] * 2,
        out_specs=(one, one),
        compiler_params=pltpu.CompilerParams(vmem_limit_bytes=60 << 20),
        cost_estimate=SMALL,
    )(rows, grads, act, gpre)


def leave_kernel(
    members,
    hidden_ref, cot_ref, gain_ref, flat_ref, ids_ref, wproj_ref, att_ref, *refs,
):
    blocks = refs[:members]
    gh_ref, da_ref, ggain_ref, gproj_ref, total_ref = refs[members:]
    step = pl.program_id(0)
    share = blocks[0].shape[0]
    grad = jnp.zeros(hidden_ref.shape, F32)
    for k in range(members):
        hit = flat_ref[...] == ids_ref[:, k * share : (k + 1) * share]
        grad = grad + nn_dot(jnp.where(hit, 1.0, 0.0).astype(BF16), blocks[k][...])
    hidden = hidden_ref[...]
    inverse = lax.rsqrt(jnp.mean(hidden * hidden, -1, keepdims=True) + 1e-06)
    unit = hidden * inverse
    scaled = gain_ref[...] * grad
    back = inverse * (scaled - unit * jnp.mean(unit * scaled, -1, keepdims=True))
    total = cot_ref[...].astype(F32) + back
    gh_ref[...] = total
    low = total.astype(BF16)
    da_ref[...] = nt_dot(low, wproj_ref[...]).astype(BF16)

    @pl.when(step == 0)
    def _():
        ggain_ref[...] = jnp.zeros_like(ggain_ref)
        total_ref[...] = jnp.zeros_like(total_ref)

    ggain_ref[...] += jnp.sum(grad * unit, 0, keepdims=True)
    total_ref[...] += nn_dot(att_ref[...], low)

    @pl.when(step == pl.num_programs(0) - 1)
    def _():
        gproj_ref[...] = total_ref[...].astype(BF16)


def leave_experts(hidden1, cotangent, gain, flat_id, ids, w_proj, attended_t, blocks):
    length, width = hidden1.shape
    inner = attended_t.shape[0]
    members = len(blocks)
    share = blocks[0].shape[0]
    return pl.pallas_call(
        functools.partial(leave_kernel, members),
        grid=(length // RB,),
        out_shape=(
            jax.ShapeDtypeStruct((length, width), F32),
            jax.ShapeDtypeStruct((length, PAD), BF16),
            jax.ShapeDtypeStruct((1, width), F32),
            jax.ShapeDtypeStruct((inner, width), BF16),
        ),
        in_specs=[
            rows_of(RB, width),
            rows_of(RB, width),
            whole_of(1, width),
            rows_of(RB, 1),
            whole_of(1, members * share),
            whole_of(PAD, width),
            pl.BlockSpec((inner, RB), lambda i: (0, i)),
        ]
        + [whole_of(share, width)] * members,
        out_specs=(
            rows_of(RB, width),
            rows_of(RB, PAD),
            whole_of(1, width),
            whole_of(inner, width),
        ),
        scratch_shapes=[pltpu.VMEM((inner, width), F32)],
        compiler_params=pltpu.CompilerParams(vmem_limit_bytes=60 << 20),
        cost_estimate=SMALL,
    )(
        hidden1, cotangent, gain, flat_id, ids, w_proj, attended_t, *blocks,
    )


def output_kernel(members, hidden_ref, gate_ref, flat_ref, ids_ref, *refs):
    blocks, out_ref = refs[:members], refs[members]
    share = blocks[0].shape[0]
    reply = jnp.zeros(hidden_ref.shape, F32)
    for k in range(members):
        hit = flat_ref[...] == ids_ref[:, k * share : (k + 1) * share]
        reply = reply + nn_dot(jnp.where(hit, 1.0, 0.0).astype(BF16), blocks[k][...])
    out_ref[...] = (hidden_ref[...] + gate_ref[...] * reply).astype(BF16)


def output_rows(hidden1, gate, flat_id, ids, blocks):
    length, width = hidden1.shape
    members = len(blocks)
    share = blocks[0].shape[0]
    return pl.pallas_call(
        functools.partial(output_kernel, members),
        grid=(length // RB,),
        out_shape=jax.ShapeDtypeStruct((length, width), BF16),
        in_specs=[rows_of(RB, width), rows_of(RB, 1), rows_of(RB, 1), whole_of(1, members * share)]
        + [whole_of(share, width)] * members,
        out_specs=rows_of(RB, width),
        compiler_params=pltpu.CompilerParams(vmem_limit_bytes=60 << 20),
        cost_estimate=SMALL,
    )(hidden1, gate, flat_id, ids, *blocks)


def chosen_half(halves, kept_ref, other_ref, low_ref):
    mine = pl.program_id(0) // halves == low_ref[0]
    return jnp.where(mine, kept_ref[...].astype(F32), other_ref[...].astype(F32))


def gain_kernel(halves, kept_ref, other_ref, x_ref, low_ref, ggain_ref):
    part = chosen_half(halves, kept_ref, other_ref, low_ref)
    x = x_ref[...].astype(F32)
    inverse = lax.rsqrt(jnp.mean(x * x, -1, keepdims=True) + 1e-06)

    @pl.when(pl.program_id(0) == 0)
    def _():
        ggain_ref[...] = jnp.zeros_like(ggain_ref)

    ggain_ref[...] += jnp.sum(part * (x * inverse), 0, keepdims=True)


def input_kernel(halves, kept_ref, other_ref, x_ref, gain_ref, gh_ref, low_ref, out_ref):
    part = chosen_half(halves, kept_ref, other_ref, low_ref)
    x = x_ref[...].astype(F32)
    inverse = lax.rsqrt(jnp.mean(x * x, -1, keepdims=True) + 1e-06)
    unit = x * inverse
    scaled = gain_ref[...] * part
    out_ref[...] = gh_ref[...] + inverse * (scaled - unit * jnp.mean(unit * scaled, -1, keepdims=True))


def gain_grads(kept, other, tokens, low_bit):
    length, width = tokens.shape
    halves = kept.shape[0] // QB
    half = pl.BlockSpec((QB, width), lambda i: (i % halves, 0))
    return pl.pallas_call(
        functools.partial(gain_kernel, halves),
        grid=(length // QB,),
        out_shape=jax.ShapeDtypeStruct((1, width), F32),
        in_specs=[half, half, rows_of(QB, width), pl.BlockSpec(memory_space=pltpu.SMEM)],
        out_specs=whole_of(1, width),
        compiler_params=pltpu.CompilerParams(vmem_limit_bytes=60 << 20),
        cost_estimate=SMALL,
    )(kept, other, tokens, low_bit)


def input_grads(kept, other, tokens, gain, grad_hidden1, low_bit):
    length, width = tokens.shape
    halves = kept.shape[0] // QB
    half = pl.BlockSpec((QB, width), lambda i: (i % halves, 0))
    return pl.pallas_call(
        functools.partial(input_kernel, halves),
        grid=(length // QB,),
        out_shape=jax.ShapeDtypeStruct((length, width), F32),
        in_specs=[
            half,
            half,
            rows_of(QB, width),
            whole_of(1, width),
            rows_of(QB, width),
            pl.BlockSpec(memory_space=pltpu.SMEM),
        ],
        out_specs=rows_of(QB, width),
        compiler_params=pltpu.CompilerParams(vmem_limit_bytes=60 << 20),
        cost_estimate=SMALL,
    )(kept, other, tokens, gain[None, :], grad_hidden1, low_bit)


def copies_kernel(came_ref, small_ref, ggain_ref, out_ref, mine_ref):
    groups, large = came_ref.shape[:2]

    @pl.when(pl.program_id(0) == 0)
    def _():
        total = came_ref[0].astype(F32)
        for g in range(1, groups):
            total = total + came_ref[g].astype(F32)
        mine_ref[:large, :] = total.astype(BF16)
        row = lax.broadcasted_iota(jnp.int32, small_ref.shape, 0)
        mine_ref[large:, :] = (small_ref[...] + jnp.where(row == 2, ggain_ref[...], 0.0)).astype(BF16)

    out_ref[0] = mine_ref[...]


def sum_copies(came, small, ggain):
    groups, large, width = came.shape
    count = large + small.shape[0]
    return pl.pallas_call(
        copies_kernel,
        grid=(groups,),
        out_shape=jax.ShapeDtypeStruct((groups, count, width), BF16),
        in_specs=whole_like(came, small, ggain),
        out_specs=pl.BlockSpec((1, count, width), lambda i: (i, 0, 0)),
        scratch_shapes=[pltpu.VMEM((count, width), BF16)],
        compiler_params=pltpu.CompilerParams(vmem_limit_bytes=60 << 20),
        cost_estimate=SMALL,
    )(came, small, ggain)


def final_kernel(large, inner, totals_ref, qkv_ref, proj_ref, gffn_ref, rel_ref, gattn_ref, router_ref):
    groups = totals_ref.shape[0]
    split = 3 * inner
    small = totals_ref[0, large:, :].astype(F32)
    for g in range(groups):
        start, stop = g * large, (g + 1) * large
        if start < split:
            count = min(stop, split) - start
            qkv_ref[start : start + count, :] = totals_ref[g, :count, :].astype(F32)
        if stop > split:
            skip = max(start, split) - start
            proj_ref[start + skip - split : stop - split, :] = totals_ref[g, skip:large, :].astype(F32)
        if g:
            small = small + totals_ref[g, large:, :].astype(F32)
    gffn_ref[...] = small[0:1]
    rel_ref[...] = small[1:2]
    gattn_ref[...] = small[2:3]
    router_ref[...] = small[3 : 3 + router_ref.shape[0]]


def final_weights(totals, large, inner, experts):
    groups, count, width = totals.shape
    results = (
        jax.ShapeDtypeStruct((3 * inner, width), F32),
        jax.ShapeDtypeStruct((inner, width), F32),
        jax.ShapeDtypeStruct((1, width), F32),
        jax.ShapeDtypeStruct((1, width), F32),
        jax.ShapeDtypeStruct((1, width), F32),
        jax.ShapeDtypeStruct((experts, width), F32),
    )
    return pl.pallas_call(
        functools.partial(final_kernel, large, inner),
        grid=(1,),
        out_shape=results,
        in_specs=whole_like(totals),
        out_specs=tuple(whole_like(*results)),
        compiler_params=pltpu.CompilerParams(vmem_limit_bytes=16 << 20),
        cost_estimate=SMALL,
    )(totals)


def shards(
    tokens,
    gain_attn,
    w_qkv,
    w_proj,
    rel_bias,
    gain_ffn,
    w_router,
    w_in,
    w_out,
    routes,
    segment_ids,
    cotangent,
):
    length, width = tokens.shape
    experts = w_router.shape[1]
    capacity = max(2, 3 * length // (2 * experts))
    inner_here = w_proj.shape[0]
    members = lax.axis_size("tensor")
    groups = lax.axis_size("expert")
    member = lax.axis_index("tensor")
    group = lax.axis_index("expert")
    share = capacity // members
    route = routes[:, 0]

    def swap(value, bit):
        return lax.ppermute(value, "tensor", [(i, i ^ bit) for i in range(members)])

    bits = [1 << i for i in range(members.bit_length() - 1)]

    def gather_far(value):
        blocks = {0: value}
        for bit in reversed(bits[1:]):
            blocks.update({k ^ bit: swap(block, bit) for k, block in blocks.items()})
        return blocks

    def gather_near(blocks):
        blocks = dict(blocks)
        for bit in bits[:1]:
            blocks.update({k ^ bit: swap(block, bit) for k, block in blocks.items()})
        return [blocks[k] for k in range(members)]

    def gather_members(value):
        return gather_near(gather_far(value))

    def gather_groups(value):
        copies = jnp.broadcast_to(value[None], (groups,) + value.shape)
        return exchange(copies)

    def exchange(value):
        return lax.all_to_all(value, "expert", split_axis=0, concat_axis=0, tiled=True)

    tie = lax.optimization_barrier

    expert_ids = jnp.arange(experts, dtype=jnp.int32)
    onehot_low = (route[:, None] == expert_ids[None, :]).astype(BF16)
    onehot = onehot_low.astype(F32)
    positions = jnp.arange(length, dtype=jnp.int32)
    lower_ones = (positions[:, None] >= positions[None, :]).astype(BF16)
    running = nn_dot(lower_ones, onehot_low)
    slot = (jnp.sum(running * onehot, 1) - 1.0).astype(jnp.int32)
    flat_id = route * capacity + slot

    def ids_of(owner):
        slots = owner * share + jnp.arange(share, dtype=jnp.int32)
        return (expert_ids[:, None] * capacity + slots[None, :]).reshape(-1)

    send_table = (ids_of(member)[:, None] == flat_id[None, :]).astype(BF16)
    all_ids = jnp.concatenate([ids_of(member ^ k) for k in range(members)])

    def dispatch(rows):
        out = nn_dot(send_table, rows).astype(BF16).reshape(groups, -1, width)
        return exchange(out).reshape(-1, width)

    cot_share = dispatch(cotangent)
    w_proj_far = gather_far(w_proj)
    w_in_far = gather_far(w_in[0])
    w_qkv_t = jnp.swapaxes(w_qkv, 1, 2)
    attended_t, lse, proj, keys_t, normed1 = attend(tokens, gain_attn, w_qkv_t, segment_ids, rel_bias)
    attended_t, w_in_far, cot_share = tie((attended_t, w_in_far, cot_share))

    attended_far = gather_far(attended_t)
    gain_row = gain_ffn[None, :]
    router = jnp.pad(w_router, ((0, 0), (0, 128 - experts)))
    w_proj_pad = jnp.pad(w_proj, ((0, PAD - inner_here), (0, 0)))
    flat_row, flat_column = flat_id[None, :], flat_id[:, None]
    send_ids, back_ids = ids_of(member)[:, None], all_ids[None, :]
    (
        attended_far, w_proj_far, w_out_here, gain_row, router, w_proj_pad,
        flat_row, flat_column, send_ids, back_ids,
    ) = tie((
        attended_far, w_proj_far, w_out[0], gain_row, router, w_proj_pad,
        flat_row, flat_column, send_ids, back_ids,
    ))
    attended_blocks = gather_near(attended_far)
    w_proj_blocks = gather_near(w_proj_far)
    w_in_all = gather_near(w_in_far)
    w_out_far = gather_far(w_out_here)
    hidden1, gate, leaving = enter_experts(
        tokens, experts, gain_row, router, routes, flat_row, send_ids, attended_blocks, w_proj_blocks
    )
    rows = exchange(leaving.reshape(groups, -1, width)).reshape(-1, width)
    rows, w_out_far, w_in_all = tie((rows, w_out_far, w_in_all))
    w_out_all = gather_near(w_out_far)

    reply, grad_share, act, grad_pre, grad_rows, grad_router = expert_step(
        rows, cot_share, experts, router, group[None], w_in_all, w_out_all
    )
    grad_back = exchange(grad_share.reshape(groups, -1, width)).reshape(-1, width)
    grad_router = grad_router[:experts]
    for bit in bits:
        grad_router = grad_router + swap(grad_router, bit)
    kept_weights, sent_weights = weight_grads(rows, grad_rows, act, grad_pre)
    grad_back, reply, kept_weights, sent_weights, grad_router = tie(
        (grad_back, reply, kept_weights, sent_weights, grad_router)
    )
    near_weights = swap(sent_weights, 1)
    grad_far = gather_far(grad_back)
    third = width // 3

    def pair(k, rows_cut):
        return kept_weights[k, rows_cut].astype(F32) + near_weights[k, rows_cut].astype(F32)

    out_sent = pair(1, slice(0, width)).astype(BF16)
    in_sent = [pair(3, slice(i * third, (i + 1) * third)).astype(BF16) for i in range(3)]
    grad_far, out_sent, in_sent = tie((grad_far, out_sent, in_sent))
    out_came, fore_came = swap(out_sent, 2), swap(in_sent[0], 2)
    grad_blocks = gather_near(grad_far)
    reply_back = exchange(reply.reshape(groups, -1, width)).reshape(-1, width)
    grad_hidden1, attended_grad, grad_gain_ffn, grad_proj = leave_experts(
        hidden1, cotangent, gain_row, flat_column, back_ids, w_proj_pad, attended_t, grad_blocks
    )

    low_bit = (member & 1)[None]
    grads, kept, sent, rel_parts = attend_back(
        proj, keys_t, lse, attended_grad, normed1, w_qkv_t, grad_proj, rel_bias, low_bit, segment_ids
    )
    grads, kept, sent, reply_back, out_came, fore_came, in_sent = tie(
        (grads, kept, sent, reply_back, out_came, fore_came, in_sent)
    )
    kept = kept + swap(sent, 1).astype(F32)
    far = swap(kept.astype(BF16), 2)
    came = exchange(grads.reshape(groups, -1, width))
    grad_w_out = pair(0, slice(0, width)) + out_came.astype(F32)
    rel_row = jnp.sum(rel_parts, -1).reshape(1, -1)
    rel_row = jnp.pad(rel_row, ((0, 0), (0, width - rel_row.shape[1])))
    small = jnp.concatenate([grad_gain_ffn, rel_row, jnp.zeros((1, width), F32), grad_router], 0)
    small = jnp.pad(small, ((0, -small.shape[0] % 16), (0, 0)))
    far, grad_w_out, reply_back, in_sent, small = tie((far, grad_w_out, reply_back, in_sent, small))
    middle_came = swap(in_sent[1], 2)
    kept = (kept + far.astype(F32)).astype(BF16)
    other = swap(kept, 1)
    gain_part = gain_grads(kept, other, tokens, low_bit)

    large = came.shape[1]
    if large % 16 == 0:
        copies = sum_copies(came, small, gain_part)
    else:
        small = small.at[2].add(gain_part[0])
        copies = jnp.concatenate([jnp.sum(came.astype(F32), 0), small], 0).astype(BF16)
        copies = jnp.broadcast_to(copies[None], (groups,) + copies.shape)
    copies, middle_came, reply_back, kept, other = tie((copies, middle_came, reply_back, kept, other))
    totals = exchange(copies)

    reply_far = gather_far(reply_back)
    grad_input = input_grads(kept, other, tokens, gain_attn, grad_hidden1, low_bit)
    reply_far, rest_sent, grad_input = tie((reply_far, in_sent[2], grad_input))
    rest_came = swap(rest_sent, 2)
    in_came = jnp.concatenate([fore_came, middle_came, rest_came], 0)
    grad_w_in = pair(2, slice(0, width)) + in_came.astype(F32)
    output = output_rows(hidden1, gate, flat_column, back_ids, gather_near(reply_far))
    if large % 16 == 0:
        grad_qkv_t, grad_proj, grad_gain_ffn, rel_row, grad_gain_attn, grad_router = final_weights(
            totals, large, inner_here, experts
        )
    else:
        shared = totals[:, :large].reshape(-1, width).astype(F32)
        grad_qkv_t, grad_proj = shared[: 3 * inner_here], shared[3 * inner_here :]
        small = jnp.sum(totals[:, large:].astype(F32), 0)
        grad_gain_ffn, rel_row, grad_gain_attn = small[0], small[1], small[2]
        grad_router = small[3 : 3 + experts]
    grad_qkv = jnp.swapaxes(grad_qkv_t.reshape(3, inner_here, width), 1, 2)
    grad_gain_ffn, grad_gain_attn = grad_gain_ffn.reshape(-1), grad_gain_attn.reshape(-1)
    grad_rel = rel_row.reshape(-1)[: rel_bias.size].reshape(rel_bias.shape)
    grad_router = grad_router.T
    return (
        output,
        grad_input,
        grad_gain_attn,
        grad_qkv,
        grad_proj,
        grad_rel,
        grad_gain_ffn,
        grad_router,
        grad_w_in[None],
        grad_w_out[None],
    )


def solution(mesh):
    placed = (
        P("expert", None),
        P(),
        P(None, None, "tensor"),
        P("tensor", None),
        P("tensor", None),
        P(),
        P(),
        P("expert", None, "tensor"),
        P("expert", "tensor", None),
        P("expert", None),
        P("expert", None),
        P("expert", None),
    )
    return jax.shard_map(
        shards,
        mesh=mesh,
        in_specs=placed,
        out_specs=(
            P("expert", None),
            P("expert", None),
            P(),
            P(None, None, "tensor"),
            P("tensor", None),
            P("tensor", None),
            P(),
            P(),
            P("expert", None, "tensor"),
            P("expert", "tensor", None),
        ),
        check_vma=False,
    )
```

```python
import functools

import jax
import jax.numpy as jnp
from jax import lax
from jax.experimental import pallas as pl
from jax.experimental.pallas import tpu as pltpu
from jax.sharding import PartitionSpec as P

FAR_LIMITS = (12, 16, 23, 32, 46, 64, 91)
HIGH = lax.Precision.HIGHEST
F32 = jnp.float32
BF16 = jnp.bfloat16
MASKED = -1e30
QB = 256
RB = 512
PAD = 256
FAR = FAR_LIMITS[-1]
SMALL = pl.CostEstimate(flops=1 << 20, bytes_accessed=1 << 16, transcendentals=0)

STEPS = (
    [(1 - limit, 14 - i) for i, limit in enumerate(reversed(FAR_LIMITS))]
    + [(-n, n) for n in range(7, -1, -1)]
    + [(n, 16 + n) for n in range(1, 8)]
    + [(8, 24)]
    + [(limit, 25 + i) for i, limit in enumerate(FAR_LIMITS)]
)


def norm_rows(values, gain):
    return values * lax.rsqrt(jnp.mean(values * values, -1, keepdims=True) + 1e-06) * gain


def nt_dot(left, right):
    return lax.dot_general(left, right, (((1,), (1,)), ((), ())), preferred_element_type=F32)


def nn_dot(left, right):
    return jnp.dot(left, right, preferred_element_type=F32)


def strip_shape(length):
    return 2 * length - QB


def near_rows(length):
    base = length - QB
    first = (base - FAR) // 32 * 32
    last = -(-(base + 127 + FAR) // 32) * 32
    return base, first, last


def build_strip(strip_ref, bias_ref, length, heads):
    total = strip_shape(length)
    base, first, last = near_rows(length)
    for h in range(heads):
        low = jnp.full((8, 128), bias_ref[h, 15], F32)
        high = jnp.full((8, 128), bias_ref[h, 31], F32)
        for half in range(QB // 128):
            cols = slice(half * 128, half * 128 + 128)
            lo_end, hi_start = first + half * 128, last + half * 128
            strip_ref[h, 0:lo_end, cols] = jnp.broadcast_to(low[:1], (lo_end, 128))
            strip_ref[h, hi_start:total, cols] = jnp.broadcast_to(high[:1], (total - hi_start, 128))
    for start in range(first, last, 32):
        offset = (
            lax.broadcasted_iota(jnp.int32, (32, 128), 0)
            - lax.broadcasted_iota(jnp.int32, (32, 128), 1)
            + (start - base)
        )
        tiles = [jnp.full((32, 128), bias_ref[h, 15], F32) for h in range(heads)]
        for begin, bucket in STEPS:
            reached = offset >= begin
            tiles = [jnp.where(reached, bias_ref[h, bucket], tiles[h]) for h in range(heads)]
        for h in range(heads):
            for half in range(QB // 128):
                at = start + half * 128
                strip_ref[h, at : at + 32, half * 128 : half * 128 + 128] = tiles[h]


def head_lanes(rows, h, dim, keep_tail, heads):
    lane = lax.broadcasted_iota(jnp.int32, (rows, PAD), 1)
    inside = (lane >= h * dim) & (lane < (h + 1) * dim)
    if keep_tail:
        inside = inside | (lane >= heads * dim)
    return inside


def shares(seg_ref, b, j):
    return (seg_ref[0, j * QB] <= seg_ref[0, b * QB + QB - 1]) & (
        seg_ref[0, b * QB] <= seg_ref[0, j * QB + QB - 1]
    )


def attend_kernel(
    length, heads, dim,
    x_ref, gain_ref, w_ref, doc_ref, bias_ref, seg_ref,
    att_ref, lse_ref, proj_ref, kt_ref, normed_ref,
    kh_ref, strip_ref, vt_ref, pad_ref, score_ref, top_ref, sum_ref, out_ref,
):
    inner = heads * dim
    build_strip(strip_ref, bias_ref, length, heads)
    lane = lax.broadcasted_iota(jnp.int32, (QB, PAD), 1) - inner
    pad_ref[...] = jnp.zeros_like(pad_ref)
    for t in range(3):
        pad_ref[t * PAD : t * PAD + inner, :] = w_ref[t]

    def project(b, carry):
        at = pl.multiple_of(b * QB, QB)
        here = x_ref[pl.ds(at, QB), :].astype(F32)
        normed = norm_rows(here, gain_ref[...]).astype(BF16)
        normed_ref[pl.ds(at, QB), :] = normed
        every = nt_dot(normed, pad_ref[...])
        same = doc_ref[pl.ds(at, QB), :] == lane
        queries = (every[:, 0:PAD].astype(BF16) * jnp.bfloat16(dim ** (-0.5))).astype(F32)
        queries = queries + jnp.where((lane < 0) | same, 0.0, MASKED)
        keys = every[:, PAD : 2 * PAD]
        values = every[:, 2 * PAD : 3 * PAD]
        proj_ref[pl.ds(at, QB), 0:PAD] = queries.astype(BF16)
        proj_ref[pl.ds(at, QB), PAD : 2 * PAD] = (keys + jnp.where(same, 1.0, 0.0)).astype(BF16)
        proj_ref[pl.ds(at, QB), 2 * PAD : 3 * PAD] = values.astype(BF16)
        kt_ref[:, pl.ds(at, QB)] = keys.T[:inner].astype(BF16)
        vt_ref[:, pl.ds(at, QB)] = values.T[:inner].astype(BF16)
        return carry

    lax.fori_loop(0, length // QB, project, 0)
    keys = proj_ref[:, PAD : 2 * PAD]
    for h in range(heads):
        kh_ref[h] = jnp.where(head_lanes(length, h, dim, True, heads), keys, jnp.zeros_like(keys))

    def block(b, carry):
        at = pl.multiple_of(b * QB, QB)
        queries = proj_ref[pl.ds(at, QB), 0:PAD]
        top_ref[...] = jnp.full_like(top_ref, -3e38)
        sum_ref[...] = jnp.zeros_like(sum_ref)
        out_ref[...] = jnp.zeros_like(out_ref)

        def score(j, carry):
            @pl.when(shares(seg_ref, b, j))
            def _():
                rows = pl.ds(pl.multiple_of(j * QB, QB), QB)
                bias = pl.ds(pl.multiple_of(length - QB + (j - b) * QB, QB), QB)
                for h in range(heads):
                    scores = nt_dot(kh_ref[h, rows, :], queries) + strip_ref[h, bias, :]
                    score_ref[h, rows, :] = scores
                    top = jnp.max(scores, 0, keepdims=True)
                    top_ref[h : h + 1, :] = jnp.maximum(top_ref[h : h + 1, :], top)

            return carry

        def spread(j, carry):
            @pl.when(shares(seg_ref, b, j))
            def _():
                rows = pl.ds(pl.multiple_of(j * QB, QB), QB)
                for h in range(heads):
                    probs = jnp.exp(score_ref[h, rows, :] - top_ref[h : h + 1, :])
                    sum_ref[h : h + 1, :] += jnp.sum(probs, 0, keepdims=True)
                    mine = slice(h * dim, (h + 1) * dim)
                    out_ref[mine, :] += nn_dot(vt_ref[mine, rows], probs.astype(BF16))

            return carry

        lax.fori_loop(0, length // QB, score, 0)
        lax.fori_loop(0, length // QB, spread, 0)
        for h in range(heads):
            mine = slice(h * dim, (h + 1) * dim)
            total = sum_ref[h : h + 1, :]
            att_ref[mine, pl.ds(at, QB)] = (out_ref[mine, :] / total).astype(BF16)
            lse_ref[h : h + 1, pl.ds(at, QB)] = top_ref[h : h + 1, :] + jnp.log(total)
        return carry

    lax.fori_loop(0, length // QB, block, 0)


def attend_back_kernel(
    length, heads, dim,
    proj_ref, kt_ref, lse_ref, da_ref, normed_ref, w_ref, gproj_ref, bias_ref, low_ref, seg_ref,
    grad_ref, kept_ref, sent_ref, drel_ref,
    kh_ref, vh_ref, strip_ref, dstrip_ref, pcat_ref, dcat_ref, dacat_ref, qcat_ref, dk_ref, dv_ref, dqt_ref,
    dq_ref, pad_ref, probs_ref, weighted_ref, delta_ref,
):
    inner = heads * dim
    scale = dim ** (-0.5)
    total = strip_shape(length)
    base, first, last = near_rows(length)
    build_strip(strip_ref, bias_ref, length, heads)
    dstrip_ref[...] = jnp.zeros_like(dstrip_ref)
    dk_ref[...] = jnp.zeros_like(dk_ref)
    dv_ref[...] = jnp.zeros_like(dv_ref)
    dqt_ref[...] = jnp.zeros_like(dqt_ref)
    keys = proj_ref[:, PAD : 2 * PAD]
    values = proj_ref[:, 2 * PAD : 3 * PAD]
    for h in range(heads):
        kh_ref[h] = jnp.where(head_lanes(length, h, dim, True, heads), keys, jnp.zeros_like(keys))
        vh_ref[h] = jnp.where(head_lanes(length, h, dim, False, heads), values, jnp.zeros_like(values))

    def block(b, carry):
        at = pl.multiple_of(b * QB, QB)
        queries = proj_ref[pl.ds(at, QB), 0:PAD]
        grads = da_ref[pl.ds(at, QB), :]
        delta_ref[...] = jnp.zeros_like(delta_ref)
        dqt_ref[...] = jnp.zeros_like(dqt_ref)
        for h in range(heads):
            mine = head_lanes(QB, h, dim, False, heads)
            cols = slice(h * QB, (h + 1) * QB)
            qcat_ref[cols, :] = jnp.where(mine, queries, jnp.zeros_like(queries))
            dacat_ref[cols, :] = jnp.where(mine, grads, jnp.zeros_like(grads))

        def weigh(j, carry):
            @pl.when(shares(seg_ref, b, j))
            def _():
                rows = pl.ds(pl.multiple_of(j * QB, QB), QB)
                bias = pl.ds(pl.multiple_of(length - QB + (j - b) * QB, QB), QB)
                for h in range(heads):
                    scores = nt_dot(kh_ref[h, rows, :], queries) + strip_ref[h, bias, :]
                    probs = jnp.exp(scores - lse_ref[h : h + 1, pl.ds(at, QB)])
                    weighted = probs * nt_dot(vh_ref[h, rows, :], grads)
                    delta_ref[h : h + 1, :] += jnp.sum(weighted, 0, keepdims=True)
                    probs_ref[h, rows, :] = probs
                    weighted_ref[h, rows, :] = weighted

            return carry

        def gather(j, carry):
            @pl.when(shares(seg_ref, b, j))
            def _():
                rows = pl.ds(pl.multiple_of(j * QB, QB), QB)
                bias = pl.ds(pl.multiple_of(length - QB + (j - b) * QB, QB), QB)
                for h in range(heads):
                    cols = slice(h * QB, (h + 1) * QB)
                    mine = slice(h * dim, (h + 1) * dim)
                    probs = probs_ref[h, rows, :]
                    dscore = weighted_ref[h, rows, :] - probs * delta_ref[h : h + 1, :]
                    dstrip_ref[h, bias, :] += dscore
                    dlow = dscore.astype(BF16)
                    pcat_ref[:, cols] = probs.astype(BF16)
                    dcat_ref[:, cols] = dlow
                    dqt_ref[mine, :] += nn_dot(kt_ref[mine, rows], dlow)
                dk_ref[rows, :] += nn_dot(dcat_ref[...], qcat_ref[...])
                dv_ref[rows, :] += nn_dot(pcat_ref[...], dacat_ref[...])

            return carry

        lax.fori_loop(0, length // QB, weigh, 0)
        lax.fori_loop(0, length // QB, gather, 0)
        dq_ref[pl.ds(at, QB), :] = dqt_ref[...].T * scale
        return carry

    lax.fori_loop(0, length // QB, block, 0)

    for t, ref in enumerate((dq_ref, dk_ref, dv_ref)):
        turned = ref[...].T[:inner].astype(BF16)
        grad_ref[t * inner : (t + 1) * inner, :] = nn_dot(turned, normed_ref[...]).astype(BF16)

    grad_ref[3 * inner :, :] = gproj_ref[...]

    pad_ref[...] = jnp.zeros_like(pad_ref)
    for t in range(3):
        pad_ref[t, 0:inner, :] = w_ref[t]
    half = length // 2

    def part(start):
        total = jnp.zeros((QB, w_ref.shape[2]), F32)
        for t, ref in enumerate((dq_ref, dk_ref, dv_ref)):
            total = total + nn_dot(ref[pl.ds(start, QB), :].astype(BF16), pad_ref[t])
        return total

    for i in range(half // QB):
        rows = slice(i * QB, (i + 1) * QB)
        kept_ref[rows, :] = part(pl.multiple_of(low_ref[0] * half + i * QB, QB))
        sent_ref[rows, :] = part(pl.multiple_of((1 - low_ref[0]) * half + i * QB, QB)).astype(BF16)

    offset = (
        lax.broadcasted_iota(jnp.int32, (last - first, 128), 0)
        - lax.broadcasted_iota(jnp.int32, (last - first, 128), 1)
        + (first - base)
    )
    begins = [-(1 << 20)] + [begin for begin, bucket in STEPS] + [1 << 20]
    buckets = [15] + [bucket for begin, bucket in STEPS]
    for h in range(heads):
        near = jnp.zeros((last - first, 128), F32)
        low = jnp.zeros((1, 128), F32)
        high = jnp.zeros((1, 128), F32)
        for half in range(QB // 128):
            cols = slice(half * 128, half * 128 + 128)
            lo_end, hi_start = first + half * 128, last + half * 128
            near = near + dstrip_ref[h, lo_end:hi_start, cols]
            low = low + jnp.sum(dstrip_ref[h, 0:lo_end, cols], 0, keepdims=True)
            high = high + jnp.sum(dstrip_ref[h, hi_start:total, cols], 0, keepdims=True)
        drel_ref[h, 16:17, :] = jnp.zeros((1, 128), F32)
        for i, bucket in enumerate(buckets):
            inside = (offset >= begins[i]) & (offset < begins[i + 1])
            row = jnp.sum(jnp.where(inside, near, 0.0), 0, keepdims=True)
            if bucket == 15:
                row = row + low
            if bucket == 31:
                row = row + high
            drel_ref[h, bucket : bucket + 1, :] = row


def rows_of(count, columns):
    return pl.BlockSpec((count, columns), lambda i: (i, 0))


def whole_of(*shape):
    return pl.BlockSpec(shape, lambda i: (0,) * len(shape))


def whole_like(*arrays):
    return [whole_of(*array.shape) for array in arrays]


def attend(tokens, gain, w_qkv, segments, rel_bias):
    length, width = tokens.shape
    heads = rel_bias.shape[0]
    inner = w_qkv.shape[1]
    operands = (tokens, gain[None, :], w_qkv, segments.reshape(-1, 1))
    results = (
        jax.ShapeDtypeStruct((inner, length), BF16),
        jax.ShapeDtypeStruct((8, length), F32),
        jax.ShapeDtypeStruct((length, 3 * PAD), BF16),
        jax.ShapeDtypeStruct((inner, length), BF16),
        jax.ShapeDtypeStruct((length, width), BF16),
    )
    return pl.pallas_call(
        functools.partial(attend_kernel, length, heads, inner // heads),
        grid=(1,),
        out_shape=results,
        in_specs=whole_like(*operands) + [pl.BlockSpec(memory_space=pltpu.SMEM)] * 2,
        out_specs=tuple(whole_like(*results)),
        scratch_shapes=[
            pltpu.VMEM((heads, length, PAD), BF16),
            pltpu.VMEM((heads, strip_shape(length), QB), F32),
            pltpu.VMEM((inner, length), BF16),
            pltpu.VMEM((3 * PAD, width), BF16),
            pltpu.VMEM((heads, length, QB), F32),
            pltpu.VMEM((8, QB), F32),
            pltpu.VMEM((8, QB), F32),
            pltpu.VMEM((inner, QB), F32),
        ],
        compiler_params=pltpu.CompilerParams(vmem_limit_bytes=60 << 20),
        cost_estimate=SMALL,
    )(*operands, rel_bias, segments)


def attend_back(proj, kt, lse, da, normed, w_qkv, grad_proj, rel_bias, low_bit, segments):
    length, width = normed.shape
    heads, buckets = rel_bias.shape
    inner = w_qkv.shape[1]
    operands = (proj, kt, lse, da, normed, w_qkv, grad_proj)
    results = (
        jax.ShapeDtypeStruct((4 * inner, width), BF16),
        jax.ShapeDtypeStruct((length // 2, width), F32),
        jax.ShapeDtypeStruct((length // 2, width), BF16),
        jax.ShapeDtypeStruct((heads, buckets, 128), F32),
    )
    return pl.pallas_call(
        functools.partial(attend_back_kernel, length, heads, inner // heads),
        grid=(1,),
        out_shape=results,
        in_specs=whole_like(*operands) + [pl.BlockSpec(memory_space=pltpu.SMEM)] * 3,
        out_specs=tuple(whole_like(*results)),
        scratch_shapes=[
            pltpu.VMEM((heads, length, PAD), BF16),
            pltpu.VMEM((heads, length, PAD), BF16),
            pltpu.VMEM((heads, strip_shape(length), QB), F32),
            pltpu.VMEM((heads, strip_shape(length), QB), F32),
            pltpu.VMEM((QB, heads * QB), BF16),
            pltpu.VMEM((QB, heads * QB), BF16),
            pltpu.VMEM((heads * QB, PAD), BF16),
            pltpu.VMEM((heads * QB, PAD), BF16),
            pltpu.VMEM((length, PAD), F32),
            pltpu.VMEM((length, PAD), F32),
            pltpu.VMEM((PAD, QB), F32),
            pltpu.VMEM((length, PAD), F32),
            pltpu.VMEM((3, PAD, width), BF16),
            pltpu.VMEM((heads, length, QB), F32),
            pltpu.VMEM((heads, length, QB), F32),
            pltpu.VMEM((8, QB), F32),
        ],
        compiler_params=pltpu.CompilerParams(vmem_limit_bytes=60 << 20),
        cost_estimate=SMALL,
    )(*operands, rel_bias, low_bit, segments)


def gelu_pair(v):
    inner = 0.7978845608028654 * (v + 0.044715 * (v * v * v))
    bend = jnp.tanh(inner)
    half = 0.5 * (1.0 + bend)
    slope = half + 0.5 * v * (1.0 - bend * bend) * (0.7978845608028654 * (1.0 + 0.134145 * (v * v)))
    return v * half, slope


def expert_kernel(
    members, experts,
    rows_ref, cot_ref, router_ref, group_ref, *refs,
):
    first, second = refs[:members], refs[members : 2 * members]
    reply_ref, share_ref, act_ref, gpre_ref, grad_ref, grouter_ref = refs[2 * members :]
    rows = rows_ref[...]
    count = rows.shape[0]
    lane = lax.broadcasted_iota(jnp.int32, (count, 128), 1)
    logits = jnp.where(lane < experts, nn_dot(rows, router_ref[...]), MASKED)
    raised = jnp.exp(logits - jnp.max(logits, -1, keepdims=True))
    probs = raised / jnp.sum(raised, -1, keepdims=True)
    own = jnp.where(lane == group_ref[0], 1.0, 0.0)
    gate = jnp.sum(probs * own, -1, keepdims=True)
    cot = cot_ref[...].astype(F32)
    grads = (gate * cot).astype(BF16)
    grad_ref[...] = grads
    reply = jnp.zeros(rows.shape, F32)
    share = jnp.zeros(rows.shape, F32)
    for k in range(members):
        act, slope = gelu_pair(nn_dot(rows, first[k][...]))
        act = act.astype(BF16)
        act_ref[k] = act
        reply = reply + nn_dot(act, second[k][...])
        gpre = (nt_dot(grads, second[k][...]) * slope).astype(BF16)
        gpre_ref[k] = gpre
        share = share + nt_dot(gpre, first[k][...])
    reply = reply.astype(BF16)
    reply_ref[...] = reply
    gate_grad = jnp.sum(cot * reply.astype(F32), -1, keepdims=True)
    logit_grad = probs * (own - gate) * gate_grad
    share_ref[...] = (share + nt_dot(logit_grad.astype(BF16), router_ref[...])).astype(BF16)
    grouter_ref[...] = nn_dot(logit_grad.T.astype(BF16), rows)


def expert_step(rows, cot, experts, router, group, first, second):
    members = len(first)
    count, width = rows.shape
    hidden = first[0].shape[1]
    weights = (*first, *second)
    results = (
        jax.ShapeDtypeStruct((count, width), BF16),
        jax.ShapeDtypeStruct((count, width), BF16),
        jax.ShapeDtypeStruct((members, count, hidden), BF16),
        jax.ShapeDtypeStruct((members, count, hidden), BF16),
        jax.ShapeDtypeStruct((count, width), BF16),
        jax.ShapeDtypeStruct((128, width), F32),
    )
    return pl.pallas_call(
        functools.partial(expert_kernel, members, experts),
        grid=(1,),
        out_shape=results,
        in_specs=whole_like(rows, cot, router)
        + [pl.BlockSpec(memory_space=pltpu.SMEM)]
        + whole_like(*weights),
        out_specs=tuple(whole_like(*results)),
        compiler_params=pltpu.CompilerParams(vmem_limit_bytes=60 << 20),
        cost_estimate=SMALL,
    )(rows, cot, router, group, *weights)


def enter_kernel(
    members, experts,
    x_ref, gain_ref, router_ref, route_ref, flat_ref, ids_ref, *refs,
):
    att, proj = refs[:members], refs[members : 2 * members]
    hidden_ref, gate_ref, leave_ref, total_ref = refs[2 * members :]
    step = pl.program_id(0)
    hidden = x_ref[...].astype(F32)
    for k in range(members):
        hidden = hidden + lax.dot_general(
            att[k][...], proj[k][...], (((0,), (0,)), ((), ())), preferred_element_type=F32
        )
    hidden_ref[...] = hidden
    normed = norm_rows(hidden, gain_ref[...]).astype(BF16)
    lane = lax.broadcasted_iota(jnp.int32, (RB, 128), 1)
    logits = jnp.where(lane < experts, nn_dot(normed, router_ref[...]), MASKED)
    raised = jnp.exp(logits - jnp.max(logits, -1, keepdims=True))
    chosen = jnp.sum(jnp.where(lane == route_ref[...], raised, 0.0), -1, keepdims=True)
    gate_ref[...] = chosen / jnp.sum(raised, -1, keepdims=True)
    table = jnp.where(ids_ref[...] == flat_ref[...], 1.0, 0.0).astype(BF16)

    @pl.when(step == 0)
    def _():
        total_ref[...] = jnp.zeros_like(total_ref)

    total_ref[...] += nn_dot(table, normed)

    @pl.when(step == pl.num_programs(0) - 1)
    def _():
        leave_ref[...] = total_ref[...].astype(BF16)


def enter_experts(tokens, experts, gain, router, route, flat_id, ids, att, proj):
    length, width = tokens.shape
    members = len(att)
    inner = att[0].shape[0]
    count = ids.shape[0]
    return pl.pallas_call(
        functools.partial(enter_kernel, members, experts),
        grid=(length // RB,),
        out_shape=(
            jax.ShapeDtypeStruct((length, width), F32),
            jax.ShapeDtypeStruct((length, 1), F32),
            jax.ShapeDtypeStruct((count, width), BF16),
        ),
        in_specs=[
            rows_of(RB, width),
            whole_of(1, width),
            whole_of(width, 128),
            rows_of(RB, 1),
            pl.BlockSpec((1, RB), lambda i: (0, i)),
            whole_of(count, 1),
        ]
        + [pl.BlockSpec((inner, RB), lambda i: (0, i))] * members
        + [whole_of(inner, width)] * members,
        out_specs=(rows_of(RB, width), rows_of(RB, 1), whole_of(count, width)),
        scratch_shapes=[pltpu.VMEM((count, width), F32)],
        compiler_params=pltpu.CompilerParams(vmem_limit_bytes=60 << 20),
        cost_estimate=SMALL,
    )(
        tokens, gain, router, route, flat_id, ids, *att, *proj,
    )


def weight_kernel(half, rows_ref, grads_ref, act_ref, gpre_ref, kept_ref, sent_ref):
    step = pl.program_id(0)

    def product(left, right):
        return lax.dot_general(
            left, right, (((0,), (0,)), ((), ())), preferred_element_type=F32
        ).astype(BF16)

    @pl.when(step < half)
    def _():
        k = 2 * step
        kept_ref[0] = product(act_ref[k], grads_ref[...])
        sent_ref[0] = product(act_ref[k + 1], grads_ref[...])

    @pl.when(step >= half)
    def _():
        k = 2 * (step - half)
        kept_ref[0] = product(rows_ref[...], gpre_ref[k])
        sent_ref[0] = product(rows_ref[...], gpre_ref[k + 1])


def weight_grads(rows, grads, act, gpre):
    members, count, hidden = act.shape
    width = rows.shape[1]
    assert hidden == width
    one = pl.BlockSpec((1, width, width), lambda i: (i, 0, 0))
    return pl.pallas_call(
        functools.partial(weight_kernel, members // 2),
        grid=(members,),
        out_shape=(
            jax.ShapeDtypeStruct((members, width, width), BF16),
            jax.ShapeDtypeStruct((members, width, width), BF16),
        ),
        in_specs=[whole_of(count, width)] * 2 + [whole_of(members, count, hidden)] * 2,
        out_specs=(one, one),
        compiler_params=pltpu.CompilerParams(vmem_limit_bytes=60 << 20),
        cost_estimate=SMALL,
    )(rows, grads, act, gpre)


def leave_kernel(
    members,
    hidden_ref, cot_ref, gain_ref, flat_ref, ids_ref, wproj_ref, att_ref, *refs,
):
    blocks = refs[:members]
    gh_ref, da_ref, ggain_ref, gproj_ref, total_ref = refs[members:]
    step = pl.program_id(0)
    share = blocks[0].shape[0]
    grad = jnp.zeros(hidden_ref.shape, F32)
    for k in range(members):
        hit = flat_ref[...] == ids_ref[:, k * share : (k + 1) * share]
        grad = grad + nn_dot(jnp.where(hit, 1.0, 0.0).astype(BF16), blocks[k][...])
    hidden = hidden_ref[...]
    inverse = lax.rsqrt(jnp.mean(hidden * hidden, -1, keepdims=True) + 1e-06)
    unit = hidden * inverse
    scaled = gain_ref[...] * grad
    back = inverse * (scaled - unit * jnp.mean(unit * scaled, -1, keepdims=True))
    total = cot_ref[...].astype(F32) + back
    gh_ref[...] = total
    low = total.astype(BF16)
    da_ref[...] = nt_dot(low, wproj_ref[...]).astype(BF16)

    @pl.when(step == 0)
    def _():
        ggain_ref[...] = jnp.zeros_like(ggain_ref)
        total_ref[...] = jnp.zeros_like(total_ref)

    ggain_ref[...] += jnp.sum(grad * unit, 0, keepdims=True)
    total_ref[...] += nn_dot(att_ref[...], low)

    @pl.when(step == pl.num_programs(0) - 1)
    def _():
        gproj_ref[...] = total_ref[...].astype(BF16)


def leave_experts(hidden1, cotangent, gain, flat_id, ids, w_proj, attended_t, blocks):
    length, width = hidden1.shape
    inner = attended_t.shape[0]
    members = len(blocks)
    share = blocks[0].shape[0]
    return pl.pallas_call(
        functools.partial(leave_kernel, members),
        grid=(length // RB,),
        out_shape=(
            jax.ShapeDtypeStruct((length, width), F32),
            jax.ShapeDtypeStruct((length, PAD), BF16),
            jax.ShapeDtypeStruct((1, width), F32),
            jax.ShapeDtypeStruct((inner, width), BF16),
        ),
        in_specs=[
            rows_of(RB, width),
            rows_of(RB, width),
            whole_of(1, width),
            rows_of(RB, 1),
            whole_of(1, members * share),
            whole_of(PAD, width),
            pl.BlockSpec((inner, RB), lambda i: (0, i)),
        ]
        + [whole_of(share, width)] * members,
        out_specs=(
            rows_of(RB, width),
            rows_of(RB, PAD),
            whole_of(1, width),
            whole_of(inner, width),
        ),
        scratch_shapes=[pltpu.VMEM((inner, width), F32)],
        compiler_params=pltpu.CompilerParams(vmem_limit_bytes=60 << 20),
        cost_estimate=SMALL,
    )(
        hidden1, cotangent, gain, flat_id, ids, w_proj, attended_t, *blocks,
    )


def output_kernel(members, hidden_ref, gate_ref, flat_ref, ids_ref, *refs):
    blocks, out_ref = refs[:members], refs[members]
    share = blocks[0].shape[0]
    reply = jnp.zeros(hidden_ref.shape, F32)
    for k in range(members):
        hit = flat_ref[...] == ids_ref[:, k * share : (k + 1) * share]
        reply = reply + nn_dot(jnp.where(hit, 1.0, 0.0).astype(BF16), blocks[k][...])
    out_ref[...] = (hidden_ref[...] + gate_ref[...] * reply).astype(BF16)


def output_rows(hidden1, gate, flat_id, ids, blocks):
    length, width = hidden1.shape
    members = len(blocks)
    share = blocks[0].shape[0]
    return pl.pallas_call(
        functools.partial(output_kernel, members),
        grid=(length // RB,),
        out_shape=jax.ShapeDtypeStruct((length, width), BF16),
        in_specs=[rows_of(RB, width), rows_of(RB, 1), rows_of(RB, 1), whole_of(1, members * share)]
        + [whole_of(share, width)] * members,
        out_specs=rows_of(RB, width),
        compiler_params=pltpu.CompilerParams(vmem_limit_bytes=60 << 20),
        cost_estimate=SMALL,
    )(hidden1, gate, flat_id, ids, *blocks)


def chosen_half(halves, kept_ref, other_ref, low_ref):
    mine = pl.program_id(0) // halves == low_ref[0]
    return jnp.where(mine, kept_ref[...].astype(F32), other_ref[...].astype(F32))


def gain_kernel(halves, kept_ref, other_ref, x_ref, low_ref, ggain_ref):
    part = chosen_half(halves, kept_ref, other_ref, low_ref)
    x = x_ref[...].astype(F32)
    inverse = lax.rsqrt(jnp.mean(x * x, -1, keepdims=True) + 1e-06)

    @pl.when(pl.program_id(0) == 0)
    def _():
        ggain_ref[...] = jnp.zeros_like(ggain_ref)

    ggain_ref[...] += jnp.sum(part * (x * inverse), 0, keepdims=True)


def input_kernel(halves, kept_ref, other_ref, x_ref, gain_ref, gh_ref, low_ref, out_ref):
    part = chosen_half(halves, kept_ref, other_ref, low_ref)
    x = x_ref[...].astype(F32)
    inverse = lax.rsqrt(jnp.mean(x * x, -1, keepdims=True) + 1e-06)
    unit = x * inverse
    scaled = gain_ref[...] * part
    out_ref[...] = gh_ref[...] + inverse * (scaled - unit * jnp.mean(unit * scaled, -1, keepdims=True))


def gain_grads(kept, other, tokens, low_bit):
    length, width = tokens.shape
    halves = kept.shape[0] // QB
    half = pl.BlockSpec((QB, width), lambda i: (i % halves, 0))
    return pl.pallas_call(
        functools.partial(gain_kernel, halves),
        grid=(length // QB,),
        out_shape=jax.ShapeDtypeStruct((1, width), F32),
        in_specs=[half, half, rows_of(QB, width), pl.BlockSpec(memory_space=pltpu.SMEM)],
        out_specs=whole_of(1, width),
        compiler_params=pltpu.CompilerParams(vmem_limit_bytes=60 << 20),
        cost_estimate=SMALL,
    )(kept, other, tokens, low_bit)


def input_grads(kept, other, tokens, gain, grad_hidden1, low_bit):
    length, width = tokens.shape
    halves = kept.shape[0] // QB
    half = pl.BlockSpec((QB, width), lambda i: (i % halves, 0))
    return pl.pallas_call(
        functools.partial(input_kernel, halves),
        grid=(length // QB,),
        out_shape=jax.ShapeDtypeStruct((length, width), F32),
        in_specs=[
            half,
            half,
            rows_of(QB, width),
            whole_of(1, width),
            rows_of(QB, width),
            pl.BlockSpec(memory_space=pltpu.SMEM),
        ],
        out_specs=rows_of(QB, width),
        compiler_params=pltpu.CompilerParams(vmem_limit_bytes=60 << 20),
        cost_estimate=SMALL,
    )(kept, other, tokens, gain[None, :], grad_hidden1, low_bit)


def copies_kernel(came_ref, small_ref, ggain_ref, out_ref, mine_ref):
    groups, large = came_ref.shape[:2]

    @pl.when(pl.program_id(0) == 0)
    def _():
        total = came_ref[0].astype(F32)
        for g in range(1, groups):
            total = total + came_ref[g].astype(F32)
        mine_ref[:large, :] = total.astype(BF16)
        row = lax.broadcasted_iota(jnp.int32, small_ref.shape, 0)
        mine_ref[large:, :] = (small_ref[...] + jnp.where(row == 2, ggain_ref[...], 0.0)).astype(BF16)

    out_ref[0] = mine_ref[...]


def sum_copies(came, small, ggain):
    groups, large, width = came.shape
    count = large + small.shape[0]
    return pl.pallas_call(
        copies_kernel,
        grid=(groups,),
        out_shape=jax.ShapeDtypeStruct((groups, count, width), BF16),
        in_specs=whole_like(came, small, ggain),
        out_specs=pl.BlockSpec((1, count, width), lambda i: (i, 0, 0)),
        scratch_shapes=[pltpu.VMEM((count, width), BF16)],
        compiler_params=pltpu.CompilerParams(vmem_limit_bytes=60 << 20),
        cost_estimate=SMALL,
    )(came, small, ggain)


def final_kernel(large, inner, totals_ref, qkv_ref, proj_ref, gffn_ref, rel_ref, gattn_ref, router_ref):
    groups = totals_ref.shape[0]
    split = 3 * inner
    small = totals_ref[0, large:, :].astype(F32)
    for g in range(groups):
        start, stop = g * large, (g + 1) * large
        if start < split:
            count = min(stop, split) - start
            qkv_ref[start : start + count, :] = totals_ref[g, :count, :].astype(F32)
        if stop > split:
            skip = max(start, split) - start
            proj_ref[start + skip - split : stop - split, :] = totals_ref[g, skip:large, :].astype(F32)
        if g:
            small = small + totals_ref[g, large:, :].astype(F32)
    gffn_ref[...] = small[0:1]
    rel_ref[...] = small[1:2]
    gattn_ref[...] = small[2:3]
    router_ref[...] = small[3 : 3 + router_ref.shape[0]]


def final_weights(totals, large, inner, experts):
    groups, count, width = totals.shape
    results = (
        jax.ShapeDtypeStruct((3 * inner, width), F32),
        jax.ShapeDtypeStruct((inner, width), F32),
        jax.ShapeDtypeStruct((1, width), F32),
        jax.ShapeDtypeStruct((1, width), F32),
        jax.ShapeDtypeStruct((1, width), F32),
        jax.ShapeDtypeStruct((experts, width), F32),
    )
    return pl.pallas_call(
        functools.partial(final_kernel, large, inner),
        grid=(1,),
        out_shape=results,
        in_specs=whole_like(totals),
        out_specs=tuple(whole_like(*results)),
        compiler_params=pltpu.CompilerParams(vmem_limit_bytes=16 << 20),
        cost_estimate=SMALL,
    )(totals)


def shards(
    tokens,
    gain_attn,
    w_qkv,
    w_proj,
    rel_bias,
    gain_ffn,
    w_router,
    w_in,
    w_out,
    routes,
    segment_ids,
    cotangent,
):
    length, width = tokens.shape
    experts = w_router.shape[1]
    capacity = max(2, 3 * length // (2 * experts))
    inner_here = w_proj.shape[0]
    members = lax.axis_size("tensor")
    groups = lax.axis_size("expert")
    member = lax.axis_index("tensor")
    group = lax.axis_index("expert")
    share = capacity // members
    route = routes[:, 0]

    def swap(value, bit):
        return lax.ppermute(value, "tensor", [(i, i ^ bit) for i in range(members)])

    bits = [1 << i for i in range(members.bit_length() - 1)]

    def gather_far(value):
        blocks = {0: value}
        for bit in reversed(bits[1:]):
            blocks.update({k ^ bit: swap(block, bit) for k, block in blocks.items()})
        return blocks

    def gather_near(blocks):
        blocks = dict(blocks)
        for bit in bits[:1]:
            blocks.update({k ^ bit: swap(block, bit) for k, block in blocks.items()})
        return [blocks[k] for k in range(members)]

    def gather_members(value):
        return gather_near(gather_far(value))

    def gather_groups(value):
        copies = jnp.broadcast_to(value[None], (groups,) + value.shape)
        return exchange(copies)

    def exchange(value):
        return lax.all_to_all(value, "expert", split_axis=0, concat_axis=0, tiled=True)

    tie = lax.optimization_barrier

    expert_ids = jnp.arange(experts, dtype=jnp.int32)
    onehot_low = (route[:, None] == expert_ids[None, :]).astype(BF16)
    onehot = onehot_low.astype(F32)
    positions = jnp.arange(length, dtype=jnp.int32)
    lower_ones = (positions[:, None] >= positions[None, :]).astype(BF16)
    running = nn_dot(lower_ones, onehot_low)
    slot = (jnp.sum(running * onehot, 1) - 1.0).astype(jnp.int32)
    flat_id = route * capacity + slot

    def ids_of(owner):
        slots = owner * share + jnp.arange(share, dtype=jnp.int32)
        return (expert_ids[:, None] * capacity + slots[None, :]).reshape(-1)

    send_table = (ids_of(member)[:, None] == flat_id[None, :]).astype(BF16)
    all_ids = jnp.concatenate([ids_of(member ^ k) for k in range(members)])

    def dispatch(rows):
        out = nn_dot(send_table, rows).astype(BF16).reshape(groups, -1, width)
        return exchange(out).reshape(-1, width)

    cot_share = dispatch(cotangent)
    w_proj_far = gather_far(w_proj)
    w_in_far = gather_far(w_in[0])
    w_qkv_t = jnp.swapaxes(w_qkv, 1, 2)
    attended_t, lse, proj, keys_t, normed1 = attend(tokens, gain_attn, w_qkv_t, segment_ids, rel_bias)
    attended_t, w_in_far, cot_share = tie((attended_t, w_in_far, cot_share))

    attended_far = gather_far(attended_t)
    gain_row = gain_ffn[None, :]
    router = jnp.pad(w_router, ((0, 0), (0, 128 - experts)))
    w_proj_pad = jnp.pad(w_proj, ((0, PAD - inner_here), (0, 0)))
    flat_row, flat_column = flat_id[None, :], flat_id[:, None]
    send_ids, back_ids = ids_of(member)[:, None], all_ids[None, :]
    (
        attended_far, w_proj_far, w_out_here, gain_row, router, w_proj_pad,
        flat_row, flat_column, send_ids, back_ids,
    ) = tie((
        attended_far, w_proj_far, w_out[0], gain_row, router, w_proj_pad,
        flat_row, flat_column, send_ids, back_ids,
    ))
    attended_blocks = gather_near(attended_far)
    w_proj_blocks = gather_near(w_proj_far)
    w_in_all = gather_near(w_in_far)
    w_out_far = gather_far(w_out_here)
    hidden1, gate, leaving = enter_experts(
        tokens, experts, gain_row, router, routes, flat_row, send_ids, attended_blocks, w_proj_blocks
    )
    rows = exchange(leaving.reshape(groups, -1, width)).reshape(-1, width)
    rows, w_out_far, w_in_all = tie((rows, w_out_far, w_in_all))
    w_out_all = gather_near(w_out_far)

    reply, grad_share, act, grad_pre, grad_rows, grad_router = expert_step(
        rows, cot_share, experts, router, group[None], w_in_all, w_out_all
    )
    grad_back = exchange(grad_share.reshape(groups, -1, width)).reshape(-1, width)
    grad_router = grad_router[:experts]
    for bit in bits:
        grad_router = grad_router + swap(grad_router, bit)
    kept_weights, sent_weights = weight_grads(rows, grad_rows, act, grad_pre)
    grad_back, reply, kept_weights, sent_weights, grad_router = tie(
        (grad_back, reply, kept_weights, sent_weights, grad_router)
    )
    near_weights = swap(sent_weights, 1)
    grad_far = gather_far(grad_back)
    third = width // 3

    def pair(k, rows_cut):
        return kept_weights[k, rows_cut].astype(F32) + near_weights[k, rows_cut].astype(F32)

    out_sent = pair(1, slice(0, width)).astype(BF16)
    in_sent = [pair(3, slice(i * third, (i + 1) * third)).astype(BF16) for i in range(3)]
    grad_far, out_sent, in_sent = tie((grad_far, out_sent, in_sent))
    out_came, fore_came = swap(out_sent, 2), swap(in_sent[0], 2)
    grad_blocks = gather_near(grad_far)
    reply_back = exchange(reply.reshape(groups, -1, width)).reshape(-1, width)
    grad_hidden1, attended_grad, grad_gain_ffn, grad_proj = leave_experts(
        hidden1, cotangent, gain_row, flat_column, back_ids, w_proj_pad, attended_t, grad_blocks
    )

    low_bit = (member & 1)[None]
    grads, kept, sent, rel_parts = attend_back(
        proj, keys_t, lse, attended_grad, normed1, w_qkv_t, grad_proj, rel_bias, low_bit, segment_ids
    )
    grads, kept, sent, reply_back, out_came, fore_came, in_sent = tie(
        (grads, kept, sent, reply_back, out_came, fore_came, in_sent)
    )
    kept = kept + swap(sent, 1).astype(F32)
    far = swap(kept.astype(BF16), 2)
    came = exchange(grads.reshape(groups, -1, width))
    grad_w_out = pair(0, slice(0, width)) + out_came.astype(F32)
    rel_row = jnp.sum(rel_parts, -1).reshape(1, -1)
    rel_row = jnp.pad(rel_row, ((0, 0), (0, width - rel_row.shape[1])))
    small = jnp.concatenate([grad_gain_ffn, rel_row, jnp.zeros((1, width), F32), grad_router], 0)
    small = jnp.pad(small, ((0, -small.shape[0] % 16), (0, 0)))
    far, grad_w_out, reply_back, in_sent, small = tie((far, grad_w_out, reply_back, in_sent, small))
    middle_came = swap(in_sent[1], 2)
    kept = (kept + far.astype(F32)).astype(BF16)
    other = swap(kept, 1)
    gain_part = gain_grads(kept, other, tokens, low_bit)

    large = came.shape[1]
    if large % 16 == 0:
        copies = sum_copies(came, small, gain_part)
    else:
        small = small.at[2].add(gain_part[0])
        copies = jnp.concatenate([jnp.sum(came.astype(F32), 0), small], 0).astype(BF16)
        copies = jnp.broadcast_to(copies[None], (groups,) + copies.shape)
    copies, middle_came, reply_back, kept, other = tie((copies, middle_came, reply_back, kept, other))
    totals = exchange(copies)

    reply_far = gather_far(reply_back)
    grad_input = input_grads(kept, other, tokens, gain_attn, grad_hidden1, low_bit)
    reply_far, rest_sent, grad_input = tie((reply_far, in_sent[2], grad_input))
    rest_came = swap(rest_sent, 2)
    output = output_rows(hidden1, gate, flat_column, back_ids, gather_near(reply_far))
    rest_came, output = tie((rest_came, output))
    in_came = jnp.concatenate([fore_came, middle_came, rest_came], 0)
    grad_w_in = pair(2, slice(0, width)) + in_came.astype(F32)
    if large % 16 == 0:
        grad_qkv_t, grad_proj, grad_gain_ffn, rel_row, grad_gain_attn, grad_router = final_weights(
            totals, large, inner_here, experts
        )
    else:
        shared = totals[:, :large].reshape(-1, width).astype(F32)
        grad_qkv_t, grad_proj = shared[: 3 * inner_here], shared[3 * inner_here :]
        small = jnp.sum(totals[:, large:].astype(F32), 0)
        grad_gain_ffn, rel_row, grad_gain_attn = small[0], small[1], small[2]
        grad_router = small[3 : 3 + experts]
    grad_qkv = jnp.swapaxes(grad_qkv_t.reshape(3, inner_here, width), 1, 2)
    grad_gain_ffn, grad_gain_attn = grad_gain_ffn.reshape(-1), grad_gain_attn.reshape(-1)
    grad_rel = rel_row.reshape(-1)[: rel_bias.size].reshape(rel_bias.shape)
    grad_router = grad_router.T
    return (
        output,
        grad_input,
        grad_gain_attn,
        grad_qkv,
        grad_proj,
        grad_rel,
        grad_gain_ffn,
        grad_router,
        grad_w_in[None],
        grad_w_out[None],
    )


def solution(mesh):
    placed = (
        P("expert", None),
        P(),
        P(None, None, "tensor"),
        P("tensor", None),
        P("tensor", None),
        P(),
        P(),
        P("expert", None, "tensor"),
        P("expert", "tensor", None),
        P("expert", None),
        P("expert", None),
        P("expert", None),
    )
    return jax.shard_map(
        shards,
        mesh=mesh,
        in_specs=placed,
        out_specs=(
            P("expert", None),
            P("expert", None),
            P(),
            P(None, None, "tensor"),
            P("tensor", None),
            P("tensor", None),
            P(),
            P(),
            P("expert", None, "tensor"),
            P("expert", "tensor", None),
        ),
        check_vma=False,
    )
```
